256 devices in a mesh: gx: 8 (over z), gy: 4 (over y), gz: 8 (over x, core).
Axes of the slice: x: 4, y: 4, z: 8, core: 2. Of those that a mesh axis runs over, the one named last changes fastest.
Arguments:
- populations: float32 [19, 32, 128, 1024], P(None, 'gx', 'gy', 'gz'), may hold values from 0.02 to 0.12
- solid: int32 [32, 128, 1024], P('gx', 'gy', 'gz'), may hold values 0 or 1
- link_cell: int32 [8, 4, 8, 1024], P('gx', 'gy', 'gz'), may hold values from 0 to 16383, as said below
- link_dir: int32 [8, 4, 8, 1024], P('gx', 'gy', 'gz'), may hold values from 1 to 18
- link_store: int32 [8, 4, 8, 1024], P('gx', 'gy', 'gz'), may hold values from 0 to 32768, as said below
- store_body: int32 [32768], replicated, may hold values from 0 to 7
- motion: float32 [8, 6], replicated, may hold values from -0.75 to 0.75
- inv_mass: float32 [8], replicated, may hold values from 1 to 8
- inv_inertia: float32 [8, 3], replicated, may hold values from 1 to 8
- centre: float32 [8, 3], replicated, may hold values from 0.2 to 0.8
- rates: float32 [15], replicated, may hold values from 0.5 to 1.9
Outputs:
- moved: float32 [19, 32, 128, 1024], P(None, 'gx', 'gy', 'gz')
- store_load: float32 [6, 32768], P(None, ('gx', 'gy', 'gz'))
- motion_next: float32 [8, 6], replicated
The draws below stay inside these ranges and needn't reach their ends.
Inputs may be any that keep to these rules, and one draw needn't show every extreme that they name: `link_cell`: within one device's list the cells are distinct, counted over its 4 x 32 x 128 block with the last dimension fastest. `link_store`: the value 32768 marks an empty slot; in each device's list the live slots come first, from a quarter of 1024 to all of them, and the first device's list is full.
All inputs are finite; a program needn't handle non-finite values. No bound on the sum of `solid` on one device may be relied on, other than what follows from the above.
Results may differ from the reference program's by a relative error of at most 0.0001.
Values sent between devices are 32-bit elements; how exact they have to be, the bound alone decides.
No kernel may reach another device: no remote copies, remote signals or barrier semaphores. Data moves between devices by JAX's collectives and lax.ppermute only.
A program may use at most 64 MiB of HBM per device.

```python
import math
import jax
import jax.numpy as jnp
import numpy as np
from jax import lax

CX = 4
CY = 32
CZ = 128
LINKS = 1024
NB = 8
MOMENTS = 15
NX = 32
NY = 128
NZ = 1024
STORES = 32768
AREA = 32768
N_GX = 8
N_GY = 4
N_GZ = 8


def draw_link_cell(key, part):
    key = jax.random.fold_in(key, 11)
    device_keys = jax.random.split(key, N_GX * N_GY * N_GZ)

    def one_device(device_key):
        return jax.random.permutation(device_key, CX * CY * CZ)[:LINKS]
    chosen = jax.vmap(one_device)(device_keys).astype(jnp.int32)
    return chosen.reshape(N_GX, N_GY, N_GZ, LINKS)


def draw_link_store(key, part):
    key = jax.random.fold_in(key, 23)
    count_key, store_key = jax.random.split(key)
    devices_all = N_GX * N_GY * N_GZ
    counts = jax.random.randint(count_key, (devices_all,), LINKS // 4, LINKS + 1).astype(jnp.int32)
    counts = counts.at[0].set(LINKS)
    stores = jax.random.randint(store_key, (devices_all, LINKS), 0, STORES).astype(jnp.int32)
    positions = jnp.arange(LINKS, dtype=jnp.int32)
    filled = jnp.where(positions[None, :] < counts[:, None], stores, STORES)
    return filled.astype(jnp.int32).reshape(N_GX, N_GY, N_GZ, LINKS)


def with_ends(values, rng, least, largest):
    spot = [jax.random.randint(jax.random.fold_in(rng, axis), (), 0, length) for axis, length in enumerate(values.shape)]
    longest = values.shape.index(max(values.shape))
    neighbour = spot[:longest] + [(spot[longest] + 1) % values.shape[longest]] + spot[longest + 1:]
    return values.at[tuple(spot)].set(least).at[tuple(neighbour)].set(largest)


def shard_levels(stream_key, extent, shards, low, top_value):
    level, own = 1.0, jax.random.fold_in(stream_key, 6)
    for dim, parts in shards:
        draws = jnp.exp(jax.random.uniform(jax.random.fold_in(own, dim), (parts,), jnp.float32, low / len(shards), top_value / len(shards)))
        level = level * jnp.repeat(draws, extent[dim] // parts).reshape([-1 if axis == dim else 1 for axis in range(len(extent))])
    return level


def centred(key, dims, width, most, held_as=jnp.bfloat16):
    entries = width * jax.random.normal(key, dims, jnp.float32)
    return jnp.clip(entries, min=-most, max=most).astype(held_as)


def setup_inputs(seed: int = 0) -> dict:
    key_of = jax.random.split(jax.random.key(seed), 12)
    populations = jnp.clip(0.02 + 0.09999999776482582 * jax.random.uniform(key_of[0], (19, NX, NY, NZ), jnp.float32) ** shard_levels(key_of[0], (19, NX, NY, NZ), ((1, 8), (2, 4), (3, 8)), -0.2, 0.2), 0.02, 0.12)
    solid = with_ends((jax.random.randint(key_of[1], (NX, NY, NZ), 0, 8) < 1).astype(jnp.int32), jax.random.fold_in(key_of[1], 1), 0, 1)
    link_cell = draw_link_cell(jax.random.fold_in(key_of[11], 71), 0)
    link_dir = with_ends(jax.random.randint(key_of[3], (N_GX, N_GY, N_GZ, LINKS), 1, 19), jax.random.fold_in(key_of[3], 1), 1, 18).astype(jnp.int32)
    link_store = draw_link_store(jax.random.fold_in(key_of[11], 71), 0)
    store_body = with_ends(jax.random.randint(key_of[5], (STORES,), 0, NB), jax.random.fold_in(key_of[5], 1), 0, NB - 1).astype(jnp.int32)
    motion = centred(key_of[6], (NB, 6), 0.05, 0.75, jnp.float32)
    inv_mass = jnp.clip(jnp.exp(jax.random.uniform(key_of[7], (NB,), jnp.float32, math.log(1.0), math.log(8.0))), 1.0, 8.0)
    inv_inertia = jnp.clip(jnp.exp(jax.random.uniform(key_of[8], (NB, 3), jnp.float32, math.log(1.0), math.log(8.0))), 1.0, 8.0)
    centre = jnp.clip(jax.random.uniform(key_of[9], (NB, 3), jnp.float32, 0.2, 0.8), 0.2, 0.8)
    rates = jnp.clip(jnp.exp(jax.random.uniform(key_of[10], (MOMENTS,), jnp.float32, math.log(0.5), math.log(1.9))), 0.5, 1.9)
    return dict(populations=populations, solid=solid, link_cell=link_cell, link_dir=link_dir, link_store=link_store, store_body=store_body, motion=motion, inv_mass=inv_mass, inv_inertia=inv_inertia, centre=centre, rates=rates)


def lattice_tables():
    speed_list = [[0, 0, 0], [1, 0, 0], [-1, 0, 0], [0, 1, 0], [0, -1, 0], [0, 0, 1], [0, 0, -1], [1, 1, 0], [-1, -1, 0], [1, -1, 0], [-1, 1, 0], [1, 0, 1], [-1, 0, -1], [1, 0, -1], [-1, 0, 1], [0, 1, 1], [0, -1, -1], [0, 1, -1], [0, -1, 1]]
    speeds = np.array(speed_list) * 1.0
    weights = np.array([1.0 / 3.0] + [1.0 / 18.0] * 6 + [1.0 / 36.0] * 12)
    along_x = speeds[:, 0]
    along_y = speeds[:, 1]
    along_z = speeds[:, 2]
    square = along_x * along_x + along_y * along_y + along_z * along_z
    polynomials = np.stack([np.ones(19), along_x, along_y, along_z, square, 3 * along_x * along_x - square, along_y * along_y - along_z * along_z, along_x * along_y, along_y * along_z, along_x * along_z, along_x * square, along_y * square, along_z * square, square * square, (3 * along_x * along_x - square) * square, (along_y * along_y - along_z * along_z) * square, along_x * (along_y * along_y - along_z * along_z), along_y * (along_z * along_z - along_x * along_x), along_z * (along_x * along_x - along_y * along_y)], axis=1)
    columns = []
    for column_index in range(19):
        vector = polynomials[:, column_index] * 1.0
        for repeat in range(2):
            for earlier in columns:
                vector = vector - np.dot(earlier, vector) * earlier
        columns.append(vector / math.sqrt(float(np.dot(vector, vector))))
    return (speeds, weights, np.stack(columns))

def collide(flat, rates):
    speeds, weights, moments = lattice_tables()
    highest = lax.Precision.HIGHEST
    velocity = jnp.asarray(speeds, jnp.float32)
    weight = jnp.asarray(weights, jnp.float32)
    upper_moments = jnp.asarray(moments[4:], jnp.float32)
    relax = jnp.dot(upper_moments.T * rates[None, :], upper_moments, precision=highest, preferred_element_type=jnp.float32)
    density = lax.optimization_barrier(jnp.sum(flat, axis=0))
    momentum = jnp.dot(velocity.T, flat, precision=highest, preferred_element_type=jnp.float32)
    projected = jnp.dot(velocity, momentum, precision=highest, preferred_element_type=jnp.float32)
    magnitude = lax.optimization_barrier(jnp.sum(momentum * momentum, axis=0))
    equilibrium = weight[:, None] * (density[None, :] + 3.0 * projected + 4.5 * projected * projected - 1.5 * magnitude[None, :])
    return flat - jnp.dot(relax, flat - equilibrium, precision=highest, preferred_element_type=jnp.float32)

def stream(extended, size_x, size_y, size_z):
    speeds = lattice_tables()[0]
    result = []
    for direction in range(19):
        start_x = 1 - int(speeds[direction, 0])
        start_y = 1 - int(speeds[direction, 1])
        start_z = 1 - int(speeds[direction, 2])
        result.append(extended[direction, start_x:start_x + size_x, start_y:start_y + size_y, start_z:start_z + size_z])
    return jnp.stack(result)

def wall_terms(picked, direction, place_x, place_y, place_z, body_index, motion, centre, live, grid):
    speeds, weights, moments = lattice_tables()
    highest = lax.Precision.HIGHEST
    velocity = jnp.asarray(speeds, jnp.float32)
    weight = jnp.asarray(weights, jnp.float32)
    choose = (direction[:, None] == jnp.arange(19, dtype=jnp.int32)[None, :]).astype(jnp.float32)
    link_speed = jnp.dot(choose, velocity, precision=highest, preferred_element_type=jnp.float32)
    link_weight = jnp.dot(choose, weight, precision=highest, preferred_element_type=jnp.float32)
    pick_body = (body_index[:, None] == jnp.arange(motion.shape[0], dtype=jnp.int32)[None, :]).astype(jnp.float32)
    link_motion = jnp.dot(pick_body, motion, precision=highest, preferred_element_type=jnp.float32)
    link_centre = jnp.dot(pick_body, centre, precision=highest, preferred_element_type=jnp.float32)
    extents = jnp.asarray([grid[0], grid[1], grid[2]], jnp.float32)
    position = jnp.stack([place_x, place_y, place_z], axis=1).astype(jnp.float32) + 0.5 * link_speed
    radius = (position - link_centre * extents[None, :]) / extents[1]
    wall = link_motion[:, 0:3] + jnp.cross(link_motion[:, 3:6], radius)
    normal_speed = lax.optimization_barrier(jnp.sum(link_speed * wall, axis=1))
    values = picked - 6.0 * link_weight * normal_speed
    push = link_speed * (2.0 * picked - 6.0 * link_weight * normal_speed)[:, None]
    turn = jnp.cross(radius, push)
    loads = jnp.concatenate([push, turn], axis=1) * live.astype(jnp.float32)[:, None]
    return (values, loads, pick_body)

def advance(motion, body_load, inv_mass, inv_inertia, area):
    linear = motion[:, 0:3] + inv_mass[:, None] * body_load[:, 0:3] / area
    angular = motion[:, 3:6] + inv_inertia * body_load[:, 3:6] / area
    return jnp.concatenate([linear, angular], axis=1)

def reference(populations, solid, link_cell, link_dir, link_store, store_body, motion, inv_mass, inv_inertia, centre, rates):
    cells_all = NX * NY * NZ
    flat = populations.reshape(19, cells_all)
    post = collide(flat, rates)
    post = jnp.where(solid.reshape(1, cells_all) == 1, flat, post).reshape(19, NX, NY, NZ)
    extended = jnp.pad(post, ((0, 0), (0, 0), (0, 0), (1, 1)), mode='wrap')
    extended = jnp.pad(extended, ((0, 0), (1, 1), (1, 1), (0, 0)))
    moved = stream(extended, NX, NY, NZ)
    offset_x = (jnp.arange(N_GX, dtype=jnp.int32) * CX)[:, None, None, None]
    offset_y = (jnp.arange(N_GY, dtype=jnp.int32) * CY)[None, :, None, None]
    offset_z = (jnp.arange(N_GZ, dtype=jnp.int32) * CZ)[None, None, :, None]
    cell_x = (link_cell // (CY * CZ) + offset_x).reshape(-1)
    cell_y = (link_cell // CZ % CY + offset_y).reshape(-1)
    cell_z = (link_cell % CZ + offset_z).reshape(-1)
    direction = link_dir.reshape(-1)
    store = link_store.reshape(-1)
    live = store < STORES
    store_index = jnp.minimum(store, STORES - 1)
    body_index = store_body[store_index]
    picked = post[direction, cell_x, cell_y, cell_z]
    values, loads, pick_body = wall_terms(picked, direction, cell_x, cell_y, cell_z, body_index, motion, centre, live, (NX, NY, NZ))
    opposite = direction + 1 - 2 * ((direction + 1) % 2)
    target_x = jnp.where(live, cell_x, NX)
    moved = moved.at[opposite, target_x, cell_y, cell_z].set(values, mode='drop')
    store_sums = jax.ops.segment_sum(loads, store_index, num_segments=STORES)
    body_load = jax.ops.segment_sum(store_sums, store_body, num_segments=NB)
    motion_next = advance(motion, body_load, inv_mass, inv_inertia, AREA)
    return (moved, store_sums.T, motion_next)
```

```python
import math

import jax
import jax.numpy as jnp
import numpy as np
from jax import lax
from jax.experimental import pallas as pl
from jax.experimental.pallas import tpu as pltpu
from jax.sharding import PartitionSpec as P

F32 = jnp.float32
BF16 = jnp.bfloat16
I32 = jnp.int32

XP, XM = (1, 7, 9, 11, 13), (2, 10, 8, 14, 12)
YP, YM = (3, 7, 10, 15, 17), (4, 9, 8, 18, 16)
ZP, ZM = (5, 11, 14, 15, 18), (6, 13, 12, 17, 16)


def lattice_tables():
    speed_list = [
        [0, 0, 0],
        [1, 0, 0],
        [-1, 0, 0],
        [0, 1, 0],
        [0, -1, 0],
        [0, 0, 1],
        [0, 0, -1],
        [1, 1, 0],
        [-1, -1, 0],
        [1, -1, 0],
        [-1, 1, 0],
        [1, 0, 1],
        [-1, 0, -1],
        [1, 0, -1],
        [-1, 0, 1],
        [0, 1, 1],
        [0, -1, -1],
        [0, 1, -1],
        [0, -1, 1],
    ]
    speeds = np.array(speed_list) * 1.0
    weights = np.array([1.0 / 3.0] + [1.0 / 18.0] * 6 + [1.0 / 36.0] * 12)
    along_x = speeds[:, 0]
    along_y = speeds[:, 1]
    along_z = speeds[:, 2]
    square = along_x * along_x + along_y * along_y + along_z * along_z
    polynomials = np.stack(
        [
            np.ones(19),
            along_x,
            along_y,
            along_z,
            square,
            3 * along_x * along_x - square,
            along_y * along_y - along_z * along_z,
            along_x * along_y,
            along_y * along_z,
            along_x * along_z,
            along_x * square,
            along_y * square,
            along_z * square,
            square * square,
            (3 * along_x * along_x - square) * square,
            (along_y * along_y - along_z * along_z) * square,
            along_x * (along_y * along_y - along_z * along_z),
            along_y * (along_z * along_z - along_x * along_x),
            along_z * (along_x * along_x - along_y * along_y),
        ],
        axis=1,
    )
    columns = []
    for column_index in range(19):
        vector = polynomials[:, column_index] * 1.0
        for repeat in range(2):
            for earlier in columns:
                vector = vector - np.dot(earlier, vector) * earlier
        columns.append(vector / math.sqrt(float(np.dot(vector, vector))))
    return (speeds, weights, np.stack(columns))


def collision_scalars(rate):
    m = lattice_tables()[2]
    r = {k: rate(k - 4) for k in range(4, 19)}
    f = lambda v: float(v)
    out = {}
    for name, column in (("rest", 0), ("axis", 1), ("diag", 7)):
        for other, column2 in (("rest", 0), ("axis", 1), ("diag", 7)):
            out[name, other] = r[4] * f(m[4, column] * m[4, column2]) + r[13] * f(
                m[13, column] * m[13, column2]
            )
    a5, b5, a14, b14 = m[5, 1] / 2, m[5, 7], m[14, 1] / 2, m[14, 7]
    out["uu"] = r[5] * f(a5 * a5) + r[14] * f(a14 * a14)
    out["uv"] = r[5] * f(a5 * b5) + r[14] * f(a14 * b14)
    out["vv"] = r[5] * f(b5 * b5) + r[14] * f(b14 * b14)
    a6, b6, a15, b15 = m[6, 3], m[6, 7], m[15, 3], m[15, 7]
    out["pp"] = r[6] * f(a6 * a6) + r[15] * f(a15 * a15)
    out["pq"] = r[6] * f(a6 * b6) + r[15] * f(a15 * b15)
    out["qq"] = r[6] * f(b6 * b6) + r[15] * f(b15 * b15)
    out["sxy"] = r[7] * f(m[7, 7] ** 2)
    out["syz"] = r[8] * f(m[8, 15] ** 2)
    out["sxz"] = r[9] * f(m[9, 11] ** 2)
    for name, row, axis, diag in (("x", 10, 1, 7), ("y", 11, 3, 7), ("z", 12, 5, 11)):
        out["aa" + name] = r[row] * f(m[row, axis] ** 2)
        out["ab" + name] = r[row] * f(m[row, axis] * m[row, diag])
        out["bb" + name] = r[row] * f(m[row, diag] ** 2)
    out["tx"] = r[16] * f(m[16, 7] ** 2)
    out["ty"] = r[17] * f(m[17, 15] ** 2)
    out["tz"] = r[18] * f(m[18, 11] ** 2)
    return out


def collide(f, k):
    w1, w2 = 1.0 / 18.0, 1.0 / 36.0
    pairs = ((1, 2), (3, 4), (5, 6), (7, 8), (9, 10), (11, 12), (13, 14), (15, 16), (17, 18))
    plus = [f[i] + f[o] for i, o in pairs]
    minus = [f[i] - f[o] for i, o in pairs]
    sx, sy, sz, sa, sb, sc, sd, se, sg = plus
    dx, dy, dz, da, db, dc, dd, de, dg = minus
    density = f[0] + ((sx + sy + sz) + (sa + sb) + (sc + sd) + (se + sg))
    jx = dx + (da + db) + (dc + dd)
    jy = dy + (da - db) + (de + dg)
    jz = dz + (dc - dd) + (de - dg)
    magnitude = jx * jx + jy * jy + jz * jz
    base = density - 1.5 * magnitude
    axis_base = (2.0 * w1) * base
    diag_base = (2.0 * w2) * base
    n0 = f[0] - (1.0 / 3.0) * base
    sx = sx - (axis_base + (9.0 * w1) * (jx * jx))
    sy = sy - (axis_base + (9.0 * w1) * (jy * jy))
    sz = sz - (axis_base + (9.0 * w1) * (jz * jz))

    def diagonal(s, project):
        return s - (diag_base + (9.0 * w2) * (project * project))

    sa, sb = diagonal(sa, jx + jy), diagonal(sb, jx - jy)
    sc, sd = diagonal(sc, jx + jz), diagonal(sd, jx - jz)
    se, sg = diagonal(se, jy + jz), diagonal(sg, jy - jz)
    dx, dy, dz = dx - (6.0 * w1) * jx, dy - (6.0 * w1) * jy, dz - (6.0 * w1) * jz
    hx, hy, hz = (6.0 * w2) * jx, (6.0 * w2) * jy, (6.0 * w2) * jz
    da, db = da - (hx + hy), db - (hx - hy)
    dc, dd = dc - (hx + hz), dd - (hx - hz)
    de, dg = de - (hy + hz), dg - (hy - hz)
    exy, exz, eyz = sa + sb, sc + sd, se + sg
    axis_sum = sx + sy + sz
    diag_sum = exy + exz + eyz
    g0 = k["rest", "rest"] * n0 + k["rest", "axis"] * axis_sum + k["rest", "diag"] * diag_sum
    ga = k["axis", "rest"] * n0 + k["axis", "axis"] * axis_sum + k["axis", "diag"] * diag_sum
    gd = k["diag", "rest"] * n0 + k["diag", "axis"] * axis_sum + k["diag", "diag"] * diag_sum
    u = 2.0 * sx - sy - sz
    v = exy + exz - 2.0 * eyz
    gu = k["uu"] * u + k["uv"] * v
    gv = k["uv"] * u + k["vv"] * v
    p = sy - sz
    q = exy - exz
    gp = k["pp"] * p + k["pq"] * q
    gq = k["pq"] * p + k["qq"] * q
    ga_u, gd_v = ga - gu, gd + gv
    even = [ga + 2.0 * gu, ga_u + gp, ga_u - gp]
    gxy, gxz, gyz = gd_v + gq, gd_v - gq, gd - 2.0 * gv
    for total, one, two, rate in ((gxy, sa, sb, "sxy"), (gxz, sc, sd, "sxz"), (gyz, se, sg, "syz")):
        shear = k[rate] * (one - two)
        even += [total + shear, total - shear]
    x_xy, x_xz = da + db, dc + dd
    y_xy, y_yz = da - db, de + dg
    z_xz, z_yz = dc - dd, de - dg
    x_all, y_all, z_all = x_xy + x_xz, y_xy + y_yz, z_xz + z_yz
    ox = k["aax"] * dx + k["abx"] * x_all
    oy = k["aay"] * dy + k["aby"] * y_all
    oz = k["aaz"] * dz + k["abz"] * z_all
    bx = k["abx"] * dx + k["bbx"] * x_all
    by = k["aby"] * dy + k["bby"] * y_all
    bz = k["abz"] * dz + k["bbz"] * z_all
    tx, ty, tz = k["tx"] * (x_xy - x_xz), k["ty"] * (y_yz - y_xy), k["tz"] * (z_xz - z_yz)
    x_on_xy, x_on_xz = bx + tx, bx - tx
    y_on_yz, y_on_xy = by + ty, by - ty
    z_on_xz, z_on_yz = bz + tz, bz - tz
    odd = [ox, oy, oz]
    odd += [x_on_xy + y_on_xy, x_on_xy - y_on_xy]
    odd += [x_on_xz + z_on_xz, x_on_xz - z_on_xz]
    odd += [y_on_yz + z_on_yz, y_on_yz - z_on_yz]
    post = [f[0] - g0]
    for (i, o), even_part, odd_part in zip(pairs, even, odd):
        post += [f[i] - (even_part + odd_part), f[o] - (even_part - odd_part)]
    return post


def halves(x):
    high = x.astype(BF16)
    return high, (x - high.astype(F32)).astype(BF16)


def rows_dot(a, b):
    return lax.dot_general(a, b, (((1,), (1,)), ((), ())), preferred_element_type=F32)


def iota(shape, dim):
    return lax.broadcasted_iota(I32, shape, dim)


def pick(conditions, values, shape):
    result = jnp.zeros(shape, F32)
    for condition, value in zip(conditions, values):
        if isinstance(value, float) and value == 0.0:
            continue
        result = jnp.where(condition, value, result)
    return result


def first_kernel(
    pop_ref,
    solid_ref,
    cell_ref,
    dir_ref,
    store_ref,
    owner_ref,
    motion_ref,
    centre_ref,
    rates_ref,
    post_ref,
    bounce_ref,
    send_ref,
    xp_ref,
    xm_ref,
    yp_ref,
    ym_ref,
    xy_ref,
    picked_ref,
    column_ref,
):
    speeds, weights, _ = lattice_tables()
    links = cell_ref.shape[1]
    place_x, place_y, place_z = (lax.axis_index(a) for a in ("gx", "gy", "gz"))
    cell = cell_ref[...]
    direction = dir_ref[...]
    store = store_ref[...]
    live = store < 32768
    row = lax.shift_right_logical(cell, 7)
    lane = cell & 127
    rows_hot = (iota((128, links), 0) == row).astype(F32)
    lanes_hot = (iota((128, links), 0) == lane).astype(F32)
    rows_hot16 = rows_hot.astype(BF16)
    lanes_hot16 = lanes_hot.astype(BF16)
    store_high = lax.shift_right_logical(store, 7)
    low_hot = (iota((128, links), 0) == (store & 127)).astype(F32).astype(BF16)
    by_high = jnp.dot(
        owner_ref[...].astype(F32).astype(BF16), low_hot, preferred_element_type=F32
    )
    body = jnp.sum(
        jnp.where(iota((256, links), 0) == store_high, by_high, 0.0), axis=0, keepdims=True
    )
    is_dir = [direction == i for i in range(19)]
    shape = direction.shape
    speed = [pick(is_dir, [float(s) for s in speeds[:, a]], shape) for a in range(3)]
    weight = jnp.where(direction <= 6, float(weights[1]), float(weights[7]))
    is_body = [body == float(b) for b in range(8)]
    move = [pick(is_body, [motion_ref[b, c] for b in range(8)], shape) for c in range(6)]
    middle = [pick(is_body, [centre_ref[b, a] for b in range(8)], shape) for a in range(3)]
    place = (
        lax.shift_right_logical(cell, 12) + place_x * 4,
        (row & 31) + place_y * 32,
        lane + place_z * 128,
    )
    extents = (32.0, 128.0, 1024.0)
    radius = [
        (place[a].astype(F32) + 0.5 * speed[a] - middle[a] * extents[a]) / 128.0 for a in range(3)
    ]

    def cross(a, b):
        return [a[(i + 1) % 3] * b[(i + 2) % 3] - a[(i + 2) % 3] * b[(i + 1) % 3] for i in range(3)]

    spin = cross(move[3:], radius)
    normal = sum(speed[a] * (move[a] + spin[a]) for a in range(3))
    wall = 6.0 * weight * normal
    coded = jnp.where(live, direction, 0).astype(F32)
    wall_high, wall_low = halves(wall)
    laid = rows_dot(
        rows_hot16,
        jnp.concatenate(
            [
                (lanes_hot * coded).astype(BF16),
                lanes_hot16 * wall_high,
                lanes_hot16 * wall_low,
            ],
            axis=0,
        ),
    )
    bounce_ref[0] = laid[:, 0:128]
    bounce_ref[1] = laid[:, 128:256] + laid[:, 256:384]

    k = collision_scalars(lambda i: rates_ref[i])
    at_lane = iota((8, 128), 1)

    def block(step, carry):
        rows = pl.ds(pl.multiple_of(step * 8, 8), 8)
        f = [pop_ref[i, rows, :] for i in range(19)]
        post = collide(f, k)
        fixed = solid_ref[rows, :] == 1
        post = [jnp.where(fixed, before, after) for before, after in zip(f, post)]
        code = bounce_ref[0, rows, :]
        found = jnp.zeros((8, 128), F32)
        for i in range(19):
            post_ref[i, rows, :] = post[i]
            if i:
                found = jnp.where(code == float(i), post[i], found)
        picked_ref[rows, :] = found
        bounce_ref[1, rows, :] = found - bounce_ref[1, rows, :]
        column = jnp.zeros((8, 128), F32)
        for n in range(5):
            column = jnp.where(at_lane == n, pltpu.roll(post[ZP[n]], n + 1, 1), column)
            turned = pltpu.roll(post[ZM[n]], 8 + n, 1)
            column = jnp.where(at_lane == 8 + n, turned, column)
        column_ref[rows, :] = column
        return carry

    lax.fori_loop(0, 16, block, 0)

    for n in range(5):
        xp_ref[n] = post_ref[XP[n], 96:128, :]
        xm_ref[n] = post_ref[XM[n], 0:32, :]
        for x in range(4):
            yp_ref[4 * n + x : 4 * n + x + 1, :] = post_ref[YP[n], 32 * x + 31 : 32 * x + 32, :]
            ym_ref[4 * n + x : 4 * n + x + 1, :] = post_ref[YM[n], 32 * x : 32 * x + 1, :]
    yp_ref[20:24, :] = jnp.zeros((4, 128), F32)
    ym_ref[20:24, :] = jnp.zeros((4, 128), F32)
    xy_ref[...] = jnp.zeros((8, 128), F32)
    xy_ref[0:1, :] = post_ref[7, 127:128, :]
    xy_ref[1:2, :] = post_ref[8, 0:1, :]
    xy_ref[2:3, :] = post_ref[9, 96:97, :]
    xy_ref[3:4, :] = post_ref[10, 31:32, :]

    found_high, found_low = halves(picked_ref[...])
    by_row = jnp.dot(
        jnp.concatenate([found_high, found_low], axis=0), lanes_hot16, preferred_element_type=F32
    )
    picked = jnp.sum((by_row[0:128] + by_row[128:256]) * rows_hot, axis=0, keepdims=True)
    strength = jnp.where(live, 2.0 * picked - wall, 0.0)
    push = [speed[a] * strength for a in range(3)]
    turn = cross(radius, push)
    record = jnp.concatenate(push + turn + [store.astype(F32), body], axis=0)
    columns = jnp.transpose(column_ref[...])
    upward = lax.rem(place_z + 1, 8)
    for j in range(8):
        for tile in range(links // 128):
            send_ref[j, tile] = record[:, tile * 128 : (tile + 1) * 128]
        send_ref[j, 8] = jnp.where(upward == j, columns[0:8], columns[8:16])


def second_kernel(got_ref, xy_ref, send_ref, total_ref, body_ref):
    place_x, place_y, place_z = (lax.axis_index(a) for a in ("gx", "gy", "gz"))
    total_ref[...] = jnp.zeros_like(total_ref)
    body_ref[...] = jnp.zeros_like(body_ref)
    links = 1024

    def one(peer, carry):
        record = jnp.concatenate([got_ref[peer, tile] for tile in range(8)], axis=1)
        store = record[6:7].astype(I32)
        body = record[7:8]
        loads = jnp.where(iota((8, links), 0) < 6, record, 0.0)
        owner = lax.shift_right_logical(store, 7)
        mine = (owner & 7) == place_z
        high = jnp.where(mine, lax.shift_right_logical(owner, 4), -1)
        low = ((lax.shift_right_logical(owner, 3) & 1) * 128) + (store & 127)
        both = jnp.concatenate(halves(loads), axis=0)
        none = jnp.zeros_like(both)
        spread = jnp.concatenate([jnp.where(high == h, both, none) for h in range(16)], axis=0)
        low_hot = (iota((256, links), 0) == low).astype(F32).astype(BF16)
        total_ref[...] += rows_dot(spread, low_hot)
        for b in range(8):
            part = jnp.where(body == float(b), loads, 0.0)
            body_ref[b] += sum(part[:, 128 * t : 128 * t + 128] for t in range(8))
        return carry

    lax.fori_loop(0, 8, one, 0)

    at_lane = iota((8, 128), 1)
    at_row = iota((8, 128), 0)
    body_row = jnp.zeros((8, 128), F32)
    for b in range(8):
        column = jnp.sum(body_ref[b], axis=1, keepdims=True)
        body_row = jnp.where(at_lane == at_row * 8 + b, column, body_row)
    body_row = jnp.where(at_row < 6, body_row, 0.0)
    body_row = jnp.sum(body_row, axis=0, keepdims=True)
    for h in range(16):
        for e in range(2):
            lanes = slice(128 * e, 128 * e + 128)
            tile = total_ref[16 * h : 16 * h + 8, lanes] + total_ref[16 * h + 8 : 16 * h + 16, lanes]
            tile = jnp.where(at_row == 6, body_row, tile)
            send_ref[2 * h + e] = jnp.where(at_row == 7, 0.0, tile)

    below = got_ref[lax.rem(place_z + 7, 8), 8]
    above = got_ref[lax.rem(place_z + 1, 8), 8]
    lane = iota((1, 128), 1)

    def turned(x, by):
        return pltpu.roll(x, by, 1)

    to_xp = jnp.where(lane < 32, turned(below[1:2], 32), turned(above[1:2], 64))
    to_xm = jnp.where(lane < 32, below[2:3], turned(above[2:3], 32))
    in_row = lane & 31
    to_yp = jnp.where(in_row == 0, turned(below[3:4], 97), turned(above[3:4], 98))
    to_ym = jnp.where(in_row == 0, below[4:5], turned(above[4:5], 1))
    me = place_x * 4 + place_y
    has_xp, has_xm = place_x < 7, place_x > 0
    has_yp, has_ym = place_y < 3, place_y > 0
    for there, step, line in (
        (has_xp, 4, to_xp),
        (has_xm, -4, to_xm),
        (has_yp, 1, to_yp),
        (has_ym, -1, to_ym),
        (has_xp & has_yp, 5, xy_ref[0:1, :]),
        (has_xm & has_ym, -5, xy_ref[1:2, :]),
        (has_xp & has_ym, 3, xy_ref[2:3, :]),
        (has_xm & has_yp, -3, xy_ref[3:4, :]),
    ):

        @pl.when(there)
        def _(step=step, line=line):
            send_ref[me + step, 7:8, :] = line


def third_kernel(
    post_ref,
    bounce_ref,
    got1_ref,
    got2_ref,
    xp_ref,
    xm_ref,
    yp_ref,
    ym_ref,
    motion_ref,
    mass_ref,
    inertia_ref,
    moved_ref,
    load_ref,
    next_ref,
):
    speeds = lattice_tables()[0].astype(int)
    place_x, place_y, place_z = (lax.axis_index(a) for a in ("gx", "gy", "gz"))
    has_xp, has_xm = place_x < 7, place_x > 0
    has_yp, has_ym = place_y < 3, place_y > 0
    me = place_x * 4 + place_y
    total = got2_ref[0]
    for j in range(1, 32):
        total = total + got2_ref[j]
    load_ref[...] = total[0:6]
    at_lane = iota((8, 128), 1)
    at_row = iota((8, 128), 0)
    own = jnp.where((at_lane & 7) == at_row, total[6:7], 0.0)
    body_load = jnp.zeros((8, 128), F32)
    scale = jnp.zeros((8, 128), F32)
    for c in range(6):
        column = jnp.sum(
            jnp.where(lax.shift_right_logical(at_lane, 3) == c, own, 0.0), axis=1, keepdims=True
        )
        body_load = jnp.where(at_lane == c, column, body_load)
        for b in range(8):
            value = mass_ref[b] if c < 3 else inertia_ref[b, c - 3]
            scale = jnp.where((at_lane == c) & (at_row == b), value, scale)
    next_ref[...] = motion_ref[...] + (scale * body_load)[:, 0:6] / 32768.0

    def edge(there, step):
        line = got2_ref[jnp.where(there, me + step, me), 7:8, :]
        return jnp.where(there, line, 0.0)

    lane = iota((1, 128), 1)
    row_in_plane = lane & 31
    from_x = {1: edge(has_xm, -4), -1: edge(has_xp, 4)}
    from_y = {1: edge(has_ym, -1), -1: edge(has_yp, 1)}
    from_xy = {
        (1, 1): edge(has_xm & has_ym, -5),
        (-1, -1): edge(has_xp & has_yp, 5),
        (1, -1): edge(has_xm & has_yp, -3),
        (-1, 1): edge(has_xp & has_ym, 3),
    }
    entering = {}
    for dirs, face in (
        (ZP, got1_ref[lax.rem(place_z + 7, 8), 8]),
        (ZM, got1_ref[lax.rem(place_z + 1, 8), 8]),
    ):
        for n, i in enumerate(dirs):
            line = face[n : n + 1]
            cx, cy, cz = (int(s) for s in speeds[i])
            if cx == 1:
                came = from_x[1] if cz == 1 else pltpu.roll(from_x[1], 96, 1)
                line = jnp.where(lane < 32, came, pltpu.roll(line, 32, 1))
            if cx == -1:
                came = pltpu.roll(from_x[-1], 96 if cz == 1 else 64, 1)
                line = jnp.where(lane >= 96, came, pltpu.roll(line, 96, 1))
            if cy == 1:
                came = from_y[1] if cz == 1 else pltpu.roll(from_y[1], 127, 1)
                line = jnp.where(row_in_plane == 0, came, pltpu.roll(line, 1, 1))
            if cy == -1:
                came = pltpu.roll(from_y[-1], 31 if cz == 1 else 30, 1)
                line = jnp.where(row_in_plane == 31, came, pltpu.roll(line, 127, 1))
            entering[i] = line
    order = ZP + ZM
    lines = jnp.concatenate(
        [entering[i] for i in order] + [jnp.zeros((118, 128), F32)], axis=0
    )
    columns = jnp.transpose(lines)

    plane_lane = iota((32, 128), 1)
    plane_row = iota((32, 128), 0)
    for x in range(4):
        rows = slice(32 * x, 32 * x + 32)
        code = bounce_ref[0, rows, :]
        value = bounce_ref[1, rows, :]
        for i in range(19):
            cx, cy, cz = (int(s) for s in speeds[i])
            source = x - cx
            if 0 <= source < 4:
                plane = post_ref[i, 32 * source : 32 * source + 32, :]
            elif source < 0:
                plane = jnp.where(has_xm, xp_ref[XP.index(i)], 0.0)
            else:
                plane = jnp.where(has_xp, xm_ref[XM.index(i)], 0.0)
            if cy:
                if 0 <= source < 4:
                    face_ref, n = (yp_ref, YP.index(i)) if cy == 1 else (ym_ref, YM.index(i))
                    line = face_ref[4 * n + source : 4 * n + source + 1, :]
                    line = jnp.where(has_ym if cy == 1 else has_yp, line, 0.0)
                else:
                    line = from_xy[cx, cy]
                plane = pltpu.roll(plane, 1 if cy == 1 else 31, 0)
                plane = jnp.where(plane_row == (0 if cy == 1 else 31), line, plane)
            if cz:
                n = order.index(i)
                plane = pltpu.roll(plane, 1 if cz == 1 else 127, 1)
                at = 0 if cz == 1 else 127
                plane = jnp.where(plane_lane == at, columns[rows, n : n + 1], plane)
            if i:
                opposite = i + 1 if i % 2 else i - 1
                plane = jnp.where(code == float(opposite), value, plane)
            moved_ref[i, x] = plane


def body(
    populations,
    solid,
    link_cell,
    link_dir,
    link_store,
    store_body,
    motion,
    inv_mass,
    inv_inertia,
    centre,
    rates,
):
    vmem = pl.BlockSpec(memory_space=pltpu.VMEM)
    smem = pl.BlockSpec(memory_space=pltpu.SMEM)
    links = link_cell.shape[-1]

    def array(*shape):
        return jax.ShapeDtypeStruct(shape, F32)

    params = pltpu.CompilerParams(vmem_limit_bytes=40 * 1024 * 1024)
    post, bounce, send1, xp, xm, yp, ym, xy = pl.pallas_call(
        first_kernel,
        out_shape=(
            array(19, 128, 128),
            array(2, 128, 128),
            array(8, 9, 8, 128),
            array(5, 32, 128),
            array(5, 32, 128),
            array(24, 128),
            array(24, 128),
            array(8, 128),
        ),
        in_specs=[vmem] * 6 + [smem] * 3,
        out_specs=(vmem,) * 8,
        scratch_shapes=[pltpu.VMEM((128, 128), F32), pltpu.VMEM((128, 128), F32)],
        compiler_params=params,
        name="collide",
    )(
        populations.reshape(19, 128, 128),
        solid.reshape(128, 128),
        link_cell.reshape(1, links),
        link_dir.reshape(1, links),
        link_store.reshape(1, links),
        store_body.reshape(256, 128),
        motion,
        centre,
        rates,
    )

    def shift(x, axis, by):
        size = lax.axis_size(axis)
        return lax.ppermute(x, axis, [(i, (i + by) % size) for i in range(size)])

    xp, xm = shift(xp, "gx", 1), shift(xm, "gx", -1)
    yp, ym = shift(yp, "gy", 1), shift(ym, "gy", -1)
    got1 = lax.all_to_all(send1, "gz", 0, 0, tiled=True)
    send2 = pl.pallas_call(
        second_kernel,
        out_shape=array(32, 8, 128),
        in_specs=[vmem] * 2,
        out_specs=vmem,
        scratch_shapes=[pltpu.VMEM((256, 256), F32), pltpu.VMEM((8, 8, 128), F32)],
        compiler_params=params,
        name="bins",
    )(got1, xy)
    got2 = lax.all_to_all(send2, ("gx", "gy"), 0, 0, tiled=True)
    moved, own_loads, motion_next = pl.pallas_call(
        third_kernel,
        out_shape=(array(19, 4, 32, 128), array(6, 128), array(8, 6)),
        in_specs=[vmem] * 9 + [smem] * 2,
        out_specs=(vmem,) * 3,
        compiler_params=params,
        name="move",
    )(post, bounce, got1, got2, xp, xm, yp, ym, motion, inv_mass, inv_inertia)
    return (moved, own_loads, motion_next)


def solution(mesh):
    return jax.shard_map(
        body,
        mesh=mesh,
        in_specs=(
            P(None, "gx", "gy", "gz"),
            P("gx", "gy", "gz"),
            P("gx", "gy", "gz", None),
            P("gx", "gy", "gz", None),
            P("gx", "gy", "gz", None),
            P(),
            P(),
            P(),
            P(),
            P(),
            P(),
        ),
        out_specs=(P(None, "gx", "gy", "gz"), P(None, ("gx", "gy", "gz")), P()),
        check_vma=False,
    )
```

```python
import math

import jax
import jax.numpy as jnp
import numpy as np
from jax import lax
from jax.experimental import pallas as pl
from jax.experimental.pallas import tpu as pltpu
from jax.sharding import PartitionSpec as P

F32 = jnp.float32
BF16 = jnp.bfloat16
I32 = jnp.int32

XP, XM = (1, 7, 9, 11, 13), (2, 10, 8, 14, 12)
YP, YM = (3, 7, 10, 15, 17), (4, 9, 8, 18, 16)
ZP, ZM = (5, 11, 14, 15, 18), (6, 13, 12, 17, 16)


def lattice_tables():
    speed_list = [
        [0, 0, 0],
        [1, 0, 0],
        [-1, 0, 0],
        [0, 1, 0],
        [0, -1, 0],
        [0, 0, 1],
        [0, 0, -1],
        [1, 1, 0],
        [-1, -1, 0],
        [1, -1, 0],
        [-1, 1, 0],
        [1, 0, 1],
        [-1, 0, -1],
        [1, 0, -1],
        [-1, 0, 1],
        [0, 1, 1],
        [0, -1, -1],
        [0, 1, -1],
        [0, -1, 1],
    ]
    speeds = np.array(speed_list) * 1.0
    weights = np.array([1.0 / 3.0] + [1.0 / 18.0] * 6 + [1.0 / 36.0] * 12)
    along_x = speeds[:, 0]
    along_y = speeds[:, 1]
    along_z = speeds[:, 2]
    square = along_x * along_x + along_y * along_y + along_z * along_z
    polynomials = np.stack(
        [
            np.ones(19),
            along_x,
            along_y,
            along_z,
            square,
            3 * along_x * along_x - square,
            along_y * along_y - along_z * along_z,
            along_x * along_y,
            along_y * along_z,
            along_x * along_z,
            along_x * square,
            along_y * square,
            along_z * square,
            square * square,
            (3 * along_x * along_x - square) * square,
            (along_y * along_y - along_z * along_z) * square,
            along_x * (along_y * along_y - along_z * along_z),
            along_y * (along_z * along_z - along_x * along_x),
            along_z * (along_x * along_x - along_y * along_y),
        ],
        axis=1,
    )
    columns = []
    for column_index in range(19):
        vector = polynomials[:, column_index] * 1.0
        for repeat in range(2):
            for earlier in columns:
                vector = vector - np.dot(earlier, vector) * earlier
        columns.append(vector / math.sqrt(float(np.dot(vector, vector))))
    return (speeds, weights, np.stack(columns))


def collision_scalars(rate):
    m = lattice_tables()[2]
    r = {k: rate(k - 4) for k in range(4, 19)}
    f = lambda v: float(v)
    out = {}
    for name, column in (("rest", 0), ("axis", 1), ("diag", 7)):
        for other, column2 in (("rest", 0), ("axis", 1), ("diag", 7)):
            out[name, other] = r[4] * f(m[4, column] * m[4, column2]) + r[13] * f(
                m[13, column] * m[13, column2]
            )
    a5, b5, a14, b14 = m[5, 1] / 2, m[5, 7], m[14, 1] / 2, m[14, 7]
    out["uu"] = r[5] * f(a5 * a5) + r[14] * f(a14 * a14)
    out["uv"] = r[5] * f(a5 * b5) + r[14] * f(a14 * b14)
    out["vv"] = r[5] * f(b5 * b5) + r[14] * f(b14 * b14)
    a6, b6, a15, b15 = m[6, 3], m[6, 7], m[15, 3], m[15, 7]
    out["pp"] = r[6] * f(a6 * a6) + r[15] * f(a15 * a15)
    out["pq"] = r[6] * f(a6 * b6) + r[15] * f(a15 * b15)
    out["qq"] = r[6] * f(b6 * b6) + r[15] * f(b15 * b15)
    out["sxy"] = r[7] * f(m[7, 7] ** 2)
    out["syz"] = r[8] * f(m[8, 15] ** 2)
    out["sxz"] = r[9] * f(m[9, 11] ** 2)
    for name, row, axis, diag in (("x", 10, 1, 7), ("y", 11, 3, 7), ("z", 12, 5, 11)):
        out["aa" + name] = r[row] * f(m[row, axis] ** 2)
        out["ab" + name] = r[row] * f(m[row, axis] * m[row, diag])
        out["bb" + name] = r[row] * f(m[row, diag] ** 2)
    out["tx"] = r[16] * f(m[16, 7] ** 2)
    out["ty"] = r[17] * f(m[17, 15] ** 2)
    out["tz"] = r[18] * f(m[18, 11] ** 2)
    return out


def collide(f, k):
    w1, w2 = 1.0 / 18.0, 1.0 / 36.0
    pairs = ((1, 2), (3, 4), (5, 6), (7, 8), (9, 10), (11, 12), (13, 14), (15, 16), (17, 18))
    plus = [f[i] + f[o] for i, o in pairs]
    minus = [f[i] - f[o] for i, o in pairs]
    sx, sy, sz, sa, sb, sc, sd, se, sg = plus
    dx, dy, dz, da, db, dc, dd, de, dg = minus
    density = f[0] + ((sx + sy + sz) + (sa + sb) + (sc + sd) + (se + sg))
    jx = dx + (da + db) + (dc + dd)
    jy = dy + (da - db) + (de + dg)
    jz = dz + (dc - dd) + (de - dg)
    magnitude = jx * jx + jy * jy + jz * jz
    base = density - 1.5 * magnitude
    axis_base = (2.0 * w1) * base
    diag_base = (2.0 * w2) * base
    n0 = f[0] - (1.0 / 3.0) * base
    sx = sx - (axis_base + (9.0 * w1) * (jx * jx))
    sy = sy - (axis_base + (9.0 * w1) * (jy * jy))
    sz = sz - (axis_base + (9.0 * w1) * (jz * jz))

    def diagonal(s, project):
        return s - (diag_base + (9.0 * w2) * (project * project))

    sa, sb = diagonal(sa, jx + jy), diagonal(sb, jx - jy)
    sc, sd = diagonal(sc, jx + jz), diagonal(sd, jx - jz)
    se, sg = diagonal(se, jy + jz), diagonal(sg, jy - jz)
    dx, dy, dz = dx - (6.0 * w1) * jx, dy - (6.0 * w1) * jy, dz - (6.0 * w1) * jz
    hx, hy, hz = (6.0 * w2) * jx, (6.0 * w2) * jy, (6.0 * w2) * jz
    da, db = da - (hx + hy), db - (hx - hy)
    dc, dd = dc - (hx + hz), dd - (hx - hz)
    de, dg = de - (hy + hz), dg - (hy - hz)
    exy, exz, eyz = sa + sb, sc + sd, se + sg
    axis_sum = sx + sy + sz
    diag_sum = exy + exz + eyz
    g0 = k["rest", "rest"] * n0 + k["rest", "axis"] * axis_sum + k["rest", "diag"] * diag_sum
    ga = k["axis", "rest"] * n0 + k["axis", "axis"] * axis_sum + k["axis", "diag"] * diag_sum
    gd = k["diag", "rest"] * n0 + k["diag", "axis"] * axis_sum + k["diag", "diag"] * diag_sum
    u = 2.0 * sx - sy - sz
    v = exy + exz - 2.0 * eyz
    gu = k["uu"] * u + k["uv"] * v
    gv = k["uv"] * u + k["vv"] * v
    p = sy - sz
    q = exy - exz
    gp = k["pp"] * p + k["pq"] * q
    gq = k["pq"] * p + k["qq"] * q
    ga_u, gd_v = ga - gu, gd + gv
    even = [ga + 2.0 * gu, ga_u + gp, ga_u - gp]
    gxy, gxz, gyz = gd_v + gq, gd_v - gq, gd - 2.0 * gv
    for total, one, two, rate in ((gxy, sa, sb, "sxy"), (gxz, sc, sd, "sxz"), (gyz, se, sg, "syz")):
        shear = k[rate] * (one - two)
        even += [total + shear, total - shear]
    x_xy, x_xz = da + db, dc + dd
    y_xy, y_yz = da - db, de + dg
    z_xz, z_yz = dc - dd, de - dg
    x_all, y_all, z_all = x_xy + x_xz, y_xy + y_yz, z_xz + z_yz
    ox = k["aax"] * dx + k["abx"] * x_all
    oy = k["aay"] * dy + k["aby"] * y_all
    oz = k["aaz"] * dz + k["abz"] * z_all
    bx = k["abx"] * dx + k["bbx"] * x_all
    by = k["aby"] * dy + k["bby"] * y_all
    bz = k["abz"] * dz + k["bbz"] * z_all
    tx, ty, tz = k["tx"] * (x_xy - x_xz), k["ty"] * (y_yz - y_xy), k["tz"] * (z_xz - z_yz)
    x_on_xy, x_on_xz = bx + tx, bx - tx
    y_on_yz, y_on_xy = by + ty, by - ty
    z_on_xz, z_on_yz = bz + tz, bz - tz
    odd = [ox, oy, oz]
    odd += [x_on_xy + y_on_xy, x_on_xy - y_on_xy]
    odd += [x_on_xz + z_on_xz, x_on_xz - z_on_xz]
    odd += [y_on_yz + z_on_yz, y_on_yz - z_on_yz]
    post = [f[0] - g0]
    for (i, o), even_part, odd_part in zip(pairs, even, odd):
        post += [f[i] - (even_part + odd_part), f[o] - (even_part - odd_part)]
    return post


def halves(x):
    high = x.astype(BF16)
    return high, (x - high.astype(F32)).astype(BF16)


def rows_dot(a, b):
    return lax.dot_general(a, b, (((1,), (1,)), ((), ())), preferred_element_type=F32)


def iota(shape, dim):
    return lax.broadcasted_iota(I32, shape, dim)


def pick(conditions, values, shape):
    result = jnp.zeros(shape, F32)
    for condition, value in zip(conditions, values):
        if isinstance(value, float) and value == 0.0:
            continue
        result = jnp.where(condition, value, result)
    return result


def first_kernel(
    pop_hbm,
    solid_hbm,
    cell_hbm,
    dir_hbm,
    store_hbm,
    owner_hbm,
    motion_hbm,
    centre_hbm,
    rates_hbm,
    post_ref,
    bounce_ref,
    send_ref,
    xp_ref,
    xm_ref,
    yp_ref,
    ym_ref,
    xy_ref,
    pop_ref,
    solid_ref,
    cell_ref,
    dir_ref,
    store_ref,
    owner_ref,
    motion_ref,
    centre_ref,
    rates_ref,
    picked_ref,
    column_ref,
    pop_sem,
    sems,
):
    small = (
        (cell_hbm, cell_ref),
        (dir_hbm, dir_ref),
        (store_hbm, store_ref),
        (owner_hbm, owner_ref),
        (motion_hbm, motion_ref),
        (centre_hbm, centre_ref),
        (rates_hbm, rates_ref),
        (solid_hbm, solid_ref),
    )
    copies = [pltpu.make_async_copy(a, b, sems.at[n]) for n, (a, b) in enumerate(small)]

    def plane(x):
        rows = pl.ds(x * 32, 32)
        return pltpu.make_async_copy(
            pop_hbm.at[:, rows, :], pop_ref.at[:, rows, :], pop_sem.at[x]
        )

    for copy in copies:
        copy.start()
    for x in range(4):
        plane(x).start()
    for copy in copies:
        copy.wait()
    speeds, weights, _ = lattice_tables()
    links = cell_ref.shape[1]
    place_x, place_y, place_z = (lax.axis_index(a) for a in ("gx", "gy", "gz"))
    cell = cell_ref[...]
    direction = dir_ref[...]
    store = store_ref[...]
    live = store < 32768
    row = lax.shift_right_logical(cell, 7)
    lane = cell & 127
    rows_hot = (iota((128, links), 0) == row).astype(F32)
    lanes_hot = (iota((128, links), 0) == lane).astype(F32)
    rows_hot16 = rows_hot.astype(BF16)
    lanes_hot16 = lanes_hot.astype(BF16)
    store_high = lax.shift_right_logical(store, 7)
    low_hot = (iota((128, links), 0) == (store & 127)).astype(F32).astype(BF16)
    by_high = jnp.dot(
        owner_ref[...].astype(F32).astype(BF16), low_hot, preferred_element_type=F32
    )
    body = jnp.sum(
        jnp.where(iota((256, links), 0) == store_high, by_high, 0.0), axis=0, keepdims=True
    )
    is_dir = [direction == i for i in range(19)]
    shape = direction.shape
    speed = [pick(is_dir, [float(s) for s in speeds[:, a]], shape) for a in range(3)]
    weight = jnp.where(direction <= 6, float(weights[1]), float(weights[7]))
    is_body = [body == float(b) for b in range(8)]
    move = [pick(is_body, [motion_ref[b, c] for b in range(8)], shape) for c in range(6)]
    middle = [pick(is_body, [centre_ref[a, b] for b in range(8)], shape) for a in range(3)]
    place = (
        lax.shift_right_logical(cell, 12) + place_x * 4,
        (row & 31) + place_y * 32,
        lane + place_z * 128,
    )
    extents = (32.0, 128.0, 1024.0)
    radius = [
        (place[a].astype(F32) + 0.5 * speed[a] - middle[a] * extents[a]) / 128.0 for a in range(3)
    ]

    def cross(a, b):
        return [a[(i + 1) % 3] * b[(i + 2) % 3] - a[(i + 2) % 3] * b[(i + 1) % 3] for i in range(3)]

    spin = cross(move[3:], radius)
    normal = sum(speed[a] * (move[a] + spin[a]) for a in range(3))
    wall = 6.0 * weight * normal
    coded = jnp.where(live, direction, 0).astype(F32)
    wall_high, wall_low = halves(wall)
    laid = rows_dot(
        rows_hot16,
        jnp.concatenate(
            [
                (lanes_hot * coded).astype(BF16),
                lanes_hot16 * wall_high,
                lanes_hot16 * wall_low,
            ],
            axis=0,
        ),
    )
    bounce_ref[0] = laid[:, 0:128]
    bounce_ref[1] = laid[:, 128:256] + laid[:, 256:384]

    k = collision_scalars(lambda i: rates_ref[i])
    at_lane = iota((8, 128), 1)

    def block(step, carry):
        @pl.when((step & 3) == 0)
        def _():
            plane(lax.shift_right_logical(step, 2)).wait()

        rows = pl.ds(pl.multiple_of(step * 8, 8), 8)
        f = [pop_ref[i, rows, :] for i in range(19)]
        post = collide(f, k)
        fixed = solid_ref[rows, :] == 1
        post = [jnp.where(fixed, before, after) for before, after in zip(f, post)]
        code = bounce_ref[0, rows, :]
        found = jnp.zeros((8, 128), F32)
        for i in range(19):
            post_ref[i, rows, :] = post[i]
            if i:
                found = jnp.where(code == float(i), post[i], found)
        picked_ref[rows, :] = found
        bounce_ref[1, rows, :] = found - bounce_ref[1, rows, :]
        column = jnp.zeros((8, 128), F32)
        for n in range(5):
            column = jnp.where(at_lane == n, pltpu.roll(post[ZP[n]], n + 1, 1), column)
            turned = pltpu.roll(post[ZM[n]], 8 + n, 1)
            column = jnp.where(at_lane == 8 + n, turned, column)
        column_ref[rows, :] = column
        return carry

    lax.fori_loop(0, 16, block, 0)

    for n in range(5):
        xp_ref[n] = post_ref[XP[n], 96:128, :]
        xm_ref[n] = post_ref[XM[n], 0:32, :]
        for x in range(4):
            yp_ref[4 * n + x : 4 * n + x + 1, :] = post_ref[YP[n], 32 * x + 31 : 32 * x + 32, :]
            ym_ref[4 * n + x : 4 * n + x + 1, :] = post_ref[YM[n], 32 * x : 32 * x + 1, :]
    yp_ref[20:24, :] = jnp.zeros((4, 128), F32)
    ym_ref[20:24, :] = jnp.zeros((4, 128), F32)
    xy_ref[...] = jnp.zeros((8, 128), F32)
    xy_ref[0:1, :] = post_ref[7, 127:128, :]
    xy_ref[1:2, :] = post_ref[8, 0:1, :]
    xy_ref[2:3, :] = post_ref[9, 96:97, :]
    xy_ref[3:4, :] = post_ref[10, 31:32, :]

    found_high, found_low = halves(picked_ref[...])
    by_row = jnp.dot(
        jnp.concatenate([found_high, found_low], axis=0), lanes_hot16, preferred_element_type=F32
    )
    picked = jnp.sum((by_row[0:128] + by_row[128:256]) * rows_hot, axis=0, keepdims=True)
    strength = jnp.where(live, 2.0 * picked - wall, 0.0)
    push = [speed[a] * strength for a in range(3)]
    turn = cross(radius, push)
    record = jnp.concatenate(push + turn + [store.astype(F32), body], axis=0)
    columns = jnp.transpose(column_ref[...])
    upward = lax.rem(place_z + 1, 8)
    for j in range(8):
        for tile in range(links // 128):
            send_ref[j, tile] = record[:, tile * 128 : (tile + 1) * 128]
        send_ref[j, 8] = jnp.where(upward == j, columns[0:8], columns[8:16])


def second_kernel(got_ref, xy_ref, send_ref, total_ref, body_ref):
    place_x, place_y, place_z = (lax.axis_index(a) for a in ("gx", "gy", "gz"))
    total_ref[...] = jnp.zeros_like(total_ref)
    body_ref[...] = jnp.zeros_like(body_ref)
    links = 1024

    def one(peer, carry):
        record = jnp.concatenate([got_ref[peer, tile] for tile in range(8)], axis=1)
        store = record[6:7].astype(I32)
        body = record[7:8]
        loads = jnp.where(iota((8, links), 0) < 6, record, 0.0)
        owner = lax.shift_right_logical(store, 7)
        mine = (owner & 7) == place_z
        high = jnp.where(mine, lax.shift_right_logical(owner, 4), -1)
        low = ((lax.shift_right_logical(owner, 3) & 1) * 128) + (store & 127)
        both = jnp.concatenate(halves(loads), axis=0)
        none = jnp.zeros_like(both)
        high = jnp.broadcast_to(high.astype(F32), (16, links)).astype(BF16)
        spread = jnp.concatenate(
            [jnp.where(high == jnp.bfloat16(h), both, none) for h in range(16)], axis=0
        )
        low = jnp.broadcast_to(low.astype(F32), (16, links)).astype(BF16)
        one = jnp.ones((16, links), BF16)
        low_hot = jnp.concatenate(
            [
                jnp.where(low == (iota((16, links), 0) + 16 * g).astype(F32).astype(BF16), one, none)
                for g in range(16)
            ],
            axis=0,
        )
        total_ref[...] += rows_dot(spread, low_hot)
        for b in range(8):
            part = jnp.where(body == float(b), loads, 0.0)
            body_ref[b] += sum(part[:, 128 * t : 128 * t + 128] for t in range(8))
        return carry

    lax.fori_loop(0, 8, one, 0)

    at_lane = iota((8, 128), 1)
    at_row = iota((8, 128), 0)
    body_row = jnp.zeros((8, 128), F32)
    for b in range(8):
        column = jnp.sum(body_ref[b], axis=1, keepdims=True)
        body_row = jnp.where(at_lane == at_row * 8 + b, column, body_row)
    body_row = jnp.where(at_row < 6, body_row, 0.0)
    body_row = jnp.sum(body_row, axis=0, keepdims=True)
    for h in range(16):
        for e in range(2):
            lanes = slice(128 * e, 128 * e + 128)
            tile = total_ref[16 * h : 16 * h + 8, lanes] + total_ref[16 * h + 8 : 16 * h + 16, lanes]
            tile = jnp.where(at_row == 6, body_row, tile)
            send_ref[2 * h + e] = jnp.where(at_row == 7, 0.0, tile)

    below = got_ref[lax.rem(place_z + 7, 8), 8]
    above = got_ref[lax.rem(place_z + 1, 8), 8]
    lane = iota((1, 128), 1)

    def turned(x, by):
        return pltpu.roll(x, by, 1)

    to_xp = jnp.where(lane < 32, turned(below[1:2], 32), turned(above[1:2], 64))
    to_xm = jnp.where(lane < 32, below[2:3], turned(above[2:3], 32))
    in_row = lane & 31
    to_yp = jnp.where(in_row == 0, turned(below[3:4], 97), turned(above[3:4], 98))
    to_ym = jnp.where(in_row == 0, below[4:5], turned(above[4:5], 1))
    me = place_x * 4 + place_y
    has_xp, has_xm = place_x < 7, place_x > 0
    has_yp, has_ym = place_y < 3, place_y > 0
    for there, step, line in (
        (has_xp, 4, to_xp),
        (has_xm, -4, to_xm),
        (has_yp, 1, to_yp),
        (has_ym, -1, to_ym),
        (has_xp & has_yp, 5, xy_ref[0:1, :]),
        (has_xm & has_ym, -5, xy_ref[1:2, :]),
        (has_xp & has_ym, 3, xy_ref[2:3, :]),
        (has_xm & has_yp, -3, xy_ref[3:4, :]),
    ):

        @pl.when(there)
        def _(step=step, line=line):
            send_ref[me + step, 7:8, :] = line


def third_kernel(
    post_ref,
    bounce_ref,
    got1_ref,
    got2_ref,
    xp_ref,
    xm_ref,
    yp_ref,
    ym_ref,
    motion_ref,
    mass_ref,
    inertia_ref,
    moved_ref,
    load_ref,
    next_ref,
):
    speeds = lattice_tables()[0].astype(int)
    place_x, place_y, place_z = (lax.axis_index(a) for a in ("gx", "gy", "gz"))
    has_xp, has_xm = place_x < 7, place_x > 0
    has_yp, has_ym = place_y < 3, place_y > 0
    me = place_x * 4 + place_y
    total = got2_ref[0]
    for j in range(1, 32):
        total = total + got2_ref[j]
    load_ref[...] = total[0:6]
    at_lane = iota((8, 128), 1)
    at_row = iota((8, 128), 0)
    own = jnp.where((at_lane & 7) == at_row, total[6:7], 0.0)
    body_load = jnp.zeros((8, 128), F32)
    scale = jnp.zeros((8, 128), F32)
    for c in range(6):
        column = jnp.sum(
            jnp.where(lax.shift_right_logical(at_lane, 3) == c, own, 0.0), axis=1, keepdims=True
        )
        body_load = jnp.where(at_lane == c, column, body_load)
        for b in range(8):
            value = mass_ref[b] if c < 3 else inertia_ref[c - 3, b]
            scale = jnp.where((at_lane == c) & (at_row == b), value, scale)
    next_ref[...] = motion_ref[...] + (scale * body_load)[:, 0:6] / 32768.0

    def edge(there, step):
        line = got2_ref[jnp.where(there, me + step, me), 7:8, :]
        return jnp.where(there, line, 0.0)

    lane = iota((1, 128), 1)
    row_in_plane = lane & 31
    from_x = {1: edge(has_xm, -4), -1: edge(has_xp, 4)}
    from_y = {1: edge(has_ym, -1), -1: edge(has_yp, 1)}
    from_xy = {
        (1, 1): edge(has_xm & has_ym, -5),
        (-1, -1): edge(has_xp & has_yp, 5),
        (1, -1): edge(has_xm & has_yp, -3),
        (-1, 1): edge(has_xp & has_ym, 3),
    }
    entering = {}
    for dirs, face in (
        (ZP, got1_ref[lax.rem(place_z + 7, 8), 8]),
        (ZM, got1_ref[lax.rem(place_z + 1, 8), 8]),
    ):
        for n, i in enumerate(dirs):
            line = face[n : n + 1]
            cx, cy, cz = (int(s) for s in speeds[i])
            if cx == 1:
                came = from_x[1] if cz == 1 else pltpu.roll(from_x[1], 96, 1)
                line = jnp.where(lane < 32, came, pltpu.roll(line, 32, 1))
            if cx == -1:
                came = pltpu.roll(from_x[-1], 96 if cz == 1 else 64, 1)
                line = jnp.where(lane >= 96, came, pltpu.roll(line, 96, 1))
            if cy == 1:
                came = from_y[1] if cz == 1 else pltpu.roll(from_y[1], 127, 1)
                line = jnp.where(row_in_plane == 0, came, pltpu.roll(line, 1, 1))
            if cy == -1:
                came = pltpu.roll(from_y[-1], 31 if cz == 1 else 30, 1)
                line = jnp.where(row_in_plane == 31, came, pltpu.roll(line, 127, 1))
            entering[i] = line
    order = ZP + ZM
    lines = jnp.concatenate(
        [entering[i] for i in order] + [jnp.zeros((118, 128), F32)], axis=0
    )
    columns = jnp.transpose(lines)

    plane_lane = iota((32, 128), 1)
    plane_row = iota((32, 128), 0)
    for x in range(4):
        rows = slice(32 * x, 32 * x + 32)
        code = bounce_ref[0, rows, :]
        value = bounce_ref[1, rows, :]
        for i in range(19):
            cx, cy, cz = (int(s) for s in speeds[i])
            source = x - cx
            if 0 <= source < 4:
                plane = post_ref[i, 32 * source : 32 * source + 32, :]
            elif source < 0:
                plane = jnp.where(has_xm, xp_ref[XP.index(i)], 0.0)
            else:
                plane = jnp.where(has_xp, xm_ref[XM.index(i)], 0.0)
            if cy:
                if 0 <= source < 4:
                    face_ref, n = (yp_ref, YP.index(i)) if cy == 1 else (ym_ref, YM.index(i))
                    line = face_ref[4 * n + source : 4 * n + source + 1, :]
                    line = jnp.where(has_ym if cy == 1 else has_yp, line, 0.0)
                else:
                    line = from_xy[cx, cy]
                plane = pltpu.roll(plane, 1 if cy == 1 else 31, 0)
                plane = jnp.where(plane_row == (0 if cy == 1 else 31), line, plane)
            if cz:
                n = order.index(i)
                plane = pltpu.roll(plane, 1 if cz == 1 else 127, 1)
                at = 0 if cz == 1 else 127
                plane = jnp.where(plane_lane == at, columns[rows, n : n + 1], plane)
            if i:
                opposite = i + 1 if i % 2 else i - 1
                plane = jnp.where(code == float(opposite), value, plane)
            moved_ref[i, x] = plane


def body(
    populations,
    solid,
    link_cell,
    link_dir,
    link_store,
    store_body,
    motion,
    inv_mass,
    inv_inertia,
    centre,
    rates,
):
    vmem = pl.BlockSpec(memory_space=pltpu.VMEM)
    smem = pl.BlockSpec(memory_space=pltpu.SMEM)
    links = link_cell.shape[-1]

    def array(*shape):
        return jax.ShapeDtypeStruct(shape, F32)

    params = pltpu.CompilerParams(vmem_limit_bytes=40 * 1024 * 1024)
    post, bounce, send1, xp, xm, yp, ym, xy = pl.pallas_call(
        first_kernel,
        out_shape=(
            array(19, 128, 128),
            array(2, 128, 128),
            array(8, 9, 8, 128),
            array(5, 32, 128),
            array(5, 32, 128),
            array(24, 128),
            array(24, 128),
            array(8, 128),
        ),
        in_specs=[pl.BlockSpec(memory_space=pltpu.HBM)] * 9,
        out_specs=(vmem,) * 8,
        scratch_shapes=[
            pltpu.VMEM((19, 128, 128), F32),
            pltpu.VMEM((128, 128), I32),
            pltpu.VMEM((1, links), I32),
            pltpu.VMEM((1, links), I32),
            pltpu.VMEM((1, links), I32),
            pltpu.VMEM((256, 128), I32),
            pltpu.SMEM((8, 6), F32),
            pltpu.SMEM((3, 8), F32),
            pltpu.SMEM((15,), F32),
            pltpu.VMEM((128, 128), F32),
            pltpu.VMEM((128, 128), F32),
            pltpu.SemaphoreType.DMA((4,)),
            pltpu.SemaphoreType.DMA((8,)),
        ],
        compiler_params=params,
        name="collide",
    )(
        *(
            pltpu.with_memory_space_constraint(x, pltpu.HBM)
            for x in (
                populations.reshape(19, 128, 128),
                solid.reshape(128, 128),
                link_cell.reshape(1, links),
                link_dir.reshape(1, links),
                link_store.reshape(1, links),
                store_body.reshape(256, 128),
                motion,
                centre.T,
                rates,
            )
        )
    )

    def shift(x, axis, by):
        size = lax.axis_size(axis)
        return lax.ppermute(x, axis, [(i, (i + by) % size) for i in range(size)])

    after = lax.optimization_barrier
    xp = shift(xp, "gx", 1)
    yp = shift(yp, "gy", 1)
    got1 = lax.all_to_all(send1, "gz", 0, 0, tiled=True)
    xm, ym, got1 = after((xm, ym, got1))
    xm = shift(xm, "gx", -1)
    ym = shift(ym, "gy", -1)
    send2 = pl.pallas_call(
        second_kernel,
        out_shape=array(32, 8, 128),
        in_specs=[vmem] * 2,
        out_specs=vmem,
        scratch_shapes=[pltpu.VMEM((256, 256), F32), pltpu.VMEM((8, 8, 128), F32)],
        compiler_params=params,
        cost_estimate=pl.CostEstimate(
            flops=2 * 256 * 256 * 8192, bytes_accessed=4 * 8 * 8192, transcendentals=0
        ),
        name="bins",
    )(got1, xy)
    send2, xp, xm, yp, ym = after((send2, xp, xm, yp, ym))
    got2 = lax.all_to_all(send2, ("gx", "gy"), 0, 0, tiled=True)
    moved, own_loads, motion_next = pl.pallas_call(
        third_kernel,
        out_shape=(array(19, 4, 32, 128), array(6, 128), array(8, 6)),
        in_specs=[vmem] * 9 + [smem] * 2,
        out_specs=(vmem,) * 3,
        compiler_params=params,
        name="move",
    )(post, bounce, got1, got2, xp, xm, yp, ym, motion, inv_mass, inv_inertia.T)
    return (moved, own_loads, motion_next)


def solution(mesh):
    return jax.shard_map(
        body,
        mesh=mesh,
        in_specs=(
            P(None, "gx", "gy", "gz"),
            P("gx", "gy", "gz"),
            P("gx", "gy", "gz", None),
            P("gx", "gy", "gz", None),
            P("gx", "gy", "gz", None),
            P(),
            P(),
            P(),
            P(),
            P(),
            P(),
        ),
        out_specs=(P(None, "gx", "gy", "gz"), P(None, ("gx", "gy", "gz")), P()),
        check_vma=False,
    )
```

```python
import math

import jax
import jax.numpy as jnp
import numpy as np
from jax import lax
from jax.experimental import pallas as pl
from jax.experimental.pallas import tpu as pltpu
from jax.sharding import PartitionSpec as P

F32 = jnp.float32
BF16 = jnp.bfloat16
I32 = jnp.int32

XP, XM = (1, 7, 9, 11, 13), (2, 10, 8, 14, 12)
YP, YM = (3, 7, 10, 15, 17), (4, 9, 8, 18, 16)
ZP, ZM = (5, 11, 14, 15, 18), (6, 13, 12, 17, 16)


def lattice_tables():
    speed_list = [
        [0, 0, 0],
        [1, 0, 0],
        [-1, 0, 0],
        [0, 1, 0],
        [0, -1, 0],
        [0, 0, 1],
        [0, 0, -1],
        [1, 1, 0],
        [-1, -1, 0],
        [1, -1, 0],
        [-1, 1, 0],
        [1, 0, 1],
        [-1, 0, -1],
        [1, 0, -1],
        [-1, 0, 1],
        [0, 1, 1],
        [0, -1, -1],
        [0, 1, -1],
        [0, -1, 1],
    ]
    speeds = np.array(speed_list) * 1.0
    weights = np.array([1.0 / 3.0] + [1.0 / 18.0] * 6 + [1.0 / 36.0] * 12)
    along_x = speeds[:, 0]
    along_y = speeds[:, 1]
    along_z = speeds[:, 2]
    square = along_x * along_x + along_y * along_y + along_z * along_z
    polynomials = np.stack(
        [
            np.ones(19),
            along_x,
            along_y,
            along_z,
            square,
            3 * along_x * along_x - square,
            along_y * along_y - along_z * along_z,
            along_x * along_y,
            along_y * along_z,
            along_x * along_z,
            along_x * square,
            along_y * square,
            along_z * square,
            square * square,
            (3 * along_x * along_x - square) * square,
            (along_y * along_y - along_z * along_z) * square,
            along_x * (along_y * along_y - along_z * along_z),
            along_y * (along_z * along_z - along_x * along_x),
            along_z * (along_x * along_x - along_y * along_y),
        ],
        axis=1,
    )
    columns = []
    for column_index in range(19):
        vector = polynomials[:, column_index] * 1.0
        for repeat in range(2):
            for earlier in columns:
                vector = vector - np.dot(earlier, vector) * earlier
        columns.append(vector / math.sqrt(float(np.dot(vector, vector))))
    return (speeds, weights, np.stack(columns))


def collision_scalars(rate):
    m = lattice_tables()[2]
    r = {k: rate(k - 4) for k in range(4, 19)}
    f = lambda v: float(v)
    out = {}
    for name, column in (("rest", 0), ("axis", 1), ("diag", 7)):
        for other, column2 in (("rest", 0), ("axis", 1), ("diag", 7)):
            out[name, other] = r[4] * f(m[4, column] * m[4, column2]) + r[13] * f(
                m[13, column] * m[13, column2]
            )
    a5, b5, a14, b14 = m[5, 1] / 2, m[5, 7], m[14, 1] / 2, m[14, 7]
    out["uu"] = r[5] * f(a5 * a5) + r[14] * f(a14 * a14)
    out["uv"] = r[5] * f(a5 * b5) + r[14] * f(a14 * b14)
    out["vv"] = r[5] * f(b5 * b5) + r[14] * f(b14 * b14)
    a6, b6, a15, b15 = m[6, 3], m[6, 7], m[15, 3], m[15, 7]
    out["pp"] = r[6] * f(a6 * a6) + r[15] * f(a15 * a15)
    out["pq"] = r[6] * f(a6 * b6) + r[15] * f(a15 * b15)
    out["qq"] = r[6] * f(b6 * b6) + r[15] * f(b15 * b15)
    out["sxy"] = r[7] * f(m[7, 7] ** 2)
    out["syz"] = r[8] * f(m[8, 15] ** 2)
    out["sxz"] = r[9] * f(m[9, 11] ** 2)
    for name, row, axis, diag in (("x", 10, 1, 7), ("y", 11, 3, 7), ("z", 12, 5, 11)):
        out["aa" + name] = r[row] * f(m[row, axis] ** 2)
        out["ab" + name] = r[row] * f(m[row, axis] * m[row, diag])
        out["bb" + name] = r[row] * f(m[row, diag] ** 2)
    out["tx"] = r[16] * f(m[16, 7] ** 2)
    out["ty"] = r[17] * f(m[17, 15] ** 2)
    out["tz"] = r[18] * f(m[18, 11] ** 2)
    return out


def collide(f, k):
    w1, w2 = 1.0 / 18.0, 1.0 / 36.0
    pairs = ((1, 2), (3, 4), (5, 6), (7, 8), (9, 10), (11, 12), (13, 14), (15, 16), (17, 18))
    plus = [f[i] + f[o] for i, o in pairs]
    minus = [f[i] - f[o] for i, o in pairs]
    sx, sy, sz, sa, sb, sc, sd, se, sg = plus
    dx, dy, dz, da, db, dc, dd, de, dg = minus
    density = f[0] + ((sx + sy + sz) + (sa + sb) + (sc + sd) + (se + sg))
    jx = dx + (da + db) + (dc + dd)
    jy = dy + (da - db) + (de + dg)
    jz = dz + (dc - dd) + (de - dg)
    magnitude = jx * jx + jy * jy + jz * jz
    base = density - 1.5 * magnitude
    axis_base = (2.0 * w1) * base
    diag_base = (2.0 * w2) * base
    n0 = f[0] - (1.0 / 3.0) * base
    sx = sx - (axis_base + (9.0 * w1) * (jx * jx))
    sy = sy - (axis_base + (9.0 * w1) * (jy * jy))
    sz = sz - (axis_base + (9.0 * w1) * (jz * jz))

    def diagonal(s, project):
        return s - (diag_base + (9.0 * w2) * (project * project))

    sa, sb = diagonal(sa, jx + jy), diagonal(sb, jx - jy)
    sc, sd = diagonal(sc, jx + jz), diagonal(sd, jx - jz)
    se, sg = diagonal(se, jy + jz), diagonal(sg, jy - jz)
    dx, dy, dz = dx - (6.0 * w1) * jx, dy - (6.0 * w1) * jy, dz - (6.0 * w1) * jz
    hx, hy, hz = (6.0 * w2) * jx, (6.0 * w2) * jy, (6.0 * w2) * jz
    da, db = da - (hx + hy), db - (hx - hy)
    dc, dd = dc - (hx + hz), dd - (hx - hz)
    de, dg = de - (hy + hz), dg - (hy - hz)
    exy, exz, eyz = sa + sb, sc + sd, se + sg
    axis_sum = sx + sy + sz
    diag_sum = exy + exz + eyz
    g0 = k["rest", "rest"] * n0 + k["rest", "axis"] * axis_sum + k["rest", "diag"] * diag_sum
    ga = k["axis", "rest"] * n0 + k["axis", "axis"] * axis_sum + k["axis", "diag"] * diag_sum
    gd = k["diag", "rest"] * n0 + k["diag", "axis"] * axis_sum + k["diag", "diag"] * diag_sum
    u = 2.0 * sx - sy - sz
    v = exy + exz - 2.0 * eyz
    gu = k["uu"] * u + k["uv"] * v
    gv = k["uv"] * u + k["vv"] * v
    p = sy - sz
    q = exy - exz
    gp = k["pp"] * p + k["pq"] * q
    gq = k["pq"] * p + k["qq"] * q
    ga_u, gd_v = ga - gu, gd + gv
    even = [ga + 2.0 * gu, ga_u + gp, ga_u - gp]
    gxy, gxz, gyz = gd_v + gq, gd_v - gq, gd - 2.0 * gv
    for total, one, two, rate in ((gxy, sa, sb, "sxy"), (gxz, sc, sd, "sxz"), (gyz, se, sg, "syz")):
        shear = k[rate] * (one - two)
        even += [total + shear, total - shear]
    x_xy, x_xz = da + db, dc + dd
    y_xy, y_yz = da - db, de + dg
    z_xz, z_yz = dc - dd, de - dg
    x_all, y_all, z_all = x_xy + x_xz, y_xy + y_yz, z_xz + z_yz
    ox = k["aax"] * dx + k["abx"] * x_all
    oy = k["aay"] * dy + k["aby"] * y_all
    oz = k["aaz"] * dz + k["abz"] * z_all
    bx = k["abx"] * dx + k["bbx"] * x_all
    by = k["aby"] * dy + k["bby"] * y_all
    bz = k["abz"] * dz + k["bbz"] * z_all
    tx, ty, tz = k["tx"] * (x_xy - x_xz), k["ty"] * (y_yz - y_xy), k["tz"] * (z_xz - z_yz)
    x_on_xy, x_on_xz = bx + tx, bx - tx
    y_on_yz, y_on_xy = by + ty, by - ty
    z_on_xz, z_on_yz = bz + tz, bz - tz
    odd = [ox, oy, oz]
    odd += [x_on_xy + y_on_xy, x_on_xy - y_on_xy]
    odd += [x_on_xz + z_on_xz, x_on_xz - z_on_xz]
    odd += [y_on_yz + z_on_yz, y_on_yz - z_on_yz]
    post = [f[0] - g0]
    for (i, o), even_part, odd_part in zip(pairs, even, odd):
        post += [f[i] - (even_part + odd_part), f[o] - (even_part - odd_part)]
    return post


def halves(x):
    high = x.astype(BF16)
    return high, (x - high.astype(F32)).astype(BF16)


def rows_dot(a, b):
    return lax.dot_general(a, b, (((1,), (1,)), ((), ())), preferred_element_type=F32)


def iota(shape, dim):
    return lax.broadcasted_iota(I32, shape, dim)


def pick(conditions, values, shape):
    result = jnp.zeros(shape, F32)
    for condition, value in zip(conditions, values):
        if isinstance(value, float) and value == 0.0:
            continue
        result = jnp.where(condition, value, result)
    return result


def first_kernel(
    pop_hbm,
    solid_hbm,
    cell_hbm,
    dir_hbm,
    store_hbm,
    owner_hbm,
    motion_hbm,
    centre_hbm,
    rates_hbm,
    post_ref,
    bounce_ref,
    send_ref,
    xp_ref,
    xm_ref,
    yp_ref,
    ym_ref,
    xy_ref,
    pop_ref,
    solid_ref,
    cell_ref,
    dir_ref,
    store_ref,
    owner_ref,
    motion_ref,
    centre_ref,
    rates_ref,
    picked_ref,
    pop_sem,
    sems,
):
    small = (
        (cell_hbm, cell_ref),
        (dir_hbm, dir_ref),
        (store_hbm, store_ref),
        (owner_hbm, owner_ref),
        (motion_hbm, motion_ref),
        (centre_hbm, centre_ref),
        (rates_hbm, rates_ref),
        (solid_hbm, solid_ref),
    )
    copies = [pltpu.make_async_copy(a, b, sems.at[n]) for n, (a, b) in enumerate(small)]

    def plane(x):
        rows = pl.ds(x * 32, 32)
        return pltpu.make_async_copy(
            pop_hbm.at[:, rows, :], pop_ref.at[:, rows, :], pop_sem.at[x]
        )

    for copy in copies:
        copy.start()
    for x in range(4):
        plane(x).start()
    for copy in copies:
        copy.wait()
    speeds, weights, _ = lattice_tables()
    links = cell_ref.shape[1]
    place_x, place_y, place_z = (lax.axis_index(a) for a in ("gx", "gy", "gz"))
    cell = cell_ref[...]
    direction = dir_ref[...]
    store = store_ref[...]
    live = store < 32768
    row = lax.shift_right_logical(cell, 7)
    lane = cell & 127
    one = jnp.ones((16, links), BF16)
    none = jnp.zeros((16, links), BF16)

    def groups(index, value):
        index = jnp.broadcast_to(index.astype(F32), (16, links)).astype(BF16)
        return [
            jnp.where(index == (iota((16, links), 0) + 16 * g).astype(F32).astype(BF16), value, none)
            for g in range(8)
        ]

    def hot(index):
        return jnp.concatenate(groups(index, one), axis=0)

    rows_hot16 = hot(row)
    lanes_hot16 = hot(lane)
    store_high = lax.shift_right_logical(store, 7)
    low_hot = hot(store & 127)
    by_high = jnp.dot(
        owner_ref[...].astype(F32).astype(BF16), low_hot, preferred_element_type=F32
    )
    body = jnp.sum(
        jnp.where(iota((256, links), 0) == store_high, by_high, 0.0), axis=0, keepdims=True
    )
    is_dir = [direction == i for i in range(19)]
    shape = direction.shape
    speed = [pick(is_dir, [float(s) for s in speeds[:, a]], shape) for a in range(3)]
    weight = jnp.where(direction <= 6, float(weights[1]), float(weights[7]))
    is_body = [body == float(b) for b in range(8)]
    move = [pick(is_body, [motion_ref[b, c] for b in range(8)], shape) for c in range(6)]
    middle = [pick(is_body, [centre_ref[a, b] for b in range(8)], shape) for a in range(3)]
    place = (
        lax.shift_right_logical(cell, 12) + place_x * 4,
        (row & 31) + place_y * 32,
        lane + place_z * 128,
    )
    extents = (32.0, 128.0, 1024.0)
    radius = [
        (place[a].astype(F32) + 0.5 * speed[a] - middle[a] * extents[a]) / 128.0 for a in range(3)
    ]

    def cross(a, b):
        return [a[(i + 1) % 3] * b[(i + 2) % 3] - a[(i + 2) % 3] * b[(i + 1) % 3] for i in range(3)]

    spin = cross(move[3:], radius)
    normal = sum(speed[a] * (move[a] + spin[a]) for a in range(3))
    wall = 6.0 * weight * normal
    coded = jnp.where(live, direction, 0).astype(F32)
    wall_high, wall_low = halves(wall)
    spread = []
    for value in (coded.astype(BF16), wall_high, wall_low):
        spread += groups(lane, jnp.broadcast_to(value.astype(F32), (16, links)).astype(BF16))
    laid = rows_dot(rows_hot16, jnp.concatenate(spread, axis=0))
    bounce_ref[0] = laid[:, 0:128]
    bounce_ref[1] = laid[:, 128:256] + laid[:, 256:384]

    k = collision_scalars(lambda i: rates_ref[i])

    def block(step, carry):
        @pl.when((step & 3) == 0)
        def _():
            plane(lax.shift_right_logical(step, 2)).wait()

        rows = pl.ds(pl.multiple_of(step * 8, 8), 8)
        f = [pop_ref[i, rows, :] for i in range(19)]
        post = collide(f, k)
        fixed = solid_ref[rows, :] == 1
        post = [jnp.where(fixed, before, after) for before, after in zip(f, post)]
        code = bounce_ref[0, rows, :]
        found = jnp.zeros((8, 128), F32)
        for i in range(19):
            post_ref[i, rows, :] = post[i]
            if i:
                found = jnp.where(code == float(i), post[i], found)
        picked_ref[rows, :] = found
        bounce_ref[1, rows, :] = found - bounce_ref[1, rows, :]
        return carry

    lax.fori_loop(0, 16, block, 0, unroll=2)

    at_lane = iota((128, 128), 1)
    column = jnp.zeros((128, 128), F32)
    for n in range(5):
        column = jnp.where(at_lane == n, pltpu.roll(post_ref[ZP[n]], n + 1, 1), column)
        column = jnp.where(at_lane == 8 + n, pltpu.roll(post_ref[ZM[n]], 8 + n, 1), column)
    columns = jnp.transpose(column)
    for n in range(5):
        xp_ref[n] = post_ref[XP[n], 96:128, :]
        xm_ref[n] = post_ref[XM[n], 0:32, :]
        for x in range(4):
            yp_ref[4 * n + x : 4 * n + x + 1, :] = post_ref[YP[n], 32 * x + 31 : 32 * x + 32, :]
            ym_ref[4 * n + x : 4 * n + x + 1, :] = post_ref[YM[n], 32 * x : 32 * x + 1, :]
    yp_ref[20:24, :] = jnp.zeros((4, 128), F32)
    ym_ref[20:24, :] = jnp.zeros((4, 128), F32)
    xy_ref[...] = jnp.zeros((8, 128), F32)
    xy_ref[0:1, :] = post_ref[7, 127:128, :]
    xy_ref[1:2, :] = post_ref[8, 0:1, :]
    xy_ref[2:3, :] = post_ref[9, 96:97, :]
    xy_ref[3:4, :] = post_ref[10, 31:32, :]

    found_high, found_low = halves(picked_ref[...])
    by_row = jnp.dot(
        jnp.concatenate([found_high, found_low], axis=0), lanes_hot16, preferred_element_type=F32
    )
    by_row = jnp.where(iota((128, links), 0) == row, by_row[0:128] + by_row[128:256], 0.0)
    picked = jnp.sum(by_row, axis=0, keepdims=True)
    strength = jnp.where(live, 2.0 * picked - wall, 0.0)
    push = [speed[a] * strength for a in range(3)]
    turn = cross(radius, push)
    record = jnp.concatenate(push + turn + [store.astype(F32), body], axis=0)
    upward = lax.rem(place_z + 1, 8)
    for j in range(8):
        for tile in range(links // 128):
            send_ref[j, tile] = record[:, tile * 128 : (tile + 1) * 128]
        send_ref[j, 8] = jnp.where(upward == j, columns[0:8], columns[8:16])


def second_kernel(got_ref, xy_ref, send_ref, total_ref, body_ref):
    place_x, place_y, place_z = (lax.axis_index(a) for a in ("gx", "gy", "gz"))
    total_ref[...] = jnp.zeros_like(total_ref)
    body_ref[...] = jnp.zeros_like(body_ref)
    links = 1024

    def one(peer, carry):
        record = jnp.concatenate([got_ref[peer, tile] for tile in range(8)], axis=1)
        store = record[6:7].astype(I32)
        body = record[7:8]
        loads = jnp.where(iota((8, links), 0) < 6, record, 0.0)
        owner = lax.shift_right_logical(store, 7)
        mine = (owner & 7) == place_z
        high = jnp.where(mine, lax.shift_right_logical(owner, 4), -1)
        low = ((lax.shift_right_logical(owner, 3) & 1) * 128) + (store & 127)
        both = jnp.concatenate(halves(loads), axis=0)
        none = jnp.zeros_like(both)
        high = jnp.broadcast_to(high.astype(F32), (16, links)).astype(BF16)
        spread = jnp.concatenate(
            [jnp.where(high == jnp.bfloat16(h), both, none) for h in range(16)], axis=0
        )
        low = jnp.broadcast_to(low.astype(F32), (16, links)).astype(BF16)
        one = jnp.ones((16, links), BF16)
        low_hot = jnp.concatenate(
            [
                jnp.where(low == (iota((16, links), 0) + 16 * g).astype(F32).astype(BF16), one, none)
                for g in range(16)
            ],
            axis=0,
        )
        total_ref[...] += rows_dot(spread, low_hot)
        for b in range(8):
            part = jnp.where(body == float(b), loads, 0.0)
            body_ref[b] += sum(part[:, 128 * t : 128 * t + 128] for t in range(8))
        return carry

    lax.fori_loop(0, 8, one, 0, unroll=4)

    at_lane = iota((8, 128), 1)
    at_row = iota((8, 128), 0)
    body_row = jnp.zeros((8, 128), F32)
    for b in range(8):
        column = jnp.sum(body_ref[b], axis=1, keepdims=True)
        body_row = jnp.where(at_lane == at_row * 8 + b, column, body_row)
    body_row = jnp.where(at_row < 6, body_row, 0.0)
    body_row = jnp.sum(body_row, axis=0, keepdims=True)
    for h in range(16):
        for e in range(2):
            lanes = slice(128 * e, 128 * e + 128)
            tile = total_ref[16 * h : 16 * h + 8, lanes] + total_ref[16 * h + 8 : 16 * h + 16, lanes]
            tile = jnp.where(at_row == 6, body_row, tile)
            send_ref[2 * h + e] = jnp.where(at_row == 7, 0.0, tile)

    below = got_ref[lax.rem(place_z + 7, 8), 8]
    above = got_ref[lax.rem(place_z + 1, 8), 8]
    lane = iota((1, 128), 1)

    def turned(x, by):
        return pltpu.roll(x, by, 1)

    to_xp = jnp.where(lane < 32, turned(below[1:2], 32), turned(above[1:2], 64))
    to_xm = jnp.where(lane < 32, below[2:3], turned(above[2:3], 32))
    in_row = lane & 31
    to_yp = jnp.where(in_row == 0, turned(below[3:4], 97), turned(above[3:4], 98))
    to_ym = jnp.where(in_row == 0, below[4:5], turned(above[4:5], 1))
    me = place_x * 4 + place_y
    has_xp, has_xm = place_x < 7, place_x > 0
    has_yp, has_ym = place_y < 3, place_y > 0
    for there, step, line in (
        (has_xp, 4, to_xp),
        (has_xm, -4, to_xm),
        (has_yp, 1, to_yp),
        (has_ym, -1, to_ym),
        (has_xp & has_yp, 5, xy_ref[0:1, :]),
        (has_xm & has_ym, -5, xy_ref[1:2, :]),
        (has_xp & has_ym, 3, xy_ref[2:3, :]),
        (has_xm & has_yp, -3, xy_ref[3:4, :]),
    ):

        @pl.when(there)
        def _(step=step, line=line):
            send_ref[me + step, 7:8, :] = line


def third_kernel(
    post_ref,
    bounce_ref,
    got1_ref,
    got2_ref,
    xp_ref,
    xm_ref,
    yp_ref,
    ym_ref,
    motion_hbm,
    mass_hbm,
    inertia_hbm,
    moved_hbm,
    load_hbm,
    next_hbm,
    moved_ref,
    load_ref,
    next_ref,
    motion_ref,
    mass_ref,
    inertia_ref,
    sems,
):
    speeds = lattice_tables()[0].astype(int)
    place_x, place_y, place_z = (lax.axis_index(a) for a in ("gx", "gy", "gz"))
    has_xp, has_xm = place_x < 7, place_x > 0
    has_yp, has_ym = place_y < 3, place_y > 0
    me = place_x * 4 + place_y
    fetches = [
        pltpu.make_async_copy(motion_hbm, motion_ref, sems.at[6]),
        pltpu.make_async_copy(mass_hbm, mass_ref, sems.at[7]),
        pltpu.make_async_copy(inertia_hbm, inertia_ref, sems.at[8]),
    ]
    for fetch in fetches:
        fetch.start()
    total = got2_ref[0]
    for j in range(1, 32):
        total = total + got2_ref[j]
    load_ref[...] = total[0:6]
    copies = [pltpu.make_async_copy(load_ref, load_hbm, sems.at[4])]
    copies[0].start()

    def advance():
        at_lane = iota((8, 128), 1)
        at_row = iota((8, 128), 0)
        own = jnp.where((at_lane & 7) == at_row, total[6:7], 0.0)
        body_load = jnp.zeros((8, 128), F32)
        scale = jnp.zeros((8, 128), F32)
        for c in range(6):
            here = lax.shift_right_logical(at_lane, 3) == c
            column = jnp.sum(jnp.where(here, own, 0.0), axis=1, keepdims=True)
            body_load = jnp.where(at_lane == c, column, body_load)
            for b in range(8):
                value = mass_ref[b] if c < 3 else inertia_ref[c - 3, b]
                scale = jnp.where((at_lane == c) & (at_row == b), value, scale)
        next_ref[...] = motion_ref[...] + (scale * body_load)[:, 0:6] / 32768.0
        copy = pltpu.make_async_copy(next_ref, next_hbm, sems.at[5])
        copy.start()
        copies.append(copy)

    def edge(there, step):
        line = got2_ref[jnp.where(there, me + step, me), 7:8, :]
        return jnp.where(there, line, 0.0)

    lane = iota((1, 128), 1)
    row_in_plane = lane & 31
    from_x = {1: edge(has_xm, -4), -1: edge(has_xp, 4)}
    from_y = {1: edge(has_ym, -1), -1: edge(has_yp, 1)}
    from_xy = {
        (1, 1): edge(has_xm & has_ym, -5),
        (-1, -1): edge(has_xp & has_yp, 5),
        (1, -1): edge(has_xm & has_yp, -3),
        (-1, 1): edge(has_xp & has_ym, 3),
    }
    entering = {}
    for dirs, face in (
        (ZP, got1_ref[lax.rem(place_z + 7, 8), 8]),
        (ZM, got1_ref[lax.rem(place_z + 1, 8), 8]),
    ):
        for n, i in enumerate(dirs):
            line = face[n : n + 1]
            cx, cy, cz = (int(s) for s in speeds[i])
            if cx == 1:
                came = from_x[1] if cz == 1 else pltpu.roll(from_x[1], 96, 1)
                line = jnp.where(lane < 32, came, pltpu.roll(line, 32, 1))
            if cx == -1:
                came = pltpu.roll(from_x[-1], 96 if cz == 1 else 64, 1)
                line = jnp.where(lane >= 96, came, pltpu.roll(line, 96, 1))
            if cy == 1:
                came = from_y[1] if cz == 1 else pltpu.roll(from_y[1], 127, 1)
                line = jnp.where(row_in_plane == 0, came, pltpu.roll(line, 1, 1))
            if cy == -1:
                came = pltpu.roll(from_y[-1], 31 if cz == 1 else 30, 1)
                line = jnp.where(row_in_plane == 31, came, pltpu.roll(line, 127, 1))
            entering[i] = line
    order = ZP + ZM
    lines = jnp.concatenate(
        [entering[i] for i in order] + [jnp.zeros((118, 128), F32)], axis=0
    )
    columns = jnp.transpose(lines)

    plane_lane = iota((32, 128), 1)
    plane_row = iota((32, 128), 0)
    for x in range(4):
        if x == 2:
            for fetch in fetches:
                fetch.wait()
            advance()
        rows = slice(32 * x, 32 * x + 32)
        code = bounce_ref[0, rows, :]
        value = bounce_ref[1, rows, :]
        for i in range(19):
            cx, cy, cz = (int(s) for s in speeds[i])
            source = x - cx
            if 0 <= source < 4:
                plane = post_ref[i, 32 * source : 32 * source + 32, :]
            elif source < 0:
                plane = jnp.where(has_xm, xp_ref[XP.index(i)], 0.0)
            else:
                plane = jnp.where(has_xp, xm_ref[XM.index(i)], 0.0)
            if cy:
                if 0 <= source < 4:
                    face_ref, n = (yp_ref, YP.index(i)) if cy == 1 else (ym_ref, YM.index(i))
                    line = face_ref[4 * n + source : 4 * n + source + 1, :]
                    line = jnp.where(has_ym if cy == 1 else has_yp, line, 0.0)
                else:
                    line = from_xy[cx, cy]
                plane = pltpu.roll(plane, 1 if cy == 1 else 31, 0)
                plane = jnp.where(plane_row == (0 if cy == 1 else 31), line, plane)
            if cz:
                n = order.index(i)
                plane = pltpu.roll(plane, 1 if cz == 1 else 127, 1)
                at = 0 if cz == 1 else 127
                plane = jnp.where(plane_lane == at, columns[rows, n : n + 1], plane)
            if i:
                opposite = i + 1 if i % 2 else i - 1
                plane = jnp.where(code == float(opposite), value, plane)
            moved_ref[i, x] = plane
        copy = pltpu.make_async_copy(moved_ref.at[:, x], moved_hbm.at[:, x], sems.at[x])
        copy.start()
        copies.append(copy)
    for copy in copies:
        copy.wait()


def body(
    populations,
    solid,
    link_cell,
    link_dir,
    link_store,
    store_body,
    motion,
    inv_mass,
    inv_inertia,
    centre,
    rates,
):
    vmem = pl.BlockSpec(memory_space=pltpu.VMEM)
    links = link_cell.shape[-1]

    def array(*shape):
        return jax.ShapeDtypeStruct(shape, F32)

    params = pltpu.CompilerParams(vmem_limit_bytes=40 * 1024 * 1024)
    post, bounce, send1, xp, xm, yp, ym, xy = pl.pallas_call(
        first_kernel,
        out_shape=(
            array(19, 128, 128),
            array(2, 128, 128),
            array(8, 9, 8, 128),
            array(5, 32, 128),
            array(5, 32, 128),
            array(24, 128),
            array(24, 128),
            array(8, 128),
        ),
        in_specs=[pl.BlockSpec(memory_space=pltpu.HBM)] * 9,
        out_specs=(vmem,) * 8,
        scratch_shapes=[
            pltpu.VMEM((19, 128, 128), F32),
            pltpu.VMEM((128, 128), I32),
            pltpu.VMEM((1, links), I32),
            pltpu.VMEM((1, links), I32),
            pltpu.VMEM((1, links), I32),
            pltpu.VMEM((256, 128), I32),
            pltpu.SMEM((8, 6), F32),
            pltpu.SMEM((3, 8), F32),
            pltpu.SMEM((15,), F32),
            pltpu.VMEM((128, 128), F32),
            pltpu.SemaphoreType.DMA((4,)),
            pltpu.SemaphoreType.DMA((8,)),
        ],
        compiler_params=params,
        name="collide",
    )(
        *(
            pltpu.with_memory_space_constraint(x, pltpu.HBM)
            for x in (
                populations.reshape(19, 128, 128),
                solid.reshape(128, 128),
                link_cell.reshape(1, links),
                link_dir.reshape(1, links),
                link_store.reshape(1, links),
                store_body.reshape(256, 128),
                motion,
                centre.T,
                rates,
            )
        )
    )

    def shift(x, axis, by):
        size = lax.axis_size(axis)
        return lax.ppermute(x, axis, [(i, (i + by) % size) for i in range(size)])

    after = lax.optimization_barrier
    xp = shift(xp, "gx", 1)
    yp = shift(yp, "gy", 1)
    got1 = lax.all_to_all(send1, "gz", 0, 0, tiled=True)
    xm, ym, got1 = after((xm, ym, got1))
    xm = shift(xm, "gx", -1)
    ym = shift(ym, "gy", -1)
    send2 = pl.pallas_call(
        second_kernel,
        out_shape=array(32, 8, 128),
        in_specs=[vmem] * 2,
        out_specs=vmem,
        scratch_shapes=[pltpu.VMEM((256, 256), F32), pltpu.VMEM((8, 8, 128), F32)],
        compiler_params=params,
        cost_estimate=pl.CostEstimate(
            flops=2 * 256 * 256 * 8192, bytes_accessed=4 * 8 * 8192, transcendentals=0
        ),
        name="bins",
    )(got1, xy)
    send2, xp, xm, yp, ym = after((send2, xp, xm, yp, ym))
    got2 = lax.all_to_all(send2, ("gx", "gy"), 0, 0, tiled=True)
    moved, own_loads, motion_next = pl.pallas_call(
        third_kernel,
        out_shape=(array(19, 4, 32, 128), array(6, 128), array(8, 6)),
        in_specs=[vmem] * 8 + [pl.BlockSpec(memory_space=pltpu.HBM)] * 3,
        out_specs=(pl.BlockSpec(memory_space=pltpu.HBM),) * 3,
        scratch_shapes=[
            pltpu.VMEM((19, 4, 32, 128), F32),
            pltpu.VMEM((6, 128), F32),
            pltpu.VMEM((8, 6), F32),
            pltpu.VMEM((8, 6), F32),
            pltpu.SMEM((8,), F32),
            pltpu.SMEM((3, 8), F32),
            pltpu.SemaphoreType.DMA((9,)),
        ],
        compiler_params=params,
        name="move",
    )(
        *(post, bounce, got1, got2, xp, xm, yp, ym),
        *(
            pltpu.with_memory_space_constraint(x, pltpu.HBM)
            for x in (motion, inv_mass, inv_inertia.T)
        ),
    )
    return (moved, own_loads, motion_next)


def solution(mesh):
    return jax.shard_map(
        body,
        mesh=mesh,
        in_specs=(
            P(None, "gx", "gy", "gz"),
            P("gx", "gy", "gz"),
            P("gx", "gy", "gz", None),
            P("gx", "gy", "gz", None),
            P("gx", "gy", "gz", None),
            P(),
            P(),
            P(),
            P(),
            P(),
            P(),
        ),
        out_specs=(P(None, "gx", "gy", "gz"), P(None, ("gx", "gy", "gz")), P()),
        check_vma=False,
    )
```

```python
import math

import jax
import jax.numpy as jnp
import numpy as np
from jax import lax
from jax.experimental import pallas as pl
from jax.experimental.pallas import tpu as pltpu
from jax.sharding import PartitionSpec as P

F32 = jnp.float32
BF16 = jnp.bfloat16
I32 = jnp.int32

XP, XM = (1, 7, 9, 11, 13), (2, 10, 8, 14, 12)
YP, YM = (3, 7, 10, 15, 17), (4, 9, 8, 18, 16)
ZP, ZM = (5, 11, 14, 15, 18), (6, 13, 12, 17, 16)


def lattice_tables():
    speed_list = [
        [0, 0, 0],
        [1, 0, 0],
        [-1, 0, 0],
        [0, 1, 0],
        [0, -1, 0],
        [0, 0, 1],
        [0, 0, -1],
        [1, 1, 0],
        [-1, -1, 0],
        [1, -1, 0],
        [-1, 1, 0],
        [1, 0, 1],
        [-1, 0, -1],
        [1, 0, -1],
        [-1, 0, 1],
        [0, 1, 1],
        [0, -1, -1],
        [0, 1, -1],
        [0, -1, 1],
    ]
    speeds = np.array(speed_list) * 1.0
    weights = np.array([1.0 / 3.0] + [1.0 / 18.0] * 6 + [1.0 / 36.0] * 12)
    along_x = speeds[:, 0]
    along_y = speeds[:, 1]
    along_z = speeds[:, 2]
    square = along_x * along_x + along_y * along_y + along_z * along_z
    polynomials = np.stack(
        [
            np.ones(19),
            along_x,
            along_y,
            along_z,
            square,
            3 * along_x * along_x - square,
            along_y * along_y - along_z * along_z,
            along_x * along_y,
            along_y * along_z,
            along_x * along_z,
            along_x * square,
            along_y * square,
            along_z * square,
            square * square,
            (3 * along_x * along_x - square) * square,
            (along_y * along_y - along_z * along_z) * square,
            along_x * (along_y * along_y - along_z * along_z),
            along_y * (along_z * along_z - along_x * along_x),
            along_z * (along_x * along_x - along_y * along_y),
        ],
        axis=1,
    )
    columns = []
    for column_index in range(19):
        vector = polynomials[:, column_index] * 1.0
        for repeat in range(2):
            for earlier in columns:
                vector = vector - np.dot(earlier, vector) * earlier
        columns.append(vector / math.sqrt(float(np.dot(vector, vector))))
    return (speeds, weights, np.stack(columns))


def collision_scalars(rate):
    m = lattice_tables()[2]
    r = {k: rate(k - 4) for k in range(4, 19)}
    f = lambda v: float(v)
    out = {}
    for name, column in (("rest", 0), ("axis", 1), ("diag", 7)):
        for other, column2 in (("rest", 0), ("axis", 1), ("diag", 7)):
            out[name, other] = r[4] * f(m[4, column] * m[4, column2]) + r[13] * f(
                m[13, column] * m[13, column2]
            )
    a5, b5, a14, b14 = m[5, 1] / 2, m[5, 7], m[14, 1] / 2, m[14, 7]
    out["uu"] = r[5] * f(a5 * a5) + r[14] * f(a14 * a14)
    out["uv"] = r[5] * f(a5 * b5) + r[14] * f(a14 * b14)
    out["vv"] = r[5] * f(b5 * b5) + r[14] * f(b14 * b14)
    a6, b6, a15, b15 = m[6, 3], m[6, 7], m[15, 3], m[15, 7]
    out["pp"] = r[6] * f(a6 * a6) + r[15] * f(a15 * a15)
    out["pq"] = r[6] * f(a6 * b6) + r[15] * f(a15 * b15)
    out["qq"] = r[6] * f(b6 * b6) + r[15] * f(b15 * b15)
    out["sxy"] = r[7] * f(m[7, 7] ** 2)
    out["syz"] = r[8] * f(m[8, 15] ** 2)
    out["sxz"] = r[9] * f(m[9, 11] ** 2)
    for name, row, axis, diag in (("x", 10, 1, 7), ("y", 11, 3, 7), ("z", 12, 5, 11)):
        out["aa" + name] = r[row] * f(m[row, axis] ** 2)
        out["ab" + name] = r[row] * f(m[row, axis] * m[row, diag])
        out["bb" + name] = r[row] * f(m[row, diag] ** 2)
    out["tx"] = r[16] * f(m[16, 7] ** 2)
    out["ty"] = r[17] * f(m[17, 15] ** 2)
    out["tz"] = r[18] * f(m[18, 11] ** 2)
    return out


def collide(f, k):
    w1, w2 = 1.0 / 18.0, 1.0 / 36.0
    pairs = ((1, 2), (3, 4), (5, 6), (7, 8), (9, 10), (11, 12), (13, 14), (15, 16), (17, 18))
    plus = [f[i] + f[o] for i, o in pairs]
    minus = [f[i] - f[o] for i, o in pairs]
    sx, sy, sz, sa, sb, sc, sd, se, sg = plus
    dx, dy, dz, da, db, dc, dd, de, dg = minus
    density = f[0] + ((sx + sy + sz) + (sa + sb) + (sc + sd) + (se + sg))
    jx = dx + (da + db) + (dc + dd)
    jy = dy + (da - db) + (de + dg)
    jz = dz + (dc - dd) + (de - dg)
    magnitude = jx * jx + jy * jy + jz * jz
    base = density - 1.5 * magnitude
    axis_base = (2.0 * w1) * base
    diag_base = (2.0 * w2) * base
    n0 = f[0] - (1.0 / 3.0) * base
    sx = sx - (axis_base + (9.0 * w1) * (jx * jx))
    sy = sy - (axis_base + (9.0 * w1) * (jy * jy))
    sz = sz - (axis_base + (9.0 * w1) * (jz * jz))

    def diagonal(s, project):
        return s - (diag_base + (9.0 * w2) * (project * project))

    sa, sb = diagonal(sa, jx + jy), diagonal(sb, jx - jy)
    sc, sd = diagonal(sc, jx + jz), diagonal(sd, jx - jz)
    se, sg = diagonal(se, jy + jz), diagonal(sg, jy - jz)
    dx, dy, dz = dx - (6.0 * w1) * jx, dy - (6.0 * w1) * jy, dz - (6.0 * w1) * jz
    hx, hy, hz = (6.0 * w2) * jx, (6.0 * w2) * jy, (6.0 * w2) * jz
    da, db = da - (hx + hy), db - (hx - hy)
    dc, dd = dc - (hx + hz), dd - (hx - hz)
    de, dg = de - (hy + hz), dg - (hy - hz)
    exy, exz, eyz = sa + sb, sc + sd, se + sg
    axis_sum = sx + sy + sz
    diag_sum = exy + exz + eyz
    g0 = k["rest", "rest"] * n0 + k["rest", "axis"] * axis_sum + k["rest", "diag"] * diag_sum
    ga = k["axis", "rest"] * n0 + k["axis", "axis"] * axis_sum + k["axis", "diag"] * diag_sum
    gd = k["diag", "rest"] * n0 + k["diag", "axis"] * axis_sum + k["diag", "diag"] * diag_sum
    u = 2.0 * sx - sy - sz
    v = exy + exz - 2.0 * eyz
    gu = k["uu"] * u + k["uv"] * v
    gv = k["uv"] * u + k["vv"] * v
    p = sy - sz
    q = exy - exz
    gp = k["pp"] * p + k["pq"] * q
    gq = k["pq"] * p + k["qq"] * q
    ga_u, gd_v = ga - gu, gd + gv
    even = [ga + 2.0 * gu, ga_u + gp, ga_u - gp]
    gxy, gxz, gyz = gd_v + gq, gd_v - gq, gd - 2.0 * gv
    for total, one, two, rate in ((gxy, sa, sb, "sxy"), (gxz, sc, sd, "sxz"), (gyz, se, sg, "syz")):
        shear = k[rate] * (one - two)
        even += [total + shear, total - shear]
    x_xy, x_xz = da + db, dc + dd
    y_xy, y_yz = da - db, de + dg
    z_xz, z_yz = dc - dd, de - dg
    x_all, y_all, z_all = x_xy + x_xz, y_xy + y_yz, z_xz + z_yz
    ox = k["aax"] * dx + k["abx"] * x_all
    oy = k["aay"] * dy + k["aby"] * y_all
    oz = k["aaz"] * dz + k["abz"] * z_all
    bx = k["abx"] * dx + k["bbx"] * x_all
    by = k["aby"] * dy + k["bby"] * y_all
    bz = k["abz"] * dz + k["bbz"] * z_all
    tx, ty, tz = k["tx"] * (x_xy - x_xz), k["ty"] * (y_yz - y_xy), k["tz"] * (z_xz - z_yz)
    x_on_xy, x_on_xz = bx + tx, bx - tx
    y_on_yz, y_on_xy = by + ty, by - ty
    z_on_xz, z_on_yz = bz + tz, bz - tz
    odd = [ox, oy, oz]
    odd += [x_on_xy + y_on_xy, x_on_xy - y_on_xy]
    odd += [x_on_xz + z_on_xz, x_on_xz - z_on_xz]
    odd += [y_on_yz + z_on_yz, y_on_yz - z_on_yz]
    post = [f[0] - g0]
    for (i, o), even_part, odd_part in zip(pairs, even, odd):
        post += [f[i] - (even_part + odd_part), f[o] - (even_part - odd_part)]
    return post


def halves(x):
    high = x.astype(BF16)
    return high, (x - high.astype(F32)).astype(BF16)


def rows_dot(a, b):
    return lax.dot_general(a, b, (((1,), (1,)), ((), ())), preferred_element_type=F32)


def flat(x):
    return jnp.concatenate([x[s : s + 1] for s in range(8)], axis=1)


def fold(x):
    return jnp.concatenate([x[:, 128 * s : 128 * s + 128] for s in range(8)], axis=0)


def cross(a, b):
    return [a[(i + 1) % 3] * b[(i + 2) % 3] - a[(i + 2) % 3] * b[(i + 1) % 3] for i in range(3)]


def iota(shape, dim):
    return lax.broadcasted_iota(I32, shape, dim)


def pick(conditions, values, shape):
    result = jnp.zeros(shape, F32)
    for condition, value in zip(conditions, values):
        if isinstance(value, float) and value == 0.0:
            continue
        result = jnp.where(condition, value, result)
    return result


def first_kernel(
    pop_hbm,
    solid_hbm,
    cell_hbm,
    dir_hbm,
    store_hbm,
    owner_hbm,
    motion_hbm,
    centre_hbm,
    rates_hbm,
    post_ref,
    bounce_ref,
    send_ref,
    xp_ref,
    xm_ref,
    yp_ref,
    ym_ref,
    xy_ref,
    own_ref,
    pop_ref,
    solid_ref,
    cell_ref,
    dir_ref,
    store_ref,
    owner_ref,
    motion_ref,
    centre_ref,
    rates_ref,
    picked_ref,
    pop_sem,
    sems,
):
    small = (
        (cell_hbm, cell_ref),
        (dir_hbm, dir_ref),
        (store_hbm, store_ref),
        (owner_hbm, owner_ref),
        (motion_hbm, motion_ref),
        (centre_hbm, centre_ref),
        (rates_hbm, rates_ref),
        (solid_hbm, solid_ref),
    )
    copies = [pltpu.make_async_copy(a, b, sems.at[n]) for n, (a, b) in enumerate(small)]

    def plane(x):
        rows = pl.ds(x * 32, 32)
        return pltpu.make_async_copy(
            pop_hbm.at[:, rows, :], pop_ref.at[:, rows, :], pop_sem.at[x]
        )

    for copy in copies:
        copy.start()
    for x in range(4):
        plane(x).start()
    for copy in copies:
        copy.wait()
    speeds, weights, _ = lattice_tables()
    links = 1024
    place_x, place_y, place_z = (lax.axis_index(a) for a in ("gx", "gy", "gz"))
    cell = cell_ref[...]
    direction = dir_ref[...]
    store = store_ref[...]
    live = store < 32768
    row = lax.shift_right_logical(cell, 7)
    lane = cell & 127
    flat_row = flat(row)
    one = jnp.ones((16, links), BF16)
    none = jnp.zeros((16, links), BF16)

    def groups(index, value):
        index = jnp.broadcast_to(index.astype(F32), (16, links)).astype(BF16)
        return [
            jnp.where(index == (iota((16, links), 0) + 16 * g).astype(F32).astype(BF16), value, none)
            for g in range(8)
        ]

    def hot(index):
        return jnp.concatenate(groups(index, one), axis=0)

    flat_lane = flat(lane)
    rows_hot16 = hot(flat_row)
    lanes_hot16 = hot(flat_lane)
    flat_store = flat(store)
    low_hot = hot(flat_store & 127)
    by_high = jnp.dot(
        owner_ref[...].astype(F32).astype(BF16), low_hot, preferred_element_type=F32
    )
    here = iota((256, links), 0) == lax.shift_right_logical(flat_store, 7)
    body = fold(jnp.sum(jnp.where(here, by_high, 0.0), axis=0, keepdims=True))
    is_dir = [direction == i for i in range(19)]
    shape = direction.shape
    speed = [pick(is_dir, [float(s) for s in speeds[:, a]], shape) for a in range(3)]
    weight = jnp.where(direction <= 6, float(weights[1]), float(weights[7]))
    is_body = [body == float(b) for b in range(8)]
    move = [pick(is_body, [motion_ref[b, c] for b in range(8)], shape) for c in range(6)]
    middle = [pick(is_body, [centre_ref[a, b] for b in range(8)], shape) for a in range(3)]
    place = (
        lax.shift_right_logical(cell, 12) + place_x * 4,
        (row & 31) + place_y * 32,
        lane + place_z * 128,
    )
    extents = (32.0, 128.0, 1024.0)
    radius = [
        (place[a].astype(F32) + 0.5 * speed[a] - middle[a] * extents[a]) / 128.0 for a in range(3)
    ]

    spin = cross(move[3:], radius)
    normal = sum(speed[a] * (move[a] + spin[a]) for a in range(3))
    wall = 6.0 * weight * normal
    coded = jnp.where(live, direction, 0).astype(F32)
    spread = []
    for value in (coded, *halves(wall)):
        value = jnp.broadcast_to(flat(value.astype(F32)), (16, links)).astype(BF16)
        spread += groups(flat_lane, value)
    laid = rows_dot(rows_hot16, jnp.concatenate(spread, axis=0))
    bounce_ref[0] = laid[:, 0:128]
    bounce_ref[1] = laid[:, 128:256] + laid[:, 256:384]

    k = collision_scalars(lambda i: rates_ref[i])

    def block(step, carry):
        @pl.when((step & 3) == 0)
        def _():
            plane(lax.shift_right_logical(step, 2)).wait()

        rows = pl.ds(pl.multiple_of(step * 8, 8), 8)
        f = [pop_ref[i, rows, :] for i in range(19)]
        post = collide(f, k)
        fixed = solid_ref[rows, :] == 1
        post = [jnp.where(fixed, before, after) for before, after in zip(f, post)]
        code = bounce_ref[0, rows, :]
        found = jnp.zeros((8, 128), F32)
        for i in range(19):
            post_ref[i, rows, :] = post[i]
            if i:
                found = jnp.where(code == float(i), post[i], found)
        picked_ref[rows, :] = found
        bounce_ref[1, rows, :] = found - bounce_ref[1, rows, :]
        return carry

    lax.fori_loop(0, 16, block, 0, unroll=2)

    at_lane = iota((128, 128), 1)
    column = jnp.zeros((128, 128), F32)
    for n in range(5):
        column = jnp.where(at_lane == n, pltpu.roll(post_ref[ZP[n]], n + 1, 1), column)
        column = jnp.where(at_lane == 8 + n, pltpu.roll(post_ref[ZM[n]], 8 + n, 1), column)
    columns = jnp.transpose(column)
    for n in range(5):
        xp_ref[n] = post_ref[XP[n], 96:128, :]
        xm_ref[n] = post_ref[XM[n], 0:32, :]
        for x in range(4):
            yp_ref[4 * n + x : 4 * n + x + 1, :] = post_ref[YP[n], 32 * x + 31 : 32 * x + 32, :]
            ym_ref[4 * n + x : 4 * n + x + 1, :] = post_ref[YM[n], 32 * x : 32 * x + 1, :]
    yp_ref[20:24, :] = jnp.zeros((4, 128), F32)
    ym_ref[20:24, :] = jnp.zeros((4, 128), F32)
    xy_ref[...] = jnp.zeros((8, 128), F32)
    xy_ref[0:1, :] = post_ref[7, 127:128, :]
    xy_ref[1:2, :] = post_ref[8, 0:1, :]
    xy_ref[2:3, :] = post_ref[9, 96:97, :]
    xy_ref[3:4, :] = post_ref[10, 31:32, :]

    found_high, found_low = halves(picked_ref[...])
    by_row = jnp.dot(
        jnp.concatenate([found_high, found_low], axis=0), lanes_hot16, preferred_element_type=F32
    )
    by_row = jnp.where(
        iota((128, links), 0) == flat_row, by_row[0:128] + by_row[128:256], 0.0
    )
    picked = fold(jnp.sum(by_row, axis=0, keepdims=True))
    strength = jnp.where(live, 2.0 * picked - wall, 0.0)
    push = [speed[a] * strength for a in range(3)]
    sums = []
    for load in push + cross(radius, push):
        for b in range(8):
            sums.append(jnp.sum(jnp.where(is_body[b], load, 0.0), axis=0, keepdims=True))
    sums = jnp.sum(jnp.concatenate(sums, axis=0), axis=1, keepdims=True)
    sums = jnp.where(iota((48, 128), 0) == iota((48, 128), 1), sums, 0.0)
    body_row = jnp.sum(sums, axis=0, keepdims=True)
    upward = lax.rem(place_z + 1, 8)
    records = (strength, direction.astype(F32), cell.astype(F32), store.astype(F32))
    for j in range(8):
        for n, record in enumerate(records):
            send_ref[j, n] = record
        face = jnp.where(upward == j, columns[0:8], columns[8:16])
        send_ref[j, 4] = jnp.where(iota((8, 128), 0) == 5, body_row, face)
    own = owner_ref[pl.ds((place_x * 4 + place_y) * 8 + place_z, 1), :]
    own_ref[...] = jnp.zeros((8, 128), F32)
    for a in range(3):
        middle = pick([own == b for b in range(8)], [centre_ref[a, b] for b in range(8)], (1, 128))
        own_ref[a : a + 1, :] = (middle - 0.5) * (extents[a] / 128.0)


def second_kernel(got_ref, xy_ref, send_ref, total_ref):
    speeds = lattice_tables()[0]
    place_x, place_y, place_z = (lax.axis_index(a) for a in ("gx", "gy", "gz"))
    total_ref[...] = jnp.zeros_like(total_ref)
    count = iota((16, 128), 0).astype(F32)
    counts = [(count + 16.0 * g).astype(BF16) for g in range(16)]
    one = jnp.ones((16, 128), BF16)
    none = jnp.zeros((16, 128), BF16)

    def gather(peer, carry):
        strength, direction = got_ref[peer, 0], got_ref[peer, 1]
        cell, store = got_ref[peer, 2].astype(I32), got_ref[peer, 3].astype(I32)
        is_dir = [direction == float(i) for i in range(19)]
        speed = [pick(is_dir, [float(v) for v in speeds[:, a]], (8, 128)) for a in range(3)]
        place = (
            lax.shift_right_logical(cell, 12) + (place_x * 4 - 16),
            (lax.shift_right_logical(cell, 7) & 31) + (place_y * 32 - 64),
            (cell & 127) + (peer * 128 - 512),
        )
        arm = [(place[a].astype(F32) + 0.5 * speed[a]) * (1.0 / 128.0) for a in range(3)]
        push = [speed[a] * strength for a in range(3)]
        loads = push + cross(arm, push)
        upper = [load.astype(BF16).astype(F32) for load in loads]
        rows = upper + [load - part for load, part in zip(loads, upper)]
        owner = lax.shift_right_logical(store, 7)
        mine = (owner & 7) == place_z
        high = jnp.where(mine, lax.shift_right_logical(owner, 4), 255).astype(F32)
        low = ((lax.shift_right_logical(owner, 3) & 1) * 128) + (store & 127)
        low = low.astype(F32)
        left, right = [], []
        for s in range(8):

            def line(x, s=s):
                return jnp.broadcast_to(x[s : s + 1], (16, 128)).astype(BF16)

            at = line(high) == counts[0]
            left.append(jnp.concatenate([jnp.where(at, line(x), none) for x in rows], axis=0))
            at = line(low)
            right.append(
                jnp.concatenate([jnp.where(at == number, one, none) for number in counts], axis=0)
            )
        total_ref[...] += rows_dot(
            jnp.concatenate(left, axis=1), jnp.concatenate(right, axis=1)
        )
        return carry

    lax.fori_loop(0, 8, gather, 0, unroll=4)

    body_row = sum(got_ref[peer, 4, 5:6, :] for peer in range(8))
    for c in range(6):
        for e in range(2):
            lanes = slice(128 * e, 128 * e + 128)
            upper = total_ref[16 * c : 16 * c + 16, lanes]
            both = upper + total_ref[96 + 16 * c : 112 + 16 * c, lanes]
            for h in range(16):
                send_ref[2 * h + e, c : c + 1, :] = both[h : h + 1]
    last = jnp.concatenate([body_row, jnp.zeros((1, 128), F32)], axis=0)
    for j in range(32):
        send_ref[j, 6:8, :] = last

    below = got_ref[lax.rem(place_z + 7, 8), 4]
    above = got_ref[lax.rem(place_z + 1, 8), 4]
    lane = iota((1, 128), 1)

    def turned(x, by):
        return pltpu.roll(x, by, 1)

    to_xp = jnp.where(lane < 32, turned(below[1:2], 32), turned(above[1:2], 64))
    to_xm = jnp.where(lane < 32, below[2:3], turned(above[2:3], 32))
    in_row = lane & 31
    to_yp = jnp.where(in_row == 0, turned(below[3:4], 97), turned(above[3:4], 98))
    to_ym = jnp.where(in_row == 0, below[4:5], turned(above[4:5], 1))
    me = place_x * 4 + place_y
    has_xp, has_xm = place_x < 7, place_x > 0
    has_yp, has_ym = place_y < 3, place_y > 0
    for there, step, line in (
        (has_xp, 4, to_xp),
        (has_xm, -4, to_xm),
        (has_yp, 1, to_yp),
        (has_ym, -1, to_ym),
        (has_xp & has_yp, 5, xy_ref[0:1, :]),
        (has_xm & has_ym, -5, xy_ref[1:2, :]),
        (has_xp & has_ym, 3, xy_ref[2:3, :]),
        (has_xm & has_yp, -3, xy_ref[3:4, :]),
    ):

        @pl.when(there)
        def _(step=step, line=line):
            send_ref[me + step, 7:8, :] = line


def third_kernel(
    post_ref,
    bounce_ref,
    own_ref,
    got1_ref,
    got2_ref,
    xp_ref,
    xm_ref,
    yp_ref,
    ym_ref,
    motion_hbm,
    mass_hbm,
    inertia_hbm,
    moved_hbm,
    load_hbm,
    next_hbm,
    moved_ref,
    load_ref,
    next_ref,
    motion_ref,
    mass_ref,
    inertia_ref,
    sems,
):
    speeds = lattice_tables()[0].astype(int)
    place_x, place_y, place_z = (lax.axis_index(a) for a in ("gx", "gy", "gz"))
    has_xp, has_xm = place_x < 7, place_x > 0
    has_yp, has_ym = place_y < 3, place_y > 0
    me = place_x * 4 + place_y
    fetches = [
        pltpu.make_async_copy(motion_hbm, motion_ref, sems.at[6]),
        pltpu.make_async_copy(mass_hbm, mass_ref, sems.at[7]),
        pltpu.make_async_copy(inertia_hbm, inertia_ref, sems.at[8]),
    ]
    for fetch in fetches:
        fetch.start()
    total = got2_ref[0]
    for j in range(1, 32):
        total = total + got2_ref[j]
    push = [total[a : a + 1] for a in range(3)]
    away = cross([own_ref[a : a + 1, :] for a in range(3)], push)
    turn = [total[3 + a : 4 + a] - away[a] for a in range(3)]
    load_ref[...] = jnp.concatenate(push + turn, axis=0)
    copies = [pltpu.make_async_copy(load_ref, load_hbm, sems.at[4])]
    copies[0].start()

    def advance():
        at_lane = iota((8, 128), 1)
        at_row = iota((8, 128), 0)
        own = jnp.where((at_lane & 7) == at_row, total[6:7], 0.0)
        body_load = jnp.zeros((8, 128), F32)
        scale = jnp.zeros((8, 128), F32)
        for c in range(6):
            here = lax.shift_right_logical(at_lane, 3) == c
            column = jnp.sum(jnp.where(here, own, 0.0), axis=1, keepdims=True)
            body_load = jnp.where(at_lane == c, column, body_load)
            for b in range(8):
                value = mass_ref[b] if c < 3 else inertia_ref[c - 3, b]
                scale = jnp.where((at_lane == c) & (at_row == b), value, scale)
        next_ref[...] = motion_ref[...] + (scale * body_load)[:, 0:6] / 32768.0
        copy = pltpu.make_async_copy(next_ref, next_hbm, sems.at[5])
        copy.start()
        copies.append(copy)

    def edge(there, step):
        line = got2_ref[jnp.where(there, me + step, me), 7:8, :]
        return jnp.where(there, line, 0.0)

    lane = iota((1, 128), 1)
    row_in_plane = lane & 31
    from_x = {1: edge(has_xm, -4), -1: edge(has_xp, 4)}
    from_y = {1: edge(has_ym, -1), -1: edge(has_yp, 1)}
    from_xy = {
        (1, 1): edge(has_xm & has_ym, -5),
        (-1, -1): edge(has_xp & has_yp, 5),
        (1, -1): edge(has_xm & has_yp, -3),
        (-1, 1): edge(has_xp & has_ym, 3),
    }
    entering = {}
    for dirs, face in (
        (ZP, got1_ref[lax.rem(place_z + 7, 8), 4]),
        (ZM, got1_ref[lax.rem(place_z + 1, 8), 4]),
    ):
        for n, i in enumerate(dirs):
            line = face[n : n + 1]
            cx, cy, cz = (int(s) for s in speeds[i])
            if cx == 1:
                came = from_x[1] if cz == 1 else pltpu.roll(from_x[1], 96, 1)
                line = jnp.where(lane < 32, came, pltpu.roll(line, 32, 1))
            if cx == -1:
                came = pltpu.roll(from_x[-1], 96 if cz == 1 else 64, 1)
                line = jnp.where(lane >= 96, came, pltpu.roll(line, 96, 1))
            if cy == 1:
                came = from_y[1] if cz == 1 else pltpu.roll(from_y[1], 127, 1)
                line = jnp.where(row_in_plane == 0, came, pltpu.roll(line, 1, 1))
            if cy == -1:
                came = pltpu.roll(from_y[-1], 31 if cz == 1 else 30, 1)
                line = jnp.where(row_in_plane == 31, came, pltpu.roll(line, 127, 1))
            entering[i] = line
    order = ZP + ZM
    lines = jnp.concatenate(
        [entering[i] for i in order] + [jnp.zeros((118, 128), F32)], axis=0
    )
    columns = jnp.transpose(lines)

    plane_lane = iota((32, 128), 1)
    plane_row = iota((32, 128), 0)
    for x in range(4):
        if x == 2:
            for fetch in fetches:
                fetch.wait()
            advance()
        rows = slice(32 * x, 32 * x + 32)
        code = bounce_ref[0, rows, :]
        value = bounce_ref[1, rows, :]
        for i in range(19):
            cx, cy, cz = (int(s) for s in speeds[i])
            source = x - cx
            if 0 <= source < 4:
                plane = post_ref[i, 32 * source : 32 * source + 32, :]
            elif source < 0:
                plane = jnp.where(has_xm, xp_ref[XP.index(i)], 0.0)
            else:
                plane = jnp.where(has_xp, xm_ref[XM.index(i)], 0.0)
            if cy:
                if 0 <= source < 4:
                    face_ref, n = (yp_ref, YP.index(i)) if cy == 1 else (ym_ref, YM.index(i))
                    line = face_ref[4 * n + source : 4 * n + source + 1, :]
                    line = jnp.where(has_ym if cy == 1 else has_yp, line, 0.0)
                else:
                    line = from_xy[cx, cy]
                plane = pltpu.roll(plane, 1 if cy == 1 else 31, 0)
                plane = jnp.where(plane_row == (0 if cy == 1 else 31), line, plane)
            if cz:
                n = order.index(i)
                plane = pltpu.roll(plane, 1 if cz == 1 else 127, 1)
                at = 0 if cz == 1 else 127
                plane = jnp.where(plane_lane == at, columns[rows, n : n + 1], plane)
            if i:
                opposite = i + 1 if i % 2 else i - 1
                plane = jnp.where(code == float(opposite), value, plane)
            moved_ref[i, x] = plane
        copy = pltpu.make_async_copy(moved_ref.at[:, x], moved_hbm.at[:, x], sems.at[x])
        copy.start()
        copies.append(copy)
    for copy in copies:
        copy.wait()


def body(
    populations,
    solid,
    link_cell,
    link_dir,
    link_store,
    store_body,
    motion,
    inv_mass,
    inv_inertia,
    centre,
    rates,
):
    vmem = pl.BlockSpec(memory_space=pltpu.VMEM)

    def array(*shape):
        return jax.ShapeDtypeStruct(shape, F32)

    params = pltpu.CompilerParams(vmem_limit_bytes=40 * 1024 * 1024)
    post, bounce, send1, xp, xm, yp, ym, xy, own = pl.pallas_call(
        first_kernel,
        out_shape=(
            array(19, 128, 128),
            array(2, 128, 128),
            array(8, 5, 8, 128),
            array(5, 32, 128),
            array(5, 32, 128),
            array(24, 128),
            array(24, 128),
            array(8, 128),
            array(8, 128),
        ),
        in_specs=[pl.BlockSpec(memory_space=pltpu.HBM)] * 9,
        out_specs=(vmem,) * 9,
        scratch_shapes=[
            pltpu.VMEM((19, 128, 128), F32),
            pltpu.VMEM((128, 128), I32),
            pltpu.VMEM((8, 128), I32),
            pltpu.VMEM((8, 128), I32),
            pltpu.VMEM((8, 128), I32),
            pltpu.VMEM((256, 128), I32),
            pltpu.SMEM((8, 6), F32),
            pltpu.SMEM((3, 8), F32),
            pltpu.SMEM((15,), F32),
            pltpu.VMEM((128, 128), F32),
            pltpu.SemaphoreType.DMA((4,)),
            pltpu.SemaphoreType.DMA((8,)),
        ],
        compiler_params=params,
        name="collide",
    )(
        *(
            pltpu.with_memory_space_constraint(x, pltpu.HBM)
            for x in (
                populations.reshape(19, 128, 128),
                solid.reshape(128, 128),
                link_cell.reshape(8, 128),
                link_dir.reshape(8, 128),
                link_store.reshape(8, 128),
                store_body.reshape(256, 128),
                motion,
                centre.T,
                rates,
            )
        )
    )

    def shift(x, axis, by):
        size = lax.axis_size(axis)
        return lax.ppermute(x, axis, [(i, (i + by) % size) for i in range(size)])

    after = lax.optimization_barrier
    xp, xm = shift(xp, "gx", 1), shift(xm, "gx", -1)
    got1 = lax.all_to_all(send1, "gz", 0, 0, tiled=True)
    send2 = pl.pallas_call(
        second_kernel,
        out_shape=array(32, 8, 128),
        in_specs=[vmem] * 2,
        out_specs=vmem,
        scratch_shapes=[pltpu.VMEM((192, 256), F32)],
        compiler_params=params,
        cost_estimate=pl.CostEstimate(
            flops=2 * 192 * 256 * 8192, bytes_accessed=4 * 4 * 8192, transcendentals=0
        ),
        name="bins",
    )(got1, xy)
    send2, xp, xm, yp, ym = after((send2, xp, xm, yp, ym))
    yp, ym = shift(yp, "gy", 1), shift(ym, "gy", -1)
    got2 = lax.all_to_all(send2, ("gx", "gy"), 0, 0, tiled=True)
    moved, own_loads, motion_next = pl.pallas_call(
        third_kernel,
        out_shape=(array(19, 4, 32, 128), array(6, 128), array(8, 6)),
        in_specs=[vmem] * 9 + [pl.BlockSpec(memory_space=pltpu.HBM)] * 3,
        out_specs=(pl.BlockSpec(memory_space=pltpu.HBM),) * 3,
        scratch_shapes=[
            pltpu.VMEM((19, 4, 32, 128), F32),
            pltpu.VMEM((6, 128), F32),
            pltpu.VMEM((8, 6), F32),
            pltpu.VMEM((8, 6), F32),
            pltpu.SMEM((8,), F32),
            pltpu.SMEM((3, 8), F32),
            pltpu.SemaphoreType.DMA((9,)),
        ],
        compiler_params=params,
        name="move",
    )(
        *(post, bounce, own, got1, got2, xp, xm, yp, ym),
        *(
            pltpu.with_memory_space_constraint(x, pltpu.HBM)
            for x in (motion, inv_mass, inv_inertia.T)
        ),
    )
    return (moved, own_loads, motion_next)


def solution(mesh):
    return jax.shard_map(
        body,
        mesh=mesh,
        in_specs=(
            P(None, "gx", "gy", "gz"),
            P("gx", "gy", "gz"),
            P("gx", "gy", "gz", None),
            P("gx", "gy", "gz", None),
            P("gx", "gy", "gz", None),
            P(),
            P(),
            P(),
            P(),
            P(),
            P(),
        ),
        out_specs=(P(None, "gx", "gy", "gz"), P(None, ("gx", "gy", "gz")), P()),
        check_vma=False,
    )
```

```python
import math

import jax
import jax.numpy as jnp
import numpy as np
from jax import lax
from jax.experimental import pallas as pl
from jax.experimental.pallas import tpu as pltpu
from jax.sharding import PartitionSpec as P

F32 = jnp.float32
BF16 = jnp.bfloat16
I32 = jnp.int32

XP, XM = (1, 7, 9, 11, 13), (2, 10, 8, 14, 12)
YP, YM = (3, 7, 10, 15, 17), (4, 9, 8, 18, 16)
ZP, ZM = (5, 11, 14, 15, 18), (6, 13, 12, 17, 16)


def lattice_tables():
    speed_list = [
        [0, 0, 0],
        [1, 0, 0],
        [-1, 0, 0],
        [0, 1, 0],
        [0, -1, 0],
        [0, 0, 1],
        [0, 0, -1],
        [1, 1, 0],
        [-1, -1, 0],
        [1, -1, 0],
        [-1, 1, 0],
        [1, 0, 1],
        [-1, 0, -1],
        [1, 0, -1],
        [-1, 0, 1],
        [0, 1, 1],
        [0, -1, -1],
        [0, 1, -1],
        [0, -1, 1],
    ]
    speeds = np.array(speed_list) * 1.0
    weights = np.array([1.0 / 3.0] + [1.0 / 18.0] * 6 + [1.0 / 36.0] * 12)
    along_x = speeds[:, 0]
    along_y = speeds[:, 1]
    along_z = speeds[:, 2]
    square = along_x * along_x + along_y * along_y + along_z * along_z
    polynomials = np.stack(
        [
            np.ones(19),
            along_x,
            along_y,
            along_z,
            square,
            3 * along_x * along_x - square,
            along_y * along_y - along_z * along_z,
            along_x * along_y,
            along_y * along_z,
            along_x * along_z,
            along_x * square,
            along_y * square,
            along_z * square,
            square * square,
            (3 * along_x * along_x - square) * square,
            (along_y * along_y - along_z * along_z) * square,
            along_x * (along_y * along_y - along_z * along_z),
            along_y * (along_z * along_z - along_x * along_x),
            along_z * (along_x * along_x - along_y * along_y),
        ],
        axis=1,
    )
    columns = []
    for column_index in range(19):
        vector = polynomials[:, column_index] * 1.0
        for repeat in range(2):
            for earlier in columns:
                vector = vector - np.dot(earlier, vector) * earlier
        columns.append(vector / math.sqrt(float(np.dot(vector, vector))))
    return (speeds, weights, np.stack(columns))


def collision_scalars(rate):
    m = lattice_tables()[2]
    r = {k: rate(k - 4) for k in range(4, 19)}
    f = lambda v: float(v)
    out = {}
    for name, column in (("rest", 0), ("axis", 1), ("diag", 7)):
        for other, column2 in (("rest", 0), ("axis", 1), ("diag", 7)):
            out[name, other] = r[4] * f(m[4, column] * m[4, column2]) + r[13] * f(
                m[13, column] * m[13, column2]
            )
    a5, b5, a14, b14 = m[5, 1] / 2, m[5, 7], m[14, 1] / 2, m[14, 7]
    out["uu"] = r[5] * f(a5 * a5) + r[14] * f(a14 * a14)
    out["uv"] = r[5] * f(a5 * b5) + r[14] * f(a14 * b14)
    out["vv"] = r[5] * f(b5 * b5) + r[14] * f(b14 * b14)
    a6, b6, a15, b15 = m[6, 3], m[6, 7], m[15, 3], m[15, 7]
    out["pp"] = r[6] * f(a6 * a6) + r[15] * f(a15 * a15)
    out["pq"] = r[6] * f(a6 * b6) + r[15] * f(a15 * b15)
    out["qq"] = r[6] * f(b6 * b6) + r[15] * f(b15 * b15)
    out["sxy"] = r[7] * f(m[7, 7] ** 2)
    out["syz"] = r[8] * f(m[8, 15] ** 2)
    out["sxz"] = r[9] * f(m[9, 11] ** 2)
    for name, row, axis, diag in (("x", 10, 1, 7), ("y", 11, 3, 7), ("z", 12, 5, 11)):
        out["aa" + name] = r[row] * f(m[row, axis] ** 2)
        out["ab" + name] = r[row] * f(m[row, axis] * m[row, diag])
        out["bb" + name] = r[row] * f(m[row, diag] ** 2)
    out["tx"] = r[16] * f(m[16, 7] ** 2)
    out["ty"] = r[17] * f(m[17, 15] ** 2)
    out["tz"] = r[18] * f(m[18, 11] ** 2)
    return out


def collide(f, k):
    w1, w2 = 1.0 / 18.0, 1.0 / 36.0
    pairs = ((1, 2), (3, 4), (5, 6), (7, 8), (9, 10), (11, 12), (13, 14), (15, 16), (17, 18))
    plus = [f[i] + f[o] for i, o in pairs]
    minus = [f[i] - f[o] for i, o in pairs]
    sx, sy, sz, sa, sb, sc, sd, se, sg = plus
    dx, dy, dz, da, db, dc, dd, de, dg = minus
    density = f[0] + ((sx + sy + sz) + (sa + sb) + (sc + sd) + (se + sg))
    jx = dx + (da + db) + (dc + dd)
    jy = dy + (da - db) + (de + dg)
    jz = dz + (dc - dd) + (de - dg)
    magnitude = jx * jx + jy * jy + jz * jz
    base = density - 1.5 * magnitude
    axis_base = (2.0 * w1) * base
    diag_base = (2.0 * w2) * base
    n0 = f[0] - (1.0 / 3.0) * base
    sx = sx - (axis_base + (9.0 * w1) * (jx * jx))
    sy = sy - (axis_base + (9.0 * w1) * (jy * jy))
    sz = sz - (axis_base + (9.0 * w1) * (jz * jz))

    def diagonal(s, project):
        return s - (diag_base + (9.0 * w2) * (project * project))

    sa, sb = diagonal(sa, jx + jy), diagonal(sb, jx - jy)
    sc, sd = diagonal(sc, jx + jz), diagonal(sd, jx - jz)
    se, sg = diagonal(se, jy + jz), diagonal(sg, jy - jz)
    dx, dy, dz = dx - (6.0 * w1) * jx, dy - (6.0 * w1) * jy, dz - (6.0 * w1) * jz
    hx, hy, hz = (6.0 * w2) * jx, (6.0 * w2) * jy, (6.0 * w2) * jz
    da, db = da - (hx + hy), db - (hx - hy)
    dc, dd = dc - (hx + hz), dd - (hx - hz)
    de, dg = de - (hy + hz), dg - (hy - hz)
    exy, exz, eyz = sa + sb, sc + sd, se + sg
    axis_sum = sx + sy + sz
    diag_sum = exy + exz + eyz
    g0 = k["rest", "rest"] * n0 + k["rest", "axis"] * axis_sum + k["rest", "diag"] * diag_sum
    ga = k["axis", "rest"] * n0 + k["axis", "axis"] * axis_sum + k["axis", "diag"] * diag_sum
    gd = k["diag", "rest"] * n0 + k["diag", "axis"] * axis_sum + k["diag", "diag"] * diag_sum
    u = 2.0 * sx - sy - sz
    v = exy + exz - 2.0 * eyz
    gu = k["uu"] * u + k["uv"] * v
    gv = k["uv"] * u + k["vv"] * v
    p = sy - sz
    q = exy - exz
    gp = k["pp"] * p + k["pq"] * q
    gq = k["pq"] * p + k["qq"] * q
    ga_u, gd_v = ga - gu, gd + gv
    even = [ga + 2.0 * gu, ga_u + gp, ga_u - gp]
    gxy, gxz, gyz = gd_v + gq, gd_v - gq, gd - 2.0 * gv
    for total, one, two, rate in ((gxy, sa, sb, "sxy"), (gxz, sc, sd, "sxz"), (gyz, se, sg, "syz")):
        shear = k[rate] * (one - two)
        even += [total + shear, total - shear]
    x_xy, x_xz = da + db, dc + dd
    y_xy, y_yz = da - db, de + dg
    z_xz, z_yz = dc - dd, de - dg
    x_all, y_all, z_all = x_xy + x_xz, y_xy + y_yz, z_xz + z_yz
    ox = k["aax"] * dx + k["abx"] * x_all
    oy = k["aay"] * dy + k["aby"] * y_all
    oz = k["aaz"] * dz + k["abz"] * z_all
    bx = k["abx"] * dx + k["bbx"] * x_all
    by = k["aby"] * dy + k["bby"] * y_all
    bz = k["abz"] * dz + k["bbz"] * z_all
    tx, ty, tz = k["tx"] * (x_xy - x_xz), k["ty"] * (y_yz - y_xy), k["tz"] * (z_xz - z_yz)
    x_on_xy, x_on_xz = bx + tx, bx - tx
    y_on_yz, y_on_xy = by + ty, by - ty
    z_on_xz, z_on_yz = bz + tz, bz - tz
    odd = [ox, oy, oz]
    odd += [x_on_xy + y_on_xy, x_on_xy - y_on_xy]
    odd += [x_on_xz + z_on_xz, x_on_xz - z_on_xz]
    odd += [y_on_yz + z_on_yz, y_on_yz - z_on_yz]
    post = [f[0] - g0]
    for (i, o), even_part, odd_part in zip(pairs, even, odd):
        post += [f[i] - (even_part + odd_part), f[o] - (even_part - odd_part)]
    return post


def halves(x):
    high = x.astype(BF16)
    return high, (x - high.astype(F32)).astype(BF16)


def rows_dot(a, b):
    return lax.dot_general(a, b, (((1,), (1,)), ((), ())), preferred_element_type=F32)


def flat(x):
    return jnp.concatenate([x[s : s + 1] for s in range(8)], axis=1)


def fold(x):
    return jnp.concatenate([x[:, 128 * s : 128 * s + 128] for s in range(8)], axis=0)


def cross(a, b):
    return [a[(i + 1) % 3] * b[(i + 2) % 3] - a[(i + 2) % 3] * b[(i + 1) % 3] for i in range(3)]


def iota(shape, dim):
    return lax.broadcasted_iota(I32, shape, dim)


def pick(conditions, values, shape):
    result = jnp.zeros(shape, F32)
    for condition, value in zip(conditions, values):
        if isinstance(value, float) and value == 0.0:
            continue
        result = jnp.where(condition, value, result)
    return result


def first_kernel(
    pop_hbm,
    solid_hbm,
    cell_hbm,
    dir_hbm,
    store_hbm,
    owner_hbm,
    motion_hbm,
    centre_hbm,
    rates_hbm,
    post_ref,
    bounce_ref,
    send_ref,
    xp_ref,
    xm_ref,
    yp_ref,
    ym_ref,
    xy_ref,
    own_ref,
    pop_ref,
    solid_ref,
    cell_ref,
    dir_ref,
    store_ref,
    owner_ref,
    motion_ref,
    centre_ref,
    rates_ref,
    picked_ref,
    pop_sem,
    sems,
):
    small = (
        (cell_hbm, cell_ref),
        (dir_hbm, dir_ref),
        (store_hbm, store_ref),
        (owner_hbm, owner_ref),
        (motion_hbm, motion_ref),
        (centre_hbm, centre_ref),
        (rates_hbm, rates_ref),
        (solid_hbm, solid_ref),
    )
    copies = [pltpu.make_async_copy(a, b, sems.at[n]) for n, (a, b) in enumerate(small)]

    def plane(x):
        rows = pl.ds(x * 32, 32)
        return pltpu.make_async_copy(
            pop_hbm.at[:, rows, :], pop_ref.at[:, rows, :], pop_sem.at[x]
        )

    for copy in copies:
        copy.start()
    for x in range(4):
        plane(x).start()
    for copy in copies:
        copy.wait()
    speeds, weights, _ = lattice_tables()
    links = 1024
    place_x, place_y, place_z = (lax.axis_index(a) for a in ("gx", "gy", "gz"))
    cell = cell_ref[...]
    direction = dir_ref[...]
    store = store_ref[...]
    live = store < 32768
    row = lax.shift_right_logical(cell, 7)
    lane = cell & 127
    flat_row = flat(row)
    one = jnp.ones((16, links), BF16)
    none = jnp.zeros((16, links), BF16)

    def groups(index, value):
        index = jnp.broadcast_to(index.astype(F32), (16, links)).astype(BF16)
        return [
            jnp.where(index == (iota((16, links), 0) + 16 * g).astype(F32).astype(BF16), value, none)
            for g in range(8)
        ]

    def hot(index):
        return jnp.concatenate(groups(index, one), axis=0)

    flat_lane = flat(lane)
    rows_hot16 = hot(flat_row)
    lanes_hot16 = hot(flat_lane)
    flat_store = flat(store)
    low_hot = hot(flat_store & 127)
    by_high = jnp.dot(
        owner_ref[...].astype(F32).astype(BF16), low_hot, preferred_element_type=F32
    )
    here = iota((256, links), 0) == lax.shift_right_logical(flat_store, 7)
    body = fold(jnp.sum(jnp.where(here, by_high, 0.0), axis=0, keepdims=True))
    is_dir = [direction == i for i in range(19)]
    shape = direction.shape
    speed = [pick(is_dir, [float(s) for s in speeds[:, a]], shape) for a in range(3)]
    weight = jnp.where(direction <= 6, float(weights[1]), float(weights[7]))
    is_body = [body == float(b) for b in range(8)]
    move = [pick(is_body, [motion_ref[b, c] for b in range(8)], shape) for c in range(6)]
    middle = [pick(is_body, [centre_ref[a, b] for b in range(8)], shape) for a in range(3)]
    place = (
        lax.shift_right_logical(cell, 12) + place_x * 4,
        (row & 31) + place_y * 32,
        lane + place_z * 128,
    )
    extents = (32.0, 128.0, 1024.0)
    radius = [
        (place[a].astype(F32) + 0.5 * speed[a] - middle[a] * extents[a]) / 128.0 for a in range(3)
    ]

    spin = cross(move[3:], radius)
    normal = sum(speed[a] * (move[a] + spin[a]) for a in range(3))
    wall = 6.0 * weight * normal
    coded = jnp.where(live, direction, 0).astype(F32)
    spread = []
    for value in (coded, *halves(wall)):
        value = jnp.broadcast_to(flat(value.astype(F32)), (16, links)).astype(BF16)
        spread += groups(flat_lane, value)
    laid = rows_dot(rows_hot16, jnp.concatenate(spread, axis=0))
    bounce_ref[0] = laid[:, 0:128]
    bounce_ref[1] = laid[:, 128:256] + laid[:, 256:384]

    k = collision_scalars(lambda i: rates_ref[i])

    def block(step, carry):
        @pl.when((step & 3) == 0)
        def _():
            plane(lax.shift_right_logical(step, 2)).wait()

        rows = pl.ds(pl.multiple_of(step * 8, 8), 8)
        f = [pop_ref[i, rows, :] for i in range(19)]
        post = collide(f, k)
        fixed = solid_ref[rows, :] == 1
        post = [jnp.where(fixed, before, after) for before, after in zip(f, post)]
        code = bounce_ref[0, rows, :]
        found = jnp.zeros((8, 128), F32)
        for i in range(19):
            post_ref[i, rows, :] = post[i]
            if i:
                found = jnp.where(code == float(i), post[i], found)
        picked_ref[rows, :] = found
        bounce_ref[1, rows, :] = found - bounce_ref[1, rows, :]
        return carry

    lax.fori_loop(0, 16, block, 0, unroll=2)

    at_lane = iota((128, 128), 1)
    column = jnp.zeros((128, 128), F32)
    for n in range(5):
        column = jnp.where(at_lane == n, pltpu.roll(post_ref[ZP[n]], n + 1, 1), column)
        column = jnp.where(at_lane == 8 + n, pltpu.roll(post_ref[ZM[n]], 8 + n, 1), column)
    columns = jnp.transpose(column)
    for n in range(5):
        xp_ref[n] = post_ref[XP[n], 96:128, :]
        xm_ref[n] = post_ref[XM[n], 0:32, :]
        for x in range(4):
            yp_ref[4 * n + x : 4 * n + x + 1, :] = post_ref[YP[n], 32 * x + 31 : 32 * x + 32, :]
            ym_ref[4 * n + x : 4 * n + x + 1, :] = post_ref[YM[n], 32 * x : 32 * x + 1, :]
    yp_ref[20:24, :] = jnp.zeros((4, 128), F32)
    ym_ref[20:24, :] = jnp.zeros((4, 128), F32)
    xy_ref[...] = jnp.zeros((8, 128), F32)
    xy_ref[0:1, :] = post_ref[7, 127:128, :]
    xy_ref[1:2, :] = post_ref[8, 0:1, :]
    xy_ref[2:3, :] = post_ref[9, 96:97, :]
    xy_ref[3:4, :] = post_ref[10, 31:32, :]

    found_high, found_low = halves(picked_ref[...])
    by_row = jnp.dot(
        jnp.concatenate([found_high, found_low], axis=0), lanes_hot16, preferred_element_type=F32
    )
    by_row = jnp.where(
        iota((128, links), 0) == flat_row, by_row[0:128] + by_row[128:256], 0.0
    )
    picked = fold(jnp.sum(by_row, axis=0, keepdims=True))
    strength = jnp.where(live, 2.0 * picked - wall, 0.0)
    push = [speed[a] * strength for a in range(3)]
    sums = []
    for load in push + cross(radius, push):
        for b in range(8):
            sums.append(jnp.sum(jnp.where(is_body[b], load, 0.0), axis=0, keepdims=True))
    sums = jnp.sum(jnp.concatenate(sums, axis=0), axis=1, keepdims=True)
    sums = jnp.where(iota((48, 128), 0) == iota((48, 128), 1), sums, 0.0)
    body_row = jnp.sum(sums, axis=0, keepdims=True)
    upward = lax.rem(place_z + 1, 8)
    records = (strength, direction.astype(F32), cell.astype(F32), store.astype(F32))
    for j in range(8):
        for n, record in enumerate(records):
            send_ref[j, n] = record
        face = jnp.where(upward == j, columns[0:8], columns[8:16])
        send_ref[j, 4] = jnp.where(iota((8, 128), 0) == 5, body_row, face)
    own = owner_ref[pl.ds((place_x * 4 + place_y) * 8 + place_z, 1), :]
    own_ref[...] = jnp.zeros((8, 128), F32)
    for a in range(3):
        middle = pick([own == b for b in range(8)], [centre_ref[a, b] for b in range(8)], (1, 128))
        own_ref[a : a + 1, :] = (middle - 0.5) * (extents[a] / 128.0)


def second_kernel(got_ref, xy_ref, send_ref, total_ref):
    speeds = lattice_tables()[0]
    place_x, place_y, place_z = (lax.axis_index(a) for a in ("gx", "gy", "gz"))
    total_ref[...] = jnp.zeros_like(total_ref)
    count = iota((16, 128), 0).astype(F32)
    counts = [(count + 16.0 * g).astype(BF16) for g in range(16)]
    one = jnp.ones((16, 128), BF16)
    none = jnp.zeros((16, 128), BF16)

    def gather(peer, carry):
        strength, direction = got_ref[peer, 0], got_ref[peer, 1]
        cell, store = got_ref[peer, 2].astype(I32), got_ref[peer, 3].astype(I32)
        is_dir = [direction == float(i) for i in range(19)]
        speed = [pick(is_dir, [float(v) for v in speeds[:, a]], (8, 128)) for a in range(3)]
        place = (
            lax.shift_right_logical(cell, 12) + (place_x * 4 - 16),
            (lax.shift_right_logical(cell, 7) & 31) + (place_y * 32 - 64),
            (cell & 127) + (peer * 128 - 512),
        )
        arm = [(place[a].astype(F32) + 0.5 * speed[a]) * (1.0 / 128.0) for a in range(3)]
        push = [speed[a] * strength for a in range(3)]
        loads = push + cross(arm, push)
        upper = [load.astype(BF16).astype(F32) for load in loads]
        rows = upper + [load - part for load, part in zip(loads, upper)]
        owner = lax.shift_right_logical(store, 7)
        mine = (owner & 7) == place_z
        high = jnp.where(mine, lax.shift_right_logical(owner, 4), 255).astype(F32)
        low = ((lax.shift_right_logical(owner, 3) & 1) * 128) + (store & 127)
        low = low.astype(F32)
        left, right = [], []
        for s in range(8):

            def line(x, s=s):
                return jnp.broadcast_to(x[s : s + 1], (16, 128)).astype(BF16)

            at = line(high) == counts[0]
            left.append(jnp.concatenate([jnp.where(at, line(x), none) for x in rows], axis=0))
            at = line(low)
            right.append(
                jnp.concatenate([jnp.where(at == number, one, none) for number in counts], axis=0)
            )
        total_ref[...] += rows_dot(
            jnp.concatenate(left, axis=1), jnp.concatenate(right, axis=1)
        )
        return carry

    lax.fori_loop(0, 8, gather, 0, unroll=4)

    body_row = sum(got_ref[peer, 4, 5:6, :] for peer in range(8))
    for c in range(6):
        for e in range(2):
            lanes = slice(128 * e, 128 * e + 128)
            upper = total_ref[16 * c : 16 * c + 16, lanes]
            both = upper + total_ref[96 + 16 * c : 112 + 16 * c, lanes]
            for h in range(16):
                send_ref[2 * h + e, c : c + 1, :] = both[h : h + 1]
    last = jnp.concatenate([body_row, jnp.zeros((1, 128), F32)], axis=0)
    for j in range(32):
        send_ref[j, 6:8, :] = last

    below = got_ref[lax.rem(place_z + 7, 8), 4]
    above = got_ref[lax.rem(place_z + 1, 8), 4]
    lane = iota((1, 128), 1)

    def turned(x, by):
        return pltpu.roll(x, by, 1)

    to_xp = jnp.where(lane < 32, turned(below[1:2], 32), turned(above[1:2], 64))
    to_xm = jnp.where(lane < 32, below[2:3], turned(above[2:3], 32))
    in_row = lane & 31
    to_yp = jnp.where(in_row == 0, turned(below[3:4], 97), turned(above[3:4], 98))
    to_ym = jnp.where(in_row == 0, below[4:5], turned(above[4:5], 1))
    me = place_x * 4 + place_y
    has_xp, has_xm = place_x < 7, place_x > 0
    has_yp, has_ym = place_y < 3, place_y > 0
    for there, step, line in (
        (has_xp, 4, to_xp),
        (has_xm, -4, to_xm),
        (has_yp, 1, to_yp),
        (has_ym, -1, to_ym),
        (has_xp & has_yp, 5, xy_ref[0:1, :]),
        (has_xm & has_ym, -5, xy_ref[1:2, :]),
        (has_xp & has_ym, 3, xy_ref[2:3, :]),
        (has_xm & has_yp, -3, xy_ref[3:4, :]),
    ):

        @pl.when(there)
        def _(step=step, line=line):
            send_ref[me + step, 7:8, :] = line


def arrivals(lines):
    blank = jnp.zeros((128 - len(lines), 128), F32)
    return jnp.transpose(jnp.concatenate(lines + [blank], axis=0))


def shifted(line, cx, cy):
    by = 32 * cx + cy
    return pltpu.roll(line, by % 128, 1) if by else line


def finish(block, i, column, code, value):
    cz = int(lattice_tables()[0][i, 2])
    if cz:
        block = pltpu.roll(block, 1 if cz == 1 else 127, 1)
        at = 0 if cz == 1 else 127
        block = jnp.where(iota(block.shape, 1) == at, column, block)
    if i:
        opposite = i + 1 if i % 2 else i - 1
        block = jnp.where(code == float(opposite), value, block)
    return block


def third_kernel(post_ref, bounce_ref, got1_ref, xp_ref, xm_ref, moved_hbm, moved_ref, sems):
    speeds = lattice_tables()[0].astype(int)
    place_x, place_z = lax.axis_index("gx"), lax.axis_index("gz")
    has_xp, has_xm = place_x < 7, place_x > 0
    below = got1_ref[lax.rem(place_z + 7, 8), 4]
    above = got1_ref[lax.rem(place_z + 1, 8), 4]
    order = ZP + ZM
    lines = []
    for dirs, face in ((ZP, below), (ZM, above)):
        for n, i in enumerate(dirs):
            lines.append(shifted(face[n : n + 1], int(speeds[i, 0]), int(speeds[i, 1])))
    columns = arrivals(lines)
    copies = []
    for i in range(19):
        cx, cy, cz = (int(v) for v in speeds[i])
        planes = range(4)
        if cx and cz:
            planes = range(1, 4) if cx == 1 else range(3)
        first, last = (8 if cy == 1 else 0), (24 if cy == -1 else 32)
        for x in planes:
            source = x - cx
            rows = slice(first - cy, last - cy)
            if 0 <= source < 4:
                block = post_ref[i, 32 * source + rows.start : 32 * source + rows.stop, :]
            elif source < 0:
                block = jnp.where(has_xm, xp_ref[XP.index(i), rows, :], 0.0)
            else:
                block = jnp.where(has_xp, xm_ref[XM.index(i), rows, :], 0.0)
            rows = slice(32 * x + first, 32 * x + last)
            column = None
            if cz:
                n = order.index(i)
                column = columns[rows, n : n + 1]
            code, value = bounce_ref[0, rows, :], bounce_ref[1, rows, :]
            moved_ref[i, x, first:last, :] = finish(block, i, column, code, value)
        part = (i, slice(planes[0], planes[-1] + 1), slice(first, last))
        copy = pltpu.make_async_copy(moved_ref.at[part], moved_hbm.at[part], sems.at[i])
        copy.start()
        copies.append(copy)
    for copy in copies:
        copy.wait()


def fourth_kernel(
    partly_hbm,
    post_ref,
    bounce_ref,
    own_ref,
    got1_ref,
    got2_ref,
    xp_ref,
    xm_ref,
    yp_ref,
    ym_ref,
    motion_hbm,
    mass_hbm,
    inertia_hbm,
    moved_hbm,
    load_hbm,
    next_hbm,
    row_ref,
    edge_ref,
    load_ref,
    next_ref,
    motion_ref,
    mass_ref,
    inertia_ref,
    sems,
):
    del partly_hbm
    speeds = lattice_tables()[0].astype(int)
    place_x, place_y, place_z = (lax.axis_index(a) for a in ("gx", "gy", "gz"))
    has_xp, has_xm = place_x < 7, place_x > 0
    has_yp, has_ym = place_y < 3, place_y > 0
    me = place_x * 4 + place_y
    fetches = [
        pltpu.make_async_copy(motion_hbm, motion_ref, sems.at[0]),
        pltpu.make_async_copy(mass_hbm, mass_ref, sems.at[1]),
        pltpu.make_async_copy(inertia_hbm, inertia_ref, sems.at[2]),
    ]
    for fetch in fetches:
        fetch.start()
    copies = []

    def send(source, target):
        copy = pltpu.make_async_copy(source, target, sems.at[3 + len(copies)])
        copy.start()
        copies.append(copy)

    total = got2_ref[0]
    for j in range(1, 32):
        total = total + got2_ref[j]
    push = [total[a : a + 1] for a in range(3)]
    away = cross([own_ref[a : a + 1, :] for a in range(3)], push)
    turn = [total[3 + a : 4 + a] - away[a] for a in range(3)]
    load_ref[...] = jnp.concatenate(push + turn, axis=0)
    send(load_ref, load_hbm)

    def edge(there, step):
        line = got2_ref[jnp.where(there, me + step, me), 7:8, :]
        return jnp.where(there, line, 0.0)

    lane = iota((1, 128), 1)
    row_in_plane = lane & 31
    from_x = {1: edge(has_xm, -4), -1: edge(has_xp, 4)}
    from_y = {1: edge(has_ym, -1), -1: edge(has_yp, 1)}
    from_xy = {
        (1, 1): edge(has_xm & has_ym, -5),
        (-1, -1): edge(has_xp & has_yp, 5),
        (1, -1): edge(has_xm & has_yp, -3),
        (-1, 1): edge(has_xp & has_ym, 3),
    }
    order, lines = [], []
    for dirs, face in (
        (ZP, got1_ref[lax.rem(place_z + 7, 8), 4]),
        (ZM, got1_ref[lax.rem(place_z + 1, 8), 4]),
    ):
        for n, i in enumerate(dirs):
            cx, cy, cz = (int(v) for v in speeds[i])
            if cx == 1:
                line = from_x[1] if cz == 1 else pltpu.roll(from_x[1], 96, 1)
            elif cx == -1:
                line = pltpu.roll(from_x[-1], 96 if cz == 1 else 64, 1)
            elif cy == 1:
                came = from_y[1] if cz == 1 else pltpu.roll(from_y[1], 127, 1)
                line = jnp.where(row_in_plane == 0, came, shifted(face[n : n + 1], 0, 1))
            elif cy == -1:
                came = pltpu.roll(from_y[-1], 31 if cz == 1 else 30, 1)
                line = jnp.where(row_in_plane == 31, came, shifted(face[n : n + 1], 0, -1))
            else:
                continue
            order.append(i)
            lines.append(line)
    columns = arrivals(lines)

    at_row = iota((8, 128), 0)
    for number, i in enumerate(YP + YM):
        cx, cy, cz = (int(v) for v in speeds[i])
        first = 0 if cy == 1 else 24
        face_ref, n = (yp_ref, YP.index(i)) if cy == 1 else (ym_ref, YM.index(i))
        for x in range(4):
            source = x - cx
            if 0 <= source < 4:
                block = post_ref[i, 32 * source + first : 32 * source + first + 8, :]
                line = face_ref[4 * n + source : 4 * n + source + 1, :]
                line = jnp.where(has_ym if cy == 1 else has_yp, line, 0.0)
            else:
                if source < 0:
                    block = jnp.where(has_xm, xp_ref[XP.index(i), first : first + 8, :], 0.0)
                else:
                    block = jnp.where(has_xp, xm_ref[XM.index(i), first : first + 8, :], 0.0)
                line = from_xy[cx, cy]
            block = pltpu.roll(block, 1 if cy == 1 else 7, 0)
            block = jnp.where(at_row == (0 if cy == 1 else 7), line, block)
            rows = slice(32 * x + first, 32 * x + first + 8)
            column = None
            if cz:
                m = order.index(i)
                column = columns[rows, m : m + 1]
            code, value = bounce_ref[0, rows, :], bounce_ref[1, rows, :]
            row_ref[number, x] = finish(block, i, column, code, value)
        send(row_ref.at[number], moved_hbm.at[i, :, first : first + 8, :])
    for number, i in enumerate((11, 13, 14, 12)):
        cx = int(speeds[i, 0])
        x = 0 if cx == 1 else 3
        if cx == 1:
            block = jnp.where(has_xm, xp_ref[XP.index(i)], 0.0)
        else:
            block = jnp.where(has_xp, xm_ref[XM.index(i)], 0.0)
        rows = slice(32 * x, 32 * x + 32)
        m = order.index(i)
        code, value = bounce_ref[0, rows, :], bounce_ref[1, rows, :]
        edge_ref[number] = finish(block, i, columns[rows, m : m + 1], code, value)
        send(edge_ref.at[number], moved_hbm.at[i, x])

    for fetch in fetches:
        fetch.wait()
    at_lane = iota((8, 128), 1)
    own = jnp.where((at_lane & 7) == at_row, total[6:7], 0.0)
    body_load = jnp.zeros((8, 128), F32)
    scale = jnp.zeros((8, 128), F32)
    for c in range(6):
        here = lax.shift_right_logical(at_lane, 3) == c
        column = jnp.sum(jnp.where(here, own, 0.0), axis=1, keepdims=True)
        body_load = jnp.where(at_lane == c, column, body_load)
        for b in range(8):
            value = mass_ref[b] if c < 3 else inertia_ref[c - 3, b]
            scale = jnp.where((at_lane == c) & (at_row == b), value, scale)
    next_ref[...] = motion_ref[...] + (scale * body_load)[:, 0:6] / 32768.0
    send(next_ref, next_hbm)
    for copy in copies:
        copy.wait()


def body(
    populations,
    solid,
    link_cell,
    link_dir,
    link_store,
    store_body,
    motion,
    inv_mass,
    inv_inertia,
    centre,
    rates,
):
    vmem = pl.BlockSpec(memory_space=pltpu.VMEM)

    def array(*shape):
        return jax.ShapeDtypeStruct(shape, F32)

    params = pltpu.CompilerParams(vmem_limit_bytes=40 * 1024 * 1024)
    post, bounce, send1, xp, xm, yp, ym, xy, own = pl.pallas_call(
        first_kernel,
        out_shape=(
            array(19, 128, 128),
            array(2, 128, 128),
            array(8, 5, 8, 128),
            array(5, 32, 128),
            array(5, 32, 128),
            array(24, 128),
            array(24, 128),
            array(8, 128),
            array(8, 128),
        ),
        in_specs=[pl.BlockSpec(memory_space=pltpu.HBM)] * 9,
        out_specs=(vmem,) * 9,
        scratch_shapes=[
            pltpu.VMEM((19, 128, 128), F32),
            pltpu.VMEM((128, 128), I32),
            pltpu.VMEM((8, 128), I32),
            pltpu.VMEM((8, 128), I32),
            pltpu.VMEM((8, 128), I32),
            pltpu.VMEM((256, 128), I32),
            pltpu.SMEM((8, 6), F32),
            pltpu.SMEM((3, 8), F32),
            pltpu.SMEM((15,), F32),
            pltpu.VMEM((128, 128), F32),
            pltpu.SemaphoreType.DMA((4,)),
            pltpu.SemaphoreType.DMA((8,)),
        ],
        compiler_params=params,
        name="collide",
    )(
        *(
            pltpu.with_memory_space_constraint(x, pltpu.HBM)
            for x in (
                populations.reshape(19, 128, 128),
                solid.reshape(128, 128),
                link_cell.reshape(8, 128),
                link_dir.reshape(8, 128),
                link_store.reshape(8, 128),
                store_body.reshape(256, 128),
                motion,
                centre.T,
                rates,
            )
        )
    )

    def shift(x, axis, by):
        size = lax.axis_size(axis)
        return lax.ppermute(x, axis, [(i, (i + by) % size) for i in range(size)])

    got1 = lax.all_to_all(send1, "gz", 0, 0, tiled=True)
    send2 = pl.pallas_call(
        second_kernel,
        out_shape=array(32, 8, 128),
        in_specs=[vmem] * 2,
        out_specs=vmem,
        scratch_shapes=[pltpu.VMEM((192, 256), F32)],
        compiler_params=params,
        cost_estimate=pl.CostEstimate(
            flops=2 * 192 * 256 * 8192, bytes_accessed=4 * 4 * 8192, transcendentals=0
        ),
        name="bins",
    )(got1, xy)
    xp, xm = shift(xp, "gx", 1), shift(xm, "gx", -1)
    yp, ym = shift(yp, "gy", 1), shift(ym, "gy", -1)
    got2 = lax.all_to_all(send2, ("gx", "gy"), 0, 0, tiled=True)
    hbm = pl.BlockSpec(memory_space=pltpu.HBM)
    partly = pl.pallas_call(
        third_kernel,
        out_shape=array(19, 4, 32, 128),
        in_specs=[vmem] * 5,
        out_specs=hbm,
        scratch_shapes=[pltpu.VMEM((19, 4, 32, 128), F32), pltpu.SemaphoreType.DMA((19,))],
        compiler_params=params,
        cost_estimate=pl.CostEstimate(
            flops=19 * 16384 * 4, bytes_accessed=2 * 19 * 16384 * 4, transcendentals=0
        ),
        name="move",
    )(post, bounce, got1, xp, xm)
    moved, own_loads, motion_next = pl.pallas_call(
        fourth_kernel,
        out_shape=(array(19, 4, 32, 128), array(6, 128), array(8, 6)),
        in_specs=[hbm] + [vmem] * 9 + [hbm] * 3,
        out_specs=(hbm,) * 3,
        scratch_shapes=[
            pltpu.VMEM((10, 4, 8, 128), F32),
            pltpu.VMEM((4, 32, 128), F32),
            pltpu.VMEM((6, 128), F32),
            pltpu.VMEM((8, 6), F32),
            pltpu.VMEM((8, 6), F32),
            pltpu.SMEM((8,), F32),
            pltpu.SMEM((3, 8), F32),
            pltpu.SemaphoreType.DMA((19,)),
        ],
        input_output_aliases={0: 0},
        compiler_params=params,
        name="close",
    )(
        *(partly, post, bounce, own, got1, got2, xp, xm, yp, ym),
        *(
            pltpu.with_memory_space_constraint(x, pltpu.HBM)
            for x in (motion, inv_mass, inv_inertia.T)
        ),
    )
    return (moved, own_loads, motion_next)


def solution(mesh):
    return jax.shard_map(
        body,
        mesh=mesh,
        in_specs=(
            P(None, "gx", "gy", "gz"),
            P("gx", "gy", "gz"),
            P("gx", "gy", "gz", None),
            P("gx", "gy", "gz", None),
            P("gx", "gy", "gz", None),
            P(),
            P(),
            P(),
            P(),
            P(),
            P(),
        ),
        out_specs=(P(None, "gx", "gy", "gz"), P(None, ("gx", "gy", "gz")), P()),
        check_vma=False,
    )
```

```python
import math

import jax
import jax.numpy as jnp
import numpy as np
from jax import lax
from jax.experimental import pallas as pl
from jax.experimental.pallas import tpu as pltpu
from jax.sharding import PartitionSpec as P

F32 = jnp.float32
BF16 = jnp.bfloat16
I32 = jnp.int32

XP, XM = (1, 7, 9, 11, 13), (2, 10, 8, 14, 12)
YP, YM = (3, 7, 10, 15, 17), (4, 9, 8, 18, 16)
ZP, ZM = (5, 11, 14, 15, 18), (6, 13, 12, 17, 16)


def lattice_tables():
    speed_list = [
        [0, 0, 0],
        [1, 0, 0],
        [-1, 0, 0],
        [0, 1, 0],
        [0, -1, 0],
        [0, 0, 1],
        [0, 0, -1],
        [1, 1, 0],
        [-1, -1, 0],
        [1, -1, 0],
        [-1, 1, 0],
        [1, 0, 1],
        [-1, 0, -1],
        [1, 0, -1],
        [-1, 0, 1],
        [0, 1, 1],
        [0, -1, -1],
        [0, 1, -1],
        [0, -1, 1],
    ]
    speeds = np.array(speed_list) * 1.0
    weights = np.array([1.0 / 3.0] + [1.0 / 18.0] * 6 + [1.0 / 36.0] * 12)
    along_x = speeds[:, 0]
    along_y = speeds[:, 1]
    along_z = speeds[:, 2]
    square = along_x * along_x + along_y * along_y + along_z * along_z
    polynomials = np.stack(
        [
            np.ones(19),
            along_x,
            along_y,
            along_z,
            square,
            3 * along_x * along_x - square,
            along_y * along_y - along_z * along_z,
            along_x * along_y,
            along_y * along_z,
            along_x * along_z,
            along_x * square,
            along_y * square,
            along_z * square,
            square * square,
            (3 * along_x * along_x - square) * square,
            (along_y * along_y - along_z * along_z) * square,
            along_x * (along_y * along_y - along_z * along_z),
            along_y * (along_z * along_z - along_x * along_x),
            along_z * (along_x * along_x - along_y * along_y),
        ],
        axis=1,
    )
    columns = []
    for column_index in range(19):
        vector = polynomials[:, column_index] * 1.0
        for repeat in range(2):
            for earlier in columns:
                vector = vector - np.dot(earlier, vector) * earlier
        columns.append(vector / math.sqrt(float(np.dot(vector, vector))))
    return (speeds, weights, np.stack(columns))


def collision_scalars(rate):
    m = lattice_tables()[2]
    r = {k: rate(k - 4) for k in range(4, 19)}
    f = lambda v: float(v)
    out = {}
    for name, column in (("rest", 0), ("axis", 1), ("diag", 7)):
        for other, column2 in (("rest", 0), ("axis", 1), ("diag", 7)):
            out[name, other] = r[4] * f(m[4, column] * m[4, column2]) + r[13] * f(
                m[13, column] * m[13, column2]
            )
    a5, b5, a14, b14 = m[5, 1] / 2, m[5, 7], m[14, 1] / 2, m[14, 7]
    out["uu"] = r[5] * f(a5 * a5) + r[14] * f(a14 * a14)
    out["uv"] = r[5] * f(a5 * b5) + r[14] * f(a14 * b14)
    out["vv"] = r[5] * f(b5 * b5) + r[14] * f(b14 * b14)
    a6, b6, a15, b15 = m[6, 3], m[6, 7], m[15, 3], m[15, 7]
    out["pp"] = r[6] * f(a6 * a6) + r[15] * f(a15 * a15)
    out["pq"] = r[6] * f(a6 * b6) + r[15] * f(a15 * b15)
    out["qq"] = r[6] * f(b6 * b6) + r[15] * f(b15 * b15)
    out["sxy"] = r[7] * f(m[7, 7] ** 2)
    out["syz"] = r[8] * f(m[8, 15] ** 2)
    out["sxz"] = r[9] * f(m[9, 11] ** 2)
    for name, row, axis, diag in (("x", 10, 1, 7), ("y", 11, 3, 7), ("z", 12, 5, 11)):
        out["aa" + name] = r[row] * f(m[row, axis] ** 2)
        out["ab" + name] = r[row] * f(m[row, axis] * m[row, diag])
        out["bb" + name] = r[row] * f(m[row, diag] ** 2)
    out["tx"] = r[16] * f(m[16, 7] ** 2)
    out["ty"] = r[17] * f(m[17, 15] ** 2)
    out["tz"] = r[18] * f(m[18, 11] ** 2)
    return out


def collide(f, k):
    w1, w2 = 1.0 / 18.0, 1.0 / 36.0
    pairs = ((1, 2), (3, 4), (5, 6), (7, 8), (9, 10), (11, 12), (13, 14), (15, 16), (17, 18))
    plus = [f[i] + f[o] for i, o in pairs]
    minus = [f[i] - f[o] for i, o in pairs]
    sx, sy, sz, sa, sb, sc, sd, se, sg = plus
    dx, dy, dz, da, db, dc, dd, de, dg = minus
    density = f[0] + ((sx + sy + sz) + (sa + sb) + (sc + sd) + (se + sg))
    jx = dx + (da + db) + (dc + dd)
    jy = dy + (da - db) + (de + dg)
    jz = dz + (dc - dd) + (de - dg)
    magnitude = jx * jx + jy * jy + jz * jz
    base = density - 1.5 * magnitude
    axis_base = (2.0 * w1) * base
    diag_base = (2.0 * w2) * base
    n0 = f[0] - (1.0 / 3.0) * base
    sx = sx - (axis_base + (9.0 * w1) * (jx * jx))
    sy = sy - (axis_base + (9.0 * w1) * (jy * jy))
    sz = sz - (axis_base + (9.0 * w1) * (jz * jz))

    def diagonal(s, project):
        return s - (diag_base + (9.0 * w2) * (project * project))

    sa, sb = diagonal(sa, jx + jy), diagonal(sb, jx - jy)
    sc, sd = diagonal(sc, jx + jz), diagonal(sd, jx - jz)
    se, sg = diagonal(se, jy + jz), diagonal(sg, jy - jz)
    dx, dy, dz = dx - (6.0 * w1) * jx, dy - (6.0 * w1) * jy, dz - (6.0 * w1) * jz
    hx, hy, hz = (6.0 * w2) * jx, (6.0 * w2) * jy, (6.0 * w2) * jz
    da, db = da - (hx + hy), db - (hx - hy)
    dc, dd = dc - (hx + hz), dd - (hx - hz)
    de, dg = de - (hy + hz), dg - (hy - hz)
    exy, exz, eyz = sa + sb, sc + sd, se + sg
    axis_sum = sx + sy + sz
    diag_sum = exy + exz + eyz
    g0 = k["rest", "rest"] * n0 + k["rest", "axis"] * axis_sum + k["rest", "diag"] * diag_sum
    ga = k["axis", "rest"] * n0 + k["axis", "axis"] * axis_sum + k["axis", "diag"] * diag_sum
    gd = k["diag", "rest"] * n0 + k["diag", "axis"] * axis_sum + k["diag", "diag"] * diag_sum
    u = 2.0 * sx - sy - sz
    v = exy + exz - 2.0 * eyz
    gu = k["uu"] * u + k["uv"] * v
    gv = k["uv"] * u + k["vv"] * v
    p = sy - sz
    q = exy - exz
    gp = k["pp"] * p + k["pq"] * q
    gq = k["pq"] * p + k["qq"] * q
    ga_u, gd_v = ga - gu, gd + gv
    even = [ga + 2.0 * gu, ga_u + gp, ga_u - gp]
    gxy, gxz, gyz = gd_v + gq, gd_v - gq, gd - 2.0 * gv
    for total, one, two, rate in ((gxy, sa, sb, "sxy"), (gxz, sc, sd, "sxz"), (gyz, se, sg, "syz")):
        shear = k[rate] * (one - two)
        even += [total + shear, total - shear]
    x_xy, x_xz = da + db, dc + dd
    y_xy, y_yz = da - db, de + dg
    z_xz, z_yz = dc - dd, de - dg
    x_all, y_all, z_all = x_xy + x_xz, y_xy + y_yz, z_xz + z_yz
    ox = k["aax"] * dx + k["abx"] * x_all
    oy = k["aay"] * dy + k["aby"] * y_all
    oz = k["aaz"] * dz + k["abz"] * z_all
    bx = k["abx"] * dx + k["bbx"] * x_all
    by = k["aby"] * dy + k["bby"] * y_all
    bz = k["abz"] * dz + k["bbz"] * z_all
    tx, ty, tz = k["tx"] * (x_xy - x_xz), k["ty"] * (y_yz - y_xy), k["tz"] * (z_xz - z_yz)
    x_on_xy, x_on_xz = bx + tx, bx - tx
    y_on_yz, y_on_xy = by + ty, by - ty
    z_on_xz, z_on_yz = bz + tz, bz - tz
    odd = [ox, oy, oz]
    odd += [x_on_xy + y_on_xy, x_on_xy - y_on_xy]
    odd += [x_on_xz + z_on_xz, x_on_xz - z_on_xz]
    odd += [y_on_yz + z_on_yz, y_on_yz - z_on_yz]
    post = [f[0] - g0]
    for (i, o), even_part, odd_part in zip(pairs, even, odd):
        post += [f[i] - (even_part + odd_part), f[o] - (even_part - odd_part)]
    return post


def halves(x):
    high = x.astype(BF16)
    return high, (x - high.astype(F32)).astype(BF16)


def rows_dot(a, b):
    return lax.dot_general(a, b, (((1,), (1,)), ((), ())), preferred_element_type=F32)


def flat(x):
    return jnp.concatenate([x[s : s + 1] for s in range(8)], axis=1)


def fold(x):
    return jnp.concatenate([x[:, 128 * s : 128 * s + 128] for s in range(8)], axis=0)


def cross(a, b):
    return [a[(i + 1) % 3] * b[(i + 2) % 3] - a[(i + 2) % 3] * b[(i + 1) % 3] for i in range(3)]


def iota(shape, dim):
    return lax.broadcasted_iota(I32, shape, dim)


def pick(conditions, values, shape):
    result = jnp.zeros(shape, F32)
    for condition, value in zip(conditions, values):
        if isinstance(value, float) and value == 0.0:
            continue
        result = jnp.where(condition, value, result)
    return result


def first_kernel(
    pop_hbm,
    solid_hbm,
    cell_hbm,
    dir_hbm,
    store_hbm,
    owner_hbm,
    motion_hbm,
    centre_hbm,
    rates_hbm,
    post_ref,
    bounce_ref,
    send_ref,
    xp_ref,
    xm_ref,
    yp_ref,
    ym_ref,
    xy_ref,
    own_ref,
    pop_ref,
    solid_ref,
    cell_ref,
    dir_ref,
    store_ref,
    owner_ref,
    motion_ref,
    centre_ref,
    rates_ref,
    picked_ref,
    pop_sem,
    sems,
):
    small = (
        (cell_hbm, cell_ref),
        (dir_hbm, dir_ref),
        (store_hbm, store_ref),
        (owner_hbm, owner_ref),
        (motion_hbm, motion_ref),
        (centre_hbm, centre_ref),
        (rates_hbm, rates_ref),
        (solid_hbm, solid_ref),
    )
    copies = [pltpu.make_async_copy(a, b, sems.at[n]) for n, (a, b) in enumerate(small)]

    def plane(x):
        rows = pl.ds(x * 32, 32)
        return pltpu.make_async_copy(
            pop_hbm.at[:, rows, :], pop_ref.at[:, rows, :], pop_sem.at[x]
        )

    for copy in copies:
        copy.start()
    for x in range(4):
        plane(x).start()
    for copy in copies:
        copy.wait()
    speeds, weights, _ = lattice_tables()
    links = 1024
    place_x, place_y, place_z = (lax.axis_index(a) for a in ("gx", "gy", "gz"))
    cell = cell_ref[...]
    direction = dir_ref[...]
    store = store_ref[...]
    live = store < 32768
    row = lax.shift_right_logical(cell, 7)
    lane = cell & 127
    flat_row = flat(row)
    one = jnp.ones((16, links), BF16)
    none = jnp.zeros((16, links), BF16)

    def groups(index, value):
        index = jnp.broadcast_to(index.astype(F32), (16, links)).astype(BF16)
        return [
            jnp.where(index == (iota((16, links), 0) + 16 * g).astype(F32).astype(BF16), value, none)
            for g in range(8)
        ]

    def hot(index):
        return jnp.concatenate(groups(index, one), axis=0)

    flat_lane = flat(lane)
    rows_hot16 = hot(flat_row)
    lanes_hot16 = hot(flat_lane)
    flat_store = flat(store)
    low_hot = hot(flat_store & 127)
    by_high = jnp.dot(
        owner_ref[...].astype(F32).astype(BF16), low_hot, preferred_element_type=F32
    )
    here = iota((256, links), 0) == lax.shift_right_logical(flat_store, 7)
    body = fold(jnp.sum(jnp.where(here, by_high, 0.0), axis=0, keepdims=True))
    is_dir = [direction == i for i in range(19)]
    shape = direction.shape
    speed = [pick(is_dir, [float(s) for s in speeds[:, a]], shape) for a in range(3)]
    weight = jnp.where(direction <= 6, float(weights[1]), float(weights[7]))
    is_body = [body == float(b) for b in range(8)]
    move = [pick(is_body, [motion_ref[b, c] for b in range(8)], shape) for c in range(6)]
    middle = [pick(is_body, [centre_ref[a, b] for b in range(8)], shape) for a in range(3)]
    place = (
        lax.shift_right_logical(cell, 12) + place_x * 4,
        (row & 31) + place_y * 32,
        lane + place_z * 128,
    )
    extents = (32.0, 128.0, 1024.0)
    radius = [
        (place[a].astype(F32) + 0.5 * speed[a] - middle[a] * extents[a]) / 128.0 for a in range(3)
    ]

    spin = cross(move[3:], radius)
    normal = sum(speed[a] * (move[a] + spin[a]) for a in range(3))
    wall = 6.0 * weight * normal
    coded = jnp.where(live, direction, 0).astype(F32)
    spread = []
    for value in (coded, *halves(wall)):
        value = jnp.broadcast_to(flat(value.astype(F32)), (16, links)).astype(BF16)
        spread += groups(flat_lane, value)
    laid = rows_dot(rows_hot16, jnp.concatenate(spread, axis=0))
    bounce_ref[0] = laid[:, 0:128]
    bounce_ref[1] = laid[:, 128:256] + laid[:, 256:384]

    k = collision_scalars(lambda i: rates_ref[i])

    def block(step, carry):
        @pl.when((step & 3) == 0)
        def _():
            plane(lax.shift_right_logical(step, 2)).wait()

        rows = pl.ds(pl.multiple_of(step * 8, 8), 8)
        f = [pop_ref[i, rows, :] for i in range(19)]
        post = collide(f, k)
        fixed = solid_ref[rows, :] == 1
        post = [jnp.where(fixed, before, after) for before, after in zip(f, post)]
        code = bounce_ref[0, rows, :]
        found = jnp.zeros((8, 128), F32)
        for i in range(19):
            post_ref[i, rows, :] = post[i]
            if i:
                found = jnp.where(code == float(i), post[i], found)
        picked_ref[rows, :] = found
        bounce_ref[1, rows, :] = found - bounce_ref[1, rows, :]
        return carry

    lax.fori_loop(0, 16, block, 0, unroll=2)

    at_lane = iota((128, 128), 1)
    column = jnp.zeros((128, 128), F32)
    for n in range(5):
        column = jnp.where(at_lane == n, pltpu.roll(post_ref[ZP[n]], n + 1, 1), column)
        column = jnp.where(at_lane == 8 + n, pltpu.roll(post_ref[ZM[n]], 8 + n, 1), column)
    columns = jnp.transpose(column)
    for n in range(5):
        xp_ref[n] = post_ref[XP[n], 96:128, :]
        xm_ref[n] = post_ref[XM[n], 0:32, :]
        for x in range(4):
            yp_ref[4 * n + x : 4 * n + x + 1, :] = post_ref[YP[n], 32 * x + 31 : 32 * x + 32, :]
            ym_ref[4 * n + x : 4 * n + x + 1, :] = post_ref[YM[n], 32 * x : 32 * x + 1, :]
    yp_ref[20:24, :] = jnp.zeros((4, 128), F32)
    ym_ref[20:24, :] = jnp.zeros((4, 128), F32)
    xy_ref[...] = jnp.zeros((8, 128), F32)
    xy_ref[0:1, :] = post_ref[7, 127:128, :]
    xy_ref[1:2, :] = post_ref[8, 0:1, :]
    xy_ref[2:3, :] = post_ref[9, 96:97, :]
    xy_ref[3:4, :] = post_ref[10, 31:32, :]

    found_high, found_low = halves(picked_ref[...])
    by_row = jnp.dot(
        jnp.concatenate([found_high, found_low], axis=0), lanes_hot16, preferred_element_type=F32
    )
    by_row = jnp.where(
        iota((128, links), 0) == flat_row, by_row[0:128] + by_row[128:256], 0.0
    )
    picked = fold(jnp.sum(by_row, axis=0, keepdims=True))
    strength = jnp.where(live, 2.0 * picked - wall, 0.0)
    push = [speed[a] * strength for a in range(3)]
    sums = []
    for load in push + cross(radius, push):
        for b in range(8):
            sums.append(jnp.sum(jnp.where(is_body[b], load, 0.0), axis=0, keepdims=True))
    sums = jnp.sum(jnp.concatenate(sums, axis=0), axis=1, keepdims=True)
    sums = jnp.where(iota((48, 128), 0) == iota((48, 128), 1), sums, 0.0)
    body_row = jnp.sum(sums, axis=0, keepdims=True)
    upward = lax.rem(place_z + 1, 8)
    records = (strength, direction.astype(F32), cell.astype(F32), store.astype(F32))
    for j in range(8):
        for n, record in enumerate(records):
            send_ref[j, n] = record
        face = jnp.where(upward == j, columns[0:8], columns[8:16])
        send_ref[j, 4] = jnp.where(iota((8, 128), 0) == 5, body_row, face)
    own = owner_ref[pl.ds((place_x * 4 + place_y) * 8 + place_z, 1), :]
    own_ref[...] = jnp.zeros((8, 128), F32)
    for a in range(3):
        middle = pick([own == b for b in range(8)], [centre_ref[a, b] for b in range(8)], (1, 128))
        own_ref[a : a + 1, :] = (middle - 0.5) * (extents[a] / 128.0)


def second_kernel(got_ref, xy_ref, send_ref, total_ref):
    speeds = lattice_tables()[0]
    place_x, place_y, place_z = (lax.axis_index(a) for a in ("gx", "gy", "gz"))
    total_ref[...] = jnp.zeros_like(total_ref)
    count = iota((16, 128), 0).astype(F32)
    counts = [(count + 16.0 * g).astype(BF16) for g in range(16)]
    one = jnp.ones((16, 128), BF16)
    none = jnp.zeros((16, 128), BF16)

    def gather(peer, carry):
        strength, direction = got_ref[peer, 0], got_ref[peer, 1]
        cell, store = got_ref[peer, 2].astype(I32), got_ref[peer, 3].astype(I32)
        is_dir = [direction == float(i) for i in range(19)]
        speed = [pick(is_dir, [float(v) for v in speeds[:, a]], (8, 128)) for a in range(3)]
        place = (
            lax.shift_right_logical(cell, 12) + (place_x * 4 - 16),
            (lax.shift_right_logical(cell, 7) & 31) + (place_y * 32 - 64),
            (cell & 127) + (peer * 128 - 512),
        )
        arm = [(place[a].astype(F32) + 0.5 * speed[a]) * (1.0 / 128.0) for a in range(3)]
        push = [speed[a] * strength for a in range(3)]
        loads = push + cross(arm, push)
        upper = [load.astype(BF16).astype(F32) for load in loads]
        rows = upper + [load - part for load, part in zip(loads, upper)]
        owner = lax.shift_right_logical(store, 7)
        mine = (owner & 7) == place_z
        high = jnp.where(mine, lax.shift_right_logical(owner, 4), 255).astype(F32)
        low = ((lax.shift_right_logical(owner, 3) & 1) * 128) + (store & 127)
        low = low.astype(F32)
        left, right = [], []
        for s in range(8):

            def line(x, s=s):
                return jnp.broadcast_to(x[s : s + 1], (16, 128)).astype(BF16)

            at = line(high) == counts[0]
            left.append(jnp.concatenate([jnp.where(at, line(x), none) for x in rows], axis=0))
            at = line(low)
            right.append(
                jnp.concatenate([jnp.where(at == number, one, none) for number in counts], axis=0)
            )
        total_ref[...] += rows_dot(
            jnp.concatenate(left, axis=1), jnp.concatenate(right, axis=1)
        )
        return carry

    lax.fori_loop(0, 8, gather, 0, unroll=8)

    body_row = sum(got_ref[peer, 4, 5:6, :] for peer in range(8))
    for c in range(6):
        for e in range(2):
            lanes = slice(128 * e, 128 * e + 128)
            upper = total_ref[16 * c : 16 * c + 16, lanes]
            both = upper + total_ref[96 + 16 * c : 112 + 16 * c, lanes]
            for h in range(16):
                send_ref[2 * h + e, c : c + 1, :] = both[h : h + 1]
    last = jnp.concatenate([body_row, jnp.zeros((1, 128), F32)], axis=0)
    for j in range(32):
        send_ref[j, 6:8, :] = last

    below = got_ref[lax.rem(place_z + 7, 8), 4]
    above = got_ref[lax.rem(place_z + 1, 8), 4]
    lane = iota((1, 128), 1)

    def turned(x, by):
        return pltpu.roll(x, by, 1)

    to_xp = jnp.where(lane < 32, turned(below[1:2], 32), turned(above[1:2], 64))
    to_xm = jnp.where(lane < 32, below[2:3], turned(above[2:3], 32))
    in_row = lane & 31
    to_yp = jnp.where(in_row == 0, turned(below[3:4], 97), turned(above[3:4], 98))
    to_ym = jnp.where(in_row == 0, below[4:5], turned(above[4:5], 1))
    me = place_x * 4 + place_y
    has_xp, has_xm = place_x < 7, place_x > 0
    has_yp, has_ym = place_y < 3, place_y > 0
    for there, step, line in (
        (has_xp, 4, to_xp),
        (has_xm, -4, to_xm),
        (has_yp, 1, to_yp),
        (has_ym, -1, to_ym),
        (has_xp & has_yp, 5, xy_ref[0:1, :]),
        (has_xm & has_ym, -5, xy_ref[1:2, :]),
        (has_xp & has_ym, 3, xy_ref[2:3, :]),
        (has_xm & has_yp, -3, xy_ref[3:4, :]),
    ):

        @pl.when(there)
        def _(step=step, line=line):
            send_ref[me + step, 7:8, :] = line


def arrivals(lines):
    blank = jnp.zeros((128 - len(lines), 128), F32)
    return jnp.transpose(jnp.concatenate(lines + [blank], axis=0))


def shifted(line, cx, cy):
    by = 32 * cx + cy
    return pltpu.roll(line, by % 128, 1) if by else line


def finish(block, i, column, code, value):
    cz = int(lattice_tables()[0][i, 2])
    if cz:
        block = pltpu.roll(block, 1 if cz == 1 else 127, 1)
        at = 0 if cz == 1 else 127
        block = jnp.where(iota(block.shape, 1) == at, column, block)
    if i:
        opposite = i + 1 if i % 2 else i - 1
        block = jnp.where(code == float(opposite), value, block)
    return block


def third_kernel(
    post_ref,
    bounce_ref,
    got1_ref,
    xp_ref,
    xm_ref,
    yp_ref,
    ym_ref,
    motion_hbm,
    mass_hbm,
    inertia_hbm,
    moved_hbm,
    step_ref,
    moved_ref,
    motion_ref,
    mass_ref,
    inertia_ref,
    sems,
):
    speeds = lattice_tables()[0].astype(int)
    place_x, place_y, place_z = (lax.axis_index(a) for a in ("gx", "gy", "gz"))
    has_xp, has_xm = place_x < 7, place_x > 0
    has_yp, has_ym = place_y < 3, place_y > 0
    fetches = [
        pltpu.make_async_copy(motion_hbm, motion_ref, sems.at[23]),
        pltpu.make_async_copy(mass_hbm, mass_ref, sems.at[24]),
        pltpu.make_async_copy(inertia_hbm, inertia_ref, sems.at[25]),
    ]
    for fetch in fetches:
        fetch.start()
    below = got1_ref[lax.rem(place_z + 7, 8), 4]
    above = got1_ref[lax.rem(place_z + 1, 8), 4]
    order = ZP + ZM
    lines = []
    for dirs, face in ((ZP, below), (ZM, above)):
        for n, i in enumerate(dirs):
            lines.append(shifted(face[n : n + 1], int(speeds[i, 0]), int(speeds[i, 1])))
    columns = arrivals(lines)
    copies = []

    def send(*part):
        copy = pltpu.make_async_copy(
            moved_ref.at[part], moved_hbm.at[part], sems.at[len(copies)]
        )
        copy.start()
        copies.append(copy)

    for i in range(19):
        cx, cy, cz = (int(v) for v in speeds[i])
        for x in range(4):
            source = x - cx
            outside = not 0 <= source < 4
            if cx and cz and outside:
                continue
            first, last = (1 if cy == 1 else 0), (31 if cy == -1 else 32)
            if cy and (cz or outside):
                first, last = (8 if cy == 1 else 0), (24 if cy == -1 else 32)
            rows = slice(first - cy, last - cy)
            if not outside:
                block = post_ref[i, 32 * source + rows.start : 32 * source + rows.stop, :]
            elif source < 0:
                block = jnp.where(has_xm, xp_ref[XP.index(i), rows, :], 0.0)
            else:
                block = jnp.where(has_xp, xm_ref[XM.index(i), rows, :], 0.0)
            if cy and not (cz or outside):
                face_ref, n = (yp_ref, YP.index(i)) if cy == 1 else (ym_ref, YM.index(i))
                line = face_ref[4 * n + source : 4 * n + source + 1, :]
                line = jnp.where(has_ym if cy == 1 else has_yp, line, 0.0)
                block = jnp.concatenate([line, block] if cy == 1 else [block, line], axis=0)
                first, last = 0, 32
            rows = slice(32 * x + first, 32 * x + last)
            column = None
            if cz:
                n = order.index(i)
                column = columns[rows, n : n + 1]
            code, value = bounce_ref[0, rows, :], bounce_ref[1, rows, :]
            moved_ref[i, x, first:last, :] = finish(block, i, column, code, value)
        planes = {0: slice(0, 4), 1: slice(1, 4), -1: slice(0, 3)}[cx if cy or cz else 0]
        rows = slice(0, 32)
        if cy and cz:
            rows = slice(8, 32) if cy == 1 else slice(0, 24)
        send(i, planes, rows)
        if cx and cy:
            rows = slice(8, 32) if cy == 1 else slice(0, 24)
            x = 0 if cx == 1 else 3
            send(i, slice(x, x + 1), rows)

    for fetch in fetches:
        fetch.wait()
    at_lane, at_row = iota((8, 128), 1), iota((8, 128), 0)
    scale = jnp.zeros((8, 128), F32)
    for c in range(6):
        for b in range(8):
            value = mass_ref[b] if c < 3 else inertia_ref[c - 3, b]
            scale = jnp.where((at_lane == c) & (at_row == b), value, scale)
    step_ref[0] = scale
    step_ref[1] = jnp.concatenate([motion_ref[...], jnp.zeros((8, 122), F32)], axis=1)
    for copy in copies:
        copy.wait()


def fourth_kernel(
    partly_hbm,
    post_ref,
    bounce_ref,
    own_ref,
    got1_ref,
    got2_ref,
    xp_ref,
    xm_ref,
    yp_ref,
    ym_ref,
    step_ref,
    moved_hbm,
    load_hbm,
    next_hbm,
    row_ref,
    edge_ref,
    load_ref,
    next_ref,
    sems,
):
    del partly_hbm
    speeds = lattice_tables()[0].astype(int)
    place_x, place_y, place_z = (lax.axis_index(a) for a in ("gx", "gy", "gz"))
    has_xp, has_xm = place_x < 7, place_x > 0
    has_yp, has_ym = place_y < 3, place_y > 0
    me = place_x * 4 + place_y
    copies = []

    def send(source, target):
        copy = pltpu.make_async_copy(source, target, sems.at[len(copies)])
        copy.start()
        copies.append(copy)

    parts = [got2_ref[j] for j in range(32)]
    while len(parts) > 1:
        parts = [a + b for a, b in zip(parts[0::2], parts[1::2])]
    total = parts[0]
    push = [total[a : a + 1] for a in range(3)]
    away = cross([own_ref[a : a + 1, :] for a in range(3)], push)
    turn = [total[3 + a : 4 + a] - away[a] for a in range(3)]
    load_ref[...] = jnp.concatenate(push + turn, axis=0)
    send(load_ref, load_hbm)
    at_lane, at_row = iota((8, 128), 1), iota((8, 128), 0)
    own = jnp.where((at_lane & 7) == at_row, total[6:7], 0.0)
    body_load = jnp.zeros((8, 128), F32)
    for c in range(6):
        here = lax.shift_right_logical(at_lane, 3) == c
        column = jnp.sum(jnp.where(here, own, 0.0), axis=1, keepdims=True)
        body_load = jnp.where(at_lane == c, column, body_load)
    next_ref[...] = (step_ref[1] + step_ref[0] * body_load / 32768.0)[:, 0:6]
    send(next_ref, next_hbm)

    def edge(there, step):
        line = got2_ref[jnp.where(there, me + step, me), 7:8, :]
        return jnp.where(there, line, 0.0)

    lane = iota((1, 128), 1)
    row_in_plane = lane & 31
    from_x = {1: edge(has_xm, -4), -1: edge(has_xp, 4)}
    from_y = {1: edge(has_ym, -1), -1: edge(has_yp, 1)}
    from_xy = {
        (1, 1): edge(has_xm & has_ym, -5),
        (-1, -1): edge(has_xp & has_yp, 5),
        (1, -1): edge(has_xm & has_yp, -3),
        (-1, 1): edge(has_xp & has_ym, 3),
    }
    order, lines = [], []
    for dirs, face in (
        (ZP, got1_ref[lax.rem(place_z + 7, 8), 4]),
        (ZM, got1_ref[lax.rem(place_z + 1, 8), 4]),
    ):
        for n, i in enumerate(dirs):
            cx, cy, cz = (int(v) for v in speeds[i])
            if cx == 1:
                line = from_x[1] if cz == 1 else pltpu.roll(from_x[1], 96, 1)
            elif cx == -1:
                line = pltpu.roll(from_x[-1], 96 if cz == 1 else 64, 1)
            elif cy == 1:
                came = from_y[1] if cz == 1 else pltpu.roll(from_y[1], 127, 1)
                line = jnp.where(row_in_plane == 0, came, shifted(face[n : n + 1], 0, 1))
            elif cy == -1:
                came = pltpu.roll(from_y[-1], 31 if cz == 1 else 30, 1)
                line = jnp.where(row_in_plane == 31, came, shifted(face[n : n + 1], 0, -1))
            else:
                continue
            order.append(i)
            lines.append(line)
    columns = arrivals(lines)

    for i in (7, 9, 8, 10, 15, 17, 16, 18):
        cx, cy, cz = (int(v) for v in speeds[i])
        first = 0 if cy == 1 else 24
        face_ref, n = (yp_ref, YP.index(i)) if cy == 1 else (ym_ref, YM.index(i))
        planes = range(4) if cz else ((0,) if cx == 1 else (3,))
        for x in planes:
            source = x - cx
            if cz:
                block = post_ref[i, 32 * source + first : 32 * source + first + 8, :]
                line = face_ref[4 * n + source : 4 * n + source + 1, :]
                line = jnp.where(has_ym if cy == 1 else has_yp, line, 0.0)
            else:
                if source < 0:
                    block = jnp.where(has_xm, xp_ref[XP.index(i), first : first + 8, :], 0.0)
                else:
                    block = jnp.where(has_xp, xm_ref[XM.index(i), first : first + 8, :], 0.0)
                line = from_xy[cx, cy]
            block = pltpu.roll(block, 1 if cy == 1 else 7, 0)
            block = jnp.where(at_row == (0 if cy == 1 else 7), line, block)
            rows = slice(32 * x + first, 32 * x + first + 8)
            column = None
            if cz:
                m = order.index(i)
                column = columns[rows, m : m + 1]
            code, value = bounce_ref[0, rows, :], bounce_ref[1, rows, :]
            row_ref[i - 7, x] = finish(block, i, column, code, value)
        part = slice(planes[0], planes[-1] + 1)
        send(row_ref.at[i - 7, part], moved_hbm.at[i, part, first : first + 8, :])
    for number, i in enumerate((11, 13, 14, 12)):
        cx = int(speeds[i, 0])
        x = 0 if cx == 1 else 3
        if cx == 1:
            block = jnp.where(has_xm, xp_ref[XP.index(i)], 0.0)
        else:
            block = jnp.where(has_xp, xm_ref[XM.index(i)], 0.0)
        rows = slice(32 * x, 32 * x + 32)
        m = order.index(i)
        code, value = bounce_ref[0, rows, :], bounce_ref[1, rows, :]
        edge_ref[number] = finish(block, i, columns[rows, m : m + 1], code, value)
        send(edge_ref.at[number], moved_hbm.at[i, x])

    for copy in copies:
        copy.wait()


def body(
    populations,
    solid,
    link_cell,
    link_dir,
    link_store,
    store_body,
    motion,
    inv_mass,
    inv_inertia,
    centre,
    rates,
):
    vmem = pl.BlockSpec(memory_space=pltpu.VMEM)

    def array(*shape):
        return jax.ShapeDtypeStruct(shape, F32)

    params = pltpu.CompilerParams(vmem_limit_bytes=40 * 1024 * 1024)
    post, bounce, send1, xp, xm, yp, ym, xy, own = pl.pallas_call(
        first_kernel,
        out_shape=(
            array(19, 128, 128),
            array(2, 128, 128),
            array(8, 5, 8, 128),
            array(5, 32, 128),
            array(5, 32, 128),
            array(24, 128),
            array(24, 128),
            array(8, 128),
            array(8, 128),
        ),
        in_specs=[pl.BlockSpec(memory_space=pltpu.HBM)] * 9,
        out_specs=(vmem,) * 9,
        scratch_shapes=[
            pltpu.VMEM((19, 128, 128), F32),
            pltpu.VMEM((128, 128), I32),
            pltpu.VMEM((8, 128), I32),
            pltpu.VMEM((8, 128), I32),
            pltpu.VMEM((8, 128), I32),
            pltpu.VMEM((256, 128), I32),
            pltpu.SMEM((8, 6), F32),
            pltpu.SMEM((3, 8), F32),
            pltpu.SMEM((15,), F32),
            pltpu.VMEM((128, 128), F32),
            pltpu.SemaphoreType.DMA((4,)),
            pltpu.SemaphoreType.DMA((8,)),
        ],
        compiler_params=params,
        name="collide",
    )(
        *(
            pltpu.with_memory_space_constraint(x, pltpu.HBM)
            for x in (
                populations.reshape(19, 128, 128),
                solid.reshape(128, 128),
                link_cell.reshape(8, 128),
                link_dir.reshape(8, 128),
                link_store.reshape(8, 128),
                store_body.reshape(256, 128),
                motion,
                centre.T,
                rates,
            )
        )
    )

    def shift(x, axis, by):
        size = lax.axis_size(axis)
        return lax.ppermute(x, axis, [(i, (i + by) % size) for i in range(size)])

    got1 = lax.all_to_all(send1, "gz", 0, 0, tiled=True)
    send2 = pl.pallas_call(
        second_kernel,
        out_shape=array(32, 8, 128),
        in_specs=[vmem] * 2,
        out_specs=vmem,
        scratch_shapes=[pltpu.VMEM((192, 256), F32)],
        compiler_params=params,
        cost_estimate=pl.CostEstimate(
            flops=2 * 192 * 256 * 8192, bytes_accessed=4 * 4 * 8192, transcendentals=0
        ),
        name="bins",
    )(got1, xy)
    xp, xm = shift(xp, "gx", 1), shift(xm, "gx", -1)
    yp, ym = shift(yp, "gy", 1), shift(ym, "gy", -1)
    got2 = lax.all_to_all(send2, ("gx", "gy"), 0, 0, tiled=True)
    hbm = pl.BlockSpec(memory_space=pltpu.HBM)
    partly, step = pl.pallas_call(
        third_kernel,
        out_shape=(array(19, 4, 32, 128), array(2, 8, 128)),
        in_specs=[vmem] * 7 + [hbm] * 3,
        out_specs=(hbm, vmem),
        scratch_shapes=[
            pltpu.VMEM((19, 4, 32, 128), F32),
            pltpu.VMEM((8, 6), F32),
            pltpu.SMEM((8,), F32),
            pltpu.SMEM((3, 8), F32),
            pltpu.SemaphoreType.DMA((26,)),
        ],
        compiler_params=params,
        cost_estimate=pl.CostEstimate(
            flops=19 * 16384 * 4, bytes_accessed=2 * 19 * 16384 * 4, transcendentals=0
        ),
        name="move",
    )(
        *(post, bounce, got1, xp, xm, yp, ym),
        *(
            pltpu.with_memory_space_constraint(x, pltpu.HBM)
            for x in (motion, inv_mass, inv_inertia.T)
        ),
    )
    moved, own_loads, motion_next = pl.pallas_call(
        fourth_kernel,
        out_shape=(array(19, 4, 32, 128), array(6, 128), array(8, 6)),
        in_specs=[hbm] + [vmem] * 10,
        out_specs=(hbm,) * 3,
        scratch_shapes=[
            pltpu.VMEM((12, 4, 8, 128), F32),
            pltpu.VMEM((4, 32, 128), F32),
            pltpu.VMEM((6, 128), F32),
            pltpu.VMEM((8, 6), F32),
            pltpu.SemaphoreType.DMA((14,)),
        ],
        input_output_aliases={0: 0},
        compiler_params=params,
        name="close",
    )(partly, post, bounce, own, got1, got2, xp, xm, yp, ym, step)
    return (moved, own_loads, motion_next)


def solution(mesh):
    return jax.shard_map(
        body,
        mesh=mesh,
        in_specs=(
            P(None, "gx", "gy", "gz"),
            P("gx", "gy", "gz"),
            P("gx", "gy", "gz", None),
            P("gx", "gy", "gz", None),
            P("gx", "gy", "gz", None),
            P(),
            P(),
            P(),
            P(),
            P(),
            P(),
        ),
        out_specs=(P(None, "gx", "gy", "gz"), P(None, ("gx", "gy", "gz")), P()),
        check_vma=False,
    )
```

```python
import math

import jax
import jax.numpy as jnp
import numpy as np
from jax import lax
from jax.experimental import pallas as pl
from jax.experimental.pallas import tpu as pltpu
from jax.sharding import PartitionSpec as P

F32 = jnp.float32
BF16 = jnp.bfloat16
I32 = jnp.int32

XP, XM = (1, 7, 9, 11, 13), (2, 10, 8, 14, 12)
YP, YM = (3, 7, 10, 15, 17), (4, 9, 8, 18, 16)
ZP, ZM = (5, 11, 14, 15, 18), (6, 13, 12, 17, 16)


def lattice_tables():
    speed_list = [
        [0, 0, 0],
        [1, 0, 0],
        [-1, 0, 0],
        [0, 1, 0],
        [0, -1, 0],
        [0, 0, 1],
        [0, 0, -1],
        [1, 1, 0],
        [-1, -1, 0],
        [1, -1, 0],
        [-1, 1, 0],
        [1, 0, 1],
        [-1, 0, -1],
        [1, 0, -1],
        [-1, 0, 1],
        [0, 1, 1],
        [0, -1, -1],
        [0, 1, -1],
        [0, -1, 1],
    ]
    speeds = np.array(speed_list) * 1.0
    weights = np.array([1.0 / 3.0] + [1.0 / 18.0] * 6 + [1.0 / 36.0] * 12)
    along_x = speeds[:, 0]
    along_y = speeds[:, 1]
    along_z = speeds[:, 2]
    square = along_x * along_x + along_y * along_y + along_z * along_z
    polynomials = np.stack(
        [
            np.ones(19),
            along_x,
            along_y,
            along_z,
            square,
            3 * along_x * along_x - square,
            along_y * along_y - along_z * along_z,
            along_x * along_y,
            along_y * along_z,
            along_x * along_z,
            along_x * square,
            along_y * square,
            along_z * square,
            square * square,
            (3 * along_x * along_x - square) * square,
            (along_y * along_y - along_z * along_z) * square,
            along_x * (along_y * along_y - along_z * along_z),
            along_y * (along_z * along_z - along_x * along_x),
            along_z * (along_x * along_x - along_y * along_y),
        ],
        axis=1,
    )
    columns = []
    for column_index in range(19):
        vector = polynomials[:, column_index] * 1.0
        for repeat in range(2):
            for earlier in columns:
                vector = vector - np.dot(earlier, vector) * earlier
        columns.append(vector / math.sqrt(float(np.dot(vector, vector))))
    return (speeds, weights, np.stack(columns))


def collision_scalars(rate):
    m = lattice_tables()[2]
    r = {k: rate(k - 4) for k in range(4, 19)}
    f = lambda v: float(v)
    out = {}
    for name, column in (("rest", 0), ("axis", 1), ("diag", 7)):
        for other, column2 in (("rest", 0), ("axis", 1), ("diag", 7)):
            out[name, other] = r[4] * f(m[4, column] * m[4, column2]) + r[13] * f(
                m[13, column] * m[13, column2]
            )
    a5, b5, a14, b14 = m[5, 1] / 2, m[5, 7], m[14, 1] / 2, m[14, 7]
    out["uu"] = r[5] * f(a5 * a5) + r[14] * f(a14 * a14)
    out["uv"] = r[5] * f(a5 * b5) + r[14] * f(a14 * b14)
    out["vv"] = r[5] * f(b5 * b5) + r[14] * f(b14 * b14)
    a6, b6, a15, b15 = m[6, 3], m[6, 7], m[15, 3], m[15, 7]
    out["pp"] = r[6] * f(a6 * a6) + r[15] * f(a15 * a15)
    out["pq"] = r[6] * f(a6 * b6) + r[15] * f(a15 * b15)
    out["qq"] = r[6] * f(b6 * b6) + r[15] * f(b15 * b15)
    out["sxy"] = r[7] * f(m[7, 7] ** 2)
    out["syz"] = r[8] * f(m[8, 15] ** 2)
    out["sxz"] = r[9] * f(m[9, 11] ** 2)
    for name, row, axis, diag in (("x", 10, 1, 7), ("y", 11, 3, 7), ("z", 12, 5, 11)):
        out["aa" + name] = r[row] * f(m[row, axis] ** 2)
        out["ab" + name] = r[row] * f(m[row, axis] * m[row, diag])
        out["bb" + name] = r[row] * f(m[row, diag] ** 2)
    out["tx"] = r[16] * f(m[16, 7] ** 2)
    out["ty"] = r[17] * f(m[17, 15] ** 2)
    out["tz"] = r[18] * f(m[18, 11] ** 2)
    return out


def collide(f, k):
    w1, w2 = 1.0 / 18.0, 1.0 / 36.0
    pairs = ((1, 2), (3, 4), (5, 6), (7, 8), (9, 10), (11, 12), (13, 14), (15, 16), (17, 18))
    plus = [f[i] + f[o] for i, o in pairs]
    minus = [f[i] - f[o] for i, o in pairs]
    sx, sy, sz, sa, sb, sc, sd, se, sg = plus
    dx, dy, dz, da, db, dc, dd, de, dg = minus
    density = f[0] + ((sx + sy + sz) + (sa + sb) + (sc + sd) + (se + sg))
    jx = dx + (da + db) + (dc + dd)
    jy = dy + (da - db) + (de + dg)
    jz = dz + (dc - dd) + (de - dg)
    magnitude = jx * jx + jy * jy + jz * jz
    base = density - 1.5 * magnitude
    axis_base = (2.0 * w1) * base
    diag_base = (2.0 * w2) * base
    n0 = f[0] - (1.0 / 3.0) * base
    sx = sx - (axis_base + (9.0 * w1) * (jx * jx))
    sy = sy - (axis_base + (9.0 * w1) * (jy * jy))
    sz = sz - (axis_base + (9.0 * w1) * (jz * jz))

    def diagonal(s, project):
        return s - (diag_base + (9.0 * w2) * (project * project))

    sa, sb = diagonal(sa, jx + jy), diagonal(sb, jx - jy)
    sc, sd = diagonal(sc, jx + jz), diagonal(sd, jx - jz)
    se, sg = diagonal(se, jy + jz), diagonal(sg, jy - jz)
    dx, dy, dz = dx - (6.0 * w1) * jx, dy - (6.0 * w1) * jy, dz - (6.0 * w1) * jz
    hx, hy, hz = (6.0 * w2) * jx, (6.0 * w2) * jy, (6.0 * w2) * jz
    da, db = da - (hx + hy), db - (hx - hy)
    dc, dd = dc - (hx + hz), dd - (hx - hz)
    de, dg = de - (hy + hz), dg - (hy - hz)
    exy, exz, eyz = sa + sb, sc + sd, se + sg
    axis_sum = sx + sy + sz
    diag_sum = exy + exz + eyz
    g0 = k["rest", "rest"] * n0 + k["rest", "axis"] * axis_sum + k["rest", "diag"] * diag_sum
    ga = k["axis", "rest"] * n0 + k["axis", "axis"] * axis_sum + k["axis", "diag"] * diag_sum
    gd = k["diag", "rest"] * n0 + k["diag", "axis"] * axis_sum + k["diag", "diag"] * diag_sum
    u = 2.0 * sx - sy - sz
    v = exy + exz - 2.0 * eyz
    gu = k["uu"] * u + k["uv"] * v
    gv = k["uv"] * u + k["vv"] * v
    p = sy - sz
    q = exy - exz
    gp = k["pp"] * p + k["pq"] * q
    gq = k["pq"] * p + k["qq"] * q
    ga_u, gd_v = ga - gu, gd + gv
    even = [ga + 2.0 * gu, ga_u + gp, ga_u - gp]
    gxy, gxz, gyz = gd_v + gq, gd_v - gq, gd - 2.0 * gv
    for total, one, two, rate in ((gxy, sa, sb, "sxy"), (gxz, sc, sd, "sxz"), (gyz, se, sg, "syz")):
        shear = k[rate] * (one - two)
        even += [total + shear, total - shear]
    x_xy, x_xz = da + db, dc + dd
    y_xy, y_yz = da - db, de + dg
    z_xz, z_yz = dc - dd, de - dg
    x_all, y_all, z_all = x_xy + x_xz, y_xy + y_yz, z_xz + z_yz
    ox = k["aax"] * dx + k["abx"] * x_all
    oy = k["aay"] * dy + k["aby"] * y_all
    oz = k["aaz"] * dz + k["abz"] * z_all
    bx = k["abx"] * dx + k["bbx"] * x_all
    by = k["aby"] * dy + k["bby"] * y_all
    bz = k["abz"] * dz + k["bbz"] * z_all
    tx, ty, tz = k["tx"] * (x_xy - x_xz), k["ty"] * (y_yz - y_xy), k["tz"] * (z_xz - z_yz)
    x_on_xy, x_on_xz = bx + tx, bx - tx
    y_on_yz, y_on_xy = by + ty, by - ty
    z_on_xz, z_on_yz = bz + tz, bz - tz
    odd = [ox, oy, oz]
    odd += [x_on_xy + y_on_xy, x_on_xy - y_on_xy]
    odd += [x_on_xz + z_on_xz, x_on_xz - z_on_xz]
    odd += [y_on_yz + z_on_yz, y_on_yz - z_on_yz]
    post = [f[0] - g0]
    for (i, o), even_part, odd_part in zip(pairs, even, odd):
        post += [f[i] - (even_part + odd_part), f[o] - (even_part - odd_part)]
    return post


def halves(x):
    high = x.astype(BF16)
    return high, (x - high.astype(F32)).astype(BF16)


def rows_dot(a, b):
    return lax.dot_general(a, b, (((1,), (1,)), ((), ())), preferred_element_type=F32)


def flat(x):
    return jnp.concatenate([x[s : s + 1] for s in range(8)], axis=1)


def fold(x):
    return jnp.concatenate([x[:, 128 * s : 128 * s + 128] for s in range(8)], axis=0)


def cross(a, b):
    return [a[(i + 1) % 3] * b[(i + 2) % 3] - a[(i + 2) % 3] * b[(i + 1) % 3] for i in range(3)]


def groups(index, value):
    index = jnp.broadcast_to(index.astype(F32), value.shape).astype(BF16)
    none = jnp.zeros_like(value)
    return [
        jnp.where(index == (iota(value.shape, 0) + 16 * g).astype(F32).astype(BF16), value, none)
        for g in range(8)
    ]


def hot(index):
    return jnp.concatenate(groups(index, jnp.ones((16, index.shape[1]), BF16)), axis=0)


def iota(shape, dim):
    return lax.broadcasted_iota(I32, shape, dim)


def pick(conditions, values, shape):
    result = jnp.zeros(shape, F32)
    for condition, value in zip(conditions, values):
        if isinstance(value, float) and value == 0.0:
            continue
        result = jnp.where(condition, value, result)
    return result


def first_kernel(
    pop_hbm,
    solid_hbm,
    cell_hbm,
    dir_hbm,
    store_hbm,
    owner_hbm,
    motion_hbm,
    centre_hbm,
    rates_hbm,
    post_ref,
    bounce_ref,
    send_ref,
    xp_ref,
    xm_ref,
    yp_ref,
    ym_ref,
    xy_ref,
    own_ref,
    wall_ref,
    pop_ref,
    solid_ref,
    cell_ref,
    dir_ref,
    store_ref,
    owner_ref,
    motion_ref,
    centre_ref,
    rates_ref,
    pop_sem,
    sems,
):
    small = (
        (cell_hbm, cell_ref),
        (dir_hbm, dir_ref),
        (store_hbm, store_ref),
        (owner_hbm, owner_ref),
        (motion_hbm, motion_ref),
        (centre_hbm, centre_ref),
        (rates_hbm, rates_ref),
        (solid_hbm, solid_ref),
    )
    copies = [pltpu.make_async_copy(a, b, sems.at[n]) for n, (a, b) in enumerate(small)]

    def plane(x):
        rows = pl.ds(x * 32, 32)
        return pltpu.make_async_copy(
            pop_hbm.at[:, rows, :], pop_ref.at[:, rows, :], pop_sem.at[x]
        )

    for copy in copies:
        copy.start()
    for x in range(4):
        plane(x).start()
    for copy in copies:
        copy.wait()
    speeds, weights, _ = lattice_tables()
    links = 1024
    place_x, place_y, place_z = (lax.axis_index(a) for a in ("gx", "gy", "gz"))
    cell = cell_ref[...]
    direction = dir_ref[...]
    store = store_ref[...]
    live = store < 32768
    row = lax.shift_right_logical(cell, 7)
    lane = cell & 127
    flat_row = flat(row)
    flat_lane = flat(lane)
    rows_hot16 = hot(flat_row)
    lanes_hot16 = hot(flat_lane)
    flat_store = flat(store)
    low_hot = hot(flat_store & 127)
    by_high = jnp.dot(
        owner_ref[...].astype(F32).astype(BF16), low_hot, preferred_element_type=F32
    )
    here = iota((256, links), 0) == lax.shift_right_logical(flat_store, 7)
    body = fold(jnp.sum(jnp.where(here, by_high, 0.0), axis=0, keepdims=True))
    is_dir = [direction == i for i in range(19)]
    shape = direction.shape
    speed = [pick(is_dir, [float(s) for s in speeds[:, a]], shape) for a in range(3)]
    weight = jnp.where(direction <= 6, float(weights[1]), float(weights[7]))
    is_body = [body == float(b) for b in range(8)]
    move = [pick(is_body, [motion_ref[b, c] for b in range(8)], shape) for c in range(6)]
    middle = [pick(is_body, [centre_ref[a, b] for b in range(8)], shape) for a in range(3)]
    place = (
        lax.shift_right_logical(cell, 12) + place_x * 4,
        (row & 31) + place_y * 32,
        lane + place_z * 128,
    )
    extents = (32.0, 128.0, 1024.0)
    radius = [
        (place[a].astype(F32) + 0.5 * speed[a] - middle[a] * extents[a]) / 128.0 for a in range(3)
    ]

    spin = cross(move[3:], radius)
    normal = sum(speed[a] * (move[a] + spin[a]) for a in range(3))
    wall = 6.0 * weight * normal
    wall_ref[...] = wall
    coded = flat(jnp.where(live, direction, 0).astype(F32))
    coded = jnp.broadcast_to(coded, (16, links)).astype(BF16)
    spread = jnp.concatenate(groups(flat_lane, coded), axis=0)
    bounce_ref[0] = rows_dot(rows_hot16, spread)

    k = collision_scalars(lambda i: rates_ref[i])

    def block(step, carry):
        @pl.when((step & 3) == 0)
        def _():
            plane(lax.shift_right_logical(step, 2)).wait()

        rows = pl.ds(pl.multiple_of(step * 8, 8), 8)
        f = [pop_ref[i, rows, :] for i in range(19)]
        post = collide(f, k)
        fixed = solid_ref[rows, :] == 1
        post = [jnp.where(fixed, before, after) for before, after in zip(f, post)]
        code = bounce_ref[0, rows, :]
        found = jnp.zeros((8, 128), F32)
        for i in range(19):
            post_ref[i, rows, :] = post[i]
            if i:
                found = jnp.where(code == float(i), post[i], found)
        bounce_ref[1, rows, :] = found
        return carry

    lax.fori_loop(0, 16, block, 0, unroll=2)

    at_lane = iota((128, 128), 1)
    column = jnp.zeros((128, 128), F32)
    for n in range(5):
        column = jnp.where(at_lane == n, pltpu.roll(post_ref[ZP[n]], n + 1, 1), column)
        column = jnp.where(at_lane == 8 + n, pltpu.roll(post_ref[ZM[n]], 8 + n, 1), column)
    columns = jnp.transpose(column)
    for n in range(5):
        xp_ref[n] = post_ref[XP[n], 96:128, :]
        xm_ref[n] = post_ref[XM[n], 0:32, :]
        for x in range(4):
            yp_ref[4 * n + x : 4 * n + x + 1, :] = post_ref[YP[n], 32 * x + 31 : 32 * x + 32, :]
            ym_ref[4 * n + x : 4 * n + x + 1, :] = post_ref[YM[n], 32 * x : 32 * x + 1, :]
    yp_ref[20:24, :] = jnp.zeros((4, 128), F32)
    ym_ref[20:24, :] = jnp.zeros((4, 128), F32)
    xy_ref[...] = jnp.zeros((8, 128), F32)
    xy_ref[0:1, :] = post_ref[7, 127:128, :]
    xy_ref[1:2, :] = post_ref[8, 0:1, :]
    xy_ref[2:3, :] = post_ref[9, 96:97, :]
    xy_ref[3:4, :] = post_ref[10, 31:32, :]

    found_high, found_low = halves(bounce_ref[1])
    by_row = jnp.dot(
        jnp.concatenate([found_high, found_low], axis=0), lanes_hot16, preferred_element_type=F32
    )
    by_row = jnp.where(
        iota((128, links), 0) == flat_row, by_row[0:128] + by_row[128:256], 0.0
    )
    picked = fold(jnp.sum(by_row, axis=0, keepdims=True))
    strength = jnp.where(live, 2.0 * picked - wall, 0.0)
    push = [speed[a] * strength for a in range(3)]
    sums = []
    for load in push + cross(radius, push):
        for b in range(8):
            sums.append(jnp.sum(jnp.where(is_body[b], load, 0.0), axis=0, keepdims=True))
    sums = jnp.sum(jnp.concatenate(sums, axis=0), axis=1, keepdims=True)
    sums = jnp.where(iota((48, 128), 0) == iota((48, 128), 1), sums, 0.0)
    body_row = jnp.sum(sums, axis=0, keepdims=True)
    upward = lax.rem(place_z + 1, 8)
    records = (strength, direction.astype(F32), cell.astype(F32), store.astype(F32))
    for j in range(8):
        for n, record in enumerate(records):
            send_ref[j, n] = record
        face = jnp.where(upward == j, columns[0:8], columns[8:16])
        send_ref[j, 4] = jnp.where(iota((8, 128), 0) == 5, body_row, face)
    own = owner_ref[pl.ds((place_x * 4 + place_y) * 8 + place_z, 1), :]
    own_ref[...] = jnp.zeros((8, 128), F32)
    for a in range(3):
        middle = pick([own == b for b in range(8)], [centre_ref[a, b] for b in range(8)], (1, 128))
        own_ref[a : a + 1, :] = (middle - 0.5) * (extents[a] / 128.0)


def second_kernel(got_ref, xy_ref, send_ref, total_ref):
    speeds = lattice_tables()[0]
    place_x, place_y, place_z = (lax.axis_index(a) for a in ("gx", "gy", "gz"))
    total_ref[...] = jnp.zeros_like(total_ref)
    count = iota((16, 128), 0).astype(F32)
    counts = [(count + 16.0 * g).astype(BF16) for g in range(16)]
    one = jnp.ones((16, 128), BF16)
    none = jnp.zeros((16, 128), BF16)

    def gather(peer, carry):
        strength, direction = got_ref[peer, 0], got_ref[peer, 1]
        cell, store = got_ref[peer, 2].astype(I32), got_ref[peer, 3].astype(I32)
        is_dir = [direction == float(i) for i in range(19)]
        speed = [pick(is_dir, [float(v) for v in speeds[:, a]], (8, 128)) for a in range(3)]
        place = (
            lax.shift_right_logical(cell, 12) + (place_x * 4 - 16),
            (lax.shift_right_logical(cell, 7) & 31) + (place_y * 32 - 64),
            (cell & 127) + (peer * 128 - 512),
        )
        arm = [(place[a].astype(F32) + 0.5 * speed[a]) * (1.0 / 128.0) for a in range(3)]
        push = [speed[a] * strength for a in range(3)]
        loads = push + cross(arm, push)
        upper = [load.astype(BF16).astype(F32) for load in loads]
        rows = upper + [load - part for load, part in zip(loads, upper)]
        owner = lax.shift_right_logical(store, 7)
        mine = (owner & 7) == place_z
        high = jnp.where(mine, lax.shift_right_logical(owner, 4), 255).astype(F32)
        low = ((lax.shift_right_logical(owner, 3) & 1) * 128) + (store & 127)
        low = low.astype(F32)
        left, right = [], []
        for s in range(8):

            def line(x, s=s):
                return jnp.broadcast_to(x[s : s + 1], (16, 128)).astype(BF16)

            at = line(high) == counts[0]
            left.append(jnp.concatenate([jnp.where(at, line(x), none) for x in rows], axis=0))
            at = line(low)
            right.append(
                jnp.concatenate([jnp.where(at == number, one, none) for number in counts], axis=0)
            )
        total_ref[...] += rows_dot(
            jnp.concatenate(left, axis=1), jnp.concatenate(right, axis=1)
        )
        return carry

    lax.fori_loop(0, 8, gather, 0, unroll=8)

    body_row = sum(got_ref[peer, 4, 5:6, :] for peer in range(8))
    for c in range(6):
        for e in range(2):
            lanes = slice(128 * e, 128 * e + 128)
            upper = total_ref[16 * c : 16 * c + 16, lanes]
            both = upper + total_ref[96 + 16 * c : 112 + 16 * c, lanes]
            for h in range(16):
                send_ref[2 * h + e, c : c + 1, :] = both[h : h + 1]
    last = jnp.concatenate([body_row, jnp.zeros((1, 128), F32)], axis=0)
    for j in range(32):
        send_ref[j, 6:8, :] = last

    below = got_ref[lax.rem(place_z + 7, 8), 4]
    above = got_ref[lax.rem(place_z + 1, 8), 4]
    lane = iota((1, 128), 1)

    def turned(x, by):
        return pltpu.roll(x, by, 1)

    to_xp = jnp.where(lane < 32, turned(below[1:2], 32), turned(above[1:2], 64))
    to_xm = jnp.where(lane < 32, below[2:3], turned(above[2:3], 32))
    in_row = lane & 31
    to_yp = jnp.where(in_row == 0, turned(below[3:4], 97), turned(above[3:4], 98))
    to_ym = jnp.where(in_row == 0, below[4:5], turned(above[4:5], 1))
    me = place_x * 4 + place_y
    has_xp, has_xm = place_x < 7, place_x > 0
    has_yp, has_ym = place_y < 3, place_y > 0
    for there, step, line in (
        (has_xp, 4, to_xp),
        (has_xm, -4, to_xm),
        (has_yp, 1, to_yp),
        (has_ym, -1, to_ym),
        (has_xp & has_yp, 5, xy_ref[0:1, :]),
        (has_xm & has_ym, -5, xy_ref[1:2, :]),
        (has_xp & has_ym, 3, xy_ref[2:3, :]),
        (has_xm & has_yp, -3, xy_ref[3:4, :]),
    ):

        @pl.when(there)
        def _(step=step, line=line):
            send_ref[me + step, 7:8, :] = line


def arrivals(lines):
    blank = jnp.zeros((128 - len(lines), 128), F32)
    return jnp.transpose(jnp.concatenate(lines + [blank], axis=0))


def shifted(line, cx, cy):
    by = 32 * cx + cy
    return pltpu.roll(line, by % 128, 1) if by else line


def finish(block, i, column, code, value):
    cz = int(lattice_tables()[0][i, 2])
    if cz:
        block = pltpu.roll(block, 1 if cz == 1 else 127, 1)
        at = 0 if cz == 1 else 127
        block = jnp.where(iota(block.shape, 1) == at, column, block)
    if i:
        opposite = i + 1 if i % 2 else i - 1
        block = jnp.where(code == float(opposite), value, block)
    return block


def third_kernel(
    post_ref,
    bounce_ref,
    wall_ref,
    got1_ref,
    motion_hbm,
    mass_hbm,
    inertia_hbm,
    cell_hbm,
    moved_hbm,
    value_ref,
    step_ref,
    moved_ref,
    cell_ref,
    motion_ref,
    mass_ref,
    inertia_ref,
    sems,
):
    speeds = lattice_tables()[0].astype(int)
    place_z = lax.axis_index("gz")
    fetches = [
        pltpu.make_async_copy(motion_hbm, motion_ref, sems.at[19]),
        pltpu.make_async_copy(mass_hbm, mass_ref, sems.at[20]),
        pltpu.make_async_copy(inertia_hbm, inertia_ref, sems.at[21]),
    ]
    cells = pltpu.make_async_copy(cell_hbm, cell_ref, sems.at[22])
    cells.start()
    for fetch in fetches:
        fetch.start()
    cells.wait()
    cell = flat(cell_ref[...])
    spread = []
    for part in halves(wall_ref[...]):
        part = jnp.broadcast_to(flat(part.astype(F32)), (16, 1024)).astype(BF16)
        spread += groups(cell & 127, part)
    laid = rows_dot(hot(lax.shift_right_logical(cell, 7)), jnp.concatenate(spread, axis=0))
    value_ref[...] = bounce_ref[1] - (laid[:, 0:128] + laid[:, 128:256])
    below = got1_ref[lax.rem(place_z + 7, 8), 4]
    above = got1_ref[lax.rem(place_z + 1, 8), 4]
    order = ZP + ZM
    lines = []
    for dirs, face in ((ZP, below), (ZM, above)):
        for n, i in enumerate(dirs):
            lines.append(shifted(face[n : n + 1], int(speeds[i, 0]), int(speeds[i, 1])))
    columns = arrivals(lines)
    copies = []
    for i in range(19):
        cx, cy, cz = (int(v) for v in speeds[i])
        planes = {0: (0, 4), 1: (1, 4), -1: (0, 3)}[cx]
        first, last = {0: (0, 32), 1: (8, 32), -1: (0, 24)}[cy]
        for x in range(*planes):
            source = 32 * (x - cx) - cy
            block = post_ref[i, source + first : source + last, :]
            rows = slice(32 * x + first, 32 * x + last)
            column = None
            if cz:
                n = order.index(i)
                column = columns[rows, n : n + 1]
            code, value = bounce_ref[0, rows, :], value_ref[rows, :]
            moved_ref[i, x, first:last, :] = finish(block, i, column, code, value)
        part = (i, slice(*planes), slice(first, last))
        copy = pltpu.make_async_copy(moved_ref.at[part], moved_hbm.at[part], sems.at[i])
        copy.start()
        copies.append(copy)

    for fetch in fetches:
        fetch.wait()
    at_lane, at_row = iota((8, 128), 1), iota((8, 128), 0)
    scale = jnp.zeros((8, 128), F32)
    for c in range(6):
        for b in range(8):
            value = mass_ref[b] if c < 3 else inertia_ref[c - 3, b]
            scale = jnp.where((at_lane == c) & (at_row == b), value, scale)
    step_ref[0] = scale
    step_ref[1] = jnp.concatenate([motion_ref[...], jnp.zeros((8, 122), F32)], axis=1)
    for copy in copies:
        copy.wait()


def face_kernel(
    partly_hbm,
    post_ref,
    bounce_ref,
    value_ref,
    xp_ref,
    xm_ref,
    yp_ref,
    ym_ref,
    moved_hbm,
    moved_ref,
    sems,
):
    del partly_hbm
    speeds = lattice_tables()[0].astype(int)
    place_x, place_y = lax.axis_index("gx"), lax.axis_index("gy")
    has_xp, has_xm = place_x < 7, place_x > 0
    has_yp, has_ym = place_y < 3, place_y > 0
    copies = []

    def send(*part):
        copy = pltpu.make_async_copy(
            moved_ref.at[part], moved_hbm.at[part], sems.at[len(copies)]
        )
        copy.start()
        copies.append(copy)

    for i in (1, 2, 7, 8, 9, 10):
        cx, cy = (int(v) for v in speeds[i, :2])
        x = 0 if cx == 1 else 3
        first, last = {0: (0, 32), 1: (8, 32), -1: (0, 24)}[cy]
        there, face = (has_xm, xp_ref[XP.index(i)]) if cx == 1 else (has_xp, xm_ref[XM.index(i)])
        block = jnp.where(there, face[first - cy : last - cy], 0.0)
        rows = slice(32 * x + first, 32 * x + last)
        code, value = bounce_ref[0, rows, :], value_ref[rows, :]
        moved_ref[i, x, first:last, :] = finish(block, i, None, code, value)
        send(i, x, slice(first, last))
    at_row = iota((8, 128), 0)
    for i in (3, 4, 7, 8, 9, 10):
        cx, cy = (int(v) for v in speeds[i, :2])
        planes = {0: (0, 4), 1: (1, 4), -1: (0, 3)}[cx]
        first = 0 if cy == 1 else 24
        face_ref, n = (yp_ref, YP.index(i)) if cy == 1 else (ym_ref, YM.index(i))
        for x in range(*planes):
            source = x - cx
            block = post_ref[i, 32 * source + first : 32 * source + first + 8, :]
            line = face_ref[4 * n + source : 4 * n + source + 1, :]
            line = jnp.where(has_ym if cy == 1 else has_yp, line, 0.0)
            block = pltpu.roll(block, 1 if cy == 1 else 7, 0)
            block = jnp.where(at_row == (0 if cy == 1 else 7), line, block)
            rows = slice(32 * x + first, 32 * x + first + 8)
            code, value = bounce_ref[0, rows, :], value_ref[rows, :]
            moved_ref[i, x, first : first + 8, :] = finish(block, i, None, code, value)
        send(i, slice(*planes), slice(first, first + 8))
    for copy in copies:
        copy.wait()


def fourth_kernel(
    partly_hbm,
    post_ref,
    bounce_ref,
    value_ref,
    own_ref,
    got1_ref,
    got2_ref,
    xp_ref,
    xm_ref,
    yp_ref,
    ym_ref,
    step_ref,
    moved_hbm,
    load_hbm,
    next_hbm,
    row_ref,
    edge_ref,
    load_ref,
    next_ref,
    sems,
):
    del partly_hbm
    speeds = lattice_tables()[0].astype(int)
    place_x, place_y, place_z = (lax.axis_index(a) for a in ("gx", "gy", "gz"))
    has_xp, has_xm = place_x < 7, place_x > 0
    has_yp, has_ym = place_y < 3, place_y > 0
    me = place_x * 4 + place_y
    copies = []

    def send(source, target):
        copy = pltpu.make_async_copy(source, target, sems.at[len(copies)])
        copy.start()
        copies.append(copy)

    parts = [got2_ref[j] for j in range(32)]
    while len(parts) > 1:
        parts = [a + b for a, b in zip(parts[0::2], parts[1::2])]
    total = parts[0]
    push = [total[a : a + 1] for a in range(3)]
    away = cross([own_ref[a : a + 1, :] for a in range(3)], push)
    turn = [total[3 + a : 4 + a] - away[a] for a in range(3)]
    load_ref[...] = jnp.concatenate(push + turn, axis=0)
    send(load_ref, load_hbm)
    at_lane, at_row = iota((8, 128), 1), iota((8, 128), 0)
    own = jnp.where((at_lane & 7) == at_row, total[6:7], 0.0)
    body_load = jnp.zeros((8, 128), F32)
    for c in range(6):
        here = lax.shift_right_logical(at_lane, 3) == c
        column = jnp.sum(jnp.where(here, own, 0.0), axis=1, keepdims=True)
        body_load = jnp.where(at_lane == c, column, body_load)
    next_ref[...] = (step_ref[1] + step_ref[0] * body_load / 32768.0)[:, 0:6]
    send(next_ref, next_hbm)

    def edge(there, step):
        line = got2_ref[jnp.where(there, me + step, me), 7:8, :]
        return jnp.where(there, line, 0.0)

    lane = iota((1, 128), 1)
    row_in_plane = lane & 31
    from_x = {1: edge(has_xm, -4), -1: edge(has_xp, 4)}
    from_y = {1: edge(has_ym, -1), -1: edge(has_yp, 1)}
    from_xy = {
        (1, 1): edge(has_xm & has_ym, -5),
        (-1, -1): edge(has_xp & has_yp, 5),
        (1, -1): edge(has_xm & has_yp, -3),
        (-1, 1): edge(has_xp & has_ym, 3),
    }
    order, lines = [], []
    for dirs, face in (
        (ZP, got1_ref[lax.rem(place_z + 7, 8), 4]),
        (ZM, got1_ref[lax.rem(place_z + 1, 8), 4]),
    ):
        for n, i in enumerate(dirs):
            cx, cy, cz = (int(v) for v in speeds[i])
            if cx == 1:
                line = from_x[1] if cz == 1 else pltpu.roll(from_x[1], 96, 1)
            elif cx == -1:
                line = pltpu.roll(from_x[-1], 96 if cz == 1 else 64, 1)
            elif cy == 1:
                came = from_y[1] if cz == 1 else pltpu.roll(from_y[1], 127, 1)
                line = jnp.where(row_in_plane == 0, came, shifted(face[n : n + 1], 0, 1))
            elif cy == -1:
                came = pltpu.roll(from_y[-1], 31 if cz == 1 else 30, 1)
                line = jnp.where(row_in_plane == 31, came, shifted(face[n : n + 1], 0, -1))
            else:
                continue
            order.append(i)
            lines.append(line)
    columns = arrivals(lines)

    for i in (7, 9, 8, 10, 15, 17, 16, 18):
        cx, cy, cz = (int(v) for v in speeds[i])
        first = 0 if cy == 1 else 24
        face_ref, n = (yp_ref, YP.index(i)) if cy == 1 else (ym_ref, YM.index(i))
        planes = range(4) if cz else ((0,) if cx == 1 else (3,))
        for x in planes:
            source = x - cx
            if cz:
                block = post_ref[i, 32 * source + first : 32 * source + first + 8, :]
                line = face_ref[4 * n + source : 4 * n + source + 1, :]
                line = jnp.where(has_ym if cy == 1 else has_yp, line, 0.0)
            else:
                if source < 0:
                    block = jnp.where(has_xm, xp_ref[XP.index(i), first : first + 8, :], 0.0)
                else:
                    block = jnp.where(has_xp, xm_ref[XM.index(i), first : first + 8, :], 0.0)
                line = from_xy[cx, cy]
            block = pltpu.roll(block, 1 if cy == 1 else 7, 0)
            block = jnp.where(at_row == (0 if cy == 1 else 7), line, block)
            rows = slice(32 * x + first, 32 * x + first + 8)
            column = None
            if cz:
                m = order.index(i)
                column = columns[rows, m : m + 1]
            code, value = bounce_ref[0, rows, :], value_ref[rows, :]
            row_ref[i - 7, x] = finish(block, i, column, code, value)
        part = slice(planes[0], planes[-1] + 1)
        send(row_ref.at[i - 7, part], moved_hbm.at[i, part, first : first + 8, :])
    for number, i in enumerate((11, 13, 14, 12)):
        cx = int(speeds[i, 0])
        x = 0 if cx == 1 else 3
        if cx == 1:
            block = jnp.where(has_xm, xp_ref[XP.index(i)], 0.0)
        else:
            block = jnp.where(has_xp, xm_ref[XM.index(i)], 0.0)
        rows = slice(32 * x, 32 * x + 32)
        m = order.index(i)
        code, value = bounce_ref[0, rows, :], value_ref[rows, :]
        edge_ref[number] = finish(block, i, columns[rows, m : m + 1], code, value)
        send(edge_ref.at[number], moved_hbm.at[i, x])

    for copy in copies:
        copy.wait()


def body(
    populations,
    solid,
    link_cell,
    link_dir,
    link_store,
    store_body,
    motion,
    inv_mass,
    inv_inertia,
    centre,
    rates,
):
    vmem = pl.BlockSpec(memory_space=pltpu.VMEM)

    def array(*shape):
        return jax.ShapeDtypeStruct(shape, F32)

    params = pltpu.CompilerParams(vmem_limit_bytes=40 * 1024 * 1024)
    post, bounce, send1, xp, xm, yp, ym, xy, own, wall = pl.pallas_call(
        first_kernel,
        out_shape=(
            array(19, 128, 128),
            array(2, 128, 128),
            array(8, 5, 8, 128),
            array(5, 32, 128),
            array(5, 32, 128),
            array(24, 128),
            array(24, 128),
            array(8, 128),
            array(8, 128),
            array(8, 128),
        ),
        in_specs=[pl.BlockSpec(memory_space=pltpu.HBM)] * 9,
        out_specs=(vmem,) * 10,
        scratch_shapes=[
            pltpu.VMEM((19, 128, 128), F32),
            pltpu.VMEM((128, 128), I32),
            pltpu.VMEM((8, 128), I32),
            pltpu.VMEM((8, 128), I32),
            pltpu.VMEM((8, 128), I32),
            pltpu.VMEM((256, 128), I32),
            pltpu.SMEM((8, 6), F32),
            pltpu.SMEM((3, 8), F32),
            pltpu.SMEM((15,), F32),
            pltpu.SemaphoreType.DMA((4,)),
            pltpu.SemaphoreType.DMA((8,)),
        ],
        compiler_params=params,
        name="collide",
    )(
        *(
            pltpu.with_memory_space_constraint(x, pltpu.HBM)
            for x in (
                populations.reshape(19, 128, 128),
                solid.reshape(128, 128),
                link_cell.reshape(8, 128),
                link_dir.reshape(8, 128),
                link_store.reshape(8, 128),
                store_body.reshape(256, 128),
                motion,
                centre.T,
                rates,
            )
        )
    )

    def shift(x, axis, by):
        size = lax.axis_size(axis)
        return lax.ppermute(x, axis, [(i, (i + by) % size) for i in range(size)])

    got1 = lax.all_to_all(send1, "gz", 0, 0, tiled=True)
    send2 = pl.pallas_call(
        second_kernel,
        out_shape=array(32, 8, 128),
        in_specs=[vmem] * 2,
        out_specs=vmem,
        scratch_shapes=[pltpu.VMEM((192, 256), F32)],
        compiler_params=params,
        cost_estimate=pl.CostEstimate(
            flops=2 * 192 * 256 * 8192, bytes_accessed=4 * 4 * 8192, transcendentals=0
        ),
        name="bins",
    )(got1, xy)
    xp, xm = shift(xp, "gx", 1), shift(xm, "gx", -1)
    yp, ym = shift(yp, "gy", 1), shift(ym, "gy", -1)
    got2 = lax.all_to_all(send2, ("gx", "gy"), 0, 0, tiled=True)
    hbm = pl.BlockSpec(memory_space=pltpu.HBM)
    partly, value, step = pl.pallas_call(
        third_kernel,
        out_shape=(array(19, 4, 32, 128), array(128, 128), array(2, 8, 128)),
        in_specs=[vmem] * 4 + [hbm] * 4,
        out_specs=(hbm, vmem, vmem),
        scratch_shapes=[
            pltpu.VMEM((19, 4, 32, 128), F32),
            pltpu.VMEM((8, 128), I32),
            pltpu.VMEM((8, 6), F32),
            pltpu.SMEM((8,), F32),
            pltpu.SMEM((3, 8), F32),
            pltpu.SemaphoreType.DMA((23,)),
        ],
        compiler_params=params,
        cost_estimate=pl.CostEstimate(
            flops=19 * 16384 * 4, bytes_accessed=2 * 19 * 16384 * 4, transcendentals=0
        ),
        name="move",
    )(
        *(post, bounce, wall, got1),
        *(
            pltpu.with_memory_space_constraint(x, pltpu.HBM)
            for x in (motion, inv_mass, inv_inertia.T, link_cell.reshape(8, 128))
        ),
    )
    partly = pl.pallas_call(
        face_kernel,
        out_shape=array(19, 4, 32, 128),
        in_specs=[hbm] + [vmem] * 7,
        out_specs=hbm,
        scratch_shapes=[pltpu.VMEM((19, 4, 32, 128), F32), pltpu.SemaphoreType.DMA((12,))],
        input_output_aliases={0: 0},
        compiler_params=params,
        name="faces",
    )(partly, post, bounce, value, xp, xm, yp, ym)
    moved, own_loads, motion_next = pl.pallas_call(
        fourth_kernel,
        out_shape=(array(19, 4, 32, 128), array(6, 128), array(8, 6)),
        in_specs=[hbm] + [vmem] * 11,
        out_specs=(hbm,) * 3,
        scratch_shapes=[
            pltpu.VMEM((12, 4, 8, 128), F32),
            pltpu.VMEM((4, 32, 128), F32),
            pltpu.VMEM((6, 128), F32),
            pltpu.VMEM((8, 6), F32),
            pltpu.SemaphoreType.DMA((14,)),
        ],
        input_output_aliases={0: 0},
        compiler_params=params,
        name="close",
    )(partly, post, bounce, value, own, got1, got2, xp, xm, yp, ym, step)
    return (moved, own_loads, motion_next)


def solution(mesh):
    return jax.shard_map(
        body,
        mesh=mesh,
        in_specs=(
            P(None, "gx", "gy", "gz"),
            P("gx", "gy", "gz"),
            P("gx", "gy", "gz", None),
            P("gx", "gy", "gz", None),
            P("gx", "gy", "gz", None),
            P(),
            P(),
            P(),
            P(),
            P(),
            P(),
        ),
        out_specs=(P(None, "gx", "gy", "gz"), P(None, ("gx", "gy", "gz")), P()),
        check_vma=False,
    )
```

```python
import math

import jax
import jax.numpy as jnp
import numpy as np
from jax import lax
from jax.experimental import pallas as pl
from jax.experimental.pallas import tpu as pltpu
from jax.sharding import PartitionSpec as P

F32 = jnp.float32
BF16 = jnp.bfloat16
I32 = jnp.int32

XP, XM = (1, 7, 9, 11, 13), (2, 10, 8, 14, 12)
YP, YM = (3, 7, 10, 15, 17), (4, 9, 8, 18, 16)
ZP, ZM = (5, 11, 14, 15, 18), (6, 13, 12, 17, 16)


def lattice_tables():
    speed_list = [
        [0, 0, 0],
        [1, 0, 0],
        [-1, 0, 0],
        [0, 1, 0],
        [0, -1, 0],
        [0, 0, 1],
        [0, 0, -1],
        [1, 1, 0],
        [-1, -1, 0],
        [1, -1, 0],
        [-1, 1, 0],
        [1, 0, 1],
        [-1, 0, -1],
        [1, 0, -1],
        [-1, 0, 1],
        [0, 1, 1],
        [0, -1, -1],
        [0, 1, -1],
        [0, -1, 1],
    ]
    speeds = np.array(speed_list) * 1.0
    weights = np.array([1.0 / 3.0] + [1.0 / 18.0] * 6 + [1.0 / 36.0] * 12)
    along_x = speeds[:, 0]
    along_y = speeds[:, 1]
    along_z = speeds[:, 2]
    square = along_x * along_x + along_y * along_y + along_z * along_z
    polynomials = np.stack(
        [
            np.ones(19),
            along_x,
            along_y,
            along_z,
            square,
            3 * along_x * along_x - square,
            along_y * along_y - along_z * along_z,
            along_x * along_y,
            along_y * along_z,
            along_x * along_z,
            along_x * square,
            along_y * square,
            along_z * square,
            square * square,
            (3 * along_x * along_x - square) * square,
            (along_y * along_y - along_z * along_z) * square,
            along_x * (along_y * along_y - along_z * along_z),
            along_y * (along_z * along_z - along_x * along_x),
            along_z * (along_x * along_x - along_y * along_y),
        ],
        axis=1,
    )
    columns = []
    for column_index in range(19):
        vector = polynomials[:, column_index] * 1.0
        for repeat in range(2):
            for earlier in columns:
                vector = vector - np.dot(earlier, vector) * earlier
        columns.append(vector / math.sqrt(float(np.dot(vector, vector))))
    return (speeds, weights, np.stack(columns))


def collision_scalars(rate):
    m = lattice_tables()[2]
    r = {k: rate(k - 4) for k in range(4, 19)}
    f = lambda v: float(v)
    out = {}
    for name, column in (("rest", 0), ("axis", 1), ("diag", 7)):
        for other, column2 in (("rest", 0), ("axis", 1), ("diag", 7)):
            out[name, other] = r[4] * f(m[4, column] * m[4, column2]) + r[13] * f(
                m[13, column] * m[13, column2]
            )
    a5, b5, a14, b14 = m[5, 1] / 2, m[5, 7], m[14, 1] / 2, m[14, 7]
    out["uu"] = r[5] * f(a5 * a5) + r[14] * f(a14 * a14)
    out["uv"] = r[5] * f(a5 * b5) + r[14] * f(a14 * b14)
    out["vv"] = r[5] * f(b5 * b5) + r[14] * f(b14 * b14)
    a6, b6, a15, b15 = m[6, 3], m[6, 7], m[15, 3], m[15, 7]
    out["pp"] = r[6] * f(a6 * a6) + r[15] * f(a15 * a15)
    out["pq"] = r[6] * f(a6 * b6) + r[15] * f(a15 * b15)
    out["qq"] = r[6] * f(b6 * b6) + r[15] * f(b15 * b15)
    out["sxy"] = r[7] * f(m[7, 7] ** 2)
    out["syz"] = r[8] * f(m[8, 15] ** 2)
    out["sxz"] = r[9] * f(m[9, 11] ** 2)
    for name, row, axis, diag in (("x", 10, 1, 7), ("y", 11, 3, 7), ("z", 12, 5, 11)):
        out["aa" + name] = r[row] * f(m[row, axis] ** 2)
        out["ab" + name] = r[row] * f(m[row, axis] * m[row, diag])
        out["bb" + name] = r[row] * f(m[row, diag] ** 2)
    out["tx"] = r[16] * f(m[16, 7] ** 2)
    out["ty"] = r[17] * f(m[17, 15] ** 2)
    out["tz"] = r[18] * f(m[18, 11] ** 2)
    return out


def collide(f, k):
    w1, w2 = 1.0 / 18.0, 1.0 / 36.0
    pairs = ((1, 2), (3, 4), (5, 6), (7, 8), (9, 10), (11, 12), (13, 14), (15, 16), (17, 18))
    plus = [f[i] + f[o] for i, o in pairs]
    minus = [f[i] - f[o] for i, o in pairs]
    sx, sy, sz, sa, sb, sc, sd, se, sg = plus
    dx, dy, dz, da, db, dc, dd, de, dg = minus
    density = f[0] + ((sx + sy + sz) + (sa + sb) + (sc + sd) + (se + sg))
    jx = dx + (da + db) + (dc + dd)
    jy = dy + (da - db) + (de + dg)
    jz = dz + (dc - dd) + (de - dg)
    magnitude = jx * jx + jy * jy + jz * jz
    base = density - 1.5 * magnitude
    axis_base = (2.0 * w1) * base
    diag_base = (2.0 * w2) * base
    n0 = f[0] - (1.0 / 3.0) * base
    sx = sx - (axis_base + (9.0 * w1) * (jx * jx))
    sy = sy - (axis_base + (9.0 * w1) * (jy * jy))
    sz = sz - (axis_base + (9.0 * w1) * (jz * jz))

    def diagonal(s, project):
        return s - (diag_base + (9.0 * w2) * (project * project))

    sa, sb = diagonal(sa, jx + jy), diagonal(sb, jx - jy)
    sc, sd = diagonal(sc, jx + jz), diagonal(sd, jx - jz)
    se, sg = diagonal(se, jy + jz), diagonal(sg, jy - jz)
    dx, dy, dz = dx - (6.0 * w1) * jx, dy - (6.0 * w1) * jy, dz - (6.0 * w1) * jz
    hx, hy, hz = (6.0 * w2) * jx, (6.0 * w2) * jy, (6.0 * w2) * jz
    da, db = da - (hx + hy), db - (hx - hy)
    dc, dd = dc - (hx + hz), dd - (hx - hz)
    de, dg = de - (hy + hz), dg - (hy - hz)
    exy, exz, eyz = sa + sb, sc + sd, se + sg
    axis_sum = sx + sy + sz
    diag_sum = exy + exz + eyz
    g0 = k["rest", "rest"] * n0 + k["rest", "axis"] * axis_sum + k["rest", "diag"] * diag_sum
    ga = k["axis", "rest"] * n0 + k["axis", "axis"] * axis_sum + k["axis", "diag"] * diag_sum
    gd = k["diag", "rest"] * n0 + k["diag", "axis"] * axis_sum + k["diag", "diag"] * diag_sum
    u = 2.0 * sx - sy - sz
    v = exy + exz - 2.0 * eyz
    gu = k["uu"] * u + k["uv"] * v
    gv = k["uv"] * u + k["vv"] * v
    p = sy - sz
    q = exy - exz
    gp = k["pp"] * p + k["pq"] * q
    gq = k["pq"] * p + k["qq"] * q
    ga_u, gd_v = ga - gu, gd + gv
    even = [ga + 2.0 * gu, ga_u + gp, ga_u - gp]
    gxy, gxz, gyz = gd_v + gq, gd_v - gq, gd - 2.0 * gv
    for total, one, two, rate in ((gxy, sa, sb, "sxy"), (gxz, sc, sd, "sxz"), (gyz, se, sg, "syz")):
        shear = k[rate] * (one - two)
        even += [total + shear, total - shear]
    x_xy, x_xz = da + db, dc + dd
    y_xy, y_yz = da - db, de + dg
    z_xz, z_yz = dc - dd, de - dg
    x_all, y_all, z_all = x_xy + x_xz, y_xy + y_yz, z_xz + z_yz
    ox = k["aax"] * dx + k["abx"] * x_all
    oy = k["aay"] * dy + k["aby"] * y_all
    oz = k["aaz"] * dz + k["abz"] * z_all
    bx = k["abx"] * dx + k["bbx"] * x_all
    by = k["aby"] * dy + k["bby"] * y_all
    bz = k["abz"] * dz + k["bbz"] * z_all
    tx, ty, tz = k["tx"] * (x_xy - x_xz), k["ty"] * (y_yz - y_xy), k["tz"] * (z_xz - z_yz)
    x_on_xy, x_on_xz = bx + tx, bx - tx
    y_on_yz, y_on_xy = by + ty, by - ty
    z_on_xz, z_on_yz = bz + tz, bz - tz
    odd = [ox, oy, oz]
    odd += [x_on_xy + y_on_xy, x_on_xy - y_on_xy]
    odd += [x_on_xz + z_on_xz, x_on_xz - z_on_xz]
    odd += [y_on_yz + z_on_yz, y_on_yz - z_on_yz]
    post = [f[0] - g0]
    for (i, o), even_part, odd_part in zip(pairs, even, odd):
        post += [f[i] - (even_part + odd_part), f[o] - (even_part - odd_part)]
    return post


def halves(x):
    high = x.astype(BF16)
    return high, (x - high.astype(F32)).astype(BF16)


def rows_dot(a, b):
    return lax.dot_general(a, b, (((1,), (1,)), ((), ())), preferred_element_type=F32)


def flat(x):
    return jnp.concatenate([x[s : s + 1] for s in range(8)], axis=1)


def fold(x):
    return jnp.concatenate([x[:, 128 * s : 128 * s + 128] for s in range(8)], axis=0)


def cross(a, b):
    return [a[(i + 1) % 3] * b[(i + 2) % 3] - a[(i + 2) % 3] * b[(i + 1) % 3] for i in range(3)]


def groups(index, value):
    index = jnp.broadcast_to(index.astype(F32), value.shape).astype(BF16)
    none = jnp.zeros_like(value)
    return [
        jnp.where(index == (iota(value.shape, 0) + 16 * g).astype(F32).astype(BF16), value, none)
        for g in range(8)
    ]


def hot(index):
    return jnp.concatenate(groups(index, jnp.ones((16, index.shape[1]), BF16)), axis=0)


def iota(shape, dim):
    return lax.broadcasted_iota(I32, shape, dim)


def pick(conditions, values, shape):
    result = jnp.zeros(shape, F32)
    for condition, value in zip(conditions, values):
        if isinstance(value, float) and value == 0.0:
            continue
        result = jnp.where(condition, value, result)
    return result


def first_kernel(
    pop_hbm,
    solid_hbm,
    cell_hbm,
    dir_hbm,
    store_hbm,
    owner_hbm,
    motion_hbm,
    centre_hbm,
    rates_hbm,
    post_ref,
    bounce_ref,
    send_ref,
    xp_ref,
    xm_ref,
    yp_ref,
    ym_ref,
    xy_ref,
    own_ref,
    wall_ref,
    pop_ref,
    solid_ref,
    cell_ref,
    dir_ref,
    store_ref,
    owner_ref,
    motion_ref,
    centre_ref,
    rates_ref,
    pop_sem,
    sems,
):
    small = (
        (cell_hbm, cell_ref),
        (dir_hbm, dir_ref),
        (store_hbm, store_ref),
        (owner_hbm, owner_ref),
        (motion_hbm, motion_ref),
        (centre_hbm, centre_ref),
        (rates_hbm, rates_ref),
        (solid_hbm, solid_ref),
    )
    copies = [pltpu.make_async_copy(a, b, sems.at[n]) for n, (a, b) in enumerate(small)]

    def plane(x):
        rows = pl.ds(x * 32, 32)
        return pltpu.make_async_copy(
            pop_hbm.at[:, rows, :], pop_ref.at[:, rows, :], pop_sem.at[x]
        )

    for copy in copies:
        copy.start()
    for x in range(4):
        plane(x).start()
    for copy in copies[0:3]:
        copy.wait()
    speeds, weights, _ = lattice_tables()
    links = 1024
    place_x, place_y, place_z = (lax.axis_index(a) for a in ("gx", "gy", "gz"))
    cell = cell_ref[...]
    direction = dir_ref[...]
    store = store_ref[...]
    live = store < 32768
    row = lax.shift_right_logical(cell, 7)
    lane = cell & 127
    flat_row = flat(row)
    flat_lane = flat(lane)
    rows_hot16 = hot(flat_row)
    lanes_hot16 = hot(flat_lane)
    flat_store = flat(store)
    low_hot = hot(flat_store & 127)
    for copy in copies[3:6]:
        copy.wait()
    by_high = jnp.dot(
        owner_ref[...].astype(F32).astype(BF16), low_hot, preferred_element_type=F32
    )
    here = iota((256, links), 0) == lax.shift_right_logical(flat_store, 7)
    body = fold(jnp.sum(jnp.where(here, by_high, 0.0), axis=0, keepdims=True))
    is_dir = [direction == i for i in range(19)]
    shape = direction.shape
    speed = [pick(is_dir, [float(s) for s in speeds[:, a]], shape) for a in range(3)]
    weight = jnp.where(direction <= 6, float(weights[1]), float(weights[7]))
    is_body = [body == float(b) for b in range(8)]
    move = [pick(is_body, [motion_ref[b, c] for b in range(8)], shape) for c in range(6)]
    middle = [pick(is_body, [centre_ref[a, b] for b in range(8)], shape) for a in range(3)]
    place = (
        lax.shift_right_logical(cell, 12) + place_x * 4,
        (row & 31) + place_y * 32,
        lane + place_z * 128,
    )
    extents = (32.0, 128.0, 1024.0)
    radius = [
        (place[a].astype(F32) + 0.5 * speed[a] - middle[a] * extents[a]) / 128.0 for a in range(3)
    ]

    spin = cross(move[3:], radius)
    normal = sum(speed[a] * (move[a] + spin[a]) for a in range(3))
    wall = 6.0 * weight * normal
    wall_ref[...] = wall
    coded = flat(jnp.where(live, direction, 0).astype(F32))
    coded = jnp.broadcast_to(coded, (16, links)).astype(BF16)
    spread = jnp.concatenate(groups(flat_lane, coded), axis=0)
    bounce_ref[0] = rows_dot(rows_hot16, spread)

    for copy in copies[6:8]:
        copy.wait()
    k = collision_scalars(lambda i: rates_ref[i])

    def block(step, carry):
        rows = pl.ds(pl.multiple_of(step * 8, 8), 8)
        f = [pop_ref[i, rows, :] for i in range(19)]
        post = collide(f, k)
        fixed = solid_ref[rows, :] == 1
        post = [jnp.where(fixed, before, after) for before, after in zip(f, post)]
        code = bounce_ref[0, rows, :]
        found = jnp.zeros((8, 128), F32)
        for i in range(19):
            post_ref[i, rows, :] = post[i]
            if i:
                found = jnp.where(code == float(i), post[i], found)
        bounce_ref[1, rows, :] = found
        return carry

    def slab(x, carry):
        plane(x).wait()
        for part in range(4):
            block(x * 4 + part, 0)
        return carry

    lax.fori_loop(0, 4, slab, 0)

    at_lane = iota((128, 128), 1)
    column = jnp.zeros((128, 128), F32)
    for n in range(5):
        column = jnp.where(at_lane == n, pltpu.roll(post_ref[ZP[n]], n + 1, 1), column)
        column = jnp.where(at_lane == 8 + n, pltpu.roll(post_ref[ZM[n]], 8 + n, 1), column)
    columns = jnp.transpose(column)
    for n in range(5):
        xp_ref[n] = post_ref[XP[n], 96:128, :]
        xm_ref[n] = post_ref[XM[n], 0:32, :]
        for x in range(4):
            yp_ref[4 * n + x : 4 * n + x + 1, :] = post_ref[YP[n], 32 * x + 31 : 32 * x + 32, :]
            ym_ref[4 * n + x : 4 * n + x + 1, :] = post_ref[YM[n], 32 * x : 32 * x + 1, :]
    yp_ref[20:24, :] = jnp.zeros((4, 128), F32)
    ym_ref[20:24, :] = jnp.zeros((4, 128), F32)
    xy_ref[...] = jnp.zeros((8, 128), F32)
    xy_ref[0:1, :] = post_ref[7, 127:128, :]
    xy_ref[1:2, :] = post_ref[8, 0:1, :]
    xy_ref[2:3, :] = post_ref[9, 96:97, :]
    xy_ref[3:4, :] = post_ref[10, 31:32, :]

    found_high, found_low = halves(bounce_ref[1])
    by_row = jnp.dot(
        jnp.concatenate([found_high, found_low], axis=0), lanes_hot16, preferred_element_type=F32
    )
    by_row = jnp.where(
        iota((128, links), 0) == flat_row, by_row[0:128] + by_row[128:256], 0.0
    )
    picked = fold(jnp.sum(by_row, axis=0, keepdims=True))
    strength = jnp.where(live, 2.0 * picked - wall, 0.0)
    push = [speed[a] * strength for a in range(3)]
    sums = []
    for load in push + cross(radius, push):
        for b in range(8):
            sums.append(jnp.sum(jnp.where(is_body[b], load, 0.0), axis=0, keepdims=True))
    sums = jnp.sum(jnp.concatenate(sums, axis=0), axis=1, keepdims=True)
    sums = jnp.where(iota((48, 128), 0) == iota((48, 128), 1), sums, 0.0)
    body_row = jnp.sum(sums, axis=0, keepdims=True)
    upward = lax.rem(place_z + 1, 8)
    records = (strength, direction.astype(F32), cell.astype(F32), store.astype(F32))
    for j in range(8):
        for n, record in enumerate(records):
            send_ref[j, n] = record
        face = jnp.where(upward == j, columns[0:8], columns[8:16])
        send_ref[j, 4] = jnp.where(iota((8, 128), 0) == 5, body_row, face)
    own = owner_ref[pl.ds((place_x * 4 + place_y) * 8 + place_z, 1), :]
    own_ref[...] = jnp.zeros((8, 128), F32)
    for a in range(3):
        middle = pick([own == b for b in range(8)], [centre_ref[a, b] for b in range(8)], (1, 128))
        own_ref[a : a + 1, :] = (middle - 0.5) * (extents[a] / 128.0)


def second_kernel(got_ref, xy_ref, send_ref, total_ref):
    speeds = lattice_tables()[0]
    place_x, place_y, place_z = (lax.axis_index(a) for a in ("gx", "gy", "gz"))
    total_ref[...] = jnp.zeros_like(total_ref)
    count = iota((16, 128), 0).astype(F32)
    counts = [(count + 16.0 * g).astype(BF16) for g in range(16)]
    one = jnp.ones((16, 128), BF16)
    none = jnp.zeros((16, 128), BF16)

    def gather(peer, carry):
        strength, direction = got_ref[peer, 0], got_ref[peer, 1]
        cell, store = got_ref[peer, 2].astype(I32), got_ref[peer, 3].astype(I32)
        is_dir = [direction == float(i) for i in range(19)]
        speed = [pick(is_dir, [float(v) for v in speeds[:, a]], (8, 128)) for a in range(3)]
        place = (
            lax.shift_right_logical(cell, 12) + (place_x * 4 - 16),
            (lax.shift_right_logical(cell, 7) & 31) + (place_y * 32 - 64),
            (cell & 127) + (peer * 128 - 512),
        )
        arm = [(place[a].astype(F32) + 0.5 * speed[a]) * (1.0 / 128.0) for a in range(3)]
        push = [speed[a] * strength for a in range(3)]
        loads = push + cross(arm, push)
        upper = [load.astype(BF16).astype(F32) for load in loads]
        rows = upper + [load - part for load, part in zip(loads, upper)]
        owner = lax.shift_right_logical(store, 7)
        mine = (owner & 7) == place_z
        high = jnp.where(mine, lax.shift_right_logical(owner, 4), 255).astype(F32)
        low = ((lax.shift_right_logical(owner, 3) & 1) * 128) + (store & 127)
        low = low.astype(F32)
        left, right = [], []
        for s in range(8):

            def line(x, s=s):
                return jnp.broadcast_to(x[s : s + 1], (16, 128)).astype(BF16)

            at = line(high) == counts[0]
            left.append(jnp.concatenate([jnp.where(at, line(x), none) for x in rows], axis=0))
            at = line(low)
            right.append(
                jnp.concatenate([jnp.where(at == number, one, none) for number in counts], axis=0)
            )
        total_ref[...] += rows_dot(
            jnp.concatenate(left, axis=1), jnp.concatenate(right, axis=1)
        )
        return carry

    lax.fori_loop(0, 8, gather, 0, unroll=8)

    body_row = sum(got_ref[peer, 4, 5:6, :] for peer in range(8))
    for c in range(6):
        for e in range(2):
            lanes = slice(128 * e, 128 * e + 128)
            upper = total_ref[16 * c : 16 * c + 16, lanes]
            both = upper + total_ref[96 + 16 * c : 112 + 16 * c, lanes]
            for h in range(16):
                send_ref[2 * h + e, c : c + 1, :] = both[h : h + 1]
    last = jnp.concatenate([body_row, jnp.zeros((1, 128), F32)], axis=0)
    for j in range(32):
        send_ref[j, 6:8, :] = last

    below = got_ref[lax.rem(place_z + 7, 8), 4]
    above = got_ref[lax.rem(place_z + 1, 8), 4]
    lane = iota((1, 128), 1)

    def turned(x, by):
        return pltpu.roll(x, by, 1)

    to_xp = jnp.where(lane < 32, turned(below[1:2], 32), turned(above[1:2], 64))
    to_xm = jnp.where(lane < 32, below[2:3], turned(above[2:3], 32))
    in_row = lane & 31
    to_yp = jnp.where(in_row == 0, turned(below[3:4], 97), turned(above[3:4], 98))
    to_ym = jnp.where(in_row == 0, below[4:5], turned(above[4:5], 1))
    me = place_x * 4 + place_y
    has_xp, has_xm = place_x < 7, place_x > 0
    has_yp, has_ym = place_y < 3, place_y > 0
    for there, step, line in (
        (has_xp, 4, to_xp),
        (has_xm, -4, to_xm),
        (has_yp, 1, to_yp),
        (has_ym, -1, to_ym),
        (has_xp & has_yp, 5, xy_ref[0:1, :]),
        (has_xm & has_ym, -5, xy_ref[1:2, :]),
        (has_xp & has_ym, 3, xy_ref[2:3, :]),
        (has_xm & has_yp, -3, xy_ref[3:4, :]),
    ):

        @pl.when(there)
        def _(step=step, line=line):
            send_ref[me + step, 7:8, :] = line


def arrivals(lines):
    blank = jnp.zeros((128 - len(lines), 128), F32)
    return jnp.transpose(jnp.concatenate(lines + [blank], axis=0))


def shifted(line, cx, cy):
    by = 32 * cx + cy
    return pltpu.roll(line, by % 128, 1) if by else line


def finish(block, i, column, code, value):
    cz = int(lattice_tables()[0][i, 2])
    if cz:
        block = pltpu.roll(block, 1 if cz == 1 else 127, 1)
        at = 0 if cz == 1 else 127
        block = jnp.where(iota(block.shape, 1) == at, column, block)
    if i:
        opposite = i + 1 if i % 2 else i - 1
        block = jnp.where(code == float(opposite), value, block)
    return block


def third_kernel(
    post_ref,
    bounce_ref,
    wall_ref,
    got1_ref,
    motion_hbm,
    mass_hbm,
    inertia_hbm,
    cell_hbm,
    moved_hbm,
    value_ref,
    step_ref,
    moved_ref,
    cell_ref,
    motion_ref,
    mass_ref,
    inertia_ref,
    sems,
):
    speeds = lattice_tables()[0].astype(int)
    place_z = lax.axis_index("gz")
    fetches = [
        pltpu.make_async_copy(motion_hbm, motion_ref, sems.at[19]),
        pltpu.make_async_copy(mass_hbm, mass_ref, sems.at[20]),
        pltpu.make_async_copy(inertia_hbm, inertia_ref, sems.at[21]),
    ]
    cells = pltpu.make_async_copy(cell_hbm, cell_ref, sems.at[22])
    cells.start()
    for fetch in fetches:
        fetch.start()
    cells.wait()
    cell = flat(cell_ref[...])
    spread = []
    for part in halves(wall_ref[...]):
        part = jnp.broadcast_to(flat(part.astype(F32)), (16, 1024)).astype(BF16)
        spread += groups(cell & 127, part)
    laid = rows_dot(hot(lax.shift_right_logical(cell, 7)), jnp.concatenate(spread, axis=0))
    value_ref[...] = bounce_ref[1] - (laid[:, 0:128] + laid[:, 128:256])
    below = got1_ref[lax.rem(place_z + 7, 8), 4]
    above = got1_ref[lax.rem(place_z + 1, 8), 4]
    order = ZP + ZM
    lines = []
    for dirs, face in ((ZP, below), (ZM, above)):
        for n, i in enumerate(dirs):
            lines.append(shifted(face[n : n + 1], int(speeds[i, 0]), int(speeds[i, 1])))
    columns = arrivals(lines)
    copies = []
    for i in range(19):
        cx, cy, cz = (int(v) for v in speeds[i])
        planes = {0: (0, 4), 1: (1, 4), -1: (0, 3)}[cx]
        first, last = {0: (0, 32), 1: (8, 32), -1: (0, 24)}[cy]
        for x in range(*planes):
            source = 32 * (x - cx) - cy
            block = post_ref[i, source + first : source + last, :]
            rows = slice(32 * x + first, 32 * x + last)
            column = None
            if cz:
                n = order.index(i)
                column = columns[rows, n : n + 1]
            code, value = bounce_ref[0, rows, :], value_ref[rows, :]
            moved_ref[i, x, first:last, :] = finish(block, i, column, code, value)
        part = (i, slice(*planes), slice(first, last))
        copy = pltpu.make_async_copy(moved_ref.at[part], moved_hbm.at[part], sems.at[i])
        copy.start()
        copies.append(copy)

    for fetch in fetches:
        fetch.wait()
    at_lane, at_row = iota((8, 128), 1), iota((8, 128), 0)
    scale = jnp.zeros((8, 128), F32)
    for c in range(6):
        for b in range(8):
            value = mass_ref[b] if c < 3 else inertia_ref[c - 3, b]
            scale = jnp.where((at_lane == c) & (at_row == b), value, scale)
    step_ref[0] = scale
    step_ref[1] = jnp.concatenate([motion_ref[...], jnp.zeros((8, 122), F32)], axis=1)
    for copy in copies:
        copy.wait()


def face_kernel(
    partly_hbm,
    post_ref,
    bounce_ref,
    value_ref,
    xp_ref,
    xm_ref,
    yp_ref,
    ym_ref,
    moved_hbm,
    moved_ref,
    sems,
):
    del partly_hbm
    speeds = lattice_tables()[0].astype(int)
    place_x, place_y = lax.axis_index("gx"), lax.axis_index("gy")
    has_xp, has_xm = place_x < 7, place_x > 0
    has_yp, has_ym = place_y < 3, place_y > 0
    copies = []

    def send(*part):
        copy = pltpu.make_async_copy(
            moved_ref.at[part], moved_hbm.at[part], sems.at[len(copies)]
        )
        copy.start()
        copies.append(copy)

    for i in (1, 2, 7, 8, 9, 10):
        cx, cy = (int(v) for v in speeds[i, :2])
        x = 0 if cx == 1 else 3
        first, last = {0: (0, 32), 1: (8, 32), -1: (0, 24)}[cy]
        there, face = (has_xm, xp_ref[XP.index(i)]) if cx == 1 else (has_xp, xm_ref[XM.index(i)])
        block = jnp.where(there, face[first - cy : last - cy], 0.0)
        rows = slice(32 * x + first, 32 * x + last)
        code, value = bounce_ref[0, rows, :], value_ref[rows, :]
        moved_ref[i, x, first:last, :] = finish(block, i, None, code, value)
        send(i, x, slice(first, last))
    at_row = iota((8, 128), 0)
    for i in (3, 4, 7, 8, 9, 10):
        cx, cy = (int(v) for v in speeds[i, :2])
        planes = {0: (0, 4), 1: (1, 4), -1: (0, 3)}[cx]
        first = 0 if cy == 1 else 24
        face_ref, n = (yp_ref, YP.index(i)) if cy == 1 else (ym_ref, YM.index(i))
        for x in range(*planes):
            source = x - cx
            block = post_ref[i, 32 * source + first : 32 * source + first + 8, :]
            line = face_ref[4 * n + source : 4 * n + source + 1, :]
            line = jnp.where(has_ym if cy == 1 else has_yp, line, 0.0)
            block = pltpu.roll(block, 1 if cy == 1 else 7, 0)
            block = jnp.where(at_row == (0 if cy == 1 else 7), line, block)
            rows = slice(32 * x + first, 32 * x + first + 8)
            code, value = bounce_ref[0, rows, :], value_ref[rows, :]
            moved_ref[i, x, first : first + 8, :] = finish(block, i, None, code, value)
        send(i, slice(*planes), slice(first, first + 8))
    for copy in copies:
        copy.wait()


def fourth_kernel(
    partly_hbm,
    post_ref,
    bounce_ref,
    value_ref,
    own_ref,
    got1_ref,
    got2_ref,
    xp_ref,
    xm_ref,
    yp_ref,
    ym_ref,
    step_ref,
    moved_hbm,
    load_hbm,
    next_hbm,
    row_ref,
    edge_ref,
    load_ref,
    next_ref,
    sems,
):
    del partly_hbm
    speeds = lattice_tables()[0].astype(int)
    place_x, place_y, place_z = (lax.axis_index(a) for a in ("gx", "gy", "gz"))
    has_xp, has_xm = place_x < 7, place_x > 0
    has_yp, has_ym = place_y < 3, place_y > 0
    me = place_x * 4 + place_y
    copies = []

    def send(source, target):
        copy = pltpu.make_async_copy(source, target, sems.at[len(copies)])
        copy.start()
        copies.append(copy)

    parts = [got2_ref[j] for j in range(32)]
    while len(parts) > 1:
        parts = [a + b for a, b in zip(parts[0::2], parts[1::2])]
    total = parts[0]
    push = [total[a : a + 1] for a in range(3)]
    away = cross([own_ref[a : a + 1, :] for a in range(3)], push)
    turn = [total[3 + a : 4 + a] - away[a] for a in range(3)]
    load_ref[...] = jnp.concatenate(push + turn, axis=0)
    send(load_ref, load_hbm)
    at_lane, at_row = iota((8, 128), 1), iota((8, 128), 0)
    own = jnp.where((at_lane & 7) == at_row, total[6:7], 0.0)
    body_load = jnp.zeros((8, 128), F32)
    for c in range(6):
        here = lax.shift_right_logical(at_lane, 3) == c
        column = jnp.sum(jnp.where(here, own, 0.0), axis=1, keepdims=True)
        body_load = jnp.where(at_lane == c, column, body_load)
    next_ref[...] = (step_ref[1] + step_ref[0] * body_load / 32768.0)[:, 0:6]
    send(next_ref, next_hbm)

    def edge(there, step):
        line = got2_ref[jnp.where(there, me + step, me), 7:8, :]
        return jnp.where(there, line, 0.0)

    lane = iota((1, 128), 1)
    row_in_plane = lane & 31
    from_x = {1: edge(has_xm, -4), -1: edge(has_xp, 4)}
    from_y = {1: edge(has_ym, -1), -1: edge(has_yp, 1)}
    from_xy = {
        (1, 1): edge(has_xm & has_ym, -5),
        (-1, -1): edge(has_xp & has_yp, 5),
        (1, -1): edge(has_xm & has_yp, -3),
        (-1, 1): edge(has_xp & has_ym, 3),
    }
    order, lines = [], []
    for dirs, face in (
        (ZP, got1_ref[lax.rem(place_z + 7, 8), 4]),
        (ZM, got1_ref[lax.rem(place_z + 1, 8), 4]),
    ):
        for n, i in enumerate(dirs):
            cx, cy, cz = (int(v) for v in speeds[i])
            if cx == 1:
                line = from_x[1] if cz == 1 else pltpu.roll(from_x[1], 96, 1)
            elif cx == -1:
                line = pltpu.roll(from_x[-1], 96 if cz == 1 else 64, 1)
            elif cy == 1:
                came = from_y[1] if cz == 1 else pltpu.roll(from_y[1], 127, 1)
                line = jnp.where(row_in_plane == 0, came, shifted(face[n : n + 1], 0, 1))
            elif cy == -1:
                came = pltpu.roll(from_y[-1], 31 if cz == 1 else 30, 1)
                line = jnp.where(row_in_plane == 31, came, shifted(face[n : n + 1], 0, -1))
            else:
                continue
            order.append(i)
            lines.append(line)
    columns = arrivals(lines)

    for i in (7, 9, 8, 10, 15, 17, 16, 18):
        cx, cy, cz = (int(v) for v in speeds[i])
        first = 0 if cy == 1 else 24
        face_ref, n = (yp_ref, YP.index(i)) if cy == 1 else (ym_ref, YM.index(i))
        planes = range(4) if cz else ((0,) if cx == 1 else (3,))
        for x in planes:
            source = x - cx
            if cz:
                block = post_ref[i, 32 * source + first : 32 * source + first + 8, :]
                line = face_ref[4 * n + source : 4 * n + source + 1, :]
                line = jnp.where(has_ym if cy == 1 else has_yp, line, 0.0)
            else:
                if source < 0:
                    block = jnp.where(has_xm, xp_ref[XP.index(i), first : first + 8, :], 0.0)
                else:
                    block = jnp.where(has_xp, xm_ref[XM.index(i), first : first + 8, :], 0.0)
                line = from_xy[cx, cy]
            block = pltpu.roll(block, 1 if cy == 1 else 7, 0)
            block = jnp.where(at_row == (0 if cy == 1 else 7), line, block)
            rows = slice(32 * x + first, 32 * x + first + 8)
            column = None
            if cz:
                m = order.index(i)
                column = columns[rows, m : m + 1]
            code, value = bounce_ref[0, rows, :], value_ref[rows, :]
            row_ref[i - 7, x] = finish(block, i, column, code, value)
        part = slice(planes[0], planes[-1] + 1)
        send(row_ref.at[i - 7, part], moved_hbm.at[i, part, first : first + 8, :])
    for number, i in enumerate((11, 13, 14, 12)):
        cx = int(speeds[i, 0])
        x = 0 if cx == 1 else 3
        if cx == 1:
            block = jnp.where(has_xm, xp_ref[XP.index(i)], 0.0)
        else:
            block = jnp.where(has_xp, xm_ref[XM.index(i)], 0.0)
        rows = slice(32 * x, 32 * x + 32)
        m = order.index(i)
        code, value = bounce_ref[0, rows, :], value_ref[rows, :]
        edge_ref[number] = finish(block, i, columns[rows, m : m + 1], code, value)
        send(edge_ref.at[number], moved_hbm.at[i, x])

    for copy in copies:
        copy.wait()


def body(
    populations,
    solid,
    link_cell,
    link_dir,
    link_store,
    store_body,
    motion,
    inv_mass,
    inv_inertia,
    centre,
    rates,
):
    vmem = pl.BlockSpec(memory_space=pltpu.VMEM)

    def array(*shape):
        return jax.ShapeDtypeStruct(shape, F32)

    params = pltpu.CompilerParams(vmem_limit_bytes=40 * 1024 * 1024)
    post, bounce, send1, xp, xm, yp, ym, xy, own, wall = pl.pallas_call(
        first_kernel,
        out_shape=(
            array(19, 128, 128),
            array(2, 128, 128),
            array(8, 5, 8, 128),
            array(5, 32, 128),
            array(5, 32, 128),
            array(24, 128),
            array(24, 128),
            array(8, 128),
            array(8, 128),
            array(8, 128),
        ),
        in_specs=[pl.BlockSpec(memory_space=pltpu.HBM)] * 9,
        out_specs=(vmem,) * 10,
        scratch_shapes=[
            pltpu.VMEM((19, 128, 128), F32),
            pltpu.VMEM((128, 128), I32),
            pltpu.VMEM((8, 128), I32),
            pltpu.VMEM((8, 128), I32),
            pltpu.VMEM((8, 128), I32),
            pltpu.VMEM((256, 128), I32),
            pltpu.SMEM((8, 6), F32),
            pltpu.SMEM((3, 8), F32),
            pltpu.SMEM((15,), F32),
            pltpu.SemaphoreType.DMA((4,)),
            pltpu.SemaphoreType.DMA((8,)),
        ],
        compiler_params=params,
        name="collide",
    )(
        *(
            pltpu.with_memory_space_constraint(x, pltpu.HBM)
            for x in (
                populations.reshape(19, 128, 128),
                solid.reshape(128, 128),
                link_cell.reshape(8, 128),
                link_dir.reshape(8, 128),
                link_store.reshape(8, 128),
                store_body.reshape(256, 128),
                motion,
                centre.T,
                rates,
            )
        )
    )

    def shift(x, axis, by):
        size = lax.axis_size(axis)
        return lax.ppermute(x, axis, [(i, (i + by) % size) for i in range(size)])

    got1 = lax.all_to_all(send1, "gz", 0, 0, tiled=True)
    send2 = pl.pallas_call(
        second_kernel,
        out_shape=array(32, 8, 128),
        in_specs=[vmem] * 2,
        out_specs=vmem,
        scratch_shapes=[pltpu.VMEM((192, 256), F32)],
        compiler_params=params,
        cost_estimate=pl.CostEstimate(
            flops=2 * 192 * 256 * 8192, bytes_accessed=4 * 4 * 8192, transcendentals=0
        ),
        name="bins",
    )(got1, xy)
    xp, xm = shift(xp, "gx", 1), shift(xm, "gx", -1)
    yp, ym = shift(yp, "gy", 1), shift(ym, "gy", -1)
    got2 = lax.all_to_all(send2, ("gx", "gy"), 0, 0, tiled=True)
    hbm = pl.BlockSpec(memory_space=pltpu.HBM)
    partly, value, step = pl.pallas_call(
        third_kernel,
        out_shape=(array(19, 4, 32, 128), array(128, 128), array(2, 8, 128)),
        in_specs=[vmem] * 4 + [hbm] * 4,
        out_specs=(hbm, vmem, vmem),
        scratch_shapes=[
            pltpu.VMEM((19, 4, 32, 128), F32),
            pltpu.VMEM((8, 128), I32),
            pltpu.VMEM((8, 6), F32),
            pltpu.SMEM((8,), F32),
            pltpu.SMEM((3, 8), F32),
            pltpu.SemaphoreType.DMA((23,)),
        ],
        compiler_params=params,
        cost_estimate=pl.CostEstimate(
            flops=19 * 16384 * 4, bytes_accessed=2 * 19 * 16384 * 4, transcendentals=0
        ),
        name="move",
    )(
        *(post, bounce, wall, got1),
        *(
            pltpu.with_memory_space_constraint(x, pltpu.HBM)
            for x in (motion, inv_mass, inv_inertia.T, link_cell.reshape(8, 128))
        ),
    )
    partly = pl.pallas_call(
        face_kernel,
        out_shape=array(19, 4, 32, 128),
        in_specs=[hbm] + [vmem] * 7,
        out_specs=hbm,
        scratch_shapes=[pltpu.VMEM((19, 4, 32, 128), F32), pltpu.SemaphoreType.DMA((12,))],
        input_output_aliases={0: 0},
        compiler_params=params,
        name="faces",
    )(partly, post, bounce, value, xp, xm, yp, ym)
    moved, own_loads, motion_next = pl.pallas_call(
        fourth_kernel,
        out_shape=(array(19, 4, 32, 128), array(6, 128), array(8, 6)),
        in_specs=[hbm] + [vmem] * 11,
        out_specs=(hbm,) * 3,
        scratch_shapes=[
            pltpu.VMEM((12, 4, 8, 128), F32),
            pltpu.VMEM((4, 32, 128), F32),
            pltpu.VMEM((6, 128), F32),
            pltpu.VMEM((8, 6), F32),
            pltpu.SemaphoreType.DMA((14,)),
        ],
        input_output_aliases={0: 0},
        compiler_params=params,
        name="close",
    )(partly, post, bounce, value, own, got1, got2, xp, xm, yp, ym, step)
    return (moved, own_loads, motion_next)


def solution(mesh):
    return jax.shard_map(
        body,
        mesh=mesh,
        in_specs=(
            P(None, "gx", "gy", "gz"),
            P("gx", "gy", "gz"),
            P("gx", "gy", "gz", None),
            P("gx", "gy", "gz", None),
            P("gx", "gy", "gz", None),
            P(),
            P(),
            P(),
            P(),
            P(),
            P(),
        ),
        out_specs=(P(None, "gx", "gy", "gz"), P(None, ("gx", "gy", "gz")), P()),
        check_vma=False,
    )
```

```python
import math

import jax
import jax.numpy as jnp
import numpy as np
from jax import lax
from jax.experimental import pallas as pl
from jax.experimental.pallas import tpu as pltpu
from jax.sharding import PartitionSpec as P

F32 = jnp.float32
BF16 = jnp.bfloat16
I32 = jnp.int32

XP, XM = (1, 7, 9, 11, 13), (2, 10, 8, 14, 12)
YP, YM = (3, 7, 10, 15, 17), (4, 9, 8, 18, 16)
ZP, ZM = (5, 11, 14, 15, 18), (6, 13, 12, 17, 16)


def lattice_tables():
    speed_list = [
        [0, 0, 0],
        [1, 0, 0],
        [-1, 0, 0],
        [0, 1, 0],
        [0, -1, 0],
        [0, 0, 1],
        [0, 0, -1],
        [1, 1, 0],
        [-1, -1, 0],
        [1, -1, 0],
        [-1, 1, 0],
        [1, 0, 1],
        [-1, 0, -1],
        [1, 0, -1],
        [-1, 0, 1],
        [0, 1, 1],
        [0, -1, -1],
        [0, 1, -1],
        [0, -1, 1],
    ]
    speeds = np.array(speed_list) * 1.0
    weights = np.array([1.0 / 3.0] + [1.0 / 18.0] * 6 + [1.0 / 36.0] * 12)
    along_x = speeds[:, 0]
    along_y = speeds[:, 1]
    along_z = speeds[:, 2]
    square = along_x * along_x + along_y * along_y + along_z * along_z
    polynomials = np.stack(
        [
            np.ones(19),
            along_x,
            along_y,
            along_z,
            square,
            3 * along_x * along_x - square,
            along_y * along_y - along_z * along_z,
            along_x * along_y,
            along_y * along_z,
            along_x * along_z,
            along_x * square,
            along_y * square,
            along_z * square,
            square * square,
            (3 * along_x * along_x - square) * square,
            (along_y * along_y - along_z * along_z) * square,
            along_x * (along_y * along_y - along_z * along_z),
            along_y * (along_z * along_z - along_x * along_x),
            along_z * (along_x * along_x - along_y * along_y),
        ],
        axis=1,
    )
    columns = []
    for column_index in range(19):
        vector = polynomials[:, column_index] * 1.0
        for repeat in range(2):
            for earlier in columns:
                vector = vector - np.dot(earlier, vector) * earlier
        columns.append(vector / math.sqrt(float(np.dot(vector, vector))))
    return (speeds, weights, np.stack(columns))


def collision_scalars(rate):
    m = lattice_tables()[2]
    r = {k: rate(k - 4) for k in range(4, 19)}
    f = lambda v: float(v)
    out = {}
    for name, column in (("rest", 0), ("axis", 1), ("diag", 7)):
        for other, column2 in (("rest", 0), ("axis", 1), ("diag", 7)):
            out[name, other] = r[4] * f(m[4, column] * m[4, column2]) + r[13] * f(
                m[13, column] * m[13, column2]
            )
    a5, b5, a14, b14 = m[5, 1] / 2, m[5, 7], m[14, 1] / 2, m[14, 7]
    out["uu"] = r[5] * f(a5 * a5) + r[14] * f(a14 * a14)
    out["uv"] = r[5] * f(a5 * b5) + r[14] * f(a14 * b14)
    out["vv"] = r[5] * f(b5 * b5) + r[14] * f(b14 * b14)
    a6, b6, a15, b15 = m[6, 3], m[6, 7], m[15, 3], m[15, 7]
    out["pp"] = r[6] * f(a6 * a6) + r[15] * f(a15 * a15)
    out["pq"] = r[6] * f(a6 * b6) + r[15] * f(a15 * b15)
    out["qq"] = r[6] * f(b6 * b6) + r[15] * f(b15 * b15)
    out["sxy"] = r[7] * f(m[7, 7] ** 2)
    out["syz"] = r[8] * f(m[8, 15] ** 2)
    out["sxz"] = r[9] * f(m[9, 11] ** 2)
    for name, row, axis, diag in (("x", 10, 1, 7), ("y", 11, 3, 7), ("z", 12, 5, 11)):
        out["aa" + name] = r[row] * f(m[row, axis] ** 2)
        out["ab" + name] = r[row] * f(m[row, axis] * m[row, diag])
        out["bb" + name] = r[row] * f(m[row, diag] ** 2)
    out["tx"] = r[16] * f(m[16, 7] ** 2)
    out["ty"] = r[17] * f(m[17, 15] ** 2)
    out["tz"] = r[18] * f(m[18, 11] ** 2)
    return out


def collide(f, k):
    w1, w2 = 1.0 / 18.0, 1.0 / 36.0
    pairs = ((1, 2), (3, 4), (5, 6), (7, 8), (9, 10), (11, 12), (13, 14), (15, 16), (17, 18))
    plus = [f[i] + f[o] for i, o in pairs]
    minus = [f[i] - f[o] for i, o in pairs]
    sx, sy, sz, sa, sb, sc, sd, se, sg = plus
    dx, dy, dz, da, db, dc, dd, de, dg = minus
    density = f[0] + ((sx + sy + sz) + (sa + sb) + (sc + sd) + (se + sg))
    jx = dx + (da + db) + (dc + dd)
    jy = dy + (da - db) + (de + dg)
    jz = dz + (dc - dd) + (de - dg)
    magnitude = jx * jx + jy * jy + jz * jz
    base = density - 1.5 * magnitude
    axis_base = (2.0 * w1) * base
    diag_base = (2.0 * w2) * base
    n0 = f[0] - (1.0 / 3.0) * base
    sx = sx - (axis_base + (9.0 * w1) * (jx * jx))
    sy = sy - (axis_base + (9.0 * w1) * (jy * jy))
    sz = sz - (axis_base + (9.0 * w1) * (jz * jz))

    def diagonal(s, project):
        return s - (diag_base + (9.0 * w2) * (project * project))

    sa, sb = diagonal(sa, jx + jy), diagonal(sb, jx - jy)
    sc, sd = diagonal(sc, jx + jz), diagonal(sd, jx - jz)
    se, sg = diagonal(se, jy + jz), diagonal(sg, jy - jz)
    dx, dy, dz = dx - (6.0 * w1) * jx, dy - (6.0 * w1) * jy, dz - (6.0 * w1) * jz
    hx, hy, hz = (6.0 * w2) * jx, (6.0 * w2) * jy, (6.0 * w2) * jz
    da, db = da - (hx + hy), db - (hx - hy)
    dc, dd = dc - (hx + hz), dd - (hx - hz)
    de, dg = de - (hy + hz), dg - (hy - hz)
    exy, exz, eyz = sa + sb, sc + sd, se + sg
    axis_sum = sx + sy + sz
    diag_sum = exy + exz + eyz
    g0 = k["rest", "rest"] * n0 + k["rest", "axis"] * axis_sum + k["rest", "diag"] * diag_sum
    ga = k["axis", "rest"] * n0 + k["axis", "axis"] * axis_sum + k["axis", "diag"] * diag_sum
    gd = k["diag", "rest"] * n0 + k["diag", "axis"] * axis_sum + k["diag", "diag"] * diag_sum
    u = 2.0 * sx - sy - sz
    v = exy + exz - 2.0 * eyz
    gu = k["uu"] * u + k["uv"] * v
    gv = k["uv"] * u + k["vv"] * v
    p = sy - sz
    q = exy - exz
    gp = k["pp"] * p + k["pq"] * q
    gq = k["pq"] * p + k["qq"] * q
    ga_u, gd_v = ga - gu, gd + gv
    even = [ga + 2.0 * gu, ga_u + gp, ga_u - gp]
    gxy, gxz, gyz = gd_v + gq, gd_v - gq, gd - 2.0 * gv
    for total, one, two, rate in ((gxy, sa, sb, "sxy"), (gxz, sc, sd, "sxz"), (gyz, se, sg, "syz")):
        shear = k[rate] * (one - two)
        even += [total + shear, total - shear]
    x_xy, x_xz = da + db, dc + dd
    y_xy, y_yz = da - db, de + dg
    z_xz, z_yz = dc - dd, de - dg
    x_all, y_all, z_all = x_xy + x_xz, y_xy + y_yz, z_xz + z_yz
    ox = k["aax"] * dx + k["abx"] * x_all
    oy = k["aay"] * dy + k["aby"] * y_all
    oz = k["aaz"] * dz + k["abz"] * z_all
    bx = k["abx"] * dx + k["bbx"] * x_all
    by = k["aby"] * dy + k["bby"] * y_all
    bz = k["abz"] * dz + k["bbz"] * z_all
    tx, ty, tz = k["tx"] * (x_xy - x_xz), k["ty"] * (y_yz - y_xy), k["tz"] * (z_xz - z_yz)
    x_on_xy, x_on_xz = bx + tx, bx - tx
    y_on_yz, y_on_xy = by + ty, by - ty
    z_on_xz, z_on_yz = bz + tz, bz - tz
    odd = [ox, oy, oz]
    odd += [x_on_xy + y_on_xy, x_on_xy - y_on_xy]
    odd += [x_on_xz + z_on_xz, x_on_xz - z_on_xz]
    odd += [y_on_yz + z_on_yz, y_on_yz - z_on_yz]
    post = [f[0] - g0]
    for (i, o), even_part, odd_part in zip(pairs, even, odd):
        post += [f[i] - (even_part + odd_part), f[o] - (even_part - odd_part)]
    return post


def halves(x):
    high = x.astype(BF16)
    return high, (x - high.astype(F32)).astype(BF16)


def rows_dot(a, b):
    return lax.dot_general(a, b, (((1,), (1,)), ((), ())), preferred_element_type=F32)


def flat(x):
    return jnp.concatenate([x[s : s + 1] for s in range(8)], axis=1)


def fold(x):
    return jnp.concatenate([x[:, 128 * s : 128 * s + 128] for s in range(8)], axis=0)


def cross(a, b):
    return [a[(i + 1) % 3] * b[(i + 2) % 3] - a[(i + 2) % 3] * b[(i + 1) % 3] for i in range(3)]


def groups(index, value):
    index = jnp.broadcast_to(index.astype(F32), value.shape).astype(BF16)
    none = jnp.zeros_like(value)
    return [
        jnp.where(index == (iota(value.shape, 0) + 16 * g).astype(F32).astype(BF16), value, none)
        for g in range(8)
    ]


def hot(index):
    return jnp.concatenate(groups(index, jnp.ones((16, index.shape[1]), BF16)), axis=0)


def iota(shape, dim):
    return lax.broadcasted_iota(I32, shape, dim)


def pick(conditions, values, shape):
    result = jnp.zeros(shape, F32)
    for condition, value in zip(conditions, values):
        if isinstance(value, float) and value == 0.0:
            continue
        result = jnp.where(condition, value, result)
    return result


def first_kernel(
    pop_hbm,
    solid_hbm,
    cell_hbm,
    dir_hbm,
    store_hbm,
    owner_hbm,
    motion_hbm,
    centre_hbm,
    rates_hbm,
    post_ref,
    bounce_ref,
    send_ref,
    xp_ref,
    xm_ref,
    yp_ref,
    ym_ref,
    xy_ref,
    own_ref,
    wall_ref,
    pop_ref,
    solid_ref,
    cell_ref,
    dir_ref,
    store_ref,
    owner_ref,
    motion_ref,
    centre_ref,
    rates_ref,
    pop_sem,
    sems,
):
    small = (
        (cell_hbm, cell_ref),
        (dir_hbm, dir_ref),
        (store_hbm, store_ref),
        (owner_hbm, owner_ref),
        (motion_hbm, motion_ref),
        (centre_hbm, centre_ref),
        (rates_hbm, rates_ref),
        (solid_hbm, solid_ref),
    )
    copies = [pltpu.make_async_copy(a, b, sems.at[n]) for n, (a, b) in enumerate(small)]

    def plane(x):
        rows = pl.ds(x * 32, 32)
        return pltpu.make_async_copy(
            pop_hbm.at[:, rows, :], pop_ref.at[:, rows, :], pop_sem.at[x]
        )

    for copy in copies:
        copy.start()
    for x in range(4):
        plane(x).start()
    for copy in copies[0:3]:
        copy.wait()
    speeds, weights, _ = lattice_tables()
    links = 1024
    place_x, place_y, place_z = (lax.axis_index(a) for a in ("gx", "gy", "gz"))
    cell = cell_ref[...]
    direction = dir_ref[...]
    store = store_ref[...]
    live = store < 32768
    row = lax.shift_right_logical(cell, 7)
    lane = cell & 127
    flat_row = flat(row)
    flat_lane = flat(lane)
    rows_hot16 = hot(flat_row)
    lanes_hot16 = hot(flat_lane)
    flat_store = flat(store)
    low_hot = hot(flat_store & 127)
    for copy in copies[3:6]:
        copy.wait()
    by_high = jnp.dot(
        owner_ref[...].astype(F32).astype(BF16), low_hot, preferred_element_type=F32
    )
    here = iota((256, links), 0) == lax.shift_right_logical(flat_store, 7)
    body = fold(jnp.sum(jnp.where(here, by_high, 0.0), axis=0, keepdims=True))
    is_dir = [direction == i for i in range(19)]
    shape = direction.shape
    speed = [pick(is_dir, [float(s) for s in speeds[:, a]], shape) for a in range(3)]
    weight = jnp.where(direction <= 6, float(weights[1]), float(weights[7]))
    is_body = [body == float(b) for b in range(8)]
    move = [pick(is_body, [motion_ref[b, c] for b in range(8)], shape) for c in range(6)]
    middle = [pick(is_body, [centre_ref[a, b] for b in range(8)], shape) for a in range(3)]
    place = (
        lax.shift_right_logical(cell, 12) + place_x * 4,
        (row & 31) + place_y * 32,
        lane + place_z * 128,
    )
    extents = (32.0, 128.0, 1024.0)
    radius = [
        (place[a].astype(F32) + 0.5 * speed[a] - middle[a] * extents[a]) / 128.0 for a in range(3)
    ]

    spin = cross(move[3:], radius)
    normal = sum(speed[a] * (move[a] + spin[a]) for a in range(3))
    wall = 6.0 * weight * normal
    wall_ref[...] = wall
    coded = flat(jnp.where(live, direction, 0).astype(F32))
    coded = jnp.broadcast_to(coded, (16, links)).astype(BF16)
    spread = jnp.concatenate(groups(flat_lane, coded), axis=0)
    bounce_ref[0] = rows_dot(rows_hot16, spread)

    for copy in copies[6:8]:
        copy.wait()
    k = collision_scalars(lambda i: rates_ref[i])

    def block(step, carry):
        rows = pl.ds(pl.multiple_of(step * 8, 8), 8)
        f = [pop_ref[i, rows, :] for i in range(19)]
        post = collide(f, k)
        fixed = solid_ref[rows, :] == 1
        post = [jnp.where(fixed, before, after) for before, after in zip(f, post)]
        code = bounce_ref[0, rows, :]
        found = jnp.zeros((8, 128), F32)
        for i in range(19):
            post_ref[i, rows, :] = post[i]
            if i:
                found = jnp.where(code == float(i), post[i], found)
        bounce_ref[1, rows, :] = found
        return carry

    def slab(x, carry):
        plane(x).wait()
        for part in range(4):
            block(x * 4 + part, 0)
        return carry

    lax.fori_loop(0, 4, slab, 0)

    at_lane = iota((128, 128), 1)
    column = jnp.zeros((128, 128), F32)
    for n in range(5):
        column = jnp.where(at_lane == n, pltpu.roll(post_ref[ZP[n]], n + 1, 1), column)
        column = jnp.where(at_lane == 8 + n, pltpu.roll(post_ref[ZM[n]], 8 + n, 1), column)
    columns = jnp.transpose(column)
    for n in range(5):
        xp_ref[n] = post_ref[XP[n], 96:128, :]
        xm_ref[n] = post_ref[XM[n], 0:32, :]
        for x in range(4):
            yp_ref[4 * n + x : 4 * n + x + 1, :] = post_ref[YP[n], 32 * x + 31 : 32 * x + 32, :]
            ym_ref[4 * n + x : 4 * n + x + 1, :] = post_ref[YM[n], 32 * x : 32 * x + 1, :]
    yp_ref[20:24, :] = jnp.zeros((4, 128), F32)
    ym_ref[20:24, :] = jnp.zeros((4, 128), F32)
    xy_ref[...] = jnp.zeros((8, 128), F32)
    xy_ref[0:1, :] = post_ref[7, 127:128, :]
    xy_ref[1:2, :] = post_ref[8, 0:1, :]
    xy_ref[2:3, :] = post_ref[9, 96:97, :]
    xy_ref[3:4, :] = post_ref[10, 31:32, :]

    found_high, found_low = halves(bounce_ref[1])
    by_row = jnp.dot(
        jnp.concatenate([found_high, found_low], axis=0), lanes_hot16, preferred_element_type=F32
    )
    by_row = jnp.where(
        iota((128, links), 0) == flat_row, by_row[0:128] + by_row[128:256], 0.0
    )
    picked = fold(jnp.sum(by_row, axis=0, keepdims=True))
    strength = jnp.where(live, 2.0 * picked - wall, 0.0)
    push = [speed[a] * strength for a in range(3)]
    sums = []
    for load in push + cross(radius, push):
        for b in range(8):
            sums.append(jnp.sum(jnp.where(is_body[b], load, 0.0), axis=0, keepdims=True))
    sums = jnp.sum(jnp.concatenate(sums, axis=0), axis=1, keepdims=True)
    sums = jnp.where(iota((48, 128), 0) == iota((48, 128), 1), sums, 0.0)
    body_row = jnp.sum(sums, axis=0, keepdims=True)
    upward = lax.rem(place_z + 1, 8)
    records = (strength, direction.astype(F32), cell.astype(F32), store.astype(F32))
    for j in range(8):
        for n, record in enumerate(records):
            send_ref[j, n] = record
        face = jnp.where(upward == j, columns[0:8], columns[8:16])
        send_ref[j, 4] = jnp.where(iota((8, 128), 0) == 5, body_row, face)
    own = owner_ref[pl.ds((place_x * 4 + place_y) * 8 + place_z, 1), :]
    own_ref[...] = jnp.zeros((8, 128), F32)
    for a in range(3):
        middle = pick([own == b for b in range(8)], [centre_ref[a, b] for b in range(8)], (1, 128))
        own_ref[a : a + 1, :] = (middle - 0.5) * (extents[a] / 128.0)


def second_kernel(got_ref, xy_ref, send_ref, total_ref):
    speeds = lattice_tables()[0]
    place_x, place_y, place_z = (lax.axis_index(a) for a in ("gx", "gy", "gz"))
    total_ref[...] = jnp.zeros_like(total_ref)
    count = iota((16, 128), 0).astype(F32)
    counts = [(count + 16.0 * g).astype(BF16) for g in range(16)]
    one = jnp.ones((16, 128), BF16)
    none = jnp.zeros((16, 128), BF16)

    def gather(peer, carry):
        strength, direction = got_ref[peer, 0], got_ref[peer, 1]
        cell, store = got_ref[peer, 2].astype(I32), got_ref[peer, 3].astype(I32)
        is_dir = [direction == float(i) for i in range(19)]
        speed = [pick(is_dir, [float(v) for v in speeds[:, a]], (8, 128)) for a in range(3)]
        place = (
            lax.shift_right_logical(cell, 12) + (place_x * 4 - 16),
            (lax.shift_right_logical(cell, 7) & 31) + (place_y * 32 - 64),
            (cell & 127) + (peer * 128 - 512),
        )
        arm = [(place[a].astype(F32) + 0.5 * speed[a]) * (1.0 / 128.0) for a in range(3)]
        push = [speed[a] * strength for a in range(3)]
        loads = push + cross(arm, push)
        upper = [load.astype(BF16).astype(F32) for load in loads]
        rows = upper + [load - part for load, part in zip(loads, upper)]
        owner = lax.shift_right_logical(store, 7)
        mine = (owner & 7) == place_z
        high = jnp.where(mine, lax.shift_right_logical(owner, 4), 255).astype(F32)
        low = ((lax.shift_right_logical(owner, 3) & 1) * 128) + (store & 127)
        low = low.astype(F32)
        left, right = [], []
        for s in range(8):

            def line(x, s=s):
                return jnp.broadcast_to(x[s : s + 1], (16, 128)).astype(BF16)

            at = line(high) == counts[0]
            left.append(jnp.concatenate([jnp.where(at, line(x), none) for x in rows], axis=0))
            at = line(low)
            right.append(
                jnp.concatenate([jnp.where(at == number, one, none) for number in counts], axis=0)
            )
        total_ref[...] += rows_dot(
            jnp.concatenate(left, axis=1), jnp.concatenate(right, axis=1)
        )
        return carry

    lax.fori_loop(0, 8, gather, 0, unroll=8)

    body_row = sum(got_ref[peer, 4, 5:6, :] for peer in range(8))
    for c in range(6):
        for e in range(2):
            lanes = slice(128 * e, 128 * e + 128)
            upper = total_ref[16 * c : 16 * c + 16, lanes]
            both = upper + total_ref[96 + 16 * c : 112 + 16 * c, lanes]
            for h in range(16):
                send_ref[(2 * h + e) % 4 * 8 + (2 * h + e) // 4, c : c + 1, :] = both[h : h + 1]
    last = jnp.concatenate([body_row, jnp.zeros((1, 128), F32)], axis=0)
    for j in range(32):
        send_ref[j, 6:8, :] = last

    below = got_ref[lax.rem(place_z + 7, 8), 4]
    above = got_ref[lax.rem(place_z + 1, 8), 4]
    lane = iota((1, 128), 1)

    def turned(x, by):
        return pltpu.roll(x, by, 1)

    to_xp = jnp.where(lane < 32, turned(below[1:2], 32), turned(above[1:2], 64))
    to_xm = jnp.where(lane < 32, below[2:3], turned(above[2:3], 32))
    in_row = lane & 31
    to_yp = jnp.where(in_row == 0, turned(below[3:4], 97), turned(above[3:4], 98))
    to_ym = jnp.where(in_row == 0, below[4:5], turned(above[4:5], 1))
    me = place_y * 8 + place_x
    has_xp, has_xm = place_x < 7, place_x > 0
    has_yp, has_ym = place_y < 3, place_y > 0
    for there, step, line in (
        (has_xp, 1, to_xp),
        (has_xm, -1, to_xm),
        (has_yp, 8, to_yp),
        (has_ym, -8, to_ym),
        (has_xp & has_yp, 9, xy_ref[0:1, :]),
        (has_xm & has_ym, -9, xy_ref[1:2, :]),
        (has_xp & has_ym, -7, xy_ref[2:3, :]),
        (has_xm & has_yp, 7, xy_ref[3:4, :]),
    ):

        @pl.when(there)
        def _(step=step, line=line):
            send_ref[me + step, 7:8, :] = line


def arrivals(lines):
    blank = jnp.zeros((128 - len(lines), 128), F32)
    return jnp.transpose(jnp.concatenate(lines + [blank], axis=0))


def shifted(line, cx, cy):
    by = 32 * cx + cy
    return pltpu.roll(line, by % 128, 1) if by else line


def finish(block, i, column, code, value):
    cz = int(lattice_tables()[0][i, 2])
    if cz:
        block = pltpu.roll(block, 1 if cz == 1 else 127, 1)
        at = 0 if cz == 1 else 127
        block = jnp.where(iota(block.shape, 1) == at, column, block)
    if i:
        opposite = i + 1 if i % 2 else i - 1
        block = jnp.where(code == float(opposite), value, block)
    return block


def third_kernel(
    post_ref,
    bounce_ref,
    wall_ref,
    got1_ref,
    motion_hbm,
    mass_hbm,
    inertia_hbm,
    cell_hbm,
    moved_hbm,
    value_ref,
    step_ref,
    moved_ref,
    cell_ref,
    motion_ref,
    mass_ref,
    inertia_ref,
    sems,
):
    speeds = lattice_tables()[0].astype(int)
    place_z = lax.axis_index("gz")
    fetches = [
        pltpu.make_async_copy(motion_hbm, motion_ref, sems.at[19]),
        pltpu.make_async_copy(mass_hbm, mass_ref, sems.at[20]),
        pltpu.make_async_copy(inertia_hbm, inertia_ref, sems.at[21]),
    ]
    cells = pltpu.make_async_copy(cell_hbm, cell_ref, sems.at[22])
    cells.start()
    for fetch in fetches:
        fetch.start()
    cells.wait()
    cell = flat(cell_ref[...])
    spread = []
    for part in halves(wall_ref[...]):
        part = jnp.broadcast_to(flat(part.astype(F32)), (16, 1024)).astype(BF16)
        spread += groups(cell & 127, part)
    laid = rows_dot(hot(lax.shift_right_logical(cell, 7)), jnp.concatenate(spread, axis=0))
    value_ref[...] = bounce_ref[1] - (laid[:, 0:128] + laid[:, 128:256])
    below = got1_ref[lax.rem(place_z + 7, 8), 4]
    above = got1_ref[lax.rem(place_z + 1, 8), 4]
    order = ZP + ZM
    lines = []
    for dirs, face in ((ZP, below), (ZM, above)):
        for n, i in enumerate(dirs):
            lines.append(shifted(face[n : n + 1], int(speeds[i, 0]), int(speeds[i, 1])))
    columns = arrivals(lines)
    copies = []
    for i in range(19):
        cx, cy, cz = (int(v) for v in speeds[i])
        planes = {0: (0, 4), 1: (1, 4), -1: (0, 3)}[cx]
        first, last = {0: (0, 32), 1: (8, 32), -1: (0, 24)}[cy]
        for x in range(*planes):
            source = 32 * (x - cx) - cy
            block = post_ref[i, source + first : source + last, :]
            rows = slice(32 * x + first, 32 * x + last)
            column = None
            if cz:
                n = order.index(i)
                column = columns[rows, n : n + 1]
            code, value = bounce_ref[0, rows, :], value_ref[rows, :]
            moved_ref[i, x, first:last, :] = finish(block, i, column, code, value)
        part = (i, slice(*planes), slice(first, last))
        copy = pltpu.make_async_copy(moved_ref.at[part], moved_hbm.at[part], sems.at[i])
        copy.start()
        copies.append(copy)

    for fetch in fetches:
        fetch.wait()
    at_lane, at_row = iota((8, 128), 1), iota((8, 128), 0)
    scale = jnp.zeros((8, 128), F32)
    for c in range(6):
        for b in range(8):
            value = mass_ref[b] if c < 3 else inertia_ref[c - 3, b]
            scale = jnp.where((at_lane == c) & (at_row == b), value, scale)
    step_ref[0] = scale
    step_ref[1] = jnp.concatenate([motion_ref[...], jnp.zeros((8, 122), F32)], axis=1)
    for copy in copies:
        copy.wait()


def face_kernel(
    partly_hbm,
    post_ref,
    bounce_ref,
    value_ref,
    xp_ref,
    xm_ref,
    yp_ref,
    ym_ref,
    moved_hbm,
    moved_ref,
    sems,
):
    del partly_hbm
    speeds = lattice_tables()[0].astype(int)
    place_x, place_y = lax.axis_index("gx"), lax.axis_index("gy")
    has_xp, has_xm = place_x < 7, place_x > 0
    has_yp, has_ym = place_y < 3, place_y > 0
    copies = []

    def send(*part):
        copy = pltpu.make_async_copy(
            moved_ref.at[part], moved_hbm.at[part], sems.at[len(copies)]
        )
        copy.start()
        copies.append(copy)

    for i in (1, 2, 7, 8, 9, 10):
        cx, cy = (int(v) for v in speeds[i, :2])
        x = 0 if cx == 1 else 3
        first, last = {0: (0, 32), 1: (8, 32), -1: (0, 24)}[cy]
        there, face = (has_xm, xp_ref[XP.index(i)]) if cx == 1 else (has_xp, xm_ref[XM.index(i)])
        block = jnp.where(there, face[first - cy : last - cy], 0.0)
        rows = slice(32 * x + first, 32 * x + last)
        code, value = bounce_ref[0, rows, :], value_ref[rows, :]
        moved_ref[i, x, first:last, :] = finish(block, i, None, code, value)
        send(i, x, slice(first, last))
    at_row = iota((8, 128), 0)
    for i in (3, 4, 7, 8, 9, 10):
        cx, cy = (int(v) for v in speeds[i, :2])
        planes = {0: (0, 4), 1: (1, 4), -1: (0, 3)}[cx]
        first = 0 if cy == 1 else 24
        face_ref, n = (yp_ref, YP.index(i)) if cy == 1 else (ym_ref, YM.index(i))
        for x in range(*planes):
            source = x - cx
            block = post_ref[i, 32 * source + first : 32 * source + first + 8, :]
            line = face_ref[4 * n + source : 4 * n + source + 1, :]
            line = jnp.where(has_ym if cy == 1 else has_yp, line, 0.0)
            block = pltpu.roll(block, 1 if cy == 1 else 7, 0)
            block = jnp.where(at_row == (0 if cy == 1 else 7), line, block)
            rows = slice(32 * x + first, 32 * x + first + 8)
            code, value = bounce_ref[0, rows, :], value_ref[rows, :]
            moved_ref[i, x, first : first + 8, :] = finish(block, i, None, code, value)
        send(i, slice(*planes), slice(first, first + 8))
    for copy in copies:
        copy.wait()


def fourth_kernel(
    partly_hbm,
    post_ref,
    bounce_ref,
    value_ref,
    own_ref,
    got1_ref,
    got2_ref,
    xp_ref,
    xm_ref,
    yp_ref,
    ym_ref,
    step_ref,
    moved_hbm,
    load_hbm,
    next_hbm,
    row_ref,
    edge_ref,
    load_ref,
    next_ref,
    sems,
):
    del partly_hbm
    speeds = lattice_tables()[0].astype(int)
    place_x, place_y, place_z = (lax.axis_index(a) for a in ("gx", "gy", "gz"))
    has_xp, has_xm = place_x < 7, place_x > 0
    has_yp, has_ym = place_y < 3, place_y > 0
    me = place_y * 8 + place_x
    copies = []

    def send(source, target):
        copy = pltpu.make_async_copy(source, target, sems.at[len(copies)])
        copy.start()
        copies.append(copy)

    parts = [got2_ref[j] for j in range(32)]
    while len(parts) > 1:
        parts = [a + b for a, b in zip(parts[0::2], parts[1::2])]
    total = parts[0]
    push = [total[a : a + 1] for a in range(3)]
    away = cross([own_ref[a : a + 1, :] for a in range(3)], push)
    turn = [total[3 + a : 4 + a] - away[a] for a in range(3)]
    load_ref[...] = jnp.concatenate(push + turn, axis=0)
    send(load_ref, load_hbm)
    at_lane, at_row = iota((8, 128), 1), iota((8, 128), 0)
    own = jnp.where((at_lane & 7) == at_row, total[6:7], 0.0)
    body_load = jnp.zeros((8, 128), F32)
    for c in range(6):
        here = lax.shift_right_logical(at_lane, 3) == c
        column = jnp.sum(jnp.where(here, own, 0.0), axis=1, keepdims=True)
        body_load = jnp.where(at_lane == c, column, body_load)
    next_ref[...] = (step_ref[1] + step_ref[0] * body_load / 32768.0)[:, 0:6]
    send(next_ref, next_hbm)

    def edge(there, step):
        line = got2_ref[jnp.where(there, me + step, me), 7:8, :]
        return jnp.where(there, line, 0.0)

    lane = iota((1, 128), 1)
    row_in_plane = lane & 31
    from_x = {1: edge(has_xm, -1), -1: edge(has_xp, 1)}
    from_y = {1: edge(has_ym, -8), -1: edge(has_yp, 8)}
    from_xy = {
        (1, 1): edge(has_xm & has_ym, -9),
        (-1, -1): edge(has_xp & has_yp, 9),
        (1, -1): edge(has_xm & has_yp, 7),
        (-1, 1): edge(has_xp & has_ym, -7),
    }
    order, lines = [], []
    for dirs, face in (
        (ZP, got1_ref[lax.rem(place_z + 7, 8), 4]),
        (ZM, got1_ref[lax.rem(place_z + 1, 8), 4]),
    ):
        for n, i in enumerate(dirs):
            cx, cy, cz = (int(v) for v in speeds[i])
            if cx == 1:
                line = from_x[1] if cz == 1 else pltpu.roll(from_x[1], 96, 1)
            elif cx == -1:
                line = pltpu.roll(from_x[-1], 96 if cz == 1 else 64, 1)
            elif cy == 1:
                came = from_y[1] if cz == 1 else pltpu.roll(from_y[1], 127, 1)
                line = jnp.where(row_in_plane == 0, came, shifted(face[n : n + 1], 0, 1))
            elif cy == -1:
                came = pltpu.roll(from_y[-1], 31 if cz == 1 else 30, 1)
                line = jnp.where(row_in_plane == 31, came, shifted(face[n : n + 1], 0, -1))
            else:
                continue
            order.append(i)
            lines.append(line)
    columns = arrivals(lines)

    for i in (7, 9, 8, 10, 15, 17, 16, 18):
        cx, cy, cz = (int(v) for v in speeds[i])
        first = 0 if cy == 1 else 24
        face_ref, n = (yp_ref, YP.index(i)) if cy == 1 else (ym_ref, YM.index(i))
        planes = range(4) if cz else ((0,) if cx == 1 else (3,))
        for x in planes:
            source = x - cx
            if cz:
                block = post_ref[i, 32 * source + first : 32 * source + first + 8, :]
                line = face_ref[4 * n + source : 4 * n + source + 1, :]
                line = jnp.where(has_ym if cy == 1 else has_yp, line, 0.0)
            else:
                if source < 0:
                    block = jnp.where(has_xm, xp_ref[XP.index(i), first : first + 8, :], 0.0)
                else:
                    block = jnp.where(has_xp, xm_ref[XM.index(i), first : first + 8, :], 0.0)
                line = from_xy[cx, cy]
            block = pltpu.roll(block, 1 if cy == 1 else 7, 0)
            block = jnp.where(at_row == (0 if cy == 1 else 7), line, block)
            rows = slice(32 * x + first, 32 * x + first + 8)
            column = None
            if cz:
                m = order.index(i)
                column = columns[rows, m : m + 1]
            code, value = bounce_ref[0, rows, :], value_ref[rows, :]
            row_ref[i - 7, x] = finish(block, i, column, code, value)
        part = slice(planes[0], planes[-1] + 1)
        send(row_ref.at[i - 7, part], moved_hbm.at[i, part, first : first + 8, :])
    for number, i in enumerate((11, 13, 14, 12)):
        cx = int(speeds[i, 0])
        x = 0 if cx == 1 else 3
        if cx == 1:
            block = jnp.where(has_xm, xp_ref[XP.index(i)], 0.0)
        else:
            block = jnp.where(has_xp, xm_ref[XM.index(i)], 0.0)
        rows = slice(32 * x, 32 * x + 32)
        m = order.index(i)
        code, value = bounce_ref[0, rows, :], value_ref[rows, :]
        edge_ref[number] = finish(block, i, columns[rows, m : m + 1], code, value)
        send(edge_ref.at[number], moved_hbm.at[i, x])

    for copy in copies:
        copy.wait()


def body(
    populations,
    solid,
    link_cell,
    link_dir,
    link_store,
    store_body,
    motion,
    inv_mass,
    inv_inertia,
    centre,
    rates,
):
    vmem = pl.BlockSpec(memory_space=pltpu.VMEM)

    def array(*shape):
        return jax.ShapeDtypeStruct(shape, F32)

    params = pltpu.CompilerParams(vmem_limit_bytes=40 * 1024 * 1024)
    post, bounce, send1, xp, xm, yp, ym, xy, own, wall = pl.pallas_call(
        first_kernel,
        out_shape=(
            array(19, 128, 128),
            array(2, 128, 128),
            array(8, 5, 8, 128),
            array(5, 32, 128),
            array(5, 32, 128),
            array(24, 128),
            array(24, 128),
            array(8, 128),
            array(8, 128),
            array(8, 128),
        ),
        in_specs=[pl.BlockSpec(memory_space=pltpu.HBM)] * 9,
        out_specs=(vmem,) * 10,
        scratch_shapes=[
            pltpu.VMEM((19, 128, 128), F32),
            pltpu.VMEM((128, 128), I32),
            pltpu.VMEM((8, 128), I32),
            pltpu.VMEM((8, 128), I32),
            pltpu.VMEM((8, 128), I32),
            pltpu.VMEM((256, 128), I32),
            pltpu.SMEM((8, 6), F32),
            pltpu.SMEM((3, 8), F32),
            pltpu.SMEM((15,), F32),
            pltpu.SemaphoreType.DMA((4,)),
            pltpu.SemaphoreType.DMA((8,)),
        ],
        compiler_params=params,
        name="collide",
    )(
        *(
            pltpu.with_memory_space_constraint(x, pltpu.HBM)
            for x in (
                populations.reshape(19, 128, 128),
                solid.reshape(128, 128),
                link_cell.reshape(8, 128),
                link_dir.reshape(8, 128),
                link_store.reshape(8, 128),
                store_body.reshape(256, 128),
                motion,
                centre.T,
                rates,
            )
        )
    )

    def shift(x, axis, by):
        size = lax.axis_size(axis)
        return lax.ppermute(x, axis, [(i, (i + by) % size) for i in range(size)])

    got1 = lax.all_to_all(send1, "gz", 0, 0, tiled=True)
    send2 = pl.pallas_call(
        second_kernel,
        out_shape=array(32, 8, 128),
        in_specs=[vmem] * 2,
        out_specs=vmem,
        scratch_shapes=[pltpu.VMEM((192, 256), F32)],
        compiler_params=params,
        cost_estimate=pl.CostEstimate(
            flops=2 * 192 * 256 * 8192, bytes_accessed=4 * 4 * 8192, transcendentals=0
        ),
        name="bins",
    )(got1, xy)
    xp, xm = shift(xp, "gx", 1), shift(xm, "gx", -1)
    yp, ym = shift(yp, "gy", 1), shift(ym, "gy", -1)
    got2 = lax.all_to_all(send2, ("gy", "gx"), 0, 0, tiled=True)
    hbm = pl.BlockSpec(memory_space=pltpu.HBM)
    partly, value, step = pl.pallas_call(
        third_kernel,
        out_shape=(array(19, 4, 32, 128), array(128, 128), array(2, 8, 128)),
        in_specs=[vmem] * 4 + [hbm] * 4,
        out_specs=(hbm, vmem, vmem),
        scratch_shapes=[
            pltpu.VMEM((19, 4, 32, 128), F32),
            pltpu.VMEM((8, 128), I32),
            pltpu.VMEM((8, 6), F32),
            pltpu.SMEM((8,), F32),
            pltpu.SMEM((3, 8), F32),
            pltpu.SemaphoreType.DMA((23,)),
        ],
        compiler_params=params,
        cost_estimate=pl.CostEstimate(
            flops=19 * 16384 * 4, bytes_accessed=2 * 19 * 16384 * 4, transcendentals=0
        ),
        name="move",
    )(
        *(post, bounce, wall, got1),
        *(
            pltpu.with_memory_space_constraint(x, pltpu.HBM)
            for x in (motion, inv_mass, inv_inertia.T, link_cell.reshape(8, 128))
        ),
    )
    partly = pl.pallas_call(
        face_kernel,
        out_shape=array(19, 4, 32, 128),
        in_specs=[hbm] + [vmem] * 7,
        out_specs=hbm,
        scratch_shapes=[pltpu.VMEM((19, 4, 32, 128), F32), pltpu.SemaphoreType.DMA((12,))],
        input_output_aliases={0: 0},
        compiler_params=params,
        name="faces",
    )(partly, post, bounce, value, xp, xm, yp, ym)
    moved, own_loads, motion_next = pl.pallas_call(
        fourth_kernel,
        out_shape=(array(19, 4, 32, 128), array(6, 128), array(8, 6)),
        in_specs=[hbm] + [vmem] * 11,
        out_specs=(hbm,) * 3,
        scratch_shapes=[
            pltpu.VMEM((12, 4, 8, 128), F32),
            pltpu.VMEM((4, 32, 128), F32),
            pltpu.VMEM((6, 128), F32),
            pltpu.VMEM((8, 6), F32),
            pltpu.SemaphoreType.DMA((14,)),
        ],
        input_output_aliases={0: 0},
        compiler_params=params,
        name="close",
    )(partly, post, bounce, value, own, got1, got2, xp, xm, yp, ym, step)
    return (moved, own_loads, motion_next)


def solution(mesh):
    return jax.shard_map(
        body,
        mesh=mesh,
        in_specs=(
            P(None, "gx", "gy", "gz"),
            P("gx", "gy", "gz"),
            P("gx", "gy", "gz", None),
            P("gx", "gy", "gz", None),
            P("gx", "gy", "gz", None),
            P(),
            P(),
            P(),
            P(),
            P(),
            P(),
        ),
        out_specs=(P(None, "gx", "gy", "gz"), P(None, ("gx", "gy", "gz")), P()),
        check_vma=False,
    )
```

```python
import math

import jax
import jax.numpy as jnp
import numpy as np
from jax import lax
from jax.experimental import pallas as pl
from jax.experimental.pallas import tpu as pltpu
from jax.sharding import PartitionSpec as P

F32 = jnp.float32
BF16 = jnp.bfloat16
I32 = jnp.int32

XP, XM = (1, 7, 9, 11, 13), (2, 10, 8, 14, 12)
YP, YM = (3, 7, 10, 15, 17), (4, 9, 8, 18, 16)
ZP, ZM = (5, 11, 14, 15, 18), (6, 13, 12, 17, 16)


def lattice_tables():
    speed_list = [
        [0, 0, 0],
        [1, 0, 0],
        [-1, 0, 0],
        [0, 1, 0],
        [0, -1, 0],
        [0, 0, 1],
        [0, 0, -1],
        [1, 1, 0],
        [-1, -1, 0],
        [1, -1, 0],
        [-1, 1, 0],
        [1, 0, 1],
        [-1, 0, -1],
        [1, 0, -1],
        [-1, 0, 1],
        [0, 1, 1],
        [0, -1, -1],
        [0, 1, -1],
        [0, -1, 1],
    ]
    speeds = np.array(speed_list) * 1.0
    weights = np.array([1.0 / 3.0] + [1.0 / 18.0] * 6 + [1.0 / 36.0] * 12)
    along_x = speeds[:, 0]
    along_y = speeds[:, 1]
    along_z = speeds[:, 2]
    square = along_x * along_x + along_y * along_y + along_z * along_z
    polynomials = np.stack(
        [
            np.ones(19),
            along_x,
            along_y,
            along_z,
            square,
            3 * along_x * along_x - square,
            along_y * along_y - along_z * along_z,
            along_x * along_y,
            along_y * along_z,
            along_x * along_z,
            along_x * square,
            along_y * square,
            along_z * square,
            square * square,
            (3 * along_x * along_x - square) * square,
            (along_y * along_y - along_z * along_z) * square,
            along_x * (along_y * along_y - along_z * along_z),
            along_y * (along_z * along_z - along_x * along_x),
            along_z * (along_x * along_x - along_y * along_y),
        ],
        axis=1,
    )
    columns = []
    for column_index in range(19):
        vector = polynomials[:, column_index] * 1.0
        for repeat in range(2):
            for earlier in columns:
                vector = vector - np.dot(earlier, vector) * earlier
        columns.append(vector / math.sqrt(float(np.dot(vector, vector))))
    return (speeds, weights, np.stack(columns))


def collision_scalars(rate):
    m = lattice_tables()[2]
    r = {k: rate(k - 4) for k in range(4, 19)}
    f = lambda v: float(v)
    out = {}
    for name, column in (("rest", 0), ("axis", 1), ("diag", 7)):
        for other, column2 in (("rest", 0), ("axis", 1), ("diag", 7)):
            out[name, other] = r[4] * f(m[4, column] * m[4, column2]) + r[13] * f(
                m[13, column] * m[13, column2]
            )
    a5, b5, a14, b14 = m[5, 1] / 2, m[5, 7], m[14, 1] / 2, m[14, 7]
    out["uu"] = r[5] * f(a5 * a5) + r[14] * f(a14 * a14)
    out["uv"] = r[5] * f(a5 * b5) + r[14] * f(a14 * b14)
    out["vv"] = r[5] * f(b5 * b5) + r[14] * f(b14 * b14)
    a6, b6, a15, b15 = m[6, 3], m[6, 7], m[15, 3], m[15, 7]
    out["pp"] = r[6] * f(a6 * a6) + r[15] * f(a15 * a15)
    out["pq"] = r[6] * f(a6 * b6) + r[15] * f(a15 * b15)
    out["qq"] = r[6] * f(b6 * b6) + r[15] * f(b15 * b15)
    out["sxy"] = r[7] * f(m[7, 7] ** 2)
    out["syz"] = r[8] * f(m[8, 15] ** 2)
    out["sxz"] = r[9] * f(m[9, 11] ** 2)
    for name, row, axis, diag in (("x", 10, 1, 7), ("y", 11, 3, 7), ("z", 12, 5, 11)):
        out["aa" + name] = r[row] * f(m[row, axis] ** 2)
        out["ab" + name] = r[row] * f(m[row, axis] * m[row, diag])
        out["bb" + name] = r[row] * f(m[row, diag] ** 2)
    out["tx"] = r[16] * f(m[16, 7] ** 2)
    out["ty"] = r[17] * f(m[17, 15] ** 2)
    out["tz"] = r[18] * f(m[18, 11] ** 2)
    return out


def collide(f, k):
    w1, w2 = 1.0 / 18.0, 1.0 / 36.0
    pairs = ((1, 2), (3, 4), (5, 6), (7, 8), (9, 10), (11, 12), (13, 14), (15, 16), (17, 18))
    plus = [f[i] + f[o] for i, o in pairs]
    minus = [f[i] - f[o] for i, o in pairs]
    sx, sy, sz, sa, sb, sc, sd, se, sg = plus
    dx, dy, dz, da, db, dc, dd, de, dg = minus
    density = f[0] + ((sx + sy + sz) + (sa + sb) + (sc + sd) + (se + sg))
    jx = dx + (da + db) + (dc + dd)
    jy = dy + (da - db) + (de + dg)
    jz = dz + (dc - dd) + (de - dg)
    magnitude = jx * jx + jy * jy + jz * jz
    base = density - 1.5 * magnitude
    axis_base = (2.0 * w1) * base
    diag_base = (2.0 * w2) * base
    n0 = f[0] - (1.0 / 3.0) * base
    sx = sx - (axis_base + (9.0 * w1) * (jx * jx))
    sy = sy - (axis_base + (9.0 * w1) * (jy * jy))
    sz = sz - (axis_base + (9.0 * w1) * (jz * jz))

    def diagonal(s, project):
        return s - (diag_base + (9.0 * w2) * (project * project))

    sa, sb = diagonal(sa, jx + jy), diagonal(sb, jx - jy)
    sc, sd = diagonal(sc, jx + jz), diagonal(sd, jx - jz)
    se, sg = diagonal(se, jy + jz), diagonal(sg, jy - jz)
    dx, dy, dz = dx - (6.0 * w1) * jx, dy - (6.0 * w1) * jy, dz - (6.0 * w1) * jz
    hx, hy, hz = (6.0 * w2) * jx, (6.0 * w2) * jy, (6.0 * w2) * jz
    da, db = da - (hx + hy), db - (hx - hy)
    dc, dd = dc - (hx + hz), dd - (hx - hz)
    de, dg = de - (hy + hz), dg - (hy - hz)
    exy, exz, eyz = sa + sb, sc + sd, se + sg
    axis_sum = sx + sy + sz
    diag_sum = exy + exz + eyz
    g0 = k["rest", "rest"] * n0 + k["rest", "axis"] * axis_sum + k["rest", "diag"] * diag_sum
    ga = k["axis", "rest"] * n0 + k["axis", "axis"] * axis_sum + k["axis", "diag"] * diag_sum
    gd = k["diag", "rest"] * n0 + k["diag", "axis"] * axis_sum + k["diag", "diag"] * diag_sum
    u = 2.0 * sx - sy - sz
    v = exy + exz - 2.0 * eyz
    gu = k["uu"] * u + k["uv"] * v
    gv = k["uv"] * u + k["vv"] * v
    p = sy - sz
    q = exy - exz
    gp = k["pp"] * p + k["pq"] * q
    gq = k["pq"] * p + k["qq"] * q
    ga_u, gd_v = ga - gu, gd + gv
    even = [ga + 2.0 * gu, ga_u + gp, ga_u - gp]
    gxy, gxz, gyz = gd_v + gq, gd_v - gq, gd - 2.0 * gv
    for total, one, two, rate in ((gxy, sa, sb, "sxy"), (gxz, sc, sd, "sxz"), (gyz, se, sg, "syz")):
        shear = k[rate] * (one - two)
        even += [total + shear, total - shear]
    x_xy, x_xz = da + db, dc + dd
    y_xy, y_yz = da - db, de + dg
    z_xz, z_yz = dc - dd, de - dg
    x_all, y_all, z_all = x_xy + x_xz, y_xy + y_yz, z_xz + z_yz
    ox = k["aax"] * dx + k["abx"] * x_all
    oy = k["aay"] * dy + k["aby"] * y_all
    oz = k["aaz"] * dz + k["abz"] * z_all
    bx = k["abx"] * dx + k["bbx"] * x_all
    by = k["aby"] * dy + k["bby"] * y_all
    bz = k["abz"] * dz + k["bbz"] * z_all
    tx, ty, tz = k["tx"] * (x_xy - x_xz), k["ty"] * (y_yz - y_xy), k["tz"] * (z_xz - z_yz)
    x_on_xy, x_on_xz = bx + tx, bx - tx
    y_on_yz, y_on_xy = by + ty, by - ty
    z_on_xz, z_on_yz = bz + tz, bz - tz
    odd = [ox, oy, oz]
    odd += [x_on_xy + y_on_xy, x_on_xy - y_on_xy]
    odd += [x_on_xz + z_on_xz, x_on_xz - z_on_xz]
    odd += [y_on_yz + z_on_yz, y_on_yz - z_on_yz]
    post = [f[0] - g0]
    for (i, o), even_part, odd_part in zip(pairs, even, odd):
        post += [f[i] - (even_part + odd_part), f[o] - (even_part - odd_part)]
    return post


def halves(x):
    high = x.astype(BF16)
    return high, (x - high.astype(F32)).astype(BF16)


def rows_dot(a, b):
    return lax.dot_general(a, b, (((1,), (1,)), ((), ())), preferred_element_type=F32)


PLACE_X = (0, 4, 1, 5, 2, 6, 3, 7)
PLACE_Y = (0, 1, 2, 3)
PLACE_Z = (0, 4, 2, 6, 1, 5, 3, 7)


def listed(table, index):
    return sum(jnp.where(index == n, value, 0) for n, value in enumerate(table))


def peer_at(x, y):
    return listed(PLACE_Y, y) * 8 + listed(PLACE_X, x)


def flat(x):
    return jnp.concatenate([x[s : s + 1] for s in range(8)], axis=1)


def fold(x):
    return jnp.concatenate([x[:, 128 * s : 128 * s + 128] for s in range(8)], axis=0)


def cross(a, b):
    return [a[(i + 1) % 3] * b[(i + 2) % 3] - a[(i + 2) % 3] * b[(i + 1) % 3] for i in range(3)]


def groups(index, value):
    index = jnp.broadcast_to(index.astype(F32), value.shape).astype(BF16)
    none = jnp.zeros_like(value)
    return [
        jnp.where(index == (iota(value.shape, 0) + 16 * g).astype(F32).astype(BF16), value, none)
        for g in range(8)
    ]


def hot(index):
    return jnp.concatenate(groups(index, jnp.ones((16, index.shape[1]), BF16)), axis=0)


def iota(shape, dim):
    return lax.broadcasted_iota(I32, shape, dim)


def pick(conditions, values, shape):
    result = jnp.zeros(shape, F32)
    for condition, value in zip(conditions, values):
        if isinstance(value, float) and value == 0.0:
            continue
        result = jnp.where(condition, value, result)
    return result


def first_kernel(
    pop_hbm,
    solid_hbm,
    cell_hbm,
    dir_hbm,
    store_hbm,
    owner_hbm,
    motion_hbm,
    centre_hbm,
    rates_hbm,
    post_ref,
    bounce_ref,
    send_ref,
    xp_ref,
    xm_ref,
    yp_ref,
    ym_ref,
    xy_ref,
    own_ref,
    wall_ref,
    pop_ref,
    solid_ref,
    cell_ref,
    dir_ref,
    store_ref,
    owner_ref,
    motion_ref,
    centre_ref,
    rates_ref,
    pop_sem,
    sems,
):
    small = (
        (cell_hbm, cell_ref),
        (dir_hbm, dir_ref),
        (store_hbm, store_ref),
        (owner_hbm, owner_ref),
        (motion_hbm, motion_ref),
        (centre_hbm, centre_ref),
        (rates_hbm, rates_ref),
        (solid_hbm, solid_ref),
    )
    copies = [pltpu.make_async_copy(a, b, sems.at[n]) for n, (a, b) in enumerate(small)]

    def plane(x):
        rows = pl.ds(x * 32, 32)
        return pltpu.make_async_copy(
            pop_hbm.at[:, rows, :], pop_ref.at[:, rows, :], pop_sem.at[x]
        )

    for copy in copies:
        copy.start()
    for x in range(4):
        plane(x).start()
    for copy in copies[0:3]:
        copy.wait()
    speeds, weights, _ = lattice_tables()
    links = 1024
    place_x, place_y, place_z = (lax.axis_index(a) for a in ("gx", "gy", "gz"))
    cell = cell_ref[...]
    direction = dir_ref[...]
    store = store_ref[...]
    live = store < 32768
    row = lax.shift_right_logical(cell, 7)
    lane = cell & 127
    flat_row = flat(row)
    flat_lane = flat(lane)
    rows_hot16 = hot(flat_row)
    lanes_hot16 = hot(flat_lane)
    flat_store = flat(store)
    low_hot = hot(flat_store & 127)
    for copy in copies[3:6]:
        copy.wait()
    by_high = jnp.dot(
        owner_ref[...].astype(F32).astype(BF16), low_hot, preferred_element_type=F32
    )
    here = iota((256, links), 0) == lax.shift_right_logical(flat_store, 7)
    body = fold(jnp.sum(jnp.where(here, by_high, 0.0), axis=0, keepdims=True))
    is_dir = [direction == i for i in range(19)]
    shape = direction.shape
    speed = [pick(is_dir, [float(s) for s in speeds[:, a]], shape) for a in range(3)]
    weight = jnp.where(direction <= 6, float(weights[1]), float(weights[7]))
    is_body = [body == float(b) for b in range(8)]
    move = [pick(is_body, [motion_ref[b, c] for b in range(8)], shape) for c in range(6)]
    middle = [pick(is_body, [centre_ref[a, b] for b in range(8)], shape) for a in range(3)]
    place = (
        lax.shift_right_logical(cell, 12) + place_x * 4,
        (row & 31) + place_y * 32,
        lane + place_z * 128,
    )
    extents = (32.0, 128.0, 1024.0)
    radius = [
        (place[a].astype(F32) + 0.5 * speed[a] - middle[a] * extents[a]) / 128.0 for a in range(3)
    ]

    spin = cross(move[3:], radius)
    normal = sum(speed[a] * (move[a] + spin[a]) for a in range(3))
    wall = 6.0 * weight * normal
    wall_ref[...] = wall
    coded = flat(jnp.where(live, direction, 0).astype(F32))
    coded = jnp.broadcast_to(coded, (16, links)).astype(BF16)
    spread = jnp.concatenate(groups(flat_lane, coded), axis=0)
    bounce_ref[0] = rows_dot(rows_hot16, spread)

    for copy in copies[6:8]:
        copy.wait()
    k = collision_scalars(lambda i: rates_ref[i])

    def block(step, carry):
        rows = pl.ds(pl.multiple_of(step * 8, 8), 8)
        f = [pop_ref[i, rows, :] for i in range(19)]
        post = collide(f, k)
        fixed = solid_ref[rows, :] == 1
        post = [jnp.where(fixed, before, after) for before, after in zip(f, post)]
        code = bounce_ref[0, rows, :]
        found = jnp.zeros((8, 128), F32)
        for i in range(19):
            post_ref[i, rows, :] = post[i]
            if i:
                found = jnp.where(code == float(i), post[i], found)
        bounce_ref[1, rows, :] = found
        return carry

    def slab(x, carry):
        plane(x).wait()
        for part in range(4):
            block(x * 4 + part, 0)
        return carry

    lax.fori_loop(0, 4, slab, 0)

    at_lane = iota((128, 128), 1)
    column = jnp.zeros((128, 128), F32)
    for n in range(5):
        column = jnp.where(at_lane == n, pltpu.roll(post_ref[ZP[n]], n + 1, 1), column)
        column = jnp.where(at_lane == 8 + n, pltpu.roll(post_ref[ZM[n]], 8 + n, 1), column)
    columns = jnp.transpose(column)
    for n in range(5):
        xp_ref[n] = post_ref[XP[n], 96:128, :]
        xm_ref[n] = post_ref[XM[n], 0:32, :]
        for x in range(4):
            yp_ref[4 * n + x : 4 * n + x + 1, :] = post_ref[YP[n], 32 * x + 31 : 32 * x + 32, :]
            ym_ref[4 * n + x : 4 * n + x + 1, :] = post_ref[YM[n], 32 * x : 32 * x + 1, :]
    yp_ref[20:24, :] = jnp.zeros((4, 128), F32)
    ym_ref[20:24, :] = jnp.zeros((4, 128), F32)
    xy_ref[...] = jnp.zeros((8, 128), F32)
    xy_ref[0:1, :] = post_ref[7, 127:128, :]
    xy_ref[1:2, :] = post_ref[8, 0:1, :]
    xy_ref[2:3, :] = post_ref[9, 96:97, :]
    xy_ref[3:4, :] = post_ref[10, 31:32, :]

    found_high, found_low = halves(bounce_ref[1])
    by_row = jnp.dot(
        jnp.concatenate([found_high, found_low], axis=0), lanes_hot16, preferred_element_type=F32
    )
    by_row = jnp.where(
        iota((128, links), 0) == flat_row, by_row[0:128] + by_row[128:256], 0.0
    )
    picked = fold(jnp.sum(by_row, axis=0, keepdims=True))
    strength = jnp.where(live, 2.0 * picked - wall, 0.0)
    push = [speed[a] * strength for a in range(3)]
    sums = []
    for load in push + cross(radius, push):
        for b in range(8):
            sums.append(jnp.sum(jnp.where(is_body[b], load, 0.0), axis=0, keepdims=True))
    sums = jnp.sum(jnp.concatenate(sums, axis=0), axis=1, keepdims=True)
    sums = jnp.where(iota((48, 128), 0) == iota((48, 128), 1), sums, 0.0)
    body_row = jnp.sum(sums, axis=0, keepdims=True)
    upward = lax.rem(place_z + 1, 8)
    records = (strength, direction.astype(F32), cell.astype(F32), store.astype(F32))
    for j in range(8):
        for n, record in enumerate(records):
            send_ref[j, n] = record
        face = jnp.where(upward == j, columns[0:8], columns[8:16])
        send_ref[PLACE_Z[j], 4] = jnp.where(iota((8, 128), 0) == 5, body_row, face)
    own = owner_ref[pl.ds((place_x * 4 + place_y) * 8 + place_z, 1), :]
    own_ref[...] = jnp.zeros((8, 128), F32)
    for a in range(3):
        middle = pick([own == b for b in range(8)], [centre_ref[a, b] for b in range(8)], (1, 128))
        own_ref[a : a + 1, :] = (middle - 0.5) * (extents[a] / 128.0)


def second_kernel(got_ref, xy_ref, send_ref, total_ref):
    speeds = lattice_tables()[0]
    place_x, place_y, place_z = (lax.axis_index(a) for a in ("gx", "gy", "gz"))
    total_ref[...] = jnp.zeros_like(total_ref)
    count = iota((16, 128), 0).astype(F32)
    counts = [(count + 16.0 * g).astype(BF16) for g in range(16)]
    one = jnp.ones((16, 128), BF16)
    none = jnp.zeros((16, 128), BF16)

    order = [PLACE_Z.index(n) for n in range(8)]

    def gather(peer, carry):
        strength, direction = got_ref[peer, 0], got_ref[peer, 1]
        cell, store = got_ref[peer, 2].astype(I32), got_ref[peer, 3].astype(I32)
        is_dir = [direction == float(i) for i in range(19)]
        speed = [pick(is_dir, [float(v) for v in speeds[:, a]], (8, 128)) for a in range(3)]
        place = (
            lax.shift_right_logical(cell, 12) + (place_x * 4 - 16),
            (lax.shift_right_logical(cell, 7) & 31) + (place_y * 32 - 64),
            (cell & 127) + (listed(order, peer) * 128 - 512),
        )
        arm = [(place[a].astype(F32) + 0.5 * speed[a]) * (1.0 / 128.0) for a in range(3)]
        push = [speed[a] * strength for a in range(3)]
        loads = push + cross(arm, push)
        upper = [load.astype(BF16).astype(F32) for load in loads]
        rows = upper + [load - part for load, part in zip(loads, upper)]
        owner = lax.shift_right_logical(store, 7)
        mine = (owner & 7) == place_z
        high = jnp.where(mine, lax.shift_right_logical(owner, 4), 255).astype(F32)
        low = ((lax.shift_right_logical(owner, 3) & 1) * 128) + (store & 127)
        low = low.astype(F32)
        left, right = [], []
        for s in range(8):

            def line(x, s=s):
                return jnp.broadcast_to(x[s : s + 1], (16, 128)).astype(BF16)

            at = line(high) == counts[0]
            left.append(jnp.concatenate([jnp.where(at, line(x), none) for x in rows], axis=0))
            at = line(low)
            right.append(
                jnp.concatenate([jnp.where(at == number, one, none) for number in counts], axis=0)
            )
        total_ref[...] += rows_dot(
            jnp.concatenate(left, axis=1), jnp.concatenate(right, axis=1)
        )
        return carry

    lax.fori_loop(0, 8, gather, 0, unroll=8)

    body_row = sum(got_ref[peer, 4, 5:6, :] for peer in range(8))
    for c in range(6):
        for e in range(2):
            lanes = slice(128 * e, 128 * e + 128)
            upper = total_ref[16 * c : 16 * c + 16, lanes]
            both = upper + total_ref[96 + 16 * c : 112 + 16 * c, lanes]
            for h in range(16):
                send_ref[PLACE_Y[(2 * h + e) % 4] * 8 + PLACE_X[(2 * h + e) // 4], c : c + 1, :] = both[h : h + 1]
    last = jnp.concatenate([body_row, jnp.zeros((1, 128), F32)], axis=0)
    for j in range(32):
        send_ref[j, 6:8, :] = last

    below = got_ref[listed(PLACE_Z, lax.rem(place_z + 7, 8)), 4]
    above = got_ref[listed(PLACE_Z, lax.rem(place_z + 1, 8)), 4]
    lane = iota((1, 128), 1)

    def turned(x, by):
        return pltpu.roll(x, by, 1)

    to_xp = jnp.where(lane < 32, turned(below[1:2], 32), turned(above[1:2], 64))
    to_xm = jnp.where(lane < 32, below[2:3], turned(above[2:3], 32))
    in_row = lane & 31
    to_yp = jnp.where(in_row == 0, turned(below[3:4], 97), turned(above[3:4], 98))
    to_ym = jnp.where(in_row == 0, below[4:5], turned(above[4:5], 1))
    has_xp, has_xm = place_x < 7, place_x > 0
    has_yp, has_ym = place_y < 3, place_y > 0
    for there, dx, dy, line in (
        (has_xp, 1, 0, to_xp),
        (has_xm, -1, 0, to_xm),
        (has_yp, 0, 1, to_yp),
        (has_ym, 0, -1, to_ym),
        (has_xp & has_yp, 1, 1, xy_ref[0:1, :]),
        (has_xm & has_ym, -1, -1, xy_ref[1:2, :]),
        (has_xp & has_ym, 1, -1, xy_ref[2:3, :]),
        (has_xm & has_yp, -1, 1, xy_ref[3:4, :]),
    ):

        @pl.when(there)
        def _(dx=dx, dy=dy, line=line):
            send_ref[peer_at(place_x + dx, place_y + dy), 7:8, :] = line


def arrivals(lines):
    blank = jnp.zeros((128 - len(lines), 128), F32)
    return jnp.transpose(jnp.concatenate(lines + [blank], axis=0))


def shifted(line, cx, cy):
    by = 32 * cx + cy
    return pltpu.roll(line, by % 128, 1) if by else line


def finish(block, i, column, code, value):
    cz = int(lattice_tables()[0][i, 2])
    if cz:
        block = pltpu.roll(block, 1 if cz == 1 else 127, 1)
        at = 0 if cz == 1 else 127
        block = jnp.where(iota(block.shape, 1) == at, column, block)
    if i:
        opposite = i + 1 if i % 2 else i - 1
        block = jnp.where(code == float(opposite), value, block)
    return block


def third_kernel(
    post_ref,
    bounce_ref,
    wall_ref,
    got1_ref,
    motion_hbm,
    mass_hbm,
    inertia_hbm,
    cell_hbm,
    moved_hbm,
    value_ref,
    step_ref,
    moved_ref,
    cell_ref,
    motion_ref,
    mass_ref,
    inertia_ref,
    sems,
):
    speeds = lattice_tables()[0].astype(int)
    place_z = lax.axis_index("gz")
    fetches = [
        pltpu.make_async_copy(motion_hbm, motion_ref, sems.at[19]),
        pltpu.make_async_copy(mass_hbm, mass_ref, sems.at[20]),
        pltpu.make_async_copy(inertia_hbm, inertia_ref, sems.at[21]),
    ]
    cells = pltpu.make_async_copy(cell_hbm, cell_ref, sems.at[22])
    cells.start()
    for fetch in fetches:
        fetch.start()
    cells.wait()
    cell = flat(cell_ref[...])
    spread = []
    for part in halves(wall_ref[...]):
        part = jnp.broadcast_to(flat(part.astype(F32)), (16, 1024)).astype(BF16)
        spread += groups(cell & 127, part)
    laid = rows_dot(hot(lax.shift_right_logical(cell, 7)), jnp.concatenate(spread, axis=0))
    value_ref[...] = bounce_ref[1] - (laid[:, 0:128] + laid[:, 128:256])
    below = got1_ref[listed(PLACE_Z, lax.rem(place_z + 7, 8)), 4]
    above = got1_ref[listed(PLACE_Z, lax.rem(place_z + 1, 8)), 4]
    order = ZP + ZM
    lines = []
    for dirs, face in ((ZP, below), (ZM, above)):
        for n, i in enumerate(dirs):
            lines.append(shifted(face[n : n + 1], int(speeds[i, 0]), int(speeds[i, 1])))
    columns = arrivals(lines)
    copies = []
    for i in range(19):
        cx, cy, cz = (int(v) for v in speeds[i])
        planes = {0: (0, 4), 1: (1, 4), -1: (0, 3)}[cx]
        first, last = {0: (0, 32), 1: (8, 32), -1: (0, 24)}[cy]
        for x in range(*planes):
            source = 32 * (x - cx) - cy
            block = post_ref[i, source + first : source + last, :]
            rows = slice(32 * x + first, 32 * x + last)
            column = None
            if cz:
                n = order.index(i)
                column = columns[rows, n : n + 1]
            code, value = bounce_ref[0, rows, :], value_ref[rows, :]
            moved_ref[i, x, first:last, :] = finish(block, i, column, code, value)
        part = (i, slice(*planes), slice(first, last))
        copy = pltpu.make_async_copy(moved_ref.at[part], moved_hbm.at[part], sems.at[i])
        copy.start()
        copies.append(copy)

    for fetch in fetches:
        fetch.wait()
    at_lane, at_row = iota((8, 128), 1), iota((8, 128), 0)
    scale = jnp.zeros((8, 128), F32)
    for c in range(6):
        for b in range(8):
            value = mass_ref[b] if c < 3 else inertia_ref[c - 3, b]
            scale = jnp.where((at_lane == c) & (at_row == b), value, scale)
    step_ref[0] = scale
    step_ref[1] = jnp.concatenate([motion_ref[...], jnp.zeros((8, 122), F32)], axis=1)
    for copy in copies:
        copy.wait()


def face_kernel(
    partly_hbm,
    post_ref,
    bounce_ref,
    value_ref,
    xp_ref,
    xm_ref,
    yp_ref,
    ym_ref,
    moved_hbm,
    moved_ref,
    sems,
):
    del partly_hbm
    speeds = lattice_tables()[0].astype(int)
    place_x, place_y = lax.axis_index("gx"), lax.axis_index("gy")
    has_xp, has_xm = place_x < 7, place_x > 0
    has_yp, has_ym = place_y < 3, place_y > 0
    copies = []

    def send(*part):
        copy = pltpu.make_async_copy(
            moved_ref.at[part], moved_hbm.at[part], sems.at[len(copies)]
        )
        copy.start()
        copies.append(copy)

    for i in (1, 2, 7, 8, 9, 10):
        cx, cy = (int(v) for v in speeds[i, :2])
        x = 0 if cx == 1 else 3
        first, last = {0: (0, 32), 1: (8, 32), -1: (0, 24)}[cy]
        there, face = (has_xm, xp_ref[XP.index(i)]) if cx == 1 else (has_xp, xm_ref[XM.index(i)])
        block = jnp.where(there, face[first - cy : last - cy], 0.0)
        rows = slice(32 * x + first, 32 * x + last)
        code, value = bounce_ref[0, rows, :], value_ref[rows, :]
        moved_ref[i, x, first:last, :] = finish(block, i, None, code, value)
        send(i, x, slice(first, last))
    at_row = iota((8, 128), 0)
    for i in (3, 4, 7, 8, 9, 10):
        cx, cy = (int(v) for v in speeds[i, :2])
        planes = {0: (0, 4), 1: (1, 4), -1: (0, 3)}[cx]
        first = 0 if cy == 1 else 24
        face_ref, n = (yp_ref, YP.index(i)) if cy == 1 else (ym_ref, YM.index(i))
        for x in range(*planes):
            source = x - cx
            block = post_ref[i, 32 * source + first : 32 * source + first + 8, :]
            line = face_ref[4 * n + source : 4 * n + source + 1, :]
            line = jnp.where(has_ym if cy == 1 else has_yp, line, 0.0)
            block = pltpu.roll(block, 1 if cy == 1 else 7, 0)
            block = jnp.where(at_row == (0 if cy == 1 else 7), line, block)
            rows = slice(32 * x + first, 32 * x + first + 8)
            code, value = bounce_ref[0, rows, :], value_ref[rows, :]
            moved_ref[i, x, first : first + 8, :] = finish(block, i, None, code, value)
        send(i, slice(*planes), slice(first, first + 8))
    for copy in copies:
        copy.wait()


def fourth_kernel(
    partly_hbm,
    post_ref,
    bounce_ref,
    value_ref,
    own_ref,
    got1_ref,
    got2_ref,
    xp_ref,
    xm_ref,
    yp_ref,
    ym_ref,
    step_ref,
    moved_hbm,
    load_hbm,
    next_hbm,
    row_ref,
    edge_ref,
    load_ref,
    next_ref,
    sems,
):
    del partly_hbm
    speeds = lattice_tables()[0].astype(int)
    place_x, place_y, place_z = (lax.axis_index(a) for a in ("gx", "gy", "gz"))
    has_xp, has_xm = place_x < 7, place_x > 0
    has_yp, has_ym = place_y < 3, place_y > 0
    copies = []

    def send(source, target):
        copy = pltpu.make_async_copy(source, target, sems.at[len(copies)])
        copy.start()
        copies.append(copy)

    parts = [got2_ref[j] for j in range(32)]
    while len(parts) > 1:
        parts = [a + b for a, b in zip(parts[0::2], parts[1::2])]
    total = parts[0]
    push = [total[a : a + 1] for a in range(3)]
    away = cross([own_ref[a : a + 1, :] for a in range(3)], push)
    turn = [total[3 + a : 4 + a] - away[a] for a in range(3)]
    load_ref[...] = jnp.concatenate(push + turn, axis=0)
    send(load_ref, load_hbm)
    at_lane, at_row = iota((8, 128), 1), iota((8, 128), 0)
    own = jnp.where((at_lane & 7) == at_row, total[6:7], 0.0)
    body_load = jnp.zeros((8, 128), F32)
    for c in range(6):
        here = lax.shift_right_logical(at_lane, 3) == c
        column = jnp.sum(jnp.where(here, own, 0.0), axis=1, keepdims=True)
        body_load = jnp.where(at_lane == c, column, body_load)
    next_ref[...] = (step_ref[1] + step_ref[0] * body_load / 32768.0)[:, 0:6]
    send(next_ref, next_hbm)

    def edge(there, dx, dy):
        line = got2_ref[peer_at(place_x + dx, place_y + dy), 7:8, :]
        return jnp.where(there, line, 0.0)

    lane = iota((1, 128), 1)
    row_in_plane = lane & 31
    from_x = {1: edge(has_xm, -1, 0), -1: edge(has_xp, 1, 0)}
    from_y = {1: edge(has_ym, 0, -1), -1: edge(has_yp, 0, 1)}
    from_xy = {
        (1, 1): edge(has_xm & has_ym, -1, -1),
        (-1, -1): edge(has_xp & has_yp, 1, 1),
        (1, -1): edge(has_xm & has_yp, -1, 1),
        (-1, 1): edge(has_xp & has_ym, 1, -1),
    }
    order, lines = [], []
    for dirs, face in (
        (ZP, got1_ref[listed(PLACE_Z, lax.rem(place_z + 7, 8)), 4]),
        (ZM, got1_ref[listed(PLACE_Z, lax.rem(place_z + 1, 8)), 4]),
    ):
        for n, i in enumerate(dirs):
            cx, cy, cz = (int(v) for v in speeds[i])
            if cx == 1:
                line = from_x[1] if cz == 1 else pltpu.roll(from_x[1], 96, 1)
            elif cx == -1:
                line = pltpu.roll(from_x[-1], 96 if cz == 1 else 64, 1)
            elif cy == 1:
                came = from_y[1] if cz == 1 else pltpu.roll(from_y[1], 127, 1)
                line = jnp.where(row_in_plane == 0, came, shifted(face[n : n + 1], 0, 1))
            elif cy == -1:
                came = pltpu.roll(from_y[-1], 31 if cz == 1 else 30, 1)
                line = jnp.where(row_in_plane == 31, came, shifted(face[n : n + 1], 0, -1))
            else:
                continue
            order.append(i)
            lines.append(line)
    columns = arrivals(lines)

    for i in (7, 9, 8, 10, 15, 17, 16, 18):
        cx, cy, cz = (int(v) for v in speeds[i])
        first = 0 if cy == 1 else 24
        face_ref, n = (yp_ref, YP.index(i)) if cy == 1 else (ym_ref, YM.index(i))
        planes = range(4) if cz else ((0,) if cx == 1 else (3,))
        for x in planes:
            source = x - cx
            if cz:
                block = post_ref[i, 32 * source + first : 32 * source + first + 8, :]
                line = face_ref[4 * n + source : 4 * n + source + 1, :]
                line = jnp.where(has_ym if cy == 1 else has_yp, line, 0.0)
            else:
                if source < 0:
                    block = jnp.where(has_xm, xp_ref[XP.index(i), first : first + 8, :], 0.0)
                else:
                    block = jnp.where(has_xp, xm_ref[XM.index(i), first : first + 8, :], 0.0)
                line = from_xy[cx, cy]
            block = pltpu.roll(block, 1 if cy == 1 else 7, 0)
            block = jnp.where(at_row == (0 if cy == 1 else 7), line, block)
            rows = slice(32 * x + first, 32 * x + first + 8)
            column = None
            if cz:
                m = order.index(i)
                column = columns[rows, m : m + 1]
            code, value = bounce_ref[0, rows, :], value_ref[rows, :]
            row_ref[i - 7, x] = finish(block, i, column, code, value)
        part = slice(planes[0], planes[-1] + 1)
        send(row_ref.at[i - 7, part], moved_hbm.at[i, part, first : first + 8, :])
    for number, i in enumerate((11, 13, 14, 12)):
        cx = int(speeds[i, 0])
        x = 0 if cx == 1 else 3
        if cx == 1:
            block = jnp.where(has_xm, xp_ref[XP.index(i)], 0.0)
        else:
            block = jnp.where(has_xp, xm_ref[XM.index(i)], 0.0)
        rows = slice(32 * x, 32 * x + 32)
        m = order.index(i)
        code, value = bounce_ref[0, rows, :], value_ref[rows, :]
        edge_ref[number] = finish(block, i, columns[rows, m : m + 1], code, value)
        send(edge_ref.at[number], moved_hbm.at[i, x])

    for copy in copies:
        copy.wait()


def body(
    populations,
    solid,
    link_cell,
    link_dir,
    link_store,
    store_body,
    motion,
    inv_mass,
    inv_inertia,
    centre,
    rates,
):
    vmem = pl.BlockSpec(memory_space=pltpu.VMEM)

    def array(*shape):
        return jax.ShapeDtypeStruct(shape, F32)

    params = pltpu.CompilerParams(vmem_limit_bytes=40 * 1024 * 1024)
    post, bounce, send1, xp, xm, yp, ym, xy, own, wall = pl.pallas_call(
        first_kernel,
        out_shape=(
            array(19, 128, 128),
            array(2, 128, 128),
            array(8, 5, 8, 128),
            array(5, 32, 128),
            array(5, 32, 128),
            array(24, 128),
            array(24, 128),
            array(8, 128),
            array(8, 128),
            array(8, 128),
        ),
        in_specs=[pl.BlockSpec(memory_space=pltpu.HBM)] * 9,
        out_specs=(vmem,) * 10,
        scratch_shapes=[
            pltpu.VMEM((19, 128, 128), F32),
            pltpu.VMEM((128, 128), I32),
            pltpu.VMEM((8, 128), I32),
            pltpu.VMEM((8, 128), I32),
            pltpu.VMEM((8, 128), I32),
            pltpu.VMEM((256, 128), I32),
            pltpu.SMEM((8, 6), F32),
            pltpu.SMEM((3, 8), F32),
            pltpu.SMEM((15,), F32),
            pltpu.SemaphoreType.DMA((4,)),
            pltpu.SemaphoreType.DMA((8,)),
        ],
        compiler_params=params,
        name="collide",
    )(
        *(
            pltpu.with_memory_space_constraint(x, pltpu.HBM)
            for x in (
                populations.reshape(19, 128, 128),
                solid.reshape(128, 128),
                link_cell.reshape(8, 128),
                link_dir.reshape(8, 128),
                link_store.reshape(8, 128),
                store_body.reshape(256, 128),
                motion,
                centre.T,
                rates,
            )
        )
    )

    def shift(x, axis, by):
        size = lax.axis_size(axis)
        return lax.ppermute(x, axis, [(i, (i + by) % size) for i in range(size)])

    along_z = [[PLACE_Z.index(n) for n in range(8)]]
    got1 = lax.all_to_all(send1, "gz", 0, 0, axis_index_groups=along_z, tiled=True)
    send2 = pl.pallas_call(
        second_kernel,
        out_shape=array(32, 8, 128),
        in_specs=[vmem] * 2,
        out_specs=vmem,
        scratch_shapes=[pltpu.VMEM((192, 256), F32)],
        compiler_params=params,
        cost_estimate=pl.CostEstimate(
            flops=2 * 192 * 256 * 8192, bytes_accessed=4 * 4 * 8192, transcendentals=0
        ),
        name="bins",
    )(got1, xy)
    xp, xm = shift(xp, "gx", 1), shift(xm, "gx", -1)
    yp, ym = shift(yp, "gy", 1), shift(ym, "gy", -1)
    across = [[PLACE_Y.index(n // 8) * 8 + PLACE_X.index(n % 8) for n in range(32)]]
    got2 = lax.all_to_all(send2, ("gy", "gx"), 0, 0, axis_index_groups=across, tiled=True)
    hbm = pl.BlockSpec(memory_space=pltpu.HBM)
    partly, value, step = pl.pallas_call(
        third_kernel,
        out_shape=(array(19, 4, 32, 128), array(128, 128), array(2, 8, 128)),
        in_specs=[vmem] * 4 + [hbm] * 4,
        out_specs=(hbm, vmem, vmem),
        scratch_shapes=[
            pltpu.VMEM((19, 4, 32, 128), F32),
            pltpu.VMEM((8, 128), I32),
            pltpu.VMEM((8, 6), F32),
            pltpu.SMEM((8,), F32),
            pltpu.SMEM((3, 8), F32),
            pltpu.SemaphoreType.DMA((23,)),
        ],
        compiler_params=params,
        cost_estimate=pl.CostEstimate(
            flops=19 * 16384 * 4, bytes_accessed=2 * 19 * 16384 * 4, transcendentals=0
        ),
        name="move",
    )(
        *(post, bounce, wall, got1),
        *(
            pltpu.with_memory_space_constraint(x, pltpu.HBM)
            for x in (motion, inv_mass, inv_inertia.T, link_cell.reshape(8, 128))
        ),
    )
    partly = pl.pallas_call(
        face_kernel,
        out_shape=array(19, 4, 32, 128),
        in_specs=[hbm] + [vmem] * 7,
        out_specs=hbm,
        scratch_shapes=[pltpu.VMEM((19, 4, 32, 128), F32), pltpu.SemaphoreType.DMA((12,))],
        input_output_aliases={0: 0},
        compiler_params=params,
        name="faces",
    )(partly, post, bounce, value, xp, xm, yp, ym)
    moved, own_loads, motion_next = pl.pallas_call(
        fourth_kernel,
        out_shape=(array(19, 4, 32, 128), array(6, 128), array(8, 6)),
        in_specs=[hbm] + [vmem] * 11,
        out_specs=(hbm,) * 3,
        scratch_shapes=[
            pltpu.VMEM((12, 4, 8, 128), F32),
            pltpu.VMEM((4, 32, 128), F32),
            pltpu.VMEM((6, 128), F32),
            pltpu.VMEM((8, 6), F32),
            pltpu.SemaphoreType.DMA((14,)),
        ],
        input_output_aliases={0: 0},
        compiler_params=params,
        name="close",
    )(partly, post, bounce, value, own, got1, got2, xp, xm, yp, ym, step)
    return (moved, own_loads, motion_next)


def solution(mesh):
    return jax.shard_map(
        body,
        mesh=mesh,
        in_specs=(
            P(None, "gx", "gy", "gz"),
            P("gx", "gy", "gz"),
            P("gx", "gy", "gz", None),
            P("gx", "gy", "gz", None),
            P("gx", "gy", "gz", None),
            P(),
            P(),
            P(),
            P(),
            P(),
            P(),
        ),
        out_specs=(P(None, "gx", "gy", "gz"), P(None, ("gx", "gy", "gz")), P()),
        check_vma=False,
    )
```

```python
import math

import jax
import jax.numpy as jnp
import numpy as np
from jax import lax
from jax.experimental import pallas as pl
from jax.experimental.pallas import tpu as pltpu
from jax.sharding import PartitionSpec as P

F32 = jnp.float32
BF16 = jnp.bfloat16
I32 = jnp.int32

XP, XM = (1, 7, 9, 11, 13), (2, 10, 8, 14, 12)
YP, YM = (3, 7, 10, 15, 17), (4, 9, 8, 18, 16)
ZP, ZM = (5, 11, 14, 15, 18), (6, 13, 12, 17, 16)


def lattice_tables():
    speed_list = [
        [0, 0, 0],
        [1, 0, 0],
        [-1, 0, 0],
        [0, 1, 0],
        [0, -1, 0],
        [0, 0, 1],
        [0, 0, -1],
        [1, 1, 0],
        [-1, -1, 0],
        [1, -1, 0],
        [-1, 1, 0],
        [1, 0, 1],
        [-1, 0, -1],
        [1, 0, -1],
        [-1, 0, 1],
        [0, 1, 1],
        [0, -1, -1],
        [0, 1, -1],
        [0, -1, 1],
    ]
    speeds = np.array(speed_list) * 1.0
    weights = np.array([1.0 / 3.0] + [1.0 / 18.0] * 6 + [1.0 / 36.0] * 12)
    along_x = speeds[:, 0]
    along_y = speeds[:, 1]
    along_z = speeds[:, 2]
    square = along_x * along_x + along_y * along_y + along_z * along_z
    polynomials = np.stack(
        [
            np.ones(19),
            along_x,
            along_y,
            along_z,
            square,
            3 * along_x * along_x - square,
            along_y * along_y - along_z * along_z,
            along_x * along_y,
            along_y * along_z,
            along_x * along_z,
            along_x * square,
            along_y * square,
            along_z * square,
            square * square,
            (3 * along_x * along_x - square) * square,
            (along_y * along_y - along_z * along_z) * square,
            along_x * (along_y * along_y - along_z * along_z),
            along_y * (along_z * along_z - along_x * along_x),
            along_z * (along_x * along_x - along_y * along_y),
        ],
        axis=1,
    )
    columns = []
    for column_index in range(19):
        vector = polynomials[:, column_index] * 1.0
        for repeat in range(2):
            for earlier in columns:
                vector = vector - np.dot(earlier, vector) * earlier
        columns.append(vector / math.sqrt(float(np.dot(vector, vector))))
    return (speeds, weights, np.stack(columns))


def collision_scalars(rate):
    m = lattice_tables()[2]
    r = {k: rate(k - 4) for k in range(4, 19)}
    f = lambda v: float(v)
    out = {}
    for name, column in (("rest", 0), ("axis", 1), ("diag", 7)):
        for other, column2 in (("rest", 0), ("axis", 1), ("diag", 7)):
            out[name, other] = r[4] * f(m[4, column] * m[4, column2]) + r[13] * f(
                m[13, column] * m[13, column2]
            )
    a5, b5, a14, b14 = m[5, 1] / 2, m[5, 7], m[14, 1] / 2, m[14, 7]
    out["uu"] = r[5] * f(a5 * a5) + r[14] * f(a14 * a14)
    out["uv"] = r[5] * f(a5 * b5) + r[14] * f(a14 * b14)
    out["vv"] = r[5] * f(b5 * b5) + r[14] * f(b14 * b14)
    a6, b6, a15, b15 = m[6, 3], m[6, 7], m[15, 3], m[15, 7]
    out["pp"] = r[6] * f(a6 * a6) + r[15] * f(a15 * a15)
    out["pq"] = r[6] * f(a6 * b6) + r[15] * f(a15 * b15)
    out["qq"] = r[6] * f(b6 * b6) + r[15] * f(b15 * b15)
    out["sxy"] = r[7] * f(m[7, 7] ** 2)
    out["syz"] = r[8] * f(m[8, 15] ** 2)
    out["sxz"] = r[9] * f(m[9, 11] ** 2)
    for name, row, axis, diag in (("x", 10, 1, 7), ("y", 11, 3, 7), ("z", 12, 5, 11)):
        out["aa" + name] = r[row] * f(m[row, axis] ** 2)
        out["ab" + name] = r[row] * f(m[row, axis] * m[row, diag])
        out["bb" + name] = r[row] * f(m[row, diag] ** 2)
    out["tx"] = r[16] * f(m[16, 7] ** 2)
    out["ty"] = r[17] * f(m[17, 15] ** 2)
    out["tz"] = r[18] * f(m[18, 11] ** 2)
    return out


def collide(f, k):
    w1, w2 = 1.0 / 18.0, 1.0 / 36.0
    pairs = ((1, 2), (3, 4), (5, 6), (7, 8), (9, 10), (11, 12), (13, 14), (15, 16), (17, 18))
    plus = [f[i] + f[o] for i, o in pairs]
    minus = [f[i] - f[o] for i, o in pairs]
    sx, sy, sz, sa, sb, sc, sd, se, sg = plus
    dx, dy, dz, da, db, dc, dd, de, dg = minus
    density = f[0] + ((sx + sy + sz) + (sa + sb) + (sc + sd) + (se + sg))
    jx = dx + (da + db) + (dc + dd)
    jy = dy + (da - db) + (de + dg)
    jz = dz + (dc - dd) + (de - dg)
    magnitude = jx * jx + jy * jy + jz * jz
    base = density - 1.5 * magnitude
    axis_base = (2.0 * w1) * base
    diag_base = (2.0 * w2) * base
    n0 = f[0] - (1.0 / 3.0) * base
    sx = sx - (axis_base + (9.0 * w1) * (jx * jx))
    sy = sy - (axis_base + (9.0 * w1) * (jy * jy))
    sz = sz - (axis_base + (9.0 * w1) * (jz * jz))

    def diagonal(s, project):
        return s - (diag_base + (9.0 * w2) * (project * project))

    sa, sb = diagonal(sa, jx + jy), diagonal(sb, jx - jy)
    sc, sd = diagonal(sc, jx + jz), diagonal(sd, jx - jz)
    se, sg = diagonal(se, jy + jz), diagonal(sg, jy - jz)
    dx, dy, dz = dx - (6.0 * w1) * jx, dy - (6.0 * w1) * jy, dz - (6.0 * w1) * jz
    hx, hy, hz = (6.0 * w2) * jx, (6.0 * w2) * jy, (6.0 * w2) * jz
    da, db = da - (hx + hy), db - (hx - hy)
    dc, dd = dc - (hx + hz), dd - (hx - hz)
    de, dg = de - (hy + hz), dg - (hy - hz)
    exy, exz, eyz = sa + sb, sc + sd, se + sg
    axis_sum = sx + sy + sz
    diag_sum = exy + exz + eyz
    g0 = k["rest", "rest"] * n0 + k["rest", "axis"] * axis_sum + k["rest", "diag"] * diag_sum
    ga = k["axis", "rest"] * n0 + k["axis", "axis"] * axis_sum + k["axis", "diag"] * diag_sum
    gd = k["diag", "rest"] * n0 + k["diag", "axis"] * axis_sum + k["diag", "diag"] * diag_sum
    u = 2.0 * sx - sy - sz
    v = exy + exz - 2.0 * eyz
    gu = k["uu"] * u + k["uv"] * v
    gv = k["uv"] * u + k["vv"] * v
    p = sy - sz
    q = exy - exz
    gp = k["pp"] * p + k["pq"] * q
    gq = k["pq"] * p + k["qq"] * q
    ga_u, gd_v = ga - gu, gd + gv
    even = [ga + 2.0 * gu, ga_u + gp, ga_u - gp]
    gxy, gxz, gyz = gd_v + gq, gd_v - gq, gd - 2.0 * gv
    for total, one, two, rate in ((gxy, sa, sb, "sxy"), (gxz, sc, sd, "sxz"), (gyz, se, sg, "syz")):
        shear = k[rate] * (one - two)
        even += [total + shear, total - shear]
    x_xy, x_xz = da + db, dc + dd
    y_xy, y_yz = da - db, de + dg
    z_xz, z_yz = dc - dd, de - dg
    x_all, y_all, z_all = x_xy + x_xz, y_xy + y_yz, z_xz + z_yz
    ox = k["aax"] * dx + k["abx"] * x_all
    oy = k["aay"] * dy + k["aby"] * y_all
    oz = k["aaz"] * dz + k["abz"] * z_all
    bx = k["abx"] * dx + k["bbx"] * x_all
    by = k["aby"] * dy + k["bby"] * y_all
    bz = k["abz"] * dz + k["bbz"] * z_all
    tx, ty, tz = k["tx"] * (x_xy - x_xz), k["ty"] * (y_yz - y_xy), k["tz"] * (z_xz - z_yz)
    x_on_xy, x_on_xz = bx + tx, bx - tx
    y_on_yz, y_on_xy = by + ty, by - ty
    z_on_xz, z_on_yz = bz + tz, bz - tz
    odd = [ox, oy, oz]
    odd += [x_on_xy + y_on_xy, x_on_xy - y_on_xy]
    odd += [x_on_xz + z_on_xz, x_on_xz - z_on_xz]
    odd += [y_on_yz + z_on_yz, y_on_yz - z_on_yz]
    post = [f[0] - g0]
    for (i, o), even_part, odd_part in zip(pairs, even, odd):
        post += [f[i] - (even_part + odd_part), f[o] - (even_part - odd_part)]
    return post


def halves(x):
    high = x.astype(BF16)
    return high, (x - high.astype(F32)).astype(BF16)


def rows_dot(a, b):
    return lax.dot_general(a, b, (((1,), (1,)), ((), ())), preferred_element_type=F32)


PLACE_X = (0, 4, 1, 5, 2, 6, 3, 7)
PLACE_Y = (0, 1, 2, 3)
PLACE_Z = (0, 2, 4, 6, 1, 3, 5, 7)


def listed(table, index):
    return sum(jnp.where(index == n, value, 0) for n, value in enumerate(table))


def peer_at(x, y):
    return listed(PLACE_Y, y) * 8 + listed(PLACE_X, x)


def flat(x):
    return jnp.concatenate([x[s : s + 1] for s in range(8)], axis=1)


def fold(x):
    return jnp.concatenate([x[:, 128 * s : 128 * s + 128] for s in range(8)], axis=0)


def cross(a, b):
    return [a[(i + 1) % 3] * b[(i + 2) % 3] - a[(i + 2) % 3] * b[(i + 1) % 3] for i in range(3)]


def groups(index, value):
    index = jnp.broadcast_to(index.astype(F32), value.shape).astype(BF16)
    none = jnp.zeros_like(value)
    return [
        jnp.where(index == (iota(value.shape, 0) + 16 * g).astype(F32).astype(BF16), value, none)
        for g in range(8)
    ]


def hot(index):
    return jnp.concatenate(groups(index, jnp.ones((16, index.shape[1]), BF16)), axis=0)


def iota(shape, dim):
    return lax.broadcasted_iota(I32, shape, dim)


def pick(conditions, values, shape):
    result = jnp.zeros(shape, F32)
    for condition, value in zip(conditions, values):
        if isinstance(value, float) and value == 0.0:
            continue
        result = jnp.where(condition, value, result)
    return result


def first_kernel(
    pop_hbm,
    solid_hbm,
    cell_hbm,
    dir_hbm,
    store_hbm,
    owner_hbm,
    motion_hbm,
    centre_hbm,
    rates_hbm,
    post_ref,
    bounce_ref,
    send_ref,
    xp_ref,
    xm_ref,
    yp_ref,
    ym_ref,
    xy_ref,
    own_ref,
    wall_ref,
    pop_ref,
    solid_ref,
    cell_ref,
    dir_ref,
    store_ref,
    owner_ref,
    motion_ref,
    centre_ref,
    rates_ref,
    pop_sem,
    sems,
):
    small = (
        (cell_hbm, cell_ref),
        (dir_hbm, dir_ref),
        (store_hbm, store_ref),
        (owner_hbm, owner_ref),
        (motion_hbm, motion_ref),
        (centre_hbm, centre_ref),
        (rates_hbm, rates_ref),
        (solid_hbm, solid_ref),
    )
    copies = [pltpu.make_async_copy(a, b, sems.at[n]) for n, (a, b) in enumerate(small)]

    def plane(x):
        rows = pl.ds(x * 32, 32)
        return pltpu.make_async_copy(
            pop_hbm.at[:, rows, :], pop_ref.at[:, rows, :], pop_sem.at[x]
        )

    for copy in copies:
        copy.start()
    for x in range(4):
        plane(x).start()
    for copy in copies[0:3]:
        copy.wait()
    speeds, weights, _ = lattice_tables()
    links = 1024
    place_x, place_y, place_z = (lax.axis_index(a) for a in ("gx", "gy", "gz"))
    cell = cell_ref[...]
    direction = dir_ref[...]
    store = store_ref[...]
    live = store < 32768
    row = lax.shift_right_logical(cell, 7)
    lane = cell & 127
    flat_row = flat(row)
    flat_lane = flat(lane)
    rows_hot16 = hot(flat_row)
    lanes_hot16 = hot(flat_lane)
    flat_store = flat(store)
    low_hot = hot(flat_store & 127)
    for copy in copies[3:6]:
        copy.wait()
    by_high = jnp.dot(
        owner_ref[...].astype(F32).astype(BF16), low_hot, preferred_element_type=F32
    )
    here = iota((256, links), 0) == lax.shift_right_logical(flat_store, 7)
    body = fold(jnp.sum(jnp.where(here, by_high, 0.0), axis=0, keepdims=True))
    is_dir = [direction == i for i in range(19)]
    shape = direction.shape
    speed = [pick(is_dir, [float(s) for s in speeds[:, a]], shape) for a in range(3)]
    weight = jnp.where(direction <= 6, float(weights[1]), float(weights[7]))
    is_body = [body == float(b) for b in range(8)]
    move = [pick(is_body, [motion_ref[b, c] for b in range(8)], shape) for c in range(6)]
    middle = [pick(is_body, [centre_ref[a, b] for b in range(8)], shape) for a in range(3)]
    place = (
        lax.shift_right_logical(cell, 12) + place_x * 4,
        (row & 31) + place_y * 32,
        lane + place_z * 128,
    )
    extents = (32.0, 128.0, 1024.0)
    radius = [
        (place[a].astype(F32) + 0.5 * speed[a] - middle[a] * extents[a]) / 128.0 for a in range(3)
    ]

    spin = cross(move[3:], radius)
    normal = sum(speed[a] * (move[a] + spin[a]) for a in range(3))
    wall = 6.0 * weight * normal
    wall_ref[...] = wall
    coded = flat(jnp.where(live, direction, 0).astype(F32))
    coded = jnp.broadcast_to(coded, (16, links)).astype(BF16)
    spread = jnp.concatenate(groups(flat_lane, coded), axis=0)
    bounce_ref[0] = rows_dot(rows_hot16, spread)

    for copy in copies[6:8]:
        copy.wait()
    k = collision_scalars(lambda i: rates_ref[i])

    def block(step, carry):
        rows = pl.ds(pl.multiple_of(step * 8, 8), 8)
        f = [pop_ref[i, rows, :] for i in range(19)]
        post = collide(f, k)
        fixed = solid_ref[rows, :] == 1
        post = [jnp.where(fixed, before, after) for before, after in zip(f, post)]
        code = bounce_ref[0, rows, :]
        found = jnp.zeros((8, 128), F32)
        for i in range(19):
            post_ref[i, rows, :] = post[i]
            if i:
                found = jnp.where(code == float(i), post[i], found)
        bounce_ref[1, rows, :] = found
        return carry

    def slab(x, carry):
        plane(x).wait()
        for part in range(4):
            block(x * 4 + part, 0)
        return carry

    lax.fori_loop(0, 4, slab, 0)

    at_lane = iota((128, 128), 1)
    column = jnp.zeros((128, 128), F32)
    for n in range(5):
        column = jnp.where(at_lane == n, pltpu.roll(post_ref[ZP[n]], n + 1, 1), column)
        column = jnp.where(at_lane == 8 + n, pltpu.roll(post_ref[ZM[n]], 8 + n, 1), column)
    columns = jnp.transpose(column)
    for n in range(5):
        xp_ref[n] = post_ref[XP[n], 96:128, :]
        xm_ref[n] = post_ref[XM[n], 0:32, :]
        for x in range(4):
            yp_ref[4 * n + x : 4 * n + x + 1, :] = post_ref[YP[n], 32 * x + 31 : 32 * x + 32, :]
            ym_ref[4 * n + x : 4 * n + x + 1, :] = post_ref[YM[n], 32 * x : 32 * x + 1, :]
    yp_ref[20:24, :] = jnp.zeros((4, 128), F32)
    ym_ref[20:24, :] = jnp.zeros((4, 128), F32)
    xy_ref[...] = jnp.zeros((8, 128), F32)
    xy_ref[0:1, :] = post_ref[7, 127:128, :]
    xy_ref[1:2, :] = post_ref[8, 0:1, :]
    xy_ref[2:3, :] = post_ref[9, 96:97, :]
    xy_ref[3:4, :] = post_ref[10, 31:32, :]

    found_high, found_low = halves(bounce_ref[1])
    by_row = jnp.dot(
        jnp.concatenate([found_high, found_low], axis=0), lanes_hot16, preferred_element_type=F32
    )
    by_row = jnp.where(
        iota((128, links), 0) == flat_row, by_row[0:128] + by_row[128:256], 0.0
    )
    picked = fold(jnp.sum(by_row, axis=0, keepdims=True))
    strength = jnp.where(live, 2.0 * picked - wall, 0.0)
    push = [speed[a] * strength for a in range(3)]
    sums = []
    for load in push + cross(radius, push):
        for b in range(8):
            sums.append(jnp.sum(jnp.where(is_body[b], load, 0.0), axis=0, keepdims=True))
    sums = jnp.sum(jnp.concatenate(sums, axis=0), axis=1, keepdims=True)
    sums = jnp.where(iota((48, 128), 0) == iota((48, 128), 1), sums, 0.0)
    body_row = jnp.sum(sums, axis=0, keepdims=True)
    upward = lax.rem(place_z + 1, 8)
    records = (strength, direction.astype(F32), cell.astype(F32), store.astype(F32))
    for j in range(8):
        for n, record in enumerate(records):
            send_ref[j, n] = record
        face = jnp.where(upward == j, columns[0:8], columns[8:16])
        send_ref[PLACE_Z[j], 4] = jnp.where(iota((8, 128), 0) == 5, body_row, face)
    own = owner_ref[pl.ds((place_x * 4 + place_y) * 8 + place_z, 1), :]
    own_ref[...] = jnp.zeros((8, 128), F32)
    for a in range(3):
        middle = pick([own == b for b in range(8)], [centre_ref[a, b] for b in range(8)], (1, 128))
        own_ref[a : a + 1, :] = (middle - 0.5) * (extents[a] / 128.0)


def second_kernel(got_ref, xy_ref, send_ref, total_ref):
    speeds = lattice_tables()[0]
    place_x, place_y, place_z = (lax.axis_index(a) for a in ("gx", "gy", "gz"))
    total_ref[...] = jnp.zeros_like(total_ref)
    count = iota((16, 128), 0).astype(F32)
    counts = [(count + 16.0 * g).astype(BF16) for g in range(16)]
    one = jnp.ones((16, 128), BF16)
    none = jnp.zeros((16, 128), BF16)

    order = [PLACE_Z.index(n) for n in range(8)]

    def gather(peer, carry):
        strength, direction = got_ref[peer, 0], got_ref[peer, 1]
        cell, store = got_ref[peer, 2].astype(I32), got_ref[peer, 3].astype(I32)
        is_dir = [direction == float(i) for i in range(19)]
        speed = [pick(is_dir, [float(v) for v in speeds[:, a]], (8, 128)) for a in range(3)]
        place = (
            lax.shift_right_logical(cell, 12) + (place_x * 4 - 16),
            (lax.shift_right_logical(cell, 7) & 31) + (place_y * 32 - 64),
            (cell & 127) + (listed(order, peer) * 128 - 512),
        )
        arm = [(place[a].astype(F32) + 0.5 * speed[a]) * (1.0 / 128.0) for a in range(3)]
        push = [speed[a] * strength for a in range(3)]
        loads = push + cross(arm, push)
        upper = [load.astype(BF16).astype(F32) for load in loads]
        rows = upper + [load - part for load, part in zip(loads, upper)]
        owner = lax.shift_right_logical(store, 7)
        mine = (owner & 7) == place_z
        high = jnp.where(mine, lax.shift_right_logical(owner, 4), 255).astype(F32)
        low = ((lax.shift_right_logical(owner, 3) & 1) * 128) + (store & 127)
        low = low.astype(F32)
        left, right = [], []
        for s in range(8):

            def line(x, s=s):
                return jnp.broadcast_to(x[s : s + 1], (16, 128)).astype(BF16)

            at = line(high) == counts[0]
            left.append(jnp.concatenate([jnp.where(at, line(x), none) for x in rows], axis=0))
            at = line(low)
            right.append(
                jnp.concatenate([jnp.where(at == number, one, none) for number in counts], axis=0)
            )
        total_ref[...] += rows_dot(
            jnp.concatenate(left, axis=1), jnp.concatenate(right, axis=1)
        )
        return carry

    lax.fori_loop(0, 8, gather, 0, unroll=8)

    body_row = sum(got_ref[peer, 4, 5:6, :] for peer in range(8))
    for c in range(6):
        for e in range(2):
            lanes = slice(128 * e, 128 * e + 128)
            upper = total_ref[16 * c : 16 * c + 16, lanes]
            both = upper + total_ref[96 + 16 * c : 112 + 16 * c, lanes]
            for h in range(16):
                send_ref[PLACE_Y[(2 * h + e) % 4] * 8 + PLACE_X[(2 * h + e) // 4], c : c + 1, :] = both[h : h + 1]
    last = jnp.concatenate([body_row, jnp.zeros((1, 128), F32)], axis=0)
    for j in range(32):
        send_ref[j, 6:8, :] = last

    below = got_ref[listed(PLACE_Z, lax.rem(place_z + 7, 8)), 4]
    above = got_ref[listed(PLACE_Z, lax.rem(place_z + 1, 8)), 4]
    lane = iota((1, 128), 1)

    def turned(x, by):
        return pltpu.roll(x, by, 1)

    to_xp = jnp.where(lane < 32, turned(below[1:2], 32), turned(above[1:2], 64))
    to_xm = jnp.where(lane < 32, below[2:3], turned(above[2:3], 32))
    in_row = lane & 31
    to_yp = jnp.where(in_row == 0, turned(below[3:4], 97), turned(above[3:4], 98))
    to_ym = jnp.where(in_row == 0, below[4:5], turned(above[4:5], 1))
    has_xp, has_xm = place_x < 7, place_x > 0
    has_yp, has_ym = place_y < 3, place_y > 0
    for there, dx, dy, line in (
        (has_xp, 1, 0, to_xp),
        (has_xm, -1, 0, to_xm),
        (has_yp, 0, 1, to_yp),
        (has_ym, 0, -1, to_ym),
        (has_xp & has_yp, 1, 1, xy_ref[0:1, :]),
        (has_xm & has_ym, -1, -1, xy_ref[1:2, :]),
        (has_xp & has_ym, 1, -1, xy_ref[2:3, :]),
        (has_xm & has_yp, -1, 1, xy_ref[3:4, :]),
    ):

        @pl.when(there)
        def _(dx=dx, dy=dy, line=line):
            send_ref[peer_at(place_x + dx, place_y + dy), 7:8, :] = line


def arrivals(lines):
    blank = jnp.zeros((128 - len(lines), 128), F32)
    return jnp.transpose(jnp.concatenate(lines + [blank], axis=0))


def shifted(line, cx, cy):
    by = 32 * cx + cy
    return pltpu.roll(line, by % 128, 1) if by else line


def finish(block, i, column, code, value):
    cz = int(lattice_tables()[0][i, 2])
    if cz:
        block = pltpu.roll(block, 1 if cz == 1 else 127, 1)
        at = 0 if cz == 1 else 127
        block = jnp.where(iota(block.shape, 1) == at, column, block)
    if i:
        opposite = i + 1 if i % 2 else i - 1
        block = jnp.where(code == float(opposite), value, block)
    return block


def third_kernel(
    post_ref,
    bounce_ref,
    wall_ref,
    got1_ref,
    motion_hbm,
    mass_hbm,
    inertia_hbm,
    cell_hbm,
    moved_hbm,
    value_ref,
    step_ref,
    moved_ref,
    cell_ref,
    motion_ref,
    mass_ref,
    inertia_ref,
    sems,
):
    speeds = lattice_tables()[0].astype(int)
    place_z = lax.axis_index("gz")
    fetches = [
        pltpu.make_async_copy(motion_hbm, motion_ref, sems.at[19]),
        pltpu.make_async_copy(mass_hbm, mass_ref, sems.at[20]),
        pltpu.make_async_copy(inertia_hbm, inertia_ref, sems.at[21]),
    ]
    cells = pltpu.make_async_copy(cell_hbm, cell_ref, sems.at[22])
    cells.start()
    for fetch in fetches:
        fetch.start()
    cells.wait()
    cell = flat(cell_ref[...])
    spread = []
    for part in halves(wall_ref[...]):
        part = jnp.broadcast_to(flat(part.astype(F32)), (16, 1024)).astype(BF16)
        spread += groups(cell & 127, part)
    laid = rows_dot(hot(lax.shift_right_logical(cell, 7)), jnp.concatenate(spread, axis=0))
    value_ref[...] = bounce_ref[1] - (laid[:, 0:128] + laid[:, 128:256])
    below = got1_ref[listed(PLACE_Z, lax.rem(place_z + 7, 8)), 4]
    above = got1_ref[listed(PLACE_Z, lax.rem(place_z + 1, 8)), 4]
    order = ZP + ZM
    lines = []
    for dirs, face in ((ZP, below), (ZM, above)):
        for n, i in enumerate(dirs):
            lines.append(shifted(face[n : n + 1], int(speeds[i, 0]), int(speeds[i, 1])))
    columns = arrivals(lines)
    copies = []
    for i in range(19):
        cx, cy, cz = (int(v) for v in speeds[i])
        planes = {0: (0, 4), 1: (1, 4), -1: (0, 3)}[cx]
        first, last = {0: (0, 32), 1: (8, 32), -1: (0, 24)}[cy]
        for x in range(*planes):
            source = 32 * (x - cx) - cy
            block = post_ref[i, source + first : source + last, :]
            rows = slice(32 * x + first, 32 * x + last)
            column = None
            if cz:
                n = order.index(i)
                column = columns[rows, n : n + 1]
            code, value = bounce_ref[0, rows, :], value_ref[rows, :]
            moved_ref[i, x, first:last, :] = finish(block, i, column, code, value)
        part = (i, slice(*planes), slice(first, last))
        copy = pltpu.make_async_copy(moved_ref.at[part], moved_hbm.at[part], sems.at[i])
        copy.start()
        copies.append(copy)

    for fetch in fetches:
        fetch.wait()
    at_lane, at_row = iota((8, 128), 1), iota((8, 128), 0)
    scale = jnp.zeros((8, 128), F32)
    for c in range(6):
        for b in range(8):
            value = mass_ref[b] if c < 3 else inertia_ref[c - 3, b]
            scale = jnp.where((at_lane == c) & (at_row == b), value, scale)
    step_ref[0] = scale
    step_ref[1] = jnp.concatenate([motion_ref[...], jnp.zeros((8, 122), F32)], axis=1)
    for copy in copies:
        copy.wait()


def face_kernel(
    partly_hbm,
    post_ref,
    bounce_ref,
    value_ref,
    xp_ref,
    xm_ref,
    yp_ref,
    ym_ref,
    moved_hbm,
    moved_ref,
    sems,
):
    del partly_hbm
    speeds = lattice_tables()[0].astype(int)
    place_x, place_y = lax.axis_index("gx"), lax.axis_index("gy")
    has_xp, has_xm = place_x < 7, place_x > 0
    has_yp, has_ym = place_y < 3, place_y > 0
    copies = []

    def send(*part):
        copy = pltpu.make_async_copy(
            moved_ref.at[part], moved_hbm.at[part], sems.at[len(copies)]
        )
        copy.start()
        copies.append(copy)

    for i in (1, 2, 7, 8, 9, 10):
        cx, cy = (int(v) for v in speeds[i, :2])
        x = 0 if cx == 1 else 3
        first, last = {0: (0, 32), 1: (8, 32), -1: (0, 24)}[cy]
        there, face = (has_xm, xp_ref[XP.index(i)]) if cx == 1 else (has_xp, xm_ref[XM.index(i)])
        block = jnp.where(there, face[first - cy : last - cy], 0.0)
        rows = slice(32 * x + first, 32 * x + last)
        code, value = bounce_ref[0, rows, :], value_ref[rows, :]
        moved_ref[i, x, first:last, :] = finish(block, i, None, code, value)
        send(i, x, slice(first, last))
    at_row = iota((8, 128), 0)
    for i in (3, 4, 7, 8, 9, 10):
        cx, cy = (int(v) for v in speeds[i, :2])
        planes = {0: (0, 4), 1: (1, 4), -1: (0, 3)}[cx]
        first = 0 if cy == 1 else 24
        face_ref, n = (yp_ref, YP.index(i)) if cy == 1 else (ym_ref, YM.index(i))
        for x in range(*planes):
            source = x - cx
            block = post_ref[i, 32 * source + first : 32 * source + first + 8, :]
            line = face_ref[4 * n + source : 4 * n + source + 1, :]
            line = jnp.where(has_ym if cy == 1 else has_yp, line, 0.0)
            block = pltpu.roll(block, 1 if cy == 1 else 7, 0)
            block = jnp.where(at_row == (0 if cy == 1 else 7), line, block)
            rows = slice(32 * x + first, 32 * x + first + 8)
            code, value = bounce_ref[0, rows, :], value_ref[rows, :]
            moved_ref[i, x, first : first + 8, :] = finish(block, i, None, code, value)
        send(i, slice(*planes), slice(first, first + 8))
    for copy in copies:
        copy.wait()


def fourth_kernel(
    partly_hbm,
    post_ref,
    bounce_ref,
    value_ref,
    own_ref,
    got1_ref,
    got2_ref,
    xp_ref,
    xm_ref,
    yp_ref,
    ym_ref,
    step_ref,
    moved_hbm,
    load_hbm,
    next_hbm,
    row_ref,
    edge_ref,
    load_ref,
    next_ref,
    sems,
):
    del partly_hbm
    speeds = lattice_tables()[0].astype(int)
    place_x, place_y, place_z = (lax.axis_index(a) for a in ("gx", "gy", "gz"))
    has_xp, has_xm = place_x < 7, place_x > 0
    has_yp, has_ym = place_y < 3, place_y > 0
    copies = []

    def send(source, target):
        copy = pltpu.make_async_copy(source, target, sems.at[len(copies)])
        copy.start()
        copies.append(copy)

    parts = [got2_ref[j] for j in range(32)]
    while len(parts) > 1:
        parts = [a + b for a, b in zip(parts[0::2], parts[1::2])]
    total = parts[0]
    push = [total[a : a + 1] for a in range(3)]
    away = cross([own_ref[a : a + 1, :] for a in range(3)], push)
    turn = [total[3 + a : 4 + a] - away[a] for a in range(3)]
    load_ref[...] = jnp.concatenate(push + turn, axis=0)
    send(load_ref, load_hbm)
    at_lane, at_row = iota((8, 128), 1), iota((8, 128), 0)
    own = jnp.where((at_lane & 7) == at_row, total[6:7], 0.0)
    body_load = jnp.zeros((8, 128), F32)
    for c in range(6):
        here = lax.shift_right_logical(at_lane, 3) == c
        column = jnp.sum(jnp.where(here, own, 0.0), axis=1, keepdims=True)
        body_load = jnp.where(at_lane == c, column, body_load)
    next_ref[...] = (step_ref[1] + step_ref[0] * body_load / 32768.0)[:, 0:6]
    send(next_ref, next_hbm)

    def edge(there, dx, dy):
        line = got2_ref[peer_at(place_x + dx, place_y + dy), 7:8, :]
        return jnp.where(there, line, 0.0)

    lane = iota((1, 128), 1)
    row_in_plane = lane & 31
    from_x = {1: edge(has_xm, -1, 0), -1: edge(has_xp, 1, 0)}
    from_y = {1: edge(has_ym, 0, -1), -1: edge(has_yp, 0, 1)}
    from_xy = {
        (1, 1): edge(has_xm & has_ym, -1, -1),
        (-1, -1): edge(has_xp & has_yp, 1, 1),
        (1, -1): edge(has_xm & has_yp, -1, 1),
        (-1, 1): edge(has_xp & has_ym, 1, -1),
    }
    order, lines = [], []
    for dirs, face in (
        (ZP, got1_ref[listed(PLACE_Z, lax.rem(place_z + 7, 8)), 4]),
        (ZM, got1_ref[listed(PLACE_Z, lax.rem(place_z + 1, 8)), 4]),
    ):
        for n, i in enumerate(dirs):
            cx, cy, cz = (int(v) for v in speeds[i])
            if cx == 1:
                line = from_x[1] if cz == 1 else pltpu.roll(from_x[1], 96, 1)
            elif cx == -1:
                line = pltpu.roll(from_x[-1], 96 if cz == 1 else 64, 1)
            elif cy == 1:
                came = from_y[1] if cz == 1 else pltpu.roll(from_y[1], 127, 1)
                line = jnp.where(row_in_plane == 0, came, shifted(face[n : n + 1], 0, 1))
            elif cy == -1:
                came = pltpu.roll(from_y[-1], 31 if cz == 1 else 30, 1)
                line = jnp.where(row_in_plane == 31, came, shifted(face[n : n + 1], 0, -1))
            else:
                continue
            order.append(i)
            lines.append(line)
    columns = arrivals(lines)

    for i in (7, 9, 8, 10, 15, 17, 16, 18):
        cx, cy, cz = (int(v) for v in speeds[i])
        first = 0 if cy == 1 else 24
        face_ref, n = (yp_ref, YP.index(i)) if cy == 1 else (ym_ref, YM.index(i))
        planes = range(4) if cz else ((0,) if cx == 1 else (3,))
        for x in planes:
            source = x - cx
            if cz:
                block = post_ref[i, 32 * source + first : 32 * source + first + 8, :]
                line = face_ref[4 * n + source : 4 * n + source + 1, :]
                line = jnp.where(has_ym if cy == 1 else has_yp, line, 0.0)
            else:
                if source < 0:
                    block = jnp.where(has_xm, xp_ref[XP.index(i), first : first + 8, :], 0.0)
                else:
                    block = jnp.where(has_xp, xm_ref[XM.index(i), first : first + 8, :], 0.0)
                line = from_xy[cx, cy]
            block = pltpu.roll(block, 1 if cy == 1 else 7, 0)
            block = jnp.where(at_row == (0 if cy == 1 else 7), line, block)
            rows = slice(32 * x + first, 32 * x + first + 8)
            column = None
            if cz:
                m = order.index(i)
                column = columns[rows, m : m + 1]
            code, value = bounce_ref[0, rows, :], value_ref[rows, :]
            row_ref[i - 7, x] = finish(block, i, column, code, value)
        part = slice(planes[0], planes[-1] + 1)
        send(row_ref.at[i - 7, part], moved_hbm.at[i, part, first : first + 8, :])
    for number, i in enumerate((11, 13, 14, 12)):
        cx = int(speeds[i, 0])
        x = 0 if cx == 1 else 3
        if cx == 1:
            block = jnp.where(has_xm, xp_ref[XP.index(i)], 0.0)
        else:
            block = jnp.where(has_xp, xm_ref[XM.index(i)], 0.0)
        rows = slice(32 * x, 32 * x + 32)
        m = order.index(i)
        code, value = bounce_ref[0, rows, :], value_ref[rows, :]
        edge_ref[number] = finish(block, i, columns[rows, m : m + 1], code, value)
        send(edge_ref.at[number], moved_hbm.at[i, x])

    for copy in copies:
        copy.wait()


def body(
    populations,
    solid,
    link_cell,
    link_dir,
    link_store,
    store_body,
    motion,
    inv_mass,
    inv_inertia,
    centre,
    rates,
):
    vmem = pl.BlockSpec(memory_space=pltpu.VMEM)

    def array(*shape):
        return jax.ShapeDtypeStruct(shape, F32)

    params = pltpu.CompilerParams(vmem_limit_bytes=40 * 1024 * 1024)
    post, bounce, send1, xp, xm, yp, ym, xy, own, wall = pl.pallas_call(
        first_kernel,
        out_shape=(
            array(19, 128, 128),
            array(2, 128, 128),
            array(8, 5, 8, 128),
            array(5, 32, 128),
            array(5, 32, 128),
            array(24, 128),
            array(24, 128),
            array(8, 128),
            array(8, 128),
            array(8, 128),
        ),
        in_specs=[pl.BlockSpec(memory_space=pltpu.HBM)] * 9,
        out_specs=(vmem,) * 10,
        scratch_shapes=[
            pltpu.VMEM((19, 128, 128), F32),
            pltpu.VMEM((128, 128), I32),
            pltpu.VMEM((8, 128), I32),
            pltpu.VMEM((8, 128), I32),
            pltpu.VMEM((8, 128), I32),
            pltpu.VMEM((256, 128), I32),
            pltpu.SMEM((8, 6), F32),
            pltpu.SMEM((3, 8), F32),
            pltpu.SMEM((15,), F32),
            pltpu.SemaphoreType.DMA((4,)),
            pltpu.SemaphoreType.DMA((8,)),
        ],
        compiler_params=params,
        name="collide",
    )(
        *(
            pltpu.with_memory_space_constraint(x, pltpu.HBM)
            for x in (
                populations.reshape(19, 128, 128),
                solid.reshape(128, 128),
                link_cell.reshape(8, 128),
                link_dir.reshape(8, 128),
                link_store.reshape(8, 128),
                store_body.reshape(256, 128),
                motion,
                centre.T,
                rates,
            )
        )
    )

    def shift(x, axis, by):
        size = lax.axis_size(axis)
        return lax.ppermute(x, axis, [(i, (i + by) % size) for i in range(size)])

    along_z = [[PLACE_Z.index(n) for n in range(8)]]
    got1 = lax.all_to_all(send1, "gz", 0, 0, axis_index_groups=along_z, tiled=True)
    send2 = pl.pallas_call(
        second_kernel,
        out_shape=array(32, 8, 128),
        in_specs=[vmem] * 2,
        out_specs=vmem,
        scratch_shapes=[pltpu.VMEM((192, 256), F32)],
        compiler_params=params,
        cost_estimate=pl.CostEstimate(
            flops=2 * 192 * 256 * 8192, bytes_accessed=4 * 4 * 8192, transcendentals=0
        ),
        name="bins",
    )(got1, xy)
    xp, xm = shift(xp, "gx", 1), shift(xm, "gx", -1)
    yp, ym = shift(yp, "gy", 1), shift(ym, "gy", -1)
    across = [[PLACE_Y.index(n // 8) * 8 + PLACE_X.index(n % 8) for n in range(32)]]
    got2 = lax.all_to_all(send2, ("gy", "gx"), 0, 0, axis_index_groups=across, tiled=True)
    hbm = pl.BlockSpec(memory_space=pltpu.HBM)
    partly, value, step = pl.pallas_call(
        third_kernel,
        out_shape=(array(19, 4, 32, 128), array(128, 128), array(2, 8, 128)),
        in_specs=[vmem] * 4 + [hbm] * 4,
        out_specs=(hbm, vmem, vmem),
        scratch_shapes=[
            pltpu.VMEM((19, 4, 32, 128), F32),
            pltpu.VMEM((8, 128), I32),
            pltpu.VMEM((8, 6), F32),
            pltpu.SMEM((8,), F32),
            pltpu.SMEM((3, 8), F32),
            pltpu.SemaphoreType.DMA((23,)),
        ],
        compiler_params=params,
        cost_estimate=pl.CostEstimate(
            flops=19 * 16384 * 4, bytes_accessed=2 * 19 * 16384 * 4, transcendentals=0
        ),
        name="move",
    )(
        *(post, bounce, wall, got1),
        *(
            pltpu.with_memory_space_constraint(x, pltpu.HBM)
            for x in (motion, inv_mass, inv_inertia.T, link_cell.reshape(8, 128))
        ),
    )
    partly = pl.pallas_call(
        face_kernel,
        out_shape=array(19, 4, 32, 128),
        in_specs=[hbm] + [vmem] * 7,
        out_specs=hbm,
        scratch_shapes=[pltpu.VMEM((19, 4, 32, 128), F32), pltpu.SemaphoreType.DMA((12,))],
        input_output_aliases={0: 0},
        compiler_params=params,
        name="faces",
    )(partly, post, bounce, value, xp, xm, yp, ym)
    moved, own_loads, motion_next = pl.pallas_call(
        fourth_kernel,
        out_shape=(array(19, 4, 32, 128), array(6, 128), array(8, 6)),
        in_specs=[hbm] + [vmem] * 11,
        out_specs=(hbm,) * 3,
        scratch_shapes=[
            pltpu.VMEM((12, 4, 8, 128), F32),
            pltpu.VMEM((4, 32, 128), F32),
            pltpu.VMEM((6, 128), F32),
            pltpu.VMEM((8, 6), F32),
            pltpu.SemaphoreType.DMA((14,)),
        ],
        input_output_aliases={0: 0},
        compiler_params=params,
        name="close",
    )(partly, post, bounce, value, own, got1, got2, xp, xm, yp, ym, step)
    return (moved, own_loads, motion_next)


def solution(mesh):
    return jax.shard_map(
        body,
        mesh=mesh,
        in_specs=(
            P(None, "gx", "gy", "gz"),
            P("gx", "gy", "gz"),
            P("gx", "gy", "gz", None),
            P("gx", "gy", "gz", None),
            P("gx", "gy", "gz", None),
            P(),
            P(),
            P(),
            P(),
            P(),
            P(),
        ),
        out_specs=(P(None, "gx", "gy", "gz"), P(None, ("gx", "gy", "gz")), P()),
        check_vma=False,
    )
```
